32 devices in a mesh: ex: 8 (over y, x, core), mp: 4 (over z).
Axes of the slice: x: 2, y: 2, z: 4, core: 2. Of those that a mesh axis runs over, the one named last changes fastest.
Arguments:
- acts: bfloat16 [4, 1024, 4096], P('mp', 'ex'), may hold values from -6 to 6
- grads: bfloat16 [4, 1024, 1024], P('mp', 'ex'), may hold values from -12 to 12
- down_factor: bfloat16 [4, 16, 4096], P('mp'), may hold values from -0.09375 to 0.09375
- up_factor_transposed: bfloat16 [4, 16, 1024], P('mp'), may hold values from -0.1875 to 0.1875
- input_projection: bfloat16 [4, 64, 4096], P('mp'), may hold values from -0.09375 to 0.09375
- gradient_projection: bfloat16 [4, 64, 1024], P('mp'), may hold values from -0.1875 to 0.1875
- order: int32 [4, 8, 16], P('mp', 'ex'), may hold values from 0 to 15, each once within a row
- damping: float32 [1], replicated, may hold values from 0.5 to 2
Outputs:
- features: float32 [128, 1024], P(('ex', 'mp'))
- factor_r: float32 [16, 64, 64], P('mp')
The draws below stay inside these ranges and needn't reach their ends.
Inputs may be any that keep to these rules, and one draw needn't show every extreme that they name: order[b, m] lists each of the 16 examples of shard m once: stored example e of block b is example order[b, m, e] of that shard.
All inputs are finite; a program needn't handle non-finite values.
Results may differ from the reference program's by a relative error of at most 0.0003.
Values sent between devices are 32-bit elements; how exact they have to be, the bound alone decides.
No kernel may reach another device: no remote copies, remote signals or barrier semaphores. Data moves between devices by JAX's collectives and lax.ppermute only.
A program may use at most 64 MiB of HBM per device.

```python
import math
import jax
import jax.numpy as jnp
from jax import lax

MODEL_WIDTH = 4096
KEY_WIDTH = 1024
ADAPTER_RANK = 16
KP = 64
E_DEV = 16
EXAMPLE_LENGTH = 8
LAYER_BLOCKS = 4
SHARDS = 8
TOKENS = 1024
EXAMPLES = 128


def draw_grads(key, part):
    key_base, key_scale = jax.random.split(key, 2)
    stored = TOKENS // EXAMPLE_LENGTH
    logs = jax.random.uniform(key_scale, (LAYER_BLOCKS, stored, 1), jnp.float32, math.log(0.3), math.log(3.0))
    scaling = jnp.repeat(jnp.exp(logs), EXAMPLE_LENGTH, axis=1)
    base = jax.random.normal(key_base, (LAYER_BLOCKS, TOKENS, KEY_WIDTH), jnp.float32)
    return jnp.clip(base * scaling, -12.0, 12.0).astype(jnp.bfloat16)


def levels(stream_key, shape, shards, low, top_value):
    loudness, own = 1.0, jax.random.fold_in(stream_key, 6)
    for axis_at, parts in shards:
        heights = jnp.exp(jax.random.uniform(jax.random.fold_in(own, axis_at), (parts,), jnp.float32, low / len(shards), top_value / len(shards)))
        loudness = loudness * jnp.repeat(heights, shape[axis_at] // parts).reshape([-1 if axis == axis_at else 1 for axis in range(len(shape))])
    return loudness


def gaussian(key, extent, width, limit, pieces=(), held_as=jnp.bfloat16):
    gain = levels(key, extent, pieces, -0.22, 0.18) if pieces else 1.0
    array = jax.random.normal(key, extent, jnp.float32) * width * gain
    return jnp.minimum(jnp.maximum(array, -limit), limit).astype(held_as)


def setup_inputs(seed: int = 0) -> dict:
    streams_of = jax.random.split(jax.random.key(seed), 9)
    acts = gaussian(streams_of[0], (LAYER_BLOCKS, TOKENS, MODEL_WIDTH), 1.0, 6.0, ((0, 4), (1, 8)))
    grads = draw_grads(jax.random.fold_in(streams_of[8], 71), 0)
    down_factor = gaussian(streams_of[2], (LAYER_BLOCKS, ADAPTER_RANK, MODEL_WIDTH), MODEL_WIDTH ** -0.5, 0.09375, ((0, 4),))
    up_factor_transposed = gaussian(streams_of[3], (LAYER_BLOCKS, ADAPTER_RANK, KEY_WIDTH), KEY_WIDTH ** -0.5, 0.1875, ((0, 4),))
    input_projection = gaussian(streams_of[4], (LAYER_BLOCKS, KP, MODEL_WIDTH), MODEL_WIDTH ** -0.5, 0.09375, ((0, 4),))
    gradient_projection = gaussian(streams_of[5], (LAYER_BLOCKS, KP, KEY_WIDTH), KEY_WIDTH ** -0.5, 0.1875, ((0, 4),))
    order = jax.vmap(lambda own: jax.random.permutation(own, E_DEV))(jax.random.split(streams_of[6], LAYER_BLOCKS * SHARDS)).reshape((LAYER_BLOCKS, SHARDS, E_DEV)).astype(jnp.int32)
    damping = jnp.clip(jnp.exp(jax.random.uniform(streams_of[7], (1,), jnp.float32, math.log(0.5), math.log(2.0))), 0.5, 2.0)
    return dict(acts=acts, grads=grads, down_factor=down_factor, up_factor_transposed=up_factor_transposed, input_projection=input_projection, gradient_projection=gradient_projection, order=order, damping=damping)


def block_partial(input_rows, output_gradients, weight_a, weight_b, sketch_a, sketch_g):
    reduced_gradient = jnp.dot(output_gradients.astype(jnp.float32), weight_b.T.astype(jnp.float32), preferred_element_type=jnp.float32)
    reduced_input = jnp.dot(input_rows.astype(jnp.float32), weight_a.T.astype(jnp.float32), preferred_element_type=jnp.float32)
    sketch_in = jnp.dot(input_rows.astype(jnp.float32), sketch_a.T.astype(jnp.float32), preferred_element_type=jnp.float32)
    sketch_out = jnp.dot(output_gradients.astype(jnp.float32), sketch_g.T.astype(jnp.float32), preferred_element_type=jnp.float32)
    reduced_gradient = reduced_gradient.reshape(EXAMPLES, EXAMPLE_LENGTH, ADAPTER_RANK)
    reduced_input = reduced_input.reshape(EXAMPLES, EXAMPLE_LENGTH, ADAPTER_RANK)
    sketch_in = sketch_in.reshape(EXAMPLES, EXAMPLE_LENGTH, KP)
    sketch_out = sketch_out.reshape(EXAMPLES, EXAMPLE_LENGTH, KP)
    first = jnp.einsum('etc,etk->eck', reduced_gradient, sketch_in, precision=lax.Precision.HIGHEST)
    second = jnp.einsum('etc,etk->eck', reduced_input, sketch_out, precision=lax.Precision.HIGHEST)
    return (first + second).reshape(EXAMPLES, ADAPTER_RANK * KP)

def reference(acts, grads, down_factor, up_factor_transposed, input_projection, gradient_projection, order, damping):
    feature_width = ADAPTER_RANK * KP
    scaling = 1.0 / math.sqrt(2.0 * EXAMPLE_LENGTH * LAYER_BLOCKS)
    offsets = (jnp.arange(SHARDS, dtype=jnp.int32) * E_DEV)[:, None]

    def single_block(carry, items):
        input_rows, output_gradients, weight_a, weight_b, sketch_a, sketch_g, ordering = items
        partial_value = block_partial(input_rows, output_gradients, weight_a, weight_b, sketch_a, sketch_g) * scaling
        target = (offsets + ordering.astype(jnp.int32)).reshape(-1).astype(jnp.int32)
        placed = jnp.zeros((EXAMPLES, feature_width), jnp.float32).at[target].set(partial_value)
        return (carry + placed, None)
    start_offset = jnp.zeros((EXAMPLES, feature_width), jnp.float32)
    features, unused_value = lax.scan(single_block, start_offset, (acts, grads, down_factor, up_factor_transposed, input_projection, gradient_projection, order))
    grouped = features.reshape(EXAMPLES, ADAPTER_RANK, KP)
    gram_blocks = jnp.einsum('eck,ecl->ckl', grouped, grouped, precision=lax.Precision.HIGHEST)
    system = gram_blocks / EXAMPLES + damping[0] * jnp.eye(KP, dtype=jnp.float32)[None, :, :]
    factor_r = jnp.swapaxes(jnp.linalg.cholesky(system), 1, 2)
    return (features, factor_r)
```

```python
import functools
import math

import jax
import jax.numpy as jnp
from jax import lax
from jax.experimental import pallas as pl
from jax.experimental.pallas import tpu as pltpu
from jax.sharding import PartitionSpec as P

EXAMPLE_LENGTH = 8
LANES = 128
SLOT = 32
GROUP = LANES // SLOT
PANEL = 8


def dot_nt(a, b):
    return lax.dot_general(
        a, b, (((1,), (1,)), ((), ())), preferred_element_type=jnp.float32
    )


def dot_tn(a, b):
    return lax.dot_general(
        a, b, (((0,), (0,)), ((), ())), preferred_element_type=jnp.float32
    )


def split(x):
    high = x.astype(jnp.bfloat16)
    return high, (x - high.astype(jnp.float32)).astype(jnp.bfloat16)


def partial_kernel(
    parts, scaling, acts, grads, down, up, proj_in, proj_out, order, send, low, out
):
    tokens = acts.shape[1]
    rank = down.shape[1]
    sketch = proj_in.shape[1]
    examples = tokens // EXAMPLE_LENGTH
    per = rank // parts
    halves = sketch // SLOT
    from_acts = dot_nt(jnp.concatenate([proj_in[0], down[0]], axis=0), acts[0])
    from_grads = dot_nt(jnp.concatenate([proj_out[0], up[0]], axis=0), grads[0])
    sketches = jnp.concatenate([from_acts[:sketch], from_grads[:sketch]], axis=1)
    low[0] = from_grads[sketch:] * scaling
    low[1] = from_acts[sketch:] * scaling

    rows = examples * parts
    lane = lax.broadcasted_iota(jnp.int32, (rows, 2 * tokens), 1)
    source = (lane % tokens) // EXAMPLE_LENGTH
    target = jnp.zeros((8, 2 * tokens), jnp.int32)
    for s in range(examples):
        target = jnp.where(source[:8] == s, order[0, 0, s], target)
    target = jnp.concatenate([target] * (rows // 8), axis=0)
    place = lax.broadcasted_iota(jnp.int32, (rows, 2 * tokens), 0) // parts
    mine = target == place
    highs, lows = [], []
    for c in range(per):
        chosen = jnp.concatenate(
            [low[i, pl.ds(c, parts, stride=per), :] for i in range(2)], axis=1
        )
        chosen = jnp.concatenate([chosen] * examples, axis=0)
        high, rest = split(jnp.where(mine, chosen, 0.0))
        highs.append(high)
        lows.append(rest)
    left_high = jnp.concatenate(highs, axis=0)
    left_low = jnp.concatenate(lows, axis=0)
    right = jnp.concatenate(
        [sketches[h * SLOT : (h + 1) * SLOT] for h in range(halves) for _ in range(per)],
        axis=0,
    )
    right_high, right_low = split(right)
    spread = (
        dot_nt(left_high, right_low) + dot_nt(left_low, right_high)
    ) + dot_nt(left_high, right_high)
    column = lax.broadcasted_iota(jnp.int32, (rows, per * sketch), 1)
    channel = (column // SLOT) % per
    total = spread[:rows]
    for c in range(1, per):
        total = jnp.where(channel == c, spread[c * rows : (c + 1) * rows], total)
    for start in range(0, per * sketch, LANES):
        stop = min(start + LANES, per * sketch)
        out[:, : stop - start] = total[:, start:stop]
        for g in range(parts):
            send[g, :examples, start:stop] = out[
                g * examples : (g + 1) * examples, : stop - start
            ]
            send[g, examples:, start:stop] = out[pl.ds(g, examples, stride=parts), :][
                :, : stop - start
            ]


def column_kernel(recv, columns):
    examples = columns.shape[1]
    total = jnp.sum(recv[:, examples:, :], axis=0)
    width = total.shape[1]
    for m in range(columns.shape[0]):
        columns[m, :, :width] = total
        if columns.shape[2] > width:
            columns[m, :, width:] = jnp.zeros(
                (examples, columns.shape[2] - width), jnp.float32
            )


def feature_kernel(parts, per, recv, features):
    rows_here, width = features.shape
    examples = rows_here * parts
    total = jnp.sum(recv[:, :examples, :], axis=0)
    span = width // parts
    halves = span // (per * SLOT)
    natural = jnp.concatenate(
        [
            total[:, (h * per + c) * SLOT : (h * per + c + 1) * SLOT]
            for c in range(per)
            for h in range(halves)
        ],
        axis=1,
    )
    for r in range(rows_here):
        features[r : r + 1, :] = jnp.concatenate(
            [natural[r * parts + g : r * parts + g + 1, :] for g in range(parts)], axis=1
        )


def pick_lanes(x, index):
    return jnp.take_along_axis(x, index, axis=1)


def reciprocal(x):
    guess = pl.reciprocal(x, approx=True)
    guess = guess * (2.0 - x * guess)
    return guess * (2.0 - x * guess)


def factor_kernel(rows, damping, factors):
    channels, sketch, _ = factors.shape
    halves = sketch // SLOT
    panels = sketch // PANEL
    per_half = SLOT // PANEL
    stacked = jnp.concatenate([rows[m] for m in range(rows.shape[0])], axis=0)
    examples = stacked.shape[0]
    high, rest = split(stacked)
    gram = (dot_tn(high, rest) + dot_tn(rest, high)) + dot_tn(high, high)
    lane = lax.broadcasted_iota(jnp.int32, (PANEL, LANES), 1)
    sub = lax.broadcasted_iota(jnp.int32, (PANEL, LANES), 0)
    slot = lane // SLOT
    within = lane % SLOT
    ridge = damping[0]
    tile = []
    for q in range(panels):
        hr, at = divmod(q, per_half)
        line = []
        for h in range(halves):
            value = None
            for c in range(GROUP):
                start = hr * LANES + c * SLOT + at * PANEL
                block = gram[start : start + PANEL, h * LANES : (h + 1) * LANES]
                value = block if c == 0 else jnp.where(slot == c, block, value)
            value = value * (1.0 / examples)
            if h == hr:
                value = value + jnp.where(within == at * PANEL + sub, ridge, 0.0)
            line.append(value)
        tile.append(line)

    zero = jnp.zeros((PANEL, LANES), jnp.float32)
    finished = []
    for q in range(panels):
        hq, at = divmod(q, per_half)
        column = [
            {
                j: pick_lanes(tile[j][hq], slot * SLOT + at * PANEL + r)
                for j in range(q, panels)
            }
            for r in range(PANEL)
        ]
        block = [
            [
                jnp.broadcast_to(column[r][q][s : s + 1, :], (PANEL, LANES))
                if s >= r
                else None
                for s in range(PANEL)
            ]
            for r in range(PANEL)
        ]
        line = [
            [
                jnp.broadcast_to(tile[q][h][r : r + 1, :], (PANEL, LANES))
                if h >= hq
                else None
                for h in range(halves)
            ]
            for r in range(PANEL)
        ]
        inverse = []
        for r in range(PANEL):
            inv = reciprocal(block[r][r])
            inverse.append(inv)
            for s in range(r + 1, PANEL):
                ratio = block[r][s] * inv
                for t in range(s, PANEL):
                    block[s][t] = block[s][t] - ratio * block[r][t]
                for j in range(q + 1, panels):
                    column[s][j] = column[s][j] - ratio * column[r][j]
                for h in range(hq, halves):
                    line[s][h] = line[s][h] - ratio * line[r][h]
        result = []
        for h in range(halves):
            if h < hq:
                result.append(zero)
                continue
            value = zero
            for r in range(PANEL):
                value = jnp.where(sub == r, line[r][h] * lax.rsqrt(block[r][r]), value)
            if h == hq:
                value = jnp.where(within >= at * PANEL + sub, value, 0.0)
            result.append(value)
        finished.append(result)
        for j in range(q + 1, panels):
            weights = [column[r][j] * inverse[r] for r in range(PANEL)]
            for h in range((q + 1) // per_half, halves):
                value = tile[j][h]
                for r in range(PANEL):
                    value = value - weights[r] * line[r][h]
                tile[j][h] = value

    for q in range(panels):
        for c in range(channels):
            factors[c, q * PANEL : (q + 1) * PANEL, :] = jnp.concatenate(
                [finished[q][h][:, c * SLOT : (c + 1) * SLOT] for h in range(halves)],
                axis=1,
            )


def vmem():
    return pl.BlockSpec(memory_space=pltpu.VMEM)


def smem():
    return pl.BlockSpec(memory_space=pltpu.SMEM)


def local(
    acts,
    grads,
    down_factor,
    up_factor_transposed,
    input_projection,
    gradient_projection,
    order,
    damping,
):
    parts = lax.axis_size("mp")
    shards = lax.axis_size("ex")
    tokens = acts.shape[1]
    rank = down_factor.shape[1]
    sketch = input_projection.shape[1]
    examples = tokens // EXAMPLE_LENGTH
    per = rank // parts
    span = per * sketch
    scaling = 1.0 / math.sqrt(2.0 * EXAMPLE_LENGTH * parts)
    send = pl.pallas_call(
        functools.partial(partial_kernel, parts, scaling),
        out_shape=jax.ShapeDtypeStruct((parts, 2 * examples, span), jnp.float32),
        in_specs=[vmem()] * 6 + [smem()],
        out_specs=vmem(),
        scratch_shapes=[
            pltpu.VMEM((2, rank, tokens), jnp.float32),
            pltpu.VMEM((examples * parts, LANES), jnp.float32),
        ],
        compiler_params=pltpu.CompilerParams(vmem_limit_bytes=32 * 2**20),
        name="partials",
    )(
        acts,
        grads,
        down_factor,
        up_factor_transposed,
        input_projection,
        gradient_projection,
        order,
    )
    recv = lax.all_to_all(send, "mp", split_axis=0, concat_axis=0, tiled=True)
    padded = max(span, GROUP * sketch)
    columns = pl.pallas_call(
        column_kernel,
        out_shape=jax.ShapeDtypeStruct((shards, examples, padded), jnp.float32),
        in_specs=[vmem()],
        out_specs=vmem(),
        name="columns",
    )(recv)
    rows = lax.all_to_all(columns, "ex", split_axis=0, concat_axis=0, tiled=True)
    features = pl.pallas_call(
        functools.partial(feature_kernel, parts, per),
        out_shape=jax.ShapeDtypeStruct((examples // parts, rank * sketch), jnp.float32),
        in_specs=[vmem()],
        out_specs=vmem(),
        name="features",
    )(recv)
    factors = pl.pallas_call(
        factor_kernel,
        out_shape=jax.ShapeDtypeStruct((per, sketch, sketch), jnp.float32),
        in_specs=[vmem(), smem()],
        out_specs=vmem(),
        compiler_params=pltpu.CompilerParams(vmem_limit_bytes=32 * 2**20),
        name="factors",
    )(rows, damping)
    return features, factors


def solution(mesh):
    in_specs = (
        P("mp", "ex", None),
        P("mp", "ex", None),
        P("mp", None, None),
        P("mp", None, None),
        P("mp", None, None),
        P("mp", None, None),
        P("mp", "ex", None),
        P(),
    )
    out_specs = (P(("ex", "mp"), None), P("mp", None, None))
    return jax.shard_map(
        local, mesh=mesh, in_specs=in_specs, out_specs=out_specs, check_vma=False
    )
```

```python
import functools
import math

import jax
import jax.numpy as jnp
from jax import lax
from jax.experimental import pallas as pl
from jax.experimental.pallas import tpu as pltpu
from jax.sharding import PartitionSpec as P

EXAMPLE_LENGTH = 8
LANES = 128
SLOT = 32
GROUP = LANES // SLOT
PANEL = 8
CHUNK = 1024


def dot_nt(a, b):
    return lax.dot_general(
        a, b, (((1,), (1,)), ((), ())), preferred_element_type=jnp.float32
    )


def dot_tn(a, b):
    return lax.dot_general(
        a, b, (((0,), (0,)), ((), ())), preferred_element_type=jnp.float32
    )


def split(x):
    high = x.astype(jnp.bfloat16)
    return high, (x - high.astype(jnp.float32)).astype(jnp.bfloat16)


def partial_kernel(
    parts,
    scaling,
    acts_hbm,
    grads_hbm,
    down_hbm,
    up_hbm,
    proj_in_hbm,
    proj_out_hbm,
    order_hbm,
    send,
    acts,
    grads,
    weights_in,
    weights_out,
    order,
    low,
    out,
    sems,
    order_sem,
):
    tokens, width = acts.shape
    rank = down_hbm.shape[1]
    sketch = proj_in_hbm.shape[1]
    examples = tokens // EXAMPLE_LENGTH
    per = rank // parts
    halves = sketch // SLOT

    def copies(source, target, sem, start, size):
        return pltpu.make_async_copy(
            source.at[0, :, pl.ds(start, size)],
            target.at[:, pl.ds(start, size)],
            sem,
        )

    order_copy = pltpu.make_async_copy(order_hbm.at[0], order, order_sem)
    stages = []
    for start in range(0, width, CHUNK):
        stages.append(
            [
                (acts_hbm, acts, start),
                (proj_in_hbm, weights_in.at[pl.ds(0, sketch)], start),
                (down_hbm, weights_in.at[pl.ds(sketch, rank)], start),
            ]
        )
    for start in range(0, grads.shape[1], CHUNK):
        stages.append(
            [
                (grads_hbm, grads, start),
                (proj_out_hbm, weights_out.at[pl.ds(0, sketch)], start),
                (up_hbm, weights_out.at[pl.ds(sketch, rank)], start),
            ]
        )
    pending = [
        [
            copies(source, target, sems.at[n, i], start, CHUNK)
            for i, (source, target, start) in enumerate(stage)
        ]
        for n, stage in enumerate(stages)
    ]
    for stage in pending:
        for copy in stage:
            copy.start()
    order_copy.start()

    def product(first, rows, weights):
        total = None
        for n in range(rows.shape[1] // CHUNK):
            for copy in pending[first + n]:
                copy.wait()
            here = pl.ds(n * CHUNK, CHUNK)
            term = dot_nt(weights[:, here], rows[:, here])
            total = term if total is None else total + term
        return total

    from_acts = product(0, acts, weights_in)
    from_grads = product(width // CHUNK, grads, weights_out)
    order_copy.wait()
    sketches = jnp.concatenate([from_acts[:sketch], from_grads[:sketch]], axis=1)
    low[0] = from_grads[sketch:] * scaling
    low[1] = from_acts[sketch:] * scaling

    rows = examples * parts
    lane = lax.broadcasted_iota(jnp.int32, (rows, 2 * tokens), 1)
    source = (lane % tokens) // EXAMPLE_LENGTH
    target = jnp.zeros((8, 2 * tokens), jnp.int32)
    for s in range(examples):
        target = jnp.where(source[:8] == s, order[0, s], target)
    target = jnp.concatenate([target] * (rows // 8), axis=0)
    place = lax.broadcasted_iota(jnp.int32, (rows, 2 * tokens), 0) // parts
    mine = target == place
    highs, lows = [], []
    for c in range(per):
        chosen = jnp.concatenate(
            [low[i, pl.ds(c, parts, stride=per), :] for i in range(2)], axis=1
        )
        chosen = jnp.concatenate([chosen] * examples, axis=0)
        high, rest = split(jnp.where(mine, chosen, 0.0))
        highs.append(high)
        lows.append(rest)
    left_high = jnp.concatenate(highs, axis=0)
    left_low = jnp.concatenate(lows, axis=0)
    right = jnp.concatenate(
        [sketches[h * SLOT : (h + 1) * SLOT] for h in range(halves) for _ in range(per)],
        axis=0,
    )
    right_high, right_low = split(right)
    spread = (
        dot_nt(left_high, right_low) + dot_nt(left_low, right_high)
    ) + dot_nt(left_high, right_high)
    column = lax.broadcasted_iota(jnp.int32, (rows, per * sketch), 1)
    channel = (column // SLOT) % per
    total = spread[:rows]
    for c in range(1, per):
        total = jnp.where(channel == c, spread[c * rows : (c + 1) * rows], total)
    for start in range(0, per * sketch, LANES):
        stop = min(start + LANES, per * sketch)
        out[:, : stop - start] = total[:, start:stop]
        for g in range(parts):
            send[g, :examples, start:stop] = out[
                g * examples : (g + 1) * examples, : stop - start
            ]
            send[g, examples:, start:stop] = out[pl.ds(g, examples, stride=parts), :][
                :, : stop - start
            ]


def column_kernel(recv, columns):
    examples = columns.shape[1]
    total = jnp.sum(recv[:, examples:, :], axis=0)
    width = total.shape[1]
    for m in range(columns.shape[0]):
        columns[m, :, :width] = total
        if columns.shape[2] > width:
            columns[m, :, width:] = jnp.zeros(
                (examples, columns.shape[2] - width), jnp.float32
            )


def feature_kernel(parts, per, recv, features):
    rows_here, width = features.shape
    examples = rows_here * parts
    total = jnp.sum(recv[:, :examples, :], axis=0)
    span = width // parts
    halves = span // (per * SLOT)
    natural = jnp.concatenate(
        [
            total[:, (h * per + c) * SLOT : (h * per + c + 1) * SLOT]
            for c in range(per)
            for h in range(halves)
        ],
        axis=1,
    )
    for r in range(rows_here):
        features[r : r + 1, :] = jnp.concatenate(
            [natural[r * parts + g : r * parts + g + 1, :] for g in range(parts)], axis=1
        )


def pick_lanes(x, index):
    return jnp.take_along_axis(x, index, axis=1)


def reciprocal(x):
    guess = pl.reciprocal(x, approx=True)
    guess = guess * (2.0 - x * guess)
    return guess * (2.0 - x * guess)


def factor_kernel(rows, damping, factors):
    channels, sketch, _ = factors.shape
    halves = sketch // SLOT
    panels = sketch // PANEL
    per_half = SLOT // PANEL
    stacked = jnp.concatenate([rows[m] for m in range(rows.shape[0])], axis=0)
    examples = stacked.shape[0]
    high, rest = split(stacked)
    gram = (dot_tn(high, rest) + dot_tn(rest, high)) + dot_tn(high, high)
    lane = lax.broadcasted_iota(jnp.int32, (PANEL, LANES), 1)
    sub = lax.broadcasted_iota(jnp.int32, (PANEL, LANES), 0)
    slot = lane // SLOT
    within = lane % SLOT
    ridge = damping[0]
    tile = []
    for q in range(panels):
        hr, at = divmod(q, per_half)
        line = []
        for h in range(halves):
            value = None
            for c in range(GROUP):
                start = hr * LANES + c * SLOT + at * PANEL
                block = gram[start : start + PANEL, h * LANES : (h + 1) * LANES]
                value = block if c == 0 else jnp.where(slot == c, block, value)
            value = value * (1.0 / examples)
            if h == hr:
                value = value + jnp.where(within == at * PANEL + sub, ridge, 0.0)
            line.append(value)
        tile.append(line)

    zero = jnp.zeros((PANEL, LANES), jnp.float32)
    finished = []
    for q in range(panels):
        hq, at = divmod(q, per_half)
        column = [
            {
                j: pick_lanes(tile[j][hq], slot * SLOT + at * PANEL + r)
                for j in range(q, panels)
            }
            for r in range(PANEL)
        ]
        block = [
            [
                jnp.broadcast_to(column[r][q][s : s + 1, :], (PANEL, LANES))
                if s >= r
                else None
                for s in range(PANEL)
            ]
            for r in range(PANEL)
        ]
        line = [
            [
                jnp.broadcast_to(tile[q][h][r : r + 1, :], (PANEL, LANES))
                if h >= hq
                else None
                for h in range(halves)
            ]
            for r in range(PANEL)
        ]
        inverse = []
        for r in range(PANEL):
            inv = reciprocal(block[r][r])
            inverse.append(inv)
            for s in range(r + 1, PANEL):
                ratio = block[r][s] * inv
                for t in range(s, PANEL):
                    block[s][t] = block[s][t] - ratio * block[r][t]
                for j in range(q + 1, panels):
                    column[s][j] = column[s][j] - ratio * column[r][j]
                for h in range(hq, halves):
                    line[s][h] = line[s][h] - ratio * line[r][h]
        result = []
        for h in range(halves):
            if h < hq:
                result.append(zero)
                continue
            value = zero
            for r in range(PANEL):
                value = jnp.where(sub == r, line[r][h] * lax.rsqrt(block[r][r]), value)
            if h == hq:
                value = jnp.where(within >= at * PANEL + sub, value, 0.0)
            result.append(value)
        finished.append(result)
        for j in range(q + 1, panels):
            weights = [column[r][j] * inverse[r] for r in range(PANEL)]
            for h in range((q + 1) // per_half, halves):
                value = tile[j][h]
                for r in range(PANEL):
                    value = value - weights[r] * line[r][h]
                tile[j][h] = value

    for q in range(panels):
        for c in range(channels):
            factors[c, q * PANEL : (q + 1) * PANEL, :] = jnp.concatenate(
                [finished[q][h][:, c * SLOT : (c + 1) * SLOT] for h in range(halves)],
                axis=1,
            )


def vmem():
    return pl.BlockSpec(memory_space=pltpu.VMEM)


def hbm():
    return pl.BlockSpec(memory_space=pltpu.HBM)


def smem():
    return pl.BlockSpec(memory_space=pltpu.SMEM)


def local(
    acts,
    grads,
    down_factor,
    up_factor_transposed,
    input_projection,
    gradient_projection,
    order,
    damping,
):
    parts = lax.axis_size("mp")
    shards = lax.axis_size("ex")
    tokens, width = acts.shape[1:]
    key_width = grads.shape[2]
    rank = down_factor.shape[1]
    sketch = input_projection.shape[1]
    examples = tokens // EXAMPLE_LENGTH
    per = rank // parts
    span = per * sketch
    scaling = 1.0 / math.sqrt(2.0 * EXAMPLE_LENGTH * parts)
    send = pl.pallas_call(
        functools.partial(partial_kernel, parts, scaling),
        out_shape=jax.ShapeDtypeStruct((parts, 2 * examples, span), jnp.float32),
        in_specs=[hbm()] * 7,
        out_specs=vmem(),
        scratch_shapes=[
            pltpu.VMEM((tokens, width), acts.dtype),
            pltpu.VMEM((tokens, key_width), grads.dtype),
            pltpu.VMEM((sketch + rank, width), acts.dtype),
            pltpu.VMEM((sketch + rank, key_width), grads.dtype),
            pltpu.SMEM(order.shape[1:], order.dtype),
            pltpu.VMEM((2, rank, tokens), jnp.float32),
            pltpu.VMEM((examples * parts, LANES), jnp.float32),
            pltpu.SemaphoreType.DMA(((width + key_width) // CHUNK, 3)),
            pltpu.SemaphoreType.DMA,
        ],
        compiler_params=pltpu.CompilerParams(vmem_limit_bytes=62000000),
        name="partials",
    )(
        acts,
        grads,
        down_factor,
        up_factor_transposed,
        input_projection,
        gradient_projection,
        order,
    )
    recv = lax.all_to_all(send, "mp", split_axis=0, concat_axis=0, tiled=True)
    padded = max(span, GROUP * sketch)
    columns = pl.pallas_call(
        column_kernel,
        out_shape=jax.ShapeDtypeStruct((shards, examples, padded), jnp.float32),
        in_specs=[vmem()],
        out_specs=vmem(),
        name="columns",
    )(recv)
    rows = lax.all_to_all(columns, "ex", split_axis=0, concat_axis=0, tiled=True)
    features = pl.pallas_call(
        functools.partial(feature_kernel, parts, per),
        out_shape=jax.ShapeDtypeStruct((examples // parts, rank * sketch), jnp.float32),
        in_specs=[vmem()],
        out_specs=vmem(),
        name="features",
    )(recv)
    factors = pl.pallas_call(
        factor_kernel,
        out_shape=jax.ShapeDtypeStruct((per, sketch, sketch), jnp.float32),
        in_specs=[vmem(), smem()],
        out_specs=vmem(),
        compiler_params=pltpu.CompilerParams(vmem_limit_bytes=32 * 2**20),
        name="factors",
    )(rows, damping)
    return features, factors


def solution(mesh):
    in_specs = (
        P("mp", "ex", None),
        P("mp", "ex", None),
        P("mp", None, None),
        P("mp", None, None),
        P("mp", None, None),
        P("mp", None, None),
        P("mp", "ex", None),
        P(),
    )
    out_specs = (P(("ex", "mp"), None), P("mp", None, None))
    return jax.shard_map(
        local, mesh=mesh, in_specs=in_specs, out_specs=out_specs, check_vma=False
    )
```

```python
import functools
import math

import jax
import jax.numpy as jnp
from jax import lax
from jax.experimental import pallas as pl
from jax.experimental.pallas import tpu as pltpu
from jax.sharding import PartitionSpec as P

EXAMPLE_LENGTH = 8
LANES = 128
SLOT = 32
GROUP = LANES // SLOT
PANEL = 8
CHUNK = 1024


def dot_nt(a, b):
    return lax.dot_general(
        a, b, (((1,), (1,)), ((), ())), preferred_element_type=jnp.float32
    )


def dot_tn(a, b):
    return lax.dot_general(
        a, b, (((0,), (0,)), ((), ())), preferred_element_type=jnp.float32
    )


def split(x):
    high = x.astype(jnp.bfloat16)
    return high, (x - high.astype(jnp.float32)).astype(jnp.bfloat16)


def partial_kernel(
    parts,
    scaling,
    acts_hbm,
    grads_hbm,
    down_hbm,
    up_hbm,
    proj_in_hbm,
    proj_out_hbm,
    order_hbm,
    *refs,
):
    sends, refs = refs[:parts], refs[parts:]
    acts, grads, weights_in, weights_out, order, low, out, sems, order_sem = refs
    tokens, width = acts.shape
    rank = down_hbm.shape[1]
    sketch = proj_in_hbm.shape[1]
    examples = tokens // EXAMPLE_LENGTH
    per = rank // parts
    halves = sketch // SLOT

    def copies(source, target, sem, start, size):
        return pltpu.make_async_copy(
            source.at[0, :, pl.ds(start, size)],
            target.at[:, pl.ds(start, size)],
            sem,
        )

    order_copy = pltpu.make_async_copy(order_hbm.at[0], order, order_sem)
    stages = []
    for start in range(0, width, CHUNK):
        stages.append(
            [
                (acts_hbm, acts, start),
                (proj_in_hbm, weights_in.at[pl.ds(0, sketch)], start),
                (down_hbm, weights_in.at[pl.ds(sketch, rank)], start),
            ]
        )
    for start in range(0, grads.shape[1], CHUNK):
        stages.append(
            [
                (grads_hbm, grads, start),
                (proj_out_hbm, weights_out.at[pl.ds(0, sketch)], start),
                (up_hbm, weights_out.at[pl.ds(sketch, rank)], start),
            ]
        )
    pending = [
        [
            copies(source, target, sems.at[n, i], start, CHUNK)
            for i, (source, target, start) in enumerate(stage)
        ]
        for n, stage in enumerate(stages)
    ]
    for stage in pending:
        for copy in stage:
            copy.start()
    order_copy.start()

    def product(first, rows, weights):
        total = None
        for n in range(rows.shape[1] // CHUNK):
            for copy in pending[first + n]:
                copy.wait()
            here = pl.ds(n * CHUNK, CHUNK)
            term = dot_nt(weights[:, here], rows[:, here])
            total = term if total is None else total + term
        return total

    from_acts = product(0, acts, weights_in)
    from_grads = product(width // CHUNK, grads, weights_out)
    order_copy.wait()
    sketches = jnp.concatenate([from_acts[:sketch], from_grads[:sketch]], axis=1)
    low[0] = from_grads[sketch:] * scaling
    low[1] = from_acts[sketch:] * scaling

    rows = examples * parts
    lane = lax.broadcasted_iota(jnp.int32, (rows, 2 * tokens), 1)
    source = (lane % tokens) // EXAMPLE_LENGTH
    target = jnp.zeros((8, 2 * tokens), jnp.int32)
    for s in range(examples):
        target = jnp.where(source[:8] == s, order[0, s], target)
    target = jnp.concatenate([target] * (rows // 8), axis=0)
    place = lax.broadcasted_iota(jnp.int32, (rows, 2 * tokens), 0) // parts
    mine = target == place
    highs, lows = [], []
    for c in range(per):
        chosen = jnp.concatenate(
            [low[i, pl.ds(c, parts, stride=per), :] for i in range(2)], axis=1
        )
        chosen = jnp.concatenate([chosen] * examples, axis=0)
        high, rest = split(jnp.where(mine, chosen, 0.0))
        highs.append(high)
        lows.append(rest)
    left_high = jnp.concatenate(highs, axis=0)
    left_low = jnp.concatenate(lows, axis=0)
    right = jnp.concatenate(
        [sketches[h * SLOT : (h + 1) * SLOT] for h in range(halves) for _ in range(per)],
        axis=0,
    )
    right_high, right_low = split(right)
    spread = (
        dot_nt(left_high, right_low) + dot_nt(left_low, right_high)
    ) + dot_nt(left_high, right_high)
    column = lax.broadcasted_iota(jnp.int32, (rows, per * sketch), 1)
    channel = (column // SLOT) % per
    total = spread[:rows]
    for c in range(1, per):
        total = jnp.where(channel == c, spread[c * rows : (c + 1) * rows], total)
    me = lax.axis_index("mp")
    for start in range(0, per * sketch, LANES):
        stop = min(start + LANES, per * sketch)
        out[:, : stop - start] = total[:, start:stop]
        for d in range(parts):
            g = lax.rem(me + d, parts)
            sends[d][:examples, start:stop] = out[
                pl.ds(pl.multiple_of(g * examples, examples), examples), : stop - start
            ]
            sends[d][examples:, start:stop] = out[pl.ds(g, examples, stride=parts), :][
                :, : stop - start
            ]


def column_kernel(*refs):
    chunks, columns = refs[:-1], refs[-1]
    examples, padded = columns.shape
    total = chunks[0][examples:, :]
    for chunk in chunks[1:]:
        total = total + chunk[examples:, :]
    width = total.shape[1]
    columns[:, :width] = total
    if padded > width:
        columns[:, width:] = jnp.zeros((examples, padded - width), jnp.float32)


def feature_kernel(per, *refs):
    chunks, features = refs[:-1], refs[-1]
    parts = len(chunks)
    rows_here, width = features.shape
    examples = rows_here * parts
    total = chunks[0][:examples, :]
    for chunk in chunks[1:]:
        total = total + chunk[:examples, :]
    span = width // parts
    halves = span // (per * SLOT)
    natural = jnp.concatenate(
        [
            total[:, (h * per + c) * SLOT : (h * per + c + 1) * SLOT]
            for c in range(per)
            for h in range(halves)
        ],
        axis=1,
    )
    for r in range(rows_here):
        features[r : r + 1, :] = jnp.concatenate(
            [natural[r * parts + g : r * parts + g + 1, :] for g in range(parts)], axis=1
        )


def pick_lanes(x, index):
    return jnp.take_along_axis(x, index, axis=1)


def reciprocal(x):
    guess = pl.reciprocal(x, approx=True)
    guess = guess * (2.0 - x * guess)
    return guess * (2.0 - x * guess)


def factor_kernel(damping, *refs):
    rows, factors = refs[:-1], refs[-1]
    channels, sketch, _ = factors.shape
    halves = sketch // SLOT
    panels = sketch // PANEL
    per_half = SLOT // PANEL
    stacked = jnp.concatenate([part[...] for part in rows], axis=0)
    examples = stacked.shape[0]
    high, rest = split(stacked)
    gram = (dot_tn(high, rest) + dot_tn(rest, high)) + dot_tn(high, high)
    lane = lax.broadcasted_iota(jnp.int32, (PANEL, LANES), 1)
    sub = lax.broadcasted_iota(jnp.int32, (PANEL, LANES), 0)
    slot = lane // SLOT
    within = lane % SLOT
    ridge = damping[0]
    tile = []
    for q in range(panels):
        hr, at = divmod(q, per_half)
        line = []
        for h in range(halves):
            value = None
            for c in range(GROUP):
                start = hr * LANES + c * SLOT + at * PANEL
                block = gram[start : start + PANEL, h * LANES : (h + 1) * LANES]
                value = block if c == 0 else jnp.where(slot == c, block, value)
            value = value * (1.0 / examples)
            if h == hr:
                value = value + jnp.where(within == at * PANEL + sub, ridge, 0.0)
            line.append(value)
        tile.append(line)

    zero = jnp.zeros((PANEL, LANES), jnp.float32)
    finished = []
    for q in range(panels):
        hq, at = divmod(q, per_half)
        column = [
            {
                j: pick_lanes(tile[j][hq], slot * SLOT + at * PANEL + r)
                for j in range(q, panels)
            }
            for r in range(PANEL)
        ]
        block = [
            [
                jnp.broadcast_to(column[r][q][s : s + 1, :], (PANEL, LANES))
                if s >= r
                else None
                for s in range(PANEL)
            ]
            for r in range(PANEL)
        ]
        line = [
            [
                jnp.broadcast_to(tile[q][h][r : r + 1, :], (PANEL, LANES))
                if h >= hq
                else None
                for h in range(halves)
            ]
            for r in range(PANEL)
        ]
        inverse = []
        for r in range(PANEL):
            inv = reciprocal(block[r][r])
            inverse.append(inv)
            for s in range(r + 1, PANEL):
                ratio = block[r][s] * inv
                for t in range(s, PANEL):
                    block[s][t] = block[s][t] - ratio * block[r][t]
                for j in range(q + 1, panels):
                    column[s][j] = column[s][j] - ratio * column[r][j]
                for h in range(hq, halves):
                    line[s][h] = line[s][h] - ratio * line[r][h]
        result = []
        for h in range(halves):
            if h < hq:
                result.append(zero)
                continue
            value = zero
            for r in range(PANEL):
                value = jnp.where(sub == r, line[r][h] * lax.rsqrt(block[r][r]), value)
            if h == hq:
                value = jnp.where(within >= at * PANEL + sub, value, 0.0)
            result.append(value)
        finished.append(result)
        for j in range(q + 1, panels):
            weights = [column[r][j] * inverse[r] for r in range(PANEL)]
            for h in range((q + 1) // per_half, halves):
                value = tile[j][h]
                for r in range(PANEL):
                    value = value - weights[r] * line[r][h]
                tile[j][h] = value

    for q in range(panels):
        for c in range(channels):
            factors[c, q * PANEL : (q + 1) * PANEL, :] = jnp.concatenate(
                [finished[q][h][:, c * SLOT : (c + 1) * SLOT] for h in range(halves)],
                axis=1,
            )


def shift(x, axis, distance):
    size = lax.axis_size(axis)
    return lax.ppermute(x, axis, [(i, (i + distance) % size) for i in range(size)])


def vmem():
    return pl.BlockSpec(memory_space=pltpu.VMEM)


def hbm():
    return pl.BlockSpec(memory_space=pltpu.HBM)


def smem():
    return pl.BlockSpec(memory_space=pltpu.SMEM)


def local(
    acts,
    grads,
    down_factor,
    up_factor_transposed,
    input_projection,
    gradient_projection,
    order,
    damping,
):
    parts = lax.axis_size("mp")
    shards = lax.axis_size("ex")
    tokens, width = acts.shape[1:]
    key_width = grads.shape[2]
    rank = down_factor.shape[1]
    sketch = input_projection.shape[1]
    examples = tokens // EXAMPLE_LENGTH
    per = rank // parts
    span = per * sketch
    scaling = 1.0 / math.sqrt(2.0 * EXAMPLE_LENGTH * parts)
    sends = pl.pallas_call(
        functools.partial(partial_kernel, parts, scaling),
        out_shape=[jax.ShapeDtypeStruct((2 * examples, span), jnp.float32)] * parts,
        in_specs=[hbm()] * 7,
        out_specs=[vmem()] * parts,
        scratch_shapes=[
            pltpu.VMEM((tokens, width), acts.dtype),
            pltpu.VMEM((tokens, key_width), grads.dtype),
            pltpu.VMEM((sketch + rank, width), acts.dtype),
            pltpu.VMEM((sketch + rank, key_width), grads.dtype),
            pltpu.SMEM(order.shape[1:], order.dtype),
            pltpu.VMEM((2, rank, tokens), jnp.float32),
            pltpu.VMEM((examples * parts, LANES), jnp.float32),
            pltpu.SemaphoreType.DMA(((width + key_width) // CHUNK, 3)),
            pltpu.SemaphoreType.DMA,
        ],
        compiler_params=pltpu.CompilerParams(vmem_limit_bytes=62000000),
        name="partials",
    )(
        acts,
        grads,
        down_factor,
        up_factor_transposed,
        input_projection,
        gradient_projection,
        order,
    )
    chunks = [sends[0]] + [shift(sends[d], "mp", d) for d in range(1, parts)]
    columns = pl.pallas_call(
        column_kernel,
        out_shape=jax.ShapeDtypeStruct((examples, max(span, GROUP * sketch)), jnp.float32),
        in_specs=[vmem()] * parts,
        out_specs=vmem(),
        name="columns",
    )(*chunks)
    rows = [columns] + [shift(columns, "ex", d) for d in range(1, shards)]
    features = pl.pallas_call(
        functools.partial(feature_kernel, per),
        out_shape=jax.ShapeDtypeStruct((examples // parts, rank * sketch), jnp.float32),
        in_specs=[vmem()] * parts,
        out_specs=vmem(),
        name="features",
    )(*chunks)
    factors = pl.pallas_call(
        factor_kernel,
        out_shape=jax.ShapeDtypeStruct((per, sketch, sketch), jnp.float32),
        in_specs=[smem()] + [vmem()] * shards,
        out_specs=vmem(),
        compiler_params=pltpu.CompilerParams(vmem_limit_bytes=32 * 2**20),
        name="factors",
    )(damping, *rows)
    return features, factors


def solution(mesh):
    in_specs = (
        P("mp", "ex", None),
        P("mp", "ex", None),
        P("mp", None, None),
        P("mp", None, None),
        P("mp", None, None),
        P("mp", None, None),
        P("mp", "ex", None),
        P(),
    )
    out_specs = (P(("ex", "mp"), None), P("mp", None, None))
    return jax.shard_map(
        local, mesh=mesh, in_specs=in_specs, out_specs=out_specs, check_vma=False
    )
```

```python
import functools
import math

import jax
import jax.numpy as jnp
from jax import lax
from jax.experimental import pallas as pl
from jax.experimental.pallas import tpu as pltpu
from jax.sharding import PartitionSpec as P

EXAMPLE_LENGTH = 8
LANES = 128
SLOT = 32
GROUP = LANES // SLOT
PANEL = 8
CHUNK = 1024


def dot_nt(a, b):
    return lax.dot_general(
        a, b, (((1,), (1,)), ((), ())), preferred_element_type=jnp.float32
    )


def dot_tn(a, b):
    return lax.dot_general(
        a, b, (((0,), (0,)), ((), ())), preferred_element_type=jnp.float32
    )


def split(x):
    high = x.astype(jnp.bfloat16)
    return high, (x - high.astype(jnp.float32)).astype(jnp.bfloat16)


def partial_kernel(
    parts,
    scaling,
    acts_hbm,
    grads_hbm,
    down_hbm,
    up_hbm,
    proj_in_hbm,
    proj_out_hbm,
    order_hbm,
    *refs,
):
    sends, refs = refs[:parts], refs[parts:]
    acts, grads, weights_in, weights_out, order, low, out, sems, order_sem = refs
    tokens, width = acts.shape
    rank = down_hbm.shape[1]
    sketch = proj_in_hbm.shape[1]
    examples = tokens // EXAMPLE_LENGTH
    per = rank // parts
    halves = sketch // SLOT

    def copies(source, target, sem, start, size):
        return pltpu.make_async_copy(
            source.at[0, :, pl.ds(start, size)],
            target.at[:, pl.ds(start, size)],
            sem,
        )

    order_copy = pltpu.make_async_copy(order_hbm.at[0], order, order_sem)
    stages = []
    for start in range(0, width, CHUNK):
        stages.append(
            [
                (acts_hbm, acts, start),
                (proj_in_hbm, weights_in.at[pl.ds(0, sketch)], start),
                (down_hbm, weights_in.at[pl.ds(sketch, rank)], start),
            ]
        )
    for start in range(0, grads.shape[1], CHUNK):
        stages.append(
            [
                (grads_hbm, grads, start),
                (proj_out_hbm, weights_out.at[pl.ds(0, sketch)], start),
                (up_hbm, weights_out.at[pl.ds(sketch, rank)], start),
            ]
        )
    pending = [
        [
            copies(source, target, sems.at[n, i], start, CHUNK)
            for i, (source, target, start) in enumerate(stage)
        ]
        for n, stage in enumerate(stages)
    ]
    for stage in pending:
        for copy in stage:
            copy.start()
    order_copy.start()

    def product(first, rows, weights):
        total = None
        for n in range(rows.shape[1] // CHUNK):
            for copy in pending[first + n]:
                copy.wait()
            here = pl.ds(n * CHUNK, CHUNK)
            term = dot_nt(weights[:, here], rows[:, here])
            total = term if total is None else total + term
        return total

    from_acts = product(0, acts, weights_in)
    from_grads = product(width // CHUNK, grads, weights_out)
    order_copy.wait()
    sketches = jnp.concatenate([from_acts[:sketch], from_grads[:sketch]], axis=1)
    low[0] = from_grads[sketch:] * scaling
    low[1] = from_acts[sketch:] * scaling

    rows = examples * parts
    lane = lax.broadcasted_iota(jnp.int32, (rows, 2 * tokens), 1)
    source = (lane % tokens) // EXAMPLE_LENGTH
    target = jnp.zeros((8, 2 * tokens), jnp.int32)
    for s in range(examples):
        target = jnp.where(source[:8] == s, order[0, s], target)
    target = jnp.concatenate([target] * (rows // 8), axis=0)
    place = lax.broadcasted_iota(jnp.int32, (rows, 2 * tokens), 0) // parts
    mine = target == place
    highs, lows = [], []
    for c in range(per):
        chosen = jnp.concatenate(
            [low[i, pl.ds(c, parts, stride=per), :] for i in range(2)], axis=1
        )
        chosen = jnp.concatenate([chosen] * examples, axis=0)
        high, rest = split(jnp.where(mine, chosen, 0.0))
        highs.append(high)
        lows.append(rest)
    left_high = jnp.concatenate(highs, axis=0)
    left_low = jnp.concatenate(lows, axis=0)
    right = jnp.concatenate(
        [sketches[h * SLOT : (h + 1) * SLOT] for h in range(halves) for _ in range(per)],
        axis=0,
    )
    right_high, right_low = split(right)
    spread = (
        dot_nt(left_high, right_low) + dot_nt(left_low, right_high)
    ) + dot_nt(left_high, right_high)
    column = lax.broadcasted_iota(jnp.int32, (rows, per * sketch), 1)
    channel = (column // SLOT) % per
    total = spread[:rows]
    for c in range(1, per):
        total = jnp.where(channel == c, spread[c * rows : (c + 1) * rows], total)
    me = lax.axis_index("mp")
    for start in range(0, per * sketch, LANES):
        stop = min(start + LANES, per * sketch)
        out[:, : stop - start] = total[:, start:stop]
        for d in range(parts):
            g = lax.rem(me + d, parts)
            sends[d][:examples, start:stop] = out[
                pl.ds(pl.multiple_of(g * examples, examples), examples), : stop - start
            ]
            sends[d][examples:, start:stop] = out[pl.ds(g, examples, stride=parts), :][
                :, : stop - start
            ]


def column_kernel(*refs):
    chunks, columns = refs[:-1], refs[-1]
    examples, padded = columns.shape
    total = chunks[0][examples:, :]
    for chunk in chunks[1:]:
        total = total + chunk[examples:, :]
    width = total.shape[1]
    columns[:, :width] = total
    if padded > width:
        columns[:, width:] = jnp.zeros((examples, padded - width), jnp.float32)


def write_features(chunks, per, features):
    parts = len(chunks)
    rows_here, width = features.shape
    examples = rows_here * parts
    total = chunks[0][:examples, :]
    for chunk in chunks[1:]:
        total = total + chunk[:examples, :]
    span = width // parts
    halves = span // (per * SLOT)
    natural = jnp.concatenate(
        [
            total[:, (h * per + c) * SLOT : (h * per + c + 1) * SLOT]
            for c in range(per)
            for h in range(halves)
        ],
        axis=1,
    )
    for r in range(rows_here):
        features[r : r + 1, :] = jnp.concatenate(
            [natural[r * parts + g : r * parts + g + 1, :] for g in range(parts)], axis=1
        )


def pick_lanes(x, index):
    return jnp.take_along_axis(x, index, axis=1)


def reciprocal(x):
    guess = pl.reciprocal(x, approx=True)
    guess = guess * (2.0 - x * guess)
    return guess * (2.0 - x * guess)


def factor_kernel(parts, shards, damping, *refs):
    chunks, rows = refs[:parts], refs[parts : parts + shards]
    features, factors = refs[parts + shards :]
    channels, sketch, _ = factors.shape
    write_features(chunks, channels, features)
    halves = sketch // SLOT
    panels = sketch // PANEL
    per_half = SLOT // PANEL
    stacked = jnp.concatenate([part[...] for part in rows], axis=0)
    examples = stacked.shape[0]
    high, rest = split(stacked)
    gram = (dot_tn(high, rest) + dot_tn(rest, high)) + dot_tn(high, high)
    lane = lax.broadcasted_iota(jnp.int32, (PANEL, LANES), 1)
    sub = lax.broadcasted_iota(jnp.int32, (PANEL, LANES), 0)
    slot = lane // SLOT
    within = lane % SLOT
    ridge = damping[0]
    tile = []
    for q in range(panels):
        hr, at = divmod(q, per_half)
        line = []
        for h in range(halves):
            value = None
            for c in range(GROUP):
                start = hr * LANES + c * SLOT + at * PANEL
                block = gram[start : start + PANEL, h * LANES : (h + 1) * LANES]
                value = block if c == 0 else jnp.where(slot == c, block, value)
            value = value * (1.0 / examples)
            if h == hr:
                value = value + jnp.where(within == at * PANEL + sub, ridge, 0.0)
            line.append(value)
        tile.append(line)

    zero = jnp.zeros((PANEL, LANES), jnp.float32)
    finished = []
    for q in range(panels):
        hq, at = divmod(q, per_half)
        column = [
            {
                j: pick_lanes(tile[j][hq], slot * SLOT + at * PANEL + r)
                for j in range(q, panels)
            }
            for r in range(PANEL)
        ]
        block = [
            [
                jnp.broadcast_to(column[r][q][s : s + 1, :], (PANEL, LANES))
                if s >= r
                else None
                for s in range(PANEL)
            ]
            for r in range(PANEL)
        ]
        line = [
            [
                jnp.broadcast_to(tile[q][h][r : r + 1, :], (PANEL, LANES))
                if h >= hq
                else None
                for h in range(halves)
            ]
            for r in range(PANEL)
        ]
        inverse = []
        for r in range(PANEL):
            inv = reciprocal(block[r][r])
            inverse.append(inv)
            for s in range(r + 1, PANEL):
                ratio = block[r][s] * inv
                for t in range(s, PANEL):
                    block[s][t] = block[s][t] - ratio * block[r][t]
                for j in range(q + 1, panels):
                    column[s][j] = column[s][j] - ratio * column[r][j]
                for h in range(hq, halves):
                    line[s][h] = line[s][h] - ratio * line[r][h]
        result = []
        for h in range(halves):
            if h < hq:
                result.append(zero)
                continue
            value = zero
            for r in range(PANEL):
                value = jnp.where(sub == r, line[r][h] * lax.rsqrt(block[r][r]), value)
            if h == hq:
                value = jnp.where(within >= at * PANEL + sub, value, 0.0)
            result.append(value)
        finished.append(result)
        for j in range(q + 1, panels):
            weights = [column[r][j] * inverse[r] for r in range(PANEL)]
            for h in range((q + 1) // per_half, halves):
                value = tile[j][h]
                for r in range(PANEL):
                    value = value - weights[r] * line[r][h]
                tile[j][h] = value

    for q in range(panels):
        for c in range(channels):
            factors[c, q * PANEL : (q + 1) * PANEL, :] = jnp.concatenate(
                [finished[q][h][:, c * SLOT : (c + 1) * SLOT] for h in range(halves)],
                axis=1,
            )


def shift(x, axis, distance):
    size = lax.axis_size(axis)
    return lax.ppermute(x, axis, [(i, (i + distance) % size) for i in range(size)])


def vmem():
    return pl.BlockSpec(memory_space=pltpu.VMEM)


def hbm():
    return pl.BlockSpec(memory_space=pltpu.HBM)


def in_hbm(*arrays):
    return [pltpu.with_memory_space_constraint(x, pltpu.HBM) for x in arrays]


def in_vmem(*arrays):
    return [pltpu.with_memory_space_constraint(x, pltpu.VMEM) for x in arrays]


def smem():
    return pl.BlockSpec(memory_space=pltpu.SMEM)


def local(
    acts,
    grads,
    down_factor,
    up_factor_transposed,
    input_projection,
    gradient_projection,
    order,
    damping,
):
    parts = lax.axis_size("mp")
    shards = lax.axis_size("ex")
    tokens, width = acts.shape[1:]
    key_width = grads.shape[2]
    rank = down_factor.shape[1]
    sketch = input_projection.shape[1]
    examples = tokens // EXAMPLE_LENGTH
    per = rank // parts
    span = per * sketch
    scaling = 1.0 / math.sqrt(2.0 * EXAMPLE_LENGTH * parts)
    sends = pl.pallas_call(
        functools.partial(partial_kernel, parts, scaling),
        out_shape=[pltpu.VMEM((2 * examples, span), jnp.float32)] * parts,
        in_specs=[hbm()] * 7,
        out_specs=[vmem()] * parts,
        scratch_shapes=[
            pltpu.VMEM((tokens, width), acts.dtype),
            pltpu.VMEM((tokens, key_width), grads.dtype),
            pltpu.VMEM((sketch + rank, width), acts.dtype),
            pltpu.VMEM((sketch + rank, key_width), grads.dtype),
            pltpu.SMEM(order.shape[1:], order.dtype),
            pltpu.VMEM((2, rank, tokens), jnp.float32),
            pltpu.VMEM((examples * parts, LANES), jnp.float32),
            pltpu.SemaphoreType.DMA(((width + key_width) // CHUNK, 3)),
            pltpu.SemaphoreType.DMA,
        ],
        compiler_params=pltpu.CompilerParams(vmem_limit_bytes=8 * 2**20),
        name="partials",
    )(
        *in_hbm(
            acts,
            grads,
            down_factor,
            up_factor_transposed,
            input_projection,
            gradient_projection,
            order,
        )
    )
    chunks = [sends[0]] + [shift(sends[d], "mp", d) for d in range(1, parts)]
    columns = pl.pallas_call(
        column_kernel,
        out_shape=pltpu.VMEM((examples, max(span, GROUP * sketch)), jnp.float32),
        in_specs=[vmem()] * parts,
        out_specs=vmem(),
        compiler_params=pltpu.CompilerParams(vmem_limit_bytes=2 * 2**20),
        name="columns",
    )(*in_vmem(*chunks))
    rows = [columns] + [shift(columns, "ex", d) for d in range(1, shards)]
    return pl.pallas_call(
        functools.partial(factor_kernel, parts, shards),
        out_shape=[
            jax.ShapeDtypeStruct((examples // parts, rank * sketch), jnp.float32),
            jax.ShapeDtypeStruct((per, sketch, sketch), jnp.float32),
        ],
        in_specs=[smem()] + [vmem()] * (parts + shards),
        out_specs=[vmem()] * 2,
        compiler_params=pltpu.CompilerParams(vmem_limit_bytes=8 * 2**20),
        name="factors",
    )(damping, *in_vmem(*chunks, *rows))


def solution(mesh):
    in_specs = (
        P("mp", "ex", None),
        P("mp", "ex", None),
        P("mp", None, None),
        P("mp", None, None),
        P("mp", None, None),
        P("mp", None, None),
        P("mp", "ex", None),
        P(),
    )
    out_specs = (P(("ex", "mp"), None), P("mp", None, None))
    return jax.shard_map(
        local, mesh=mesh, in_specs=in_specs, out_specs=out_specs, check_vma=False
    )
```

```python
import functools
import math

import jax
import jax.numpy as jnp
from jax import lax
from jax.experimental import pallas as pl
from jax.experimental.pallas import tpu as pltpu
from jax.sharding import PartitionSpec as P

EXAMPLE_LENGTH = 8
LANES = 128
SLOT = 32
GROUP = LANES // SLOT
PANEL = 8
CHUNK = 1024


def dot_nt(a, b):
    return lax.dot_general(
        a, b, (((1,), (1,)), ((), ())), preferred_element_type=jnp.float32
    )


def dot_tn(a, b):
    return lax.dot_general(
        a, b, (((0,), (0,)), ((), ())), preferred_element_type=jnp.float32
    )


def split(x):
    high = x.astype(jnp.bfloat16)
    return high, (x - high.astype(jnp.float32)).astype(jnp.bfloat16)


def partial_kernel(
    parts,
    scaling,
    acts_hbm,
    grads_hbm,
    down_hbm,
    up_hbm,
    proj_in_hbm,
    proj_out_hbm,
    order_hbm,
    *refs,
):
    sends, refs = refs[:parts], refs[parts:]
    acts, grads, weights_in, weights_out, order, low, out, sems, order_sem = refs
    tokens, width = acts.shape
    rank = down_hbm.shape[1]
    sketch = proj_in_hbm.shape[1]
    examples = tokens // EXAMPLE_LENGTH
    per = rank // parts
    halves = sketch // SLOT

    def copies(source, target, sem, start, size):
        return pltpu.make_async_copy(
            source.at[0, :, pl.ds(start, size)],
            target.at[:, pl.ds(start, size)],
            sem,
        )

    order_copy = pltpu.make_async_copy(order_hbm.at[0], order, order_sem)
    stages = []
    for start in range(0, width, CHUNK):
        stages.append(
            [
                (acts_hbm, acts, start),
                (proj_in_hbm, weights_in.at[pl.ds(0, sketch)], start),
                (down_hbm, weights_in.at[pl.ds(sketch, rank)], start),
            ]
        )
    for start in range(0, grads.shape[1], CHUNK):
        stages.append(
            [
                (grads_hbm, grads, start),
                (proj_out_hbm, weights_out.at[pl.ds(0, sketch)], start),
                (up_hbm, weights_out.at[pl.ds(sketch, rank)], start),
            ]
        )
    pending = [
        [
            copies(source, target, sems.at[n, i], start, CHUNK)
            for i, (source, target, start) in enumerate(stage)
        ]
        for n, stage in enumerate(stages)
    ]
    for stage in pending:
        for copy in stage:
            copy.start()
    order_copy.start()

    def product(first, rows, weights):
        total = None
        for n in range(rows.shape[1] // CHUNK):
            for copy in pending[first + n]:
                copy.wait()
            here = pl.ds(n * CHUNK, CHUNK)
            term = dot_nt(weights[:, here], rows[:, here])
            total = term if total is None else total + term
        return total

    from_acts = product(0, acts, weights_in)
    from_grads = product(width // CHUNK, grads, weights_out)
    order_copy.wait()
    sketches = jnp.concatenate([from_acts[:sketch], from_grads[:sketch]], axis=1)
    low[0] = from_grads[sketch:] * scaling
    low[1] = from_acts[sketch:] * scaling

    rows = examples * parts
    lane = lax.broadcasted_iota(jnp.int32, (rows, 2 * tokens), 1)
    source = (lane % tokens) // EXAMPLE_LENGTH
    target = jnp.zeros((8, 2 * tokens), jnp.int32)
    for s in range(examples):
        target = jnp.where(source[:8] == s, order[0, s], target)
    target = jnp.concatenate([target] * (rows // 8), axis=0)
    place = lax.broadcasted_iota(jnp.int32, (rows, 2 * tokens), 0) // parts
    mine = target == place
    highs, lows = [], []
    for c in range(per):
        chosen = jnp.concatenate(
            [low[i, pl.ds(c, parts, stride=per), :] for i in range(2)], axis=1
        )
        chosen = jnp.concatenate([chosen] * examples, axis=0)
        high, rest = split(jnp.where(mine, chosen, 0.0))
        highs.append(high)
        lows.append(rest)
    left_high = jnp.concatenate(highs, axis=0)
    left_low = jnp.concatenate(lows, axis=0)
    right = jnp.concatenate(
        [sketches[h * SLOT : (h + 1) * SLOT] for h in range(halves) for _ in range(per)],
        axis=0,
    )
    right_high, right_low = split(right)
    spread = (
        dot_nt(left_high, right_low) + dot_nt(left_low, right_high)
    ) + dot_nt(left_high, right_high)
    column = lax.broadcasted_iota(jnp.int32, (rows, per * sketch), 1)
    channel = (column // SLOT) % per
    total = spread[:rows]
    for c in range(1, per):
        total = jnp.where(channel == c, spread[c * rows : (c + 1) * rows], total)
    me = lax.axis_index("mp")
    for start in range(0, per * sketch, LANES):
        stop = min(start + LANES, per * sketch)
        out[:, : stop - start] = total[:, start:stop]
        for d in range(parts):
            g = me ^ d
            sends[d][:examples, start:stop] = out[
                pl.ds(pl.multiple_of(g * examples, examples), examples), : stop - start
            ]
            sends[d][examples:, start:stop] = out[pl.ds(g, examples, stride=parts), :][
                :, : stop - start
            ]


def column_kernel(*refs):
    chunks, columns = refs[:-1], refs[-1]
    examples, padded = columns.shape
    total = chunks[0][examples:, :]
    for chunk in chunks[1:]:
        total = total + chunk[examples:, :]
    width = total.shape[1]
    columns[:, :width] = total
    if padded > width:
        columns[:, width:] = jnp.zeros((examples, padded - width), jnp.float32)


def stack_kernel(*refs):
    rows = refs[0].shape[0]
    for n, part in enumerate(refs[:-1]):
        refs[-1][n * rows : (n + 1) * rows, :] = part[...]


def write_features(chunks, per, features):
    parts = len(chunks)
    rows_here, width = features.shape
    examples = rows_here * parts
    total = chunks[0][:examples, :]
    for chunk in chunks[1:]:
        total = total + chunk[:examples, :]
    span = width // parts
    halves = span // (per * SLOT)
    natural = jnp.concatenate(
        [
            total[:, (h * per + c) * SLOT : (h * per + c + 1) * SLOT]
            for c in range(per)
            for h in range(halves)
        ],
        axis=1,
    )
    for r in range(rows_here):
        features[r : r + 1, :] = jnp.concatenate(
            [natural[r * parts + g : r * parts + g + 1, :] for g in range(parts)], axis=1
        )


def pick_lanes(x, index):
    return jnp.take_along_axis(x, index, axis=1)


def reciprocal(x):
    guess = pl.reciprocal(x, approx=True)
    guess = guess * (2.0 - x * guess)
    return guess * (2.0 - x * guess)


def factor_kernel(parts, damping, *refs):
    chunks, rows, (features, factors) = refs[:parts], refs[parts:-2], refs[-2:]
    channels, sketch, _ = factors.shape
    write_features(chunks, channels, features)
    halves = sketch // SLOT
    panels = sketch // PANEL
    per_half = SLOT // PANEL
    stacked = jnp.concatenate([part[...] for part in rows], axis=0)
    examples = stacked.shape[0]
    high, rest = split(stacked)
    gram = (dot_tn(high, rest) + dot_tn(rest, high)) + dot_tn(high, high)
    lane = lax.broadcasted_iota(jnp.int32, (PANEL, LANES), 1)
    sub = lax.broadcasted_iota(jnp.int32, (PANEL, LANES), 0)
    slot = lane // SLOT
    within = lane % SLOT
    ridge = damping[0]
    tile = []
    for q in range(panels):
        hr, at = divmod(q, per_half)
        line = []
        for h in range(halves):
            value = None
            for c in range(GROUP):
                start = hr * LANES + c * SLOT + at * PANEL
                block = gram[start : start + PANEL, h * LANES : (h + 1) * LANES]
                value = block if c == 0 else jnp.where(slot == c, block, value)
            value = value * (1.0 / examples)
            if h == hr:
                value = value + jnp.where(within == at * PANEL + sub, ridge, 0.0)
            line.append(value)
        tile.append(line)

    zero = jnp.zeros((PANEL, LANES), jnp.float32)
    finished = []
    for q in range(panels):
        hq, at = divmod(q, per_half)
        column = [
            {
                j: pick_lanes(tile[j][hq], slot * SLOT + at * PANEL + r)
                for j in range(q, panels)
            }
            for r in range(PANEL)
        ]
        block = [
            [
                jnp.broadcast_to(column[r][q][s : s + 1, :], (PANEL, LANES))
                if s >= r
                else None
                for s in range(PANEL)
            ]
            for r in range(PANEL)
        ]
        line = [
            [
                jnp.broadcast_to(tile[q][h][r : r + 1, :], (PANEL, LANES))
                if h >= hq
                else None
                for h in range(halves)
            ]
            for r in range(PANEL)
        ]
        inverse = []
        for r in range(PANEL):
            inv = reciprocal(block[r][r])
            inverse.append(inv)
            for s in range(r + 1, PANEL):
                ratio = block[r][s] * inv
                for t in range(s, PANEL):
                    block[s][t] = block[s][t] - ratio * block[r][t]
                for j in range(q + 1, panels):
                    column[s][j] = column[s][j] - ratio * column[r][j]
                for h in range(hq, halves):
                    line[s][h] = line[s][h] - ratio * line[r][h]
        result = []
        for h in range(halves):
            if h < hq:
                result.append(zero)
                continue
            value = zero
            for r in range(PANEL):
                value = jnp.where(sub == r, line[r][h] * lax.rsqrt(block[r][r]), value)
            if h == hq:
                value = jnp.where(within >= at * PANEL + sub, value, 0.0)
            result.append(value)
        finished.append(result)
        for j in range(q + 1, panels):
            weights = [column[r][j] * inverse[r] for r in range(PANEL)]
            for h in range((q + 1) // per_half, halves):
                value = tile[j][h]
                for r in range(PANEL):
                    value = value - weights[r] * line[r][h]
                tile[j][h] = value

    for q in range(panels):
        for c in range(channels):
            factors[c, q * PANEL : (q + 1) * PANEL, :] = jnp.concatenate(
                [finished[q][h][:, c * SLOT : (c + 1) * SLOT] for h in range(halves)],
                axis=1,
            )


def exchange(x, axis, distance):
    size = lax.axis_size(axis)
    return lax.ppermute(x, axis, [(i, i ^ distance) for i in range(size)])


def vmem():
    return pl.BlockSpec(memory_space=pltpu.VMEM)


def hbm():
    return pl.BlockSpec(memory_space=pltpu.HBM)


def in_hbm(*arrays):
    return [pltpu.with_memory_space_constraint(x, pltpu.HBM) for x in arrays]


def in_vmem(*arrays):
    return [pltpu.with_memory_space_constraint(x, pltpu.VMEM) for x in arrays]


def smem():
    return pl.BlockSpec(memory_space=pltpu.SMEM)


def local(
    acts,
    grads,
    down_factor,
    up_factor_transposed,
    input_projection,
    gradient_projection,
    order,
    damping,
):
    parts = lax.axis_size("mp")
    shards = lax.axis_size("ex")
    tokens, width = acts.shape[1:]
    key_width = grads.shape[2]
    rank = down_factor.shape[1]
    sketch = input_projection.shape[1]
    examples = tokens // EXAMPLE_LENGTH
    per = rank // parts
    span = per * sketch
    scaling = 1.0 / math.sqrt(2.0 * EXAMPLE_LENGTH * parts)
    sends = pl.pallas_call(
        functools.partial(partial_kernel, parts, scaling),
        out_shape=[pltpu.VMEM((2 * examples, span), jnp.float32)] * parts,
        in_specs=[hbm()] * 7,
        out_specs=[vmem()] * parts,
        scratch_shapes=[
            pltpu.VMEM((tokens, width), acts.dtype),
            pltpu.VMEM((tokens, key_width), grads.dtype),
            pltpu.VMEM((sketch + rank, width), acts.dtype),
            pltpu.VMEM((sketch + rank, key_width), grads.dtype),
            pltpu.SMEM(order.shape[1:], order.dtype),
            pltpu.VMEM((2, rank, tokens), jnp.float32),
            pltpu.VMEM((examples * parts, LANES), jnp.float32),
            pltpu.SemaphoreType.DMA(((width + key_width) // CHUNK, 3)),
            pltpu.SemaphoreType.DMA,
        ],
        compiler_params=pltpu.CompilerParams(vmem_limit_bytes=8 * 2**20),
        name="partials",
    )(
        *in_hbm(
            acts,
            grads,
            down_factor,
            up_factor_transposed,
            input_projection,
            gradient_projection,
            order,
        )
    )
    chunks = [sends[0]] + [exchange(sends[d], "mp", d) for d in range(1, parts)]
    columns = pl.pallas_call(
        column_kernel,
        out_shape=pltpu.VMEM((examples, max(span, GROUP * sketch)), jnp.float32),
        in_specs=[vmem()] * parts,
        out_specs=vmem(),
        compiler_params=pltpu.CompilerParams(vmem_limit_bytes=2 * 2**20),
        name="columns",
    )(*in_vmem(*chunks))
    near = [columns] + [exchange(columns, "ex", d) for d in range(2, shards, 2)]
    gathered = pl.pallas_call(
        stack_kernel,
        out_shape=pltpu.VMEM((len(near) * examples, columns.shape[1]), jnp.float32),
        in_specs=[vmem()] * len(near),
        out_specs=vmem(),
        compiler_params=pltpu.CompilerParams(vmem_limit_bytes=2 * 2**20),
        name="stack",
    )(*in_vmem(*near))
    rows = [gathered, exchange(gathered, "ex", 1)]
    return pl.pallas_call(
        functools.partial(factor_kernel, parts),
        out_shape=[
            jax.ShapeDtypeStruct((examples // parts, rank * sketch), jnp.float32),
            jax.ShapeDtypeStruct((per, sketch, sketch), jnp.float32),
        ],
        in_specs=[smem()] + [vmem()] * (parts + len(rows)),
        out_specs=[vmem()] * 2,
        compiler_params=pltpu.CompilerParams(vmem_limit_bytes=8 * 2**20),
        name="factors",
    )(damping, *in_vmem(*chunks, *rows))


def solution(mesh):
    in_specs = (
        P("mp", "ex", None),
        P("mp", "ex", None),
        P("mp", None, None),
        P("mp", None, None),
        P("mp", None, None),
        P("mp", None, None),
        P("mp", "ex", None),
        P(),
    )
    out_specs = (P(("ex", "mp"), None), P("mp", None, None))
    return jax.shard_map(
        local, mesh=mesh, in_specs=in_specs, out_specs=out_specs, check_vma=False
    )
```

```python
import functools
import math

import jax
import jax.numpy as jnp
from jax import lax
from jax.experimental import pallas as pl
from jax.experimental.pallas import tpu as pltpu
from jax.sharding import PartitionSpec as P

EXAMPLE_LENGTH = 8
LANES = 128
SLOT = 32
GROUP = LANES // SLOT
PANEL = 8
CHUNK = 1024


def dot_nt(a, b):
    return lax.dot_general(
        a, b, (((1,), (1,)), ((), ())), preferred_element_type=jnp.float32
    )


def dot_tn(a, b):
    return lax.dot_general(
        a, b, (((0,), (0,)), ((), ())), preferred_element_type=jnp.float32
    )


def split(x):
    high = x.astype(jnp.bfloat16)
    return high, (x - high.astype(jnp.float32)).astype(jnp.bfloat16)


def partial_kernel(
    parts,
    scaling,
    acts_hbm,
    grads_hbm,
    down_hbm,
    up_hbm,
    proj_in_hbm,
    proj_out_hbm,
    order_hbm,
    *refs,
):
    keep, give, acts, grads, weights_in, weights_out, order, low, out, sems, order_sem = refs
    tokens, width = acts.shape
    rank = down_hbm.shape[1]
    sketch = proj_in_hbm.shape[1]
    examples = tokens // EXAMPLE_LENGTH
    per = rank // parts
    halves = sketch // SLOT

    def copies(source, target, sem, start, size):
        return pltpu.make_async_copy(
            source.at[0, :, pl.ds(start, size)],
            target.at[:, pl.ds(start, size)],
            sem,
        )

    order_copy = pltpu.make_async_copy(order_hbm.at[0], order, order_sem)
    stages = []
    for start in range(0, width, CHUNK):
        stages.append(
            [
                (acts_hbm, acts, start),
                (proj_in_hbm, weights_in.at[pl.ds(0, sketch)], start),
                (down_hbm, weights_in.at[pl.ds(sketch, rank)], start),
            ]
        )
    for start in range(0, grads.shape[1], CHUNK):
        stages.append(
            [
                (grads_hbm, grads, start),
                (proj_out_hbm, weights_out.at[pl.ds(0, sketch)], start),
                (up_hbm, weights_out.at[pl.ds(sketch, rank)], start),
            ]
        )
    pending = [
        [
            copies(source, target, sems.at[n, i], start, CHUNK)
            for i, (source, target, start) in enumerate(stage)
        ]
        for n, stage in enumerate(stages)
    ]
    for stage in pending:
        for copy in stage:
            copy.start()
    order_copy.start()

    def product(first, rows, weights):
        total = None
        for n in range(rows.shape[1] // CHUNK):
            for copy in pending[first + n]:
                copy.wait()
            here = pl.ds(n * CHUNK, CHUNK)
            term = dot_nt(weights[:, here], rows[:, here])
            total = term if total is None else total + term
        return total

    from_acts = product(0, acts, weights_in)
    from_grads = product(width // CHUNK, grads, weights_out)
    order_copy.wait()
    sketches = jnp.concatenate([from_acts[:sketch], from_grads[:sketch]], axis=1)
    low[0] = from_grads[sketch:] * scaling
    low[1] = from_acts[sketch:] * scaling

    rows = examples * parts
    lane = lax.broadcasted_iota(jnp.int32, (rows, 2 * tokens), 1)
    source = (lane % tokens) // EXAMPLE_LENGTH
    target = jnp.zeros((8, 2 * tokens), jnp.int32)
    for s in range(examples):
        target = jnp.where(source[:8] == s, order[0, s], target)
    target = jnp.concatenate([target] * (rows // 8), axis=0)
    place = lax.broadcasted_iota(jnp.int32, (rows, 2 * tokens), 0) // parts
    mine = target == place
    highs, lows = [], []
    for c in range(per):
        chosen = jnp.concatenate(
            [low[i, pl.ds(c, parts, stride=per), :] for i in range(2)], axis=1
        )
        chosen = jnp.concatenate([chosen] * examples, axis=0)
        high, rest = split(jnp.where(mine, chosen, 0.0))
        highs.append(high)
        lows.append(rest)
    left_high = jnp.concatenate(highs, axis=0)
    left_low = jnp.concatenate(lows, axis=0)
    right = jnp.concatenate(
        [sketches[h * SLOT : (h + 1) * SLOT] for h in range(halves) for _ in range(per)],
        axis=0,
    )
    right_high, right_low = split(right)
    spread = (
        dot_nt(left_high, right_low) + dot_nt(left_low, right_high)
    ) + dot_nt(left_high, right_high)
    column = lax.broadcasted_iota(jnp.int32, (rows, per * sketch), 1)
    channel = (column // SLOT) % per
    total = spread[:rows]
    for c in range(1, per):
        total = jnp.where(channel == c, spread[c * rows : (c + 1) * rows], total)
    me = lax.axis_index("mp")
    odd = lax.axis_index("ex") % 2 == 1
    for start in range(0, per * sketch, LANES):
        stop = min(start + LANES, per * sketch)
        out[:, : stop - start] = total[:, start:stop]
        for d in range(parts):
            g = me ^ d
            by_row = out[pl.ds(pl.multiple_of(g * examples, examples), examples), :]
            by_column = out[pl.ds(g, examples, stride=parts), :]
            here = pl.ds(d * examples, examples)
            keep[here, start:stop] = jnp.where(odd, by_column, by_row)[:, : stop - start]
            give[here, start:stop] = jnp.where(odd, by_row, by_column)[:, : stop - start]


def pair_kernel(keep, got, *sends):
    rows = sends[0].shape[0] // 2
    for d, send in enumerate(sends):
        send[:rows, :] = keep[d * rows : (d + 1) * rows, :]
        send[rows:, :] = got[d * rows : (d + 1) * rows, :]


def sum_kernel(*refs):
    chunks, (columns, own_rows, other_rows) = refs[:-3], refs[-3:]
    total = chunks[0][...]
    for chunk in chunks[1:]:
        total = total + chunk[...]
    width = total.shape[1]
    columns[:, :width] = total
    if columns.shape[1] > width:
        columns[:, width:] = jnp.zeros(
            (total.shape[0], columns.shape[1] - width), jnp.float32
        )
    own_rows[...] = total[: own_rows.shape[0]]
    other_rows[...] = total[own_rows.shape[0] :]


def stack_kernel(*refs):
    rows = refs[0].shape[0]
    for n, part in enumerate(refs[:-1]):
        refs[-1][n * rows : (n + 1) * rows, :] = part[...]


def write_features(total, parts, per, features):
    rows_here, width = features.shape
    span = width // parts
    halves = span // (per * SLOT)
    natural = jnp.concatenate(
        [
            total[:, (h * per + c) * SLOT : (h * per + c + 1) * SLOT]
            for c in range(per)
            for h in range(halves)
        ],
        axis=1,
    )
    for r in range(rows_here):
        features[r : r + 1, :] = jnp.concatenate(
            [natural[r * parts + g : r * parts + g + 1, :] for g in range(parts)], axis=1
        )


def pick_lanes(x, index):
    return jnp.take_along_axis(x, index, axis=1)


def reciprocal(x):
    guess = pl.reciprocal(x, approx=True)
    guess = guess * (2.0 - x * guess)
    return guess * (2.0 - x * guess)


def factor_kernel(
    parts, damping, own_rows, sent_rows, own_columns, sent_columns, features, factors
):
    channels, sketch, _ = factors.shape
    odd = lax.axis_index("ex") % 2 == 1
    write_features(
        jnp.where(odd, sent_rows[...], own_rows[...]), parts, channels, features
    )
    halves = sketch // SLOT
    panels = sketch // PANEL
    per_half = SLOT // PANEL
    stacked = jnp.where(odd, own_columns[...], sent_columns[...])
    examples = stacked.shape[0]
    high, rest = split(stacked)
    gram = (dot_tn(high, rest) + dot_tn(rest, high)) + dot_tn(high, high)
    lane = lax.broadcasted_iota(jnp.int32, (PANEL, LANES), 1)
    sub = lax.broadcasted_iota(jnp.int32, (PANEL, LANES), 0)
    slot = lane // SLOT
    within = lane % SLOT
    ridge = damping[0]
    tile = []
    for q in range(panels):
        hr, at = divmod(q, per_half)
        line = []
        for h in range(halves):
            value = None
            for c in range(GROUP):
                start = hr * LANES + c * SLOT + at * PANEL
                block = gram[start : start + PANEL, h * LANES : (h + 1) * LANES]
                value = block if c == 0 else jnp.where(slot == c, block, value)
            value = value * (1.0 / examples)
            if h == hr:
                value = value + jnp.where(within == at * PANEL + sub, ridge, 0.0)
            line.append(value)
        tile.append(line)

    zero = jnp.zeros((PANEL, LANES), jnp.float32)
    finished = []
    for q in range(panels):
        hq, at = divmod(q, per_half)
        column = [
            {
                j: pick_lanes(tile[j][hq], slot * SLOT + at * PANEL + r)
                for j in range(q, panels)
            }
            for r in range(PANEL)
        ]
        block = [
            [
                jnp.broadcast_to(column[r][q][s : s + 1, :], (PANEL, LANES))
                if s >= r
                else None
                for s in range(PANEL)
            ]
            for r in range(PANEL)
        ]
        line = [
            [
                jnp.broadcast_to(tile[q][h][r : r + 1, :], (PANEL, LANES))
                if h >= hq
                else None
                for h in range(halves)
            ]
            for r in range(PANEL)
        ]
        inverse = []
        for r in range(PANEL):
            inv = reciprocal(block[r][r])
            inverse.append(inv)
            for s in range(r + 1, PANEL):
                ratio = block[r][s] * inv
                for t in range(s, PANEL):
                    block[s][t] = block[s][t] - ratio * block[r][t]
                for j in range(q + 1, panels):
                    column[s][j] = column[s][j] - ratio * column[r][j]
                for h in range(hq, halves):
                    line[s][h] = line[s][h] - ratio * line[r][h]
        result = []
        for h in range(halves):
            if h < hq:
                result.append(zero)
                continue
            value = zero
            for r in range(PANEL):
                value = jnp.where(sub == r, line[r][h] * lax.rsqrt(block[r][r]), value)
            if h == hq:
                value = jnp.where(within >= at * PANEL + sub, value, 0.0)
            result.append(value)
        finished.append(result)
        for j in range(q + 1, panels):
            weights = [column[r][j] * inverse[r] for r in range(PANEL)]
            for h in range((q + 1) // per_half, halves):
                value = tile[j][h]
                for r in range(PANEL):
                    value = value - weights[r] * line[r][h]
                tile[j][h] = value

    for q in range(panels):
        for c in range(channels):
            factors[c, q * PANEL : (q + 1) * PANEL, :] = jnp.concatenate(
                [finished[q][h][:, c * SLOT : (c + 1) * SLOT] for h in range(halves)],
                axis=1,
            )


def exchange(x, axis, distance, part=None):
    sources = range(lax.axis_size(axis)) if part is None else range(part, lax.axis_size(axis), 2)
    return lax.ppermute(x, axis, [(i, i ^ distance) for i in sources])


def small_call(kernel, name, outs, *args):
    return pl.pallas_call(
        kernel,
        out_shape=[pltpu.VMEM(shape, jnp.float32) for shape in outs],
        in_specs=[vmem()] * len(args),
        out_specs=[vmem()] * len(outs),
        compiler_params=pltpu.CompilerParams(vmem_limit_bytes=2 * 2**20),
        name=name,
    )(*in_vmem(*args))


def vmem():
    return pl.BlockSpec(memory_space=pltpu.VMEM)


def hbm():
    return pl.BlockSpec(memory_space=pltpu.HBM)


def in_hbm(*arrays):
    return [pltpu.with_memory_space_constraint(x, pltpu.HBM) for x in arrays]


def in_vmem(*arrays):
    return [pltpu.with_memory_space_constraint(x, pltpu.VMEM) for x in arrays]


def smem():
    return pl.BlockSpec(memory_space=pltpu.SMEM)


def local(
    acts,
    grads,
    down_factor,
    up_factor_transposed,
    input_projection,
    gradient_projection,
    order,
    damping,
):
    parts = lax.axis_size("mp")
    shards = lax.axis_size("ex")
    tokens, width = acts.shape[1:]
    key_width = grads.shape[2]
    rank = down_factor.shape[1]
    sketch = input_projection.shape[1]
    examples = tokens // EXAMPLE_LENGTH
    per = rank // parts
    span = per * sketch
    scaling = 1.0 / math.sqrt(2.0 * EXAMPLE_LENGTH * parts)
    keep, give = pl.pallas_call(
        functools.partial(partial_kernel, parts, scaling),
        out_shape=[pltpu.VMEM((parts * examples, span), jnp.float32)] * 2,
        in_specs=[hbm()] * 7,
        out_specs=[vmem()] * 2,
        scratch_shapes=[
            pltpu.VMEM((tokens, width), acts.dtype),
            pltpu.VMEM((tokens, key_width), grads.dtype),
            pltpu.VMEM((sketch + rank, width), acts.dtype),
            pltpu.VMEM((sketch + rank, key_width), grads.dtype),
            pltpu.SMEM(order.shape[1:], order.dtype),
            pltpu.VMEM((2, rank, tokens), jnp.float32),
            pltpu.VMEM((examples * parts, LANES), jnp.float32),
            pltpu.SemaphoreType.DMA(((width + key_width) // CHUNK, 3)),
            pltpu.SemaphoreType.DMA,
        ],
        compiler_params=pltpu.CompilerParams(vmem_limit_bytes=8 * 2**20),
        name="partials",
    )(
        *in_hbm(
            acts,
            grads,
            down_factor,
            up_factor_transposed,
            input_projection,
            gradient_projection,
            order,
        )
    )
    got = exchange(give, "ex", 1)
    sends = small_call(
        pair_kernel, "pair", [(2 * examples, span)] * parts, keep, got
    )
    chunks = [sends[0]] + [exchange(sends[d], "mp", d) for d in range(parts - 1, 0, -1)]
    padded = max(span, GROUP * sketch)
    columns, own_rows, other_rows = small_call(
        sum_kernel,
        "sums",
        [(2 * examples, padded), (examples, span), (examples, span)],
        *chunks,
    )
    sent_rows = exchange(other_rows, "ex", 1, 0)
    near = [columns] + [exchange(columns, "ex", d, 1) for d in range(2, shards, 2)]
    (own_columns,) = small_call(
        stack_kernel, "stack", [(shards * examples, padded)], *near
    )
    sent_columns = exchange(own_columns, "ex", 1, 1)
    return pl.pallas_call(
        functools.partial(factor_kernel, parts),
        out_shape=[
            jax.ShapeDtypeStruct((examples // parts, rank * sketch), jnp.float32),
            jax.ShapeDtypeStruct((per, sketch, sketch), jnp.float32),
        ],
        in_specs=[smem()] + [vmem()] * 4,
        out_specs=[vmem()] * 2,
        compiler_params=pltpu.CompilerParams(vmem_limit_bytes=8 * 2**20),
        name="factors",
    )(damping, *in_vmem(own_rows, sent_rows, own_columns, sent_columns))


def solution(mesh):
    in_specs = (
        P("mp", "ex", None),
        P("mp", "ex", None),
        P("mp", None, None),
        P("mp", None, None),
        P("mp", None, None),
        P("mp", None, None),
        P("mp", "ex", None),
        P(),
    )
    out_specs = (P(("ex", "mp"), None), P("mp", None, None))
    return jax.shard_map(
        local, mesh=mesh, in_specs=in_specs, out_specs=out_specs, check_vma=False
    )
```

```python
import functools
import math

import jax
import jax.numpy as jnp
from jax import lax
from jax.experimental import pallas as pl
from jax.experimental.pallas import tpu as pltpu
from jax.sharding import PartitionSpec as P

EXAMPLE_LENGTH = 8
LANES = 128
SLOT = 32
GROUP = LANES // SLOT
PANEL = 8
CHUNK = 1024


def dot_nt(a, b):
    return lax.dot_general(
        a, b, (((1,), (1,)), ((), ())), preferred_element_type=jnp.float32
    )


def dot_tn(a, b):
    return lax.dot_general(
        a, b, (((0,), (0,)), ((), ())), preferred_element_type=jnp.float32
    )


def split(x):
    high = x.astype(jnp.bfloat16)
    return high, (x - high.astype(jnp.float32)).astype(jnp.bfloat16)


def partial_kernel(
    parts,
    scaling,
    acts_hbm,
    grads_hbm,
    down_hbm,
    up_hbm,
    proj_in_hbm,
    proj_out_hbm,
    order_hbm,
    *refs,
):
    keep, give, acts, grads, weights_in, weights_out, order, low, out, sems, order_sem = refs
    tokens, width = acts.shape
    rank = down_hbm.shape[1]
    sketch = proj_in_hbm.shape[1]
    examples = tokens // EXAMPLE_LENGTH
    per = rank // parts
    halves = sketch // SLOT

    def copies(source, target, sem, start, size):
        return pltpu.make_async_copy(
            source.at[0, :, pl.ds(start, size)],
            target.at[:, pl.ds(start, size)],
            sem,
        )

    order_copy = pltpu.make_async_copy(order_hbm.at[0], order, order_sem)
    stages = []
    for start in range(0, width, CHUNK):
        stages.append(
            [
                (acts_hbm, acts, start),
                (proj_in_hbm, weights_in.at[pl.ds(0, sketch)], start),
                (down_hbm, weights_in.at[pl.ds(sketch, rank)], start),
            ]
        )
    for start in range(0, grads.shape[1], CHUNK):
        stages.append(
            [
                (grads_hbm, grads, start),
                (proj_out_hbm, weights_out.at[pl.ds(0, sketch)], start),
                (up_hbm, weights_out.at[pl.ds(sketch, rank)], start),
            ]
        )
    pending = [
        [
            copies(source, target, sems.at[n, i], start, CHUNK)
            for i, (source, target, start) in enumerate(stage)
        ]
        for n, stage in enumerate(stages)
    ]
    for stage in pending:
        for copy in stage:
            copy.start()
    order_copy.start()

    def product(first, rows, weights):
        total = None
        for n in range(rows.shape[1] // CHUNK):
            for copy in pending[first + n]:
                copy.wait()
            here = pl.ds(n * CHUNK, CHUNK)
            term = dot_nt(weights[:, here], rows[:, here])
            total = term if total is None else total + term
        return total

    from_acts = product(0, acts, weights_in)
    from_grads = product(width // CHUNK, grads, weights_out)
    order_copy.wait()
    sketches = jnp.concatenate([from_acts[:sketch], from_grads[:sketch]], axis=1)
    low[0] = from_grads[sketch:] * scaling
    low[1] = from_acts[sketch:] * scaling

    rows = examples * parts
    lane = lax.broadcasted_iota(jnp.int32, (rows, 2 * tokens), 1)
    source = (lane % tokens) // EXAMPLE_LENGTH
    target = jnp.zeros((8, 2 * tokens), jnp.int32)
    for s in range(examples):
        target = jnp.where(source[:8] == s, order[0, s], target)
    target = jnp.concatenate([target] * (rows // 8), axis=0)
    place = lax.broadcasted_iota(jnp.int32, (rows, 2 * tokens), 0) // parts
    mine = target == place
    highs, lows = [], []
    for c in range(per):
        chosen = jnp.concatenate(
            [low[i, pl.ds(c, parts, stride=per), :] for i in range(2)], axis=1
        )
        chosen = jnp.concatenate([chosen] * examples, axis=0)
        high, rest = split(jnp.where(mine, chosen, 0.0))
        highs.append(high)
        lows.append(rest)
    left_high = jnp.concatenate(highs, axis=0)
    left_low = jnp.concatenate(lows, axis=0)
    right = jnp.concatenate(
        [sketches[h * SLOT : (h + 1) * SLOT] for h in range(halves) for _ in range(per)],
        axis=0,
    )
    right_high, right_low = split(right)
    spread = (
        dot_nt(left_high, right_low) + dot_nt(left_low, right_high)
    ) + dot_nt(left_high, right_high)
    column = lax.broadcasted_iota(jnp.int32, (rows, per * sketch), 1)
    channel = (column // SLOT) % per
    total = spread[:rows]
    for c in range(1, per):
        total = jnp.where(channel == c, spread[c * rows : (c + 1) * rows], total)
    me = lax.axis_index("mp")
    odd = lax.axis_index("ex") % 2 == 1
    for start in range(0, per * sketch, LANES):
        stop = min(start + LANES, per * sketch)
        out[:, : stop - start] = total[:, start:stop]
        for d in range(parts):
            g = me ^ d
            by_row = out[pl.ds(pl.multiple_of(g * examples, examples), examples), :]
            by_column = out[pl.ds(g, examples, stride=parts), :]
            here = pl.ds(d * examples, examples)
            keep[here, start:stop] = jnp.where(odd, by_column, by_row)[:, : stop - start]
            give[here, start:stop] = jnp.where(odd, by_row, by_column)[:, : stop - start]


def pair_kernel(keep, got, *sends):
    rows = sends[0].shape[0] // 2
    for d, send in enumerate(sends):
        send[:rows, :] = keep[d * rows : (d + 1) * rows, :]
        send[rows:, :] = got[d * rows : (d + 1) * rows, :]


def sum_kernel(*refs):
    chunks, columns = refs[:-1], refs[-1]
    total = chunks[0][...]
    for chunk in chunks[1:]:
        total = total + chunk[...]
    width = total.shape[1]
    columns[:, :width] = total
    if columns.shape[1] > width:
        columns[:, width:] = jnp.zeros(
            (total.shape[0], columns.shape[1] - width), jnp.float32
        )


def stack_kernel(*refs):
    rows = refs[0].shape[0]
    for n, part in enumerate(refs[:-1]):
        refs[-1][n * rows : (n + 1) * rows, :] = part[...]


def write_features(total, parts, per, features):
    rows_here, width = features.shape
    span = width // parts
    halves = span // (per * SLOT)
    natural = jnp.concatenate(
        [
            total[:, (h * per + c) * SLOT : (h * per + c + 1) * SLOT]
            for c in range(per)
            for h in range(halves)
        ],
        axis=1,
    )
    for r in range(rows_here):
        features[r : r + 1, :] = jnp.concatenate(
            [natural[r * parts + g : r * parts + g + 1, :] for g in range(parts)], axis=1
        )


def pick_lanes(x, index):
    return jnp.take_along_axis(x, index, axis=1)


def reciprocal(x):
    guess = pl.reciprocal(x, approx=True)
    guess = guess * (2.0 - x * guess)
    return guess * (2.0 - x * guess)


def factor_kernel(
    parts, damping, own, sent, features, factors
):
    channels, sketch, _ = factors.shape
    odd = lax.axis_index("ex") % 2 == 1
    rows, width = features.shape[0] * parts, features.shape[1] // parts
    own_rows = jnp.where(odd, sent[rows : 2 * rows, :width], own[:rows, :width])
    write_features(own_rows, parts, channels, features)
    halves = sketch // SLOT
    panels = sketch // PANEL
    per_half = SLOT // PANEL
    stacked = jnp.where(odd, own[...], sent[...])
    examples = stacked.shape[0]
    high, rest = split(stacked)
    gram = (dot_tn(high, rest) + dot_tn(rest, high)) + dot_tn(high, high)
    lane = lax.broadcasted_iota(jnp.int32, (PANEL, LANES), 1)
    sub = lax.broadcasted_iota(jnp.int32, (PANEL, LANES), 0)
    slot = lane // SLOT
    within = lane % SLOT
    ridge = damping[0]
    tile = []
    for q in range(panels):
        hr, at = divmod(q, per_half)
        line = []
        for h in range(halves):
            value = None
            for c in range(GROUP):
                start = hr * LANES + c * SLOT + at * PANEL
                block = gram[start : start + PANEL, h * LANES : (h + 1) * LANES]
                value = block if c == 0 else jnp.where(slot == c, block, value)
            value = value * (1.0 / examples)
            if h == hr:
                value = value + jnp.where(within == at * PANEL + sub, ridge, 0.0)
            line.append(value)
        tile.append(line)

    zero = jnp.zeros((PANEL, LANES), jnp.float32)
    finished = []
    for q in range(panels):
        hq, at = divmod(q, per_half)
        column = [
            {
                j: pick_lanes(tile[j][hq], slot * SLOT + at * PANEL + r)
                for j in range(q, panels)
            }
            for r in range(PANEL)
        ]
        block = [
            [
                jnp.broadcast_to(column[r][q][s : s + 1, :], (PANEL, LANES))
                if s >= r
                else None
                for s in range(PANEL)
            ]
            for r in range(PANEL)
        ]
        line = [
            [
                jnp.broadcast_to(tile[q][h][r : r + 1, :], (PANEL, LANES))
                if h >= hq
                else None
                for h in range(halves)
            ]
            for r in range(PANEL)
        ]
        inverse = []
        for r in range(PANEL):
            inv = reciprocal(block[r][r])
            inverse.append(inv)
            for s in range(r + 1, PANEL):
                ratio = block[r][s] * inv
                for t in range(s, PANEL):
                    block[s][t] = block[s][t] - ratio * block[r][t]
                for j in range(q + 1, panels):
                    column[s][j] = column[s][j] - ratio * column[r][j]
                for h in range(hq, halves):
                    line[s][h] = line[s][h] - ratio * line[r][h]
        result = []
        for h in range(halves):
            if h < hq:
                result.append(zero)
                continue
            value = zero
            for r in range(PANEL):
                value = jnp.where(sub == r, line[r][h] * lax.rsqrt(block[r][r]), value)
            if h == hq:
                value = jnp.where(within >= at * PANEL + sub, value, 0.0)
            result.append(value)
        finished.append(result)
        for j in range(q + 1, panels):
            weights = [column[r][j] * inverse[r] for r in range(PANEL)]
            for h in range((q + 1) // per_half, halves):
                value = tile[j][h]
                for r in range(PANEL):
                    value = value - weights[r] * line[r][h]
                tile[j][h] = value

    for q in range(panels):
        for c in range(channels):
            factors[c, q * PANEL : (q + 1) * PANEL, :] = jnp.concatenate(
                [finished[q][h][:, c * SLOT : (c + 1) * SLOT] for h in range(halves)],
                axis=1,
            )


def exchange(x, axis, distance, part=None):
    return lax.ppermute(
        x,
        axis,
        [
            (i, i if part is not None and i % 2 != part else i ^ distance)
            for i in range(lax.axis_size(axis))
        ],
    )


def small_call(kernel, name, outs, *args):
    return pl.pallas_call(
        kernel,
        out_shape=[pltpu.VMEM(shape, jnp.float32) for shape in outs],
        in_specs=[vmem()] * len(args),
        out_specs=[vmem()] * len(outs),
        compiler_params=pltpu.CompilerParams(vmem_limit_bytes=2 * 2**20),
        name=name,
    )(*in_vmem(*args))


def vmem():
    return pl.BlockSpec(memory_space=pltpu.VMEM)


def hbm():
    return pl.BlockSpec(memory_space=pltpu.HBM)


def in_hbm(*arrays):
    return [pltpu.with_memory_space_constraint(x, pltpu.HBM) for x in arrays]


def in_vmem(*arrays):
    return [pltpu.with_memory_space_constraint(x, pltpu.VMEM) for x in arrays]


def smem():
    return pl.BlockSpec(memory_space=pltpu.SMEM)


def local(
    acts,
    grads,
    down_factor,
    up_factor_transposed,
    input_projection,
    gradient_projection,
    order,
    damping,
):
    parts = lax.axis_size("mp")
    shards = lax.axis_size("ex")
    tokens, width = acts.shape[1:]
    key_width = grads.shape[2]
    rank = down_factor.shape[1]
    sketch = input_projection.shape[1]
    examples = tokens // EXAMPLE_LENGTH
    per = rank // parts
    span = per * sketch
    scaling = 1.0 / math.sqrt(2.0 * EXAMPLE_LENGTH * parts)
    keep, give = pl.pallas_call(
        functools.partial(partial_kernel, parts, scaling),
        out_shape=[pltpu.VMEM((parts * examples, span), jnp.float32)] * 2,
        in_specs=[hbm()] * 7,
        out_specs=[vmem()] * 2,
        scratch_shapes=[
            pltpu.VMEM((tokens, width), acts.dtype),
            pltpu.VMEM((tokens, key_width), grads.dtype),
            pltpu.VMEM((sketch + rank, width), acts.dtype),
            pltpu.VMEM((sketch + rank, key_width), grads.dtype),
            pltpu.SMEM(order.shape[1:], order.dtype),
            pltpu.VMEM((2, rank, tokens), jnp.float32),
            pltpu.VMEM((examples * parts, LANES), jnp.float32),
            pltpu.SemaphoreType.DMA(((width + key_width) // CHUNK, 3)),
            pltpu.SemaphoreType.DMA,
        ],
        compiler_params=pltpu.CompilerParams(vmem_limit_bytes=8 * 2**20),
        name="partials",
    )(
        *in_hbm(
            acts,
            grads,
            down_factor,
            up_factor_transposed,
            input_projection,
            gradient_projection,
            order,
        )
    )
    got = exchange(give, "ex", 1)
    sends = small_call(
        pair_kernel, "pair", [(2 * examples, span)] * parts, keep, got
    )
    chunks = [sends[0]] + [exchange(sends[d], "mp", d) for d in range(parts - 1, 0, -1)]
    padded = max(span, GROUP * sketch)
    (columns,) = small_call(sum_kernel, "sums", [(2 * examples, padded)], *chunks)
    near = [columns] + [exchange(columns, "ex", d, 1) for d in range(2, shards, 2)]
    (own,) = small_call(stack_kernel, "stack", [(shards * examples, padded)], *near)
    sent = exchange(own, "ex", 1)
    return pl.pallas_call(
        functools.partial(factor_kernel, parts),
        out_shape=[
            jax.ShapeDtypeStruct((examples // parts, rank * sketch), jnp.float32),
            jax.ShapeDtypeStruct((per, sketch, sketch), jnp.float32),
        ],
        in_specs=[smem()] + [vmem()] * 2,
        out_specs=[vmem()] * 2,
        compiler_params=pltpu.CompilerParams(vmem_limit_bytes=8 * 2**20),
        name="factors",
    )(damping, *in_vmem(own, sent))


def solution(mesh):
    in_specs = (
        P("mp", "ex", None),
        P("mp", "ex", None),
        P("mp", None, None),
        P("mp", None, None),
        P("mp", None, None),
        P("mp", None, None),
        P("mp", "ex", None),
        P(),
    )
    out_specs = (P(("ex", "mp"), None), P("mp", None, None))
    return jax.shard_map(
        local, mesh=mesh, in_specs=in_specs, out_specs=out_specs, check_vma=False
    )
```

```python
import functools
import math

import jax
import jax.numpy as jnp
from jax import lax
from jax.experimental import pallas as pl
from jax.experimental.pallas import tpu as pltpu
from jax.sharding import PartitionSpec as P

EXAMPLE_LENGTH = 8
LANES = 128
SLOT = 32
GROUP = LANES // SLOT
PANEL = 8
CHUNK = 1024


def dot_nt(a, b):
    return lax.dot_general(
        a, b, (((1,), (1,)), ((), ())), preferred_element_type=jnp.float32
    )


def dot_tn(a, b):
    return lax.dot_general(
        a, b, (((0,), (0,)), ((), ())), preferred_element_type=jnp.float32
    )


def split(x):
    high = x.astype(jnp.bfloat16)
    return high, (x - high.astype(jnp.float32)).astype(jnp.bfloat16)


def partial_kernel(
    parts,
    scaling,
    acts_hbm,
    grads_hbm,
    down_hbm,
    up_hbm,
    proj_in_hbm,
    proj_out_hbm,
    order_hbm,
    *refs,
):
    sends, refs = refs[:parts], refs[parts:]
    acts, grads, weights_in, weights_out, order, low, mask, out, sems, order_sem = refs
    tokens, width = acts.shape
    rank = down_hbm.shape[1]
    sketch = proj_in_hbm.shape[1]
    examples = tokens // EXAMPLE_LENGTH
    per = rank // parts
    halves = sketch // SLOT

    def copies(source, target, sem, start, size):
        return pltpu.make_async_copy(
            source.at[0, :, pl.ds(start, size)],
            target.at[:, pl.ds(start, size)],
            sem,
        )

    order_copy = pltpu.make_async_copy(order_hbm.at[0], order, order_sem)
    order_copy.start()
    sources = [
        (grads_hbm, grads, proj_out_hbm, up_hbm, weights_out),
        (acts_hbm, acts, proj_in_hbm, down_hbm, weights_in),
    ]
    pending = []
    for data_hbm, data, first_hbm, second_hbm, weights in sources:
        for start in range(0, data.shape[1], CHUNK):
            n = len(pending)
            pending.append(
                [
                    copies(first_hbm, weights.at[pl.ds(0, sketch)], sems.at[n, 0], start, CHUNK),
                    copies(second_hbm, weights.at[pl.ds(sketch, rank)], sems.at[n, 1], start, CHUNK),
                    copies(data_hbm, data, sems.at[n, 2], start, CHUNK),
                ]
            )
            for copy in pending[-1]:
                copy.start()

    order_copy.wait()
    rows = examples * parts
    lane = lax.broadcasted_iota(jnp.int32, (rows, 2 * tokens), 1)
    source = (lane % tokens) // EXAMPLE_LENGTH
    target = jnp.zeros((8, 2 * tokens), jnp.int32)
    for s in range(examples):
        target = jnp.where(source[:8] == s, order[0, s], target)
    target = jnp.concatenate([target] * (rows // 8), axis=0)
    place = lax.broadcasted_iota(jnp.int32, (rows, 2 * tokens), 0) // parts
    mask[...] = jnp.where(target == place, scaling, 0.0)

    def product(first, data, weights):
        total = None
        for n in range(data.shape[1] // CHUNK):
            for copy in pending[first + n]:
                copy.wait()
            here = pl.ds(n * CHUNK, CHUNK)
            term = dot_nt(weights[:, here], data[:, here])
            total = term if total is None else total + term
        return total

    from_grads = product(0, grads, weights_out)
    from_acts = product(grads.shape[1] // CHUNK, acts, weights_in)
    sketches = jnp.concatenate([from_acts[:sketch], from_grads[:sketch]], axis=1)
    low[0] = from_grads[sketch:]
    low[1] = from_acts[sketch:]

    highs, lows = [], []
    for c in range(per):
        chosen = jnp.concatenate(
            [low[i, pl.ds(c, parts, stride=per), :] for i in range(2)], axis=1
        )
        chosen = jnp.concatenate([chosen] * examples, axis=0)
        high, rest = split(chosen * mask[...])
        highs.append(high)
        lows.append(rest)
    left_high = jnp.concatenate(highs, axis=0)
    left_low = jnp.concatenate(lows, axis=0)
    right = jnp.concatenate(
        [sketches[h * SLOT : (h + 1) * SLOT] for h in range(halves) for _ in range(per)],
        axis=0,
    )
    right_high, right_low = split(right)
    spread = (
        dot_nt(left_high, right_low) + dot_nt(left_low, right_high)
    ) + dot_nt(left_high, right_high)
    column = lax.broadcasted_iota(jnp.int32, (rows, per * sketch), 1)
    channel = (column // SLOT) % per
    total = spread[:rows]
    for c in range(1, per):
        total = jnp.where(channel == c, spread[c * rows : (c + 1) * rows], total)
    me = lax.axis_index("mp")
    for start in range(0, per * sketch, LANES):
        stop = min(start + LANES, per * sketch)
        out[:, : stop - start] = total[:, start:stop]
        for d in range(parts):
            g = me ^ d
            sends[d][:examples, start:stop] = out[
                pl.ds(pl.multiple_of(g * examples, examples), examples), : stop - start
            ]
            sends[d][examples:, start:stop] = out[pl.ds(g, examples, stride=parts), :][
                :, : stop - start
            ]


def column_kernel(*refs):
    chunks, columns = refs[:-1], refs[-1]
    examples, padded = columns.shape
    total = chunks[0][examples:, :]
    for chunk in chunks[1:]:
        total = total + chunk[examples:, :]
    width = total.shape[1]
    columns[:, :width] = total
    if padded > width:
        columns[:, width:] = jnp.zeros((examples, padded - width), jnp.float32)


def stack_kernel(*refs):
    rows = refs[0].shape[0]
    for n, part in enumerate(refs[:-1]):
        refs[-1][n * rows : (n + 1) * rows, :] = part[...]


def write_features(chunks, per, features):
    parts = len(chunks)
    rows_here, width = features.shape
    examples = rows_here * parts
    total = chunks[0][:examples, :]
    for chunk in chunks[1:]:
        total = total + chunk[:examples, :]
    span = width // parts
    halves = span // (per * SLOT)
    natural = jnp.concatenate(
        [
            total[:, (h * per + c) * SLOT : (h * per + c + 1) * SLOT]
            for c in range(per)
            for h in range(halves)
        ],
        axis=1,
    )
    for r in range(rows_here):
        features[r : r + 1, :] = jnp.concatenate(
            [natural[r * parts + g : r * parts + g + 1, :] for g in range(parts)], axis=1
        )


def pick_lanes(x, index):
    return jnp.take_along_axis(x, index, axis=1)


def reciprocal(x):
    guess = pl.reciprocal(x, approx=True)
    guess = guess * (2.0 - x * guess)
    return guess * (2.0 - x * guess)


def factor_kernel(parts, damping, *refs):
    chunks, rows, (features, factors) = refs[:parts], refs[parts:-2], refs[-2:]
    channels, sketch, _ = factors.shape
    write_features(chunks, channels, features)
    halves = sketch // SLOT
    panels = sketch // PANEL
    per_half = SLOT // PANEL
    stacked = jnp.concatenate([part[...] for part in rows], axis=0)
    examples = stacked.shape[0]
    high, rest = split(stacked)
    gram = (dot_tn(high, rest) + dot_tn(rest, high)) + dot_tn(high, high)
    lane = lax.broadcasted_iota(jnp.int32, (PANEL, LANES), 1)
    sub = lax.broadcasted_iota(jnp.int32, (PANEL, LANES), 0)
    slot = lane // SLOT
    within = lane % SLOT
    ridge = damping[0]
    tile = []
    for q in range(panels):
        hr, at = divmod(q, per_half)
        line = []
        for h in range(halves):
            value = None
            for c in range(GROUP):
                start = hr * LANES + c * SLOT + at * PANEL
                block = gram[start : start + PANEL, h * LANES : (h + 1) * LANES]
                value = block if c == 0 else jnp.where(slot == c, block, value)
            value = value * (1.0 / examples)
            if h == hr:
                value = value + jnp.where(within == at * PANEL + sub, ridge, 0.0)
            line.append(value)
        tile.append(line)

    zero = jnp.zeros((PANEL, LANES), jnp.float32)
    finished = []
    for q in range(panels):
        hq, at = divmod(q, per_half)
        column = [
            {
                j: pick_lanes(tile[j][hq], slot * SLOT + at * PANEL + r)
                for j in range(q, panels)
            }
            for r in range(PANEL)
        ]
        block = [
            [
                jnp.broadcast_to(column[r][q][s : s + 1, :], (PANEL, LANES))
                if s >= r
                else None
                for s in range(PANEL)
            ]
            for r in range(PANEL)
        ]
        line = [
            [
                jnp.broadcast_to(tile[q][h][r : r + 1, :], (PANEL, LANES))
                if h >= hq
                else None
                for h in range(halves)
            ]
            for r in range(PANEL)
        ]
        inverse = []
        for r in range(PANEL):
            inv = reciprocal(block[r][r])
            inverse.append(inv)
            for s in range(r + 1, PANEL):
                ratio = block[r][s] * inv
                for t in range(s, PANEL):
                    block[s][t] = block[s][t] - ratio * block[r][t]
                for j in range(q + 1, panels):
                    column[s][j] = column[s][j] - ratio * column[r][j]
                for h in range(hq, halves):
                    line[s][h] = line[s][h] - ratio * line[r][h]
        result = []
        for h in range(halves):
            if h < hq:
                result.append(zero)
                continue
            value = zero
            for r in range(PANEL):
                value = jnp.where(sub == r, line[r][h] * lax.rsqrt(block[r][r]), value)
            if h == hq:
                value = jnp.where(within >= at * PANEL + sub, value, 0.0)
            result.append(value)
        finished.append(result)
        for j in range(q + 1, panels):
            weights = [column[r][j] * inverse[r] for r in range(PANEL)]
            for h in range((q + 1) // per_half, halves):
                value = tile[j][h]
                for r in range(PANEL):
                    value = value - weights[r] * line[r][h]
                tile[j][h] = value

    for q in range(panels):
        for c in range(channels):
            factors[c, q * PANEL : (q + 1) * PANEL, :] = jnp.concatenate(
                [finished[q][h][:, c * SLOT : (c + 1) * SLOT] for h in range(halves)],
                axis=1,
            )


def exchange(x, axis, distance):
    size = lax.axis_size(axis)
    return lax.ppermute(x, axis, [(i, i ^ distance) for i in range(size)])


def vmem():
    return pl.BlockSpec(memory_space=pltpu.VMEM)


def hbm():
    return pl.BlockSpec(memory_space=pltpu.HBM)


def in_hbm(*arrays):
    return [pltpu.with_memory_space_constraint(x, pltpu.HBM) for x in arrays]


def in_vmem(*arrays):
    return [pltpu.with_memory_space_constraint(x, pltpu.VMEM) for x in arrays]


def smem():
    return pl.BlockSpec(memory_space=pltpu.SMEM)


def local(
    acts,
    grads,
    down_factor,
    up_factor_transposed,
    input_projection,
    gradient_projection,
    order,
    damping,
):
    parts = lax.axis_size("mp")
    shards = lax.axis_size("ex")
    tokens, width = acts.shape[1:]
    key_width = grads.shape[2]
    rank = down_factor.shape[1]
    sketch = input_projection.shape[1]
    examples = tokens // EXAMPLE_LENGTH
    per = rank // parts
    span = per * sketch
    scaling = 1.0 / math.sqrt(2.0 * EXAMPLE_LENGTH * parts)
    sends = pl.pallas_call(
        functools.partial(partial_kernel, parts, scaling),
        out_shape=[pltpu.VMEM((2 * examples, span), jnp.float32)] * parts,
        in_specs=[hbm()] * 7,
        out_specs=[vmem()] * parts,
        scratch_shapes=[
            pltpu.VMEM((tokens, width), acts.dtype),
            pltpu.VMEM((tokens, key_width), grads.dtype),
            pltpu.VMEM((sketch + rank, width), acts.dtype),
            pltpu.VMEM((sketch + rank, key_width), grads.dtype),
            pltpu.SMEM(order.shape[1:], order.dtype),
            pltpu.VMEM((2, rank, tokens), jnp.float32),
            pltpu.VMEM((examples * parts, 2 * tokens), jnp.float32),
            pltpu.VMEM((examples * parts, LANES), jnp.float32),
            pltpu.SemaphoreType.DMA(((width + key_width) // CHUNK, 3)),
            pltpu.SemaphoreType.DMA,
        ],
        compiler_params=pltpu.CompilerParams(vmem_limit_bytes=8 * 2**20),
        name="partials",
    )(
        *in_hbm(
            acts,
            grads,
            down_factor,
            up_factor_transposed,
            input_projection,
            gradient_projection,
            order,
        )
    )
    chunks = [sends[0]] + [exchange(sends[d], "mp", d) for d in range(parts - 1, 0, -1)]
    columns = pl.pallas_call(
        column_kernel,
        out_shape=pltpu.VMEM((examples, max(span, GROUP * sketch)), jnp.float32),
        in_specs=[vmem()] * parts,
        out_specs=vmem(),
        compiler_params=pltpu.CompilerParams(vmem_limit_bytes=2 * 2**20),
        name="columns",
    )(*in_vmem(*chunks))
    near = [columns] + [exchange(columns, "ex", d) for d in range(2, shards, 2)]
    gathered = pl.pallas_call(
        stack_kernel,
        out_shape=pltpu.VMEM((len(near) * examples, columns.shape[1]), jnp.float32),
        in_specs=[vmem()] * len(near),
        out_specs=vmem(),
        compiler_params=pltpu.CompilerParams(vmem_limit_bytes=2 * 2**20),
        name="stack",
    )(*in_vmem(*near))
    rows = [gathered, exchange(gathered, "ex", 1)]
    return pl.pallas_call(
        functools.partial(factor_kernel, parts),
        out_shape=[
            jax.ShapeDtypeStruct((examples // parts, rank * sketch), jnp.float32),
            jax.ShapeDtypeStruct((per, sketch, sketch), jnp.float32),
        ],
        in_specs=[smem()] + [vmem()] * (parts + len(rows)),
        out_specs=[vmem()] * 2,
        compiler_params=pltpu.CompilerParams(vmem_limit_bytes=8 * 2**20),
        name="factors",
    )(damping, *in_vmem(*chunks, *rows))


def solution(mesh):
    in_specs = (
        P("mp", "ex", None),
        P("mp", "ex", None),
        P("mp", None, None),
        P("mp", None, None),
        P("mp", None, None),
        P("mp", None, None),
        P("mp", "ex", None),
        P(),
    )
    out_specs = (P(("ex", "mp"), None), P("mp", None, None))
    return jax.shard_map(
        local, mesh=mesh, in_specs=in_specs, out_specs=out_specs, check_vma=False
    )
```

```python
import functools
import math

import jax
import jax.numpy as jnp
from jax import lax
from jax.experimental import pallas as pl
from jax.experimental.pallas import tpu as pltpu
from jax.sharding import PartitionSpec as P

EXAMPLE_LENGTH = 8
LANES = 128
SLOT = 32
GROUP = LANES // SLOT
PANEL = 8
CHUNK = 1024


def dot_nt(a, b):
    return lax.dot_general(
        a, b, (((1,), (1,)), ((), ())), preferred_element_type=jnp.float32
    )


def dot_tn(a, b):
    return lax.dot_general(
        a, b, (((0,), (0,)), ((), ())), preferred_element_type=jnp.float32
    )


def split(x):
    high = x.astype(jnp.bfloat16)
    return high, (x - high.astype(jnp.float32)).astype(jnp.bfloat16)


def partial_kernel(
    parts,
    scaling,
    acts_hbm,
    grads_hbm,
    down_hbm,
    up_hbm,
    proj_in_hbm,
    proj_out_hbm,
    order_hbm,
    *refs,
):
    sends, refs = refs[:parts], refs[parts:]
    acts, grads, weights_in, weights_out, order, low, mask, out, sems, order_sem = refs
    tokens, width = acts.shape
    rank = down_hbm.shape[1]
    sketch = proj_in_hbm.shape[1]
    examples = tokens // EXAMPLE_LENGTH
    per = rank // parts
    halves = sketch // SLOT

    def copies(source, target, sem, start, size):
        return pltpu.make_async_copy(
            source.at[0, :, pl.ds(start, size)],
            target.at[:, pl.ds(start, size)],
            sem,
        )

    order_copy = pltpu.make_async_copy(order_hbm.at[0], order, order_sem)
    order_copy.start()
    sources = [
        (grads_hbm, grads, proj_out_hbm, up_hbm, weights_out),
        (acts_hbm, acts, proj_in_hbm, down_hbm, weights_in),
    ]
    pending = []
    for data_hbm, data, first_hbm, second_hbm, weights in sources:
        for start in range(0, data.shape[1], CHUNK):
            n = len(pending)
            pending.append(
                [
                    copies(first_hbm, weights.at[pl.ds(0, sketch)], sems.at[n, 0], start, CHUNK),
                    copies(second_hbm, weights.at[pl.ds(sketch, rank)], sems.at[n, 1], start, CHUNK),
                    copies(data_hbm, data, sems.at[n, 2], start, CHUNK),
                ]
            )
            for copy in pending[-1]:
                copy.start()

    order_copy.wait()
    rows = examples * parts
    lane = lax.broadcasted_iota(jnp.int32, (rows, 2 * tokens), 1)
    source = (lane % tokens) // EXAMPLE_LENGTH
    target = jnp.zeros((8, 2 * tokens), jnp.int32)
    for s in range(examples):
        target = jnp.where(source[:8] == s, order[0, s], target)
    target = jnp.concatenate([target] * (rows // 8), axis=0)
    place = lax.broadcasted_iota(jnp.int32, (rows, 2 * tokens), 0) // parts
    mask[...] = jnp.where(target == place, scaling, 0.0)

    def product(first, data, weights):
        total = None
        for n in range(data.shape[1] // CHUNK):
            for copy in pending[first + n]:
                copy.wait()
            here = pl.ds(n * CHUNK, CHUNK)
            term = dot_nt(weights[:, here], data[:, here])
            total = term if total is None else total + term
        return total

    from_grads = product(0, grads, weights_out)
    from_acts = product(grads.shape[1] // CHUNK, acts, weights_in)
    sketches = jnp.concatenate([from_acts[:sketch], from_grads[:sketch]], axis=1)
    low[0] = from_grads[sketch:]
    low[1] = from_acts[sketch:]

    highs, lows = [], []
    for c in range(per):
        chosen = jnp.concatenate(
            [low[i, pl.ds(c, parts, stride=per), :] for i in range(2)], axis=1
        )
        chosen = jnp.concatenate([chosen] * examples, axis=0)
        high, rest = split(chosen * mask[...])
        highs.append(high)
        lows.append(rest)
    left_high = jnp.concatenate(highs, axis=0)
    left_low = jnp.concatenate(lows, axis=0)
    right = jnp.concatenate(
        [sketches[h * SLOT : (h + 1) * SLOT] for h in range(halves) for _ in range(per)],
        axis=0,
    )
    right_high, right_low = split(right)
    spread = (
        dot_nt(left_high, right_low) + dot_nt(left_low, right_high)
    ) + dot_nt(left_high, right_high)
    column = lax.broadcasted_iota(jnp.int32, (rows, per * sketch), 1)
    channel = (column // SLOT) % per
    total = spread[:rows]
    for c in range(1, per):
        total = jnp.where(channel == c, spread[c * rows : (c + 1) * rows], total)
    me = lax.axis_index("mp")
    for start in range(0, per * sketch, LANES):
        stop = min(start + LANES, per * sketch)
        out[:, : stop - start] = total[:, start:stop]
        for d in range(parts):
            g = me ^ d
            sends[d][:examples, start:stop] = out[
                pl.ds(pl.multiple_of(g * examples, examples), examples), : stop - start
            ]
            sends[d][examples:, start:stop] = out[pl.ds(g, examples, stride=parts), :][
                :, : stop - start
            ]


def column_kernel(*refs):
    chunks, columns = refs[:-1], refs[-1]
    examples, padded = columns.shape
    total = chunks[0][examples:, :]
    for chunk in chunks[1:]:
        total = total + chunk[examples:, :]
    width = total.shape[1]
    columns[:, :width] = total
    if padded > width:
        columns[:, width:] = jnp.zeros((examples, padded - width), jnp.float32)


def stack_kernel(*refs):
    rows = refs[0].shape[0]
    for n, part in enumerate(refs[:-1]):
        refs[-1][n * rows : (n + 1) * rows, :] = part[...]


def write_features(chunks, per, features):
    parts = len(chunks)
    rows_here, width = features.shape
    examples = rows_here * parts
    total = chunks[0][:examples, :]
    for chunk in chunks[1:]:
        total = total + chunk[:examples, :]
    span = width // parts
    halves = span // (per * SLOT)
    natural = jnp.concatenate(
        [
            total[:, (h * per + c) * SLOT : (h * per + c + 1) * SLOT]
            for c in range(per)
            for h in range(halves)
        ],
        axis=1,
    )
    for r in range(rows_here):
        features[r : r + 1, :] = jnp.concatenate(
            [natural[r * parts + g : r * parts + g + 1, :] for g in range(parts)], axis=1
        )


def pick_lanes(x, index):
    return jnp.take_along_axis(x, index, axis=1)


def reciprocal(x):
    guess = pl.reciprocal(x, approx=True)
    return guess * (2.0 - x * guess)


def factor_kernel(parts, damping, *refs):
    chunks, rows, (features, factors) = refs[:parts], refs[parts:-2], refs[-2:]
    channels, sketch, _ = factors.shape
    write_features(chunks, channels, features)
    halves = sketch // SLOT
    panels = sketch // PANEL
    per_half = SLOT // PANEL
    stacked = jnp.concatenate([part[...] for part in rows], axis=0)
    examples = stacked.shape[0]
    high, rest = split(stacked)
    gram = (dot_tn(high, rest) + dot_tn(rest, high)) + dot_tn(high, high)
    lane = lax.broadcasted_iota(jnp.int32, (PANEL, LANES), 1)
    sub = lax.broadcasted_iota(jnp.int32, (PANEL, LANES), 0)
    slot = lane // SLOT
    within = lane % SLOT
    ridge = damping[0]
    tile = []
    for q in range(panels):
        hr, at = divmod(q, per_half)
        line = []
        for h in range(halves):
            value = None
            for c in range(GROUP):
                start = hr * LANES + c * SLOT + at * PANEL
                block = gram[start : start + PANEL, h * LANES : (h + 1) * LANES]
                value = block if c == 0 else jnp.where(slot == c, block, value)
            value = value * (1.0 / examples)
            if h == hr:
                value = value + jnp.where(within == at * PANEL + sub, ridge, 0.0)
            line.append(value)
        tile.append(line)

    zero = jnp.zeros((PANEL, LANES), jnp.float32)
    finished = []
    for q in range(panels):
        hq, at = divmod(q, per_half)
        column = [
            {
                j: pick_lanes(tile[j][hq], slot * SLOT + at * PANEL + r)
                for j in range(q, panels)
            }
            for r in range(PANEL)
        ]
        block = [
            [
                jnp.broadcast_to(column[r][q][s : s + 1, :], (PANEL, LANES))
                if s >= r
                else None
                for s in range(PANEL)
            ]
            for r in range(PANEL)
        ]
        line = [
            [
                jnp.broadcast_to(tile[q][h][r : r + 1, :], (PANEL, LANES))
                if h >= hq
                else None
                for h in range(halves)
            ]
            for r in range(PANEL)
        ]
        inverse = []

        def eliminate(r, s, inv):
            ratio = block[r][s] * inv
            for t in range(s, PANEL):
                block[s][t] = block[s][t] - ratio * block[r][t]
            for j in range(q + 1, panels):
                column[s][j] = column[s][j] - ratio * column[r][j]
            for h in range(hq, halves):
                line[s][h] = line[s][h] - ratio * line[r][h]

        for r in range(0, PANEL, 2):
            pivot = block[r][r]
            minor = pivot * block[r + 1][r + 1] - block[r][r + 1] * block[r][r + 1]
            inverse.append(reciprocal(pivot))
            inverse.append(pivot * reciprocal(minor))
            eliminate(r, r + 1, inverse[r])
            for s in range(r + 2, PANEL):
                eliminate(r, s, inverse[r])
                eliminate(r + 1, s, inverse[r + 1])
        result = []
        for h in range(halves):
            if h < hq:
                result.append(zero)
                continue
            value = zero
            for r in range(PANEL):
                value = jnp.where(sub == r, line[r][h] * lax.rsqrt(block[r][r]), value)
            if h == hq:
                value = jnp.where(within >= at * PANEL + sub, value, 0.0)
            result.append(value)
        finished.append(result)
        for j in range(q + 1, panels):
            weights = [column[r][j] * inverse[r] for r in range(PANEL)]
            for h in range((q + 1) // per_half, halves):
                value = tile[j][h]
                for r in range(PANEL):
                    value = value - weights[r] * line[r][h]
                tile[j][h] = value

    for q in range(panels):
        for c in range(channels):
            factors[c, q * PANEL : (q + 1) * PANEL, :] = jnp.concatenate(
                [finished[q][h][:, c * SLOT : (c + 1) * SLOT] for h in range(halves)],
                axis=1,
            )


def exchange(x, axis, distance):
    size = lax.axis_size(axis)
    return lax.ppermute(x, axis, [(i, i ^ distance) for i in range(size)])


def vmem():
    return pl.BlockSpec(memory_space=pltpu.VMEM)


def hbm():
    return pl.BlockSpec(memory_space=pltpu.HBM)


def in_hbm(*arrays):
    return [pltpu.with_memory_space_constraint(x, pltpu.HBM) for x in arrays]


def in_vmem(*arrays):
    return [pltpu.with_memory_space_constraint(x, pltpu.VMEM) for x in arrays]


def smem():
    return pl.BlockSpec(memory_space=pltpu.SMEM)


def local(
    acts,
    grads,
    down_factor,
    up_factor_transposed,
    input_projection,
    gradient_projection,
    order,
    damping,
):
    parts = lax.axis_size("mp")
    shards = lax.axis_size("ex")
    tokens, width = acts.shape[1:]
    key_width = grads.shape[2]
    rank = down_factor.shape[1]
    sketch = input_projection.shape[1]
    examples = tokens // EXAMPLE_LENGTH
    per = rank // parts
    span = per * sketch
    scaling = 1.0 / math.sqrt(2.0 * EXAMPLE_LENGTH * parts)
    sends = pl.pallas_call(
        functools.partial(partial_kernel, parts, scaling),
        out_shape=[pltpu.VMEM((2 * examples, span), jnp.float32)] * parts,
        in_specs=[hbm()] * 7,
        out_specs=[vmem()] * parts,
        scratch_shapes=[
            pltpu.VMEM((tokens, width), acts.dtype),
            pltpu.VMEM((tokens, key_width), grads.dtype),
            pltpu.VMEM((sketch + rank, width), acts.dtype),
            pltpu.VMEM((sketch + rank, key_width), grads.dtype),
            pltpu.SMEM(order.shape[1:], order.dtype),
            pltpu.VMEM((2, rank, tokens), jnp.float32),
            pltpu.VMEM((examples * parts, 2 * tokens), jnp.float32),
            pltpu.VMEM((examples * parts, LANES), jnp.float32),
            pltpu.SemaphoreType.DMA(((width + key_width) // CHUNK, 3)),
            pltpu.SemaphoreType.DMA,
        ],
        compiler_params=pltpu.CompilerParams(vmem_limit_bytes=8 * 2**20),
        name="partials",
    )(
        *in_hbm(
            acts,
            grads,
            down_factor,
            up_factor_transposed,
            input_projection,
            gradient_projection,
            order,
        )
    )
    chunks = [sends[0]] + [exchange(sends[d], "mp", d) for d in range(parts - 1, 0, -1)]
    columns = pl.pallas_call(
        column_kernel,
        out_shape=pltpu.VMEM((examples, max(span, GROUP * sketch)), jnp.float32),
        in_specs=[vmem()] * parts,
        out_specs=vmem(),
        compiler_params=pltpu.CompilerParams(vmem_limit_bytes=2 * 2**20),
        name="columns",
    )(*in_vmem(*chunks))
    near = [columns] + [exchange(columns, "ex", d) for d in range(3, shards, 2)]
    gathered = pl.pallas_call(
        stack_kernel,
        out_shape=pltpu.VMEM((len(near) * examples, columns.shape[1]), jnp.float32),
        in_specs=[vmem()] * len(near),
        out_specs=vmem(),
        compiler_params=pltpu.CompilerParams(vmem_limit_bytes=2 * 2**20),
        name="stack",
    )(*in_vmem(*near))
    rows = [gathered, exchange(gathered, "ex", 1)]
    return pl.pallas_call(
        functools.partial(factor_kernel, parts),
        out_shape=[
            jax.ShapeDtypeStruct((examples // parts, rank * sketch), jnp.float32),
            jax.ShapeDtypeStruct((per, sketch, sketch), jnp.float32),
        ],
        in_specs=[smem()] + [vmem()] * (parts + len(rows)),
        out_specs=[vmem()] * 2,
        compiler_params=pltpu.CompilerParams(vmem_limit_bytes=8 * 2**20),
        name="factors",
    )(damping, *in_vmem(*chunks, *rows))


def solution(mesh):
    in_specs = (
        P("mp", "ex", None),
        P("mp", "ex", None),
        P("mp", None, None),
        P("mp", None, None),
        P("mp", None, None),
        P("mp", None, None),
        P("mp", "ex", None),
        P(),
    )
    out_specs = (P(("ex", "mp"), None), P("mp", None, None))
    return jax.shard_map(
        local, mesh=mesh, in_specs=in_specs, out_specs=out_specs, check_vma=False
    )
```

```python
import functools
import math

import jax
import jax.numpy as jnp
from jax import lax
from jax.experimental import pallas as pl
from jax.experimental.pallas import tpu as pltpu
from jax.sharding import PartitionSpec as P

EXAMPLE_LENGTH = 8
LANES = 128
SLOT = 32
GROUP = LANES // SLOT
PANEL = 8
CHUNK = 1024


def dot_nt(a, b):
    return lax.dot_general(
        a, b, (((1,), (1,)), ((), ())), preferred_element_type=jnp.float32
    )


def dot_tn(a, b):
    return lax.dot_general(
        a, b, (((0,), (0,)), ((), ())), preferred_element_type=jnp.float32
    )


def split(x):
    high = x.astype(jnp.bfloat16)
    return high, (x - high.astype(jnp.float32)).astype(jnp.bfloat16)


def partial_kernel(
    parts,
    scaling,
    acts_hbm,
    grads_hbm,
    down_hbm,
    up_hbm,
    proj_in_hbm,
    proj_out_hbm,
    order_hbm,
    *refs,
):
    sends, refs = refs[:parts], refs[parts:]
    acts, grads, weights_in, weights_out, order, low, mask, out, sems, order_sem = refs
    tokens, width = acts.shape
    rank = down_hbm.shape[1]
    sketch = proj_in_hbm.shape[1]
    examples = tokens // EXAMPLE_LENGTH
    per = rank // parts
    halves = sketch // SLOT

    def copies(source, target, sem, start, size):
        return pltpu.make_async_copy(
            source.at[0, :, pl.ds(start, size)],
            target.at[:, pl.ds(start, size)],
            sem,
        )

    order_copy = pltpu.make_async_copy(order_hbm.at[0], order, order_sem)
    order_copy.start()
    sources = [
        (grads_hbm, grads, proj_out_hbm, up_hbm, weights_out),
        (acts_hbm, acts, proj_in_hbm, down_hbm, weights_in),
    ]
    pending = []
    for data_hbm, data, first_hbm, second_hbm, weights in sources:
        for start in range(0, data.shape[1], CHUNK):
            n = len(pending)
            pending.append(
                [
                    copies(first_hbm, weights.at[pl.ds(0, sketch)], sems.at[n, 0], start, CHUNK),
                    copies(second_hbm, weights.at[pl.ds(sketch, rank)], sems.at[n, 1], start, CHUNK),
                    copies(data_hbm, data, sems.at[n, 2], start, CHUNK),
                ]
            )
            for copy in pending[-1]:
                copy.start()

    order_copy.wait()
    rows = examples * parts
    lane = lax.broadcasted_iota(jnp.int32, (rows, 2 * tokens), 1)
    source = (lane % tokens) // EXAMPLE_LENGTH
    target = jnp.zeros((8, 2 * tokens), jnp.int32)
    for s in range(examples):
        target = jnp.where(source[:8] == s, order[0, s], target)
    target = jnp.concatenate([target] * (rows // 8), axis=0)
    place = lax.broadcasted_iota(jnp.int32, (rows, 2 * tokens), 0) // parts
    mask[...] = jnp.where(target == place, scaling, 0.0)

    def product(first, data, weights):
        total = None
        for n in range(data.shape[1] // CHUNK):
            for copy in pending[first + n]:
                copy.wait()
            here = pl.ds(n * CHUNK, CHUNK)
            term = dot_nt(weights[:, here], data[:, here])
            total = term if total is None else total + term
        return total

    from_grads = product(0, grads, weights_out)
    from_acts = product(grads.shape[1] // CHUNK, acts, weights_in)
    sketches = jnp.concatenate([from_acts[:sketch], from_grads[:sketch]], axis=1)
    low[0] = from_grads[sketch:]
    low[1] = from_acts[sketch:]

    highs, lows = [], []
    for c in range(per):
        chosen = jnp.concatenate(
            [low[i, pl.ds(c, parts, stride=per), :] for i in range(2)], axis=1
        )
        chosen = jnp.concatenate([chosen] * examples, axis=0)
        high, rest = split(chosen * mask[...])
        highs.append(high)
        lows.append(rest)
    left_high = jnp.concatenate(highs, axis=0)
    left_low = jnp.concatenate(lows, axis=0)
    right = jnp.concatenate(
        [sketches[h * SLOT : (h + 1) * SLOT] for h in range(halves) for _ in range(per)],
        axis=0,
    )
    right_high, right_low = split(right)
    spread = (
        dot_nt(left_high, right_low) + dot_nt(left_low, right_high)
    ) + dot_nt(left_high, right_high)
    column = lax.broadcasted_iota(jnp.int32, (rows, per * sketch), 1)
    channel = (column // SLOT) % per
    total = spread[:rows]
    for c in range(1, per):
        total = jnp.where(channel == c, spread[c * rows : (c + 1) * rows], total)
    me = lax.axis_index("mp")
    for start in range(0, per * sketch, LANES):
        stop = min(start + LANES, per * sketch)
        out[:, : stop - start] = total[:, start:stop]
        for d in range(parts):
            g = me ^ d
            sends[d][:examples, start:stop] = out[
                pl.ds(pl.multiple_of(g * examples, examples), examples), : stop - start
            ]
            sends[d][examples:, start:stop] = out[pl.ds(g, examples, stride=parts), :][
                :, : stop - start
            ]


def sum_kernel(*refs):
    chunks, (columns, feature_rows) = refs[:-2], refs[-2:]
    examples, padded = columns.shape
    total = chunks[0][...]
    for chunk in chunks[1:]:
        total = total + chunk[...]
    width = total.shape[1]
    for ref, value in ((feature_rows, total[:examples]), (columns, total[examples:])):
        ref[:, :width] = value
        if padded > width:
            ref[:, width:] = jnp.zeros((examples, padded - width), jnp.float32)


def stack_kernel(*refs):
    rows = refs[0].shape[0]
    for n, part in enumerate(refs[:-1]):
        refs[-1][n * rows : (n + 1) * rows, :] = part[...]


def write_features(total, parts, per, features):
    rows_here, width = features.shape
    span = width // parts
    halves = span // (per * SLOT)
    natural = jnp.concatenate(
        [
            total[:, (h * per + c) * SLOT : (h * per + c + 1) * SLOT]
            for c in range(per)
            for h in range(halves)
        ],
        axis=1,
    )
    for r in range(rows_here):
        features[r : r + 1, :] = jnp.concatenate(
            [natural[r * parts + g : r * parts + g + 1, :] for g in range(parts)], axis=1
        )


def pick_lanes(x, index):
    return jnp.take_along_axis(x, index, axis=1)


def reciprocal(x):
    guess = pl.reciprocal(x, approx=True)
    return guess * (2.0 - x * guess)


def factor_kernel(parts, damping, held, sent, features, factors):
    channels, sketch, _ = factors.shape
    examples = features.shape[0] * parts
    gathered = held.shape[0] - examples
    span = features.shape[1] // parts
    write_features(sent[gathered:, :span], parts, channels, features)
    halves = sketch // SLOT
    panels = sketch // PANEL
    per_half = SLOT // PANEL
    stacked = jnp.concatenate([held[:gathered, :], sent[:gathered, :]], axis=0)
    high, rest = split(stacked)
    gram = (dot_tn(high, rest) + dot_tn(rest, high)) + dot_tn(high, high)
    lane = lax.broadcasted_iota(jnp.int32, (PANEL, LANES), 1)
    sub = lax.broadcasted_iota(jnp.int32, (PANEL, LANES), 0)
    slot = lane // SLOT
    within = lane % SLOT
    ridge = damping[0]
    tile = []
    for q in range(panels):
        hr, at = divmod(q, per_half)
        line = []
        for h in range(halves):
            value = None
            for c in range(GROUP):
                start = hr * LANES + c * SLOT + at * PANEL
                block = gram[start : start + PANEL, h * LANES : (h + 1) * LANES]
                value = block if c == 0 else jnp.where(slot == c, block, value)
            value = value * (1.0 / stacked.shape[0])
            if h == hr:
                value = value + jnp.where(within == at * PANEL + sub, ridge, 0.0)
            line.append(value)
        tile.append(line)

    zero = jnp.zeros((PANEL, LANES), jnp.float32)
    finished = []
    for q in range(panels):
        hq, at = divmod(q, per_half)
        column = [
            {
                j: pick_lanes(tile[j][hq], slot * SLOT + at * PANEL + r)
                for j in range(q, panels)
            }
            for r in range(PANEL)
        ]
        block = [
            [
                jnp.broadcast_to(column[r][q][s : s + 1, :], (PANEL, LANES))
                if s >= r
                else None
                for s in range(PANEL)
            ]
            for r in range(PANEL)
        ]
        line = [
            [
                jnp.broadcast_to(tile[q][h][r : r + 1, :], (PANEL, LANES))
                if h >= hq
                else None
                for h in range(halves)
            ]
            for r in range(PANEL)
        ]
        inverse = []

        def eliminate(r, s, inv):
            ratio = block[r][s] * inv
            for t in range(s, PANEL):
                block[s][t] = block[s][t] - ratio * block[r][t]
            for j in range(q + 1, panels):
                column[s][j] = column[s][j] - ratio * column[r][j]
            for h in range(hq, halves):
                line[s][h] = line[s][h] - ratio * line[r][h]

        for r in range(0, PANEL, 2):
            pivot = block[r][r]
            minor = pivot * block[r + 1][r + 1] - block[r][r + 1] * block[r][r + 1]
            inverse.append(reciprocal(pivot))
            inverse.append(pivot * reciprocal(minor))
            eliminate(r, r + 1, inverse[r])
            for s in range(r + 2, PANEL):
                eliminate(r, s, inverse[r])
                eliminate(r + 1, s, inverse[r + 1])
        result = []
        for h in range(halves):
            if h < hq:
                result.append(zero)
                continue
            value = zero
            for r in range(PANEL):
                value = jnp.where(sub == r, line[r][h] * lax.rsqrt(block[r][r]), value)
            if h == hq:
                value = jnp.where(within >= at * PANEL + sub, value, 0.0)
            result.append(value)
        finished.append(result)
        for j in range(q + 1, panels):
            weights = [column[r][j] * inverse[r] for r in range(PANEL)]
            for h in range((q + 1) // per_half, halves):
                value = tile[j][h]
                for r in range(PANEL):
                    value = value - weights[r] * line[r][h]
                tile[j][h] = value

    for q in range(panels):
        for c in range(channels):
            factors[c, q * PANEL : (q + 1) * PANEL, :] = jnp.concatenate(
                [finished[q][h][:, c * SLOT : (c + 1) * SLOT] for h in range(halves)],
                axis=1,
            )


def exchange(x, ex_distance, mp_distance=0):
    shards, parts = lax.axis_size("ex"), lax.axis_size("mp")
    return lax.ppermute(
        x,
        ("ex", "mp"),
        [
            (m * parts + b, (m ^ ex_distance) * parts + (b ^ mp_distance))
            for m in range(shards)
            for b in range(parts)
        ],
    )


def vmem():
    return pl.BlockSpec(memory_space=pltpu.VMEM)


def hbm():
    return pl.BlockSpec(memory_space=pltpu.HBM)


def in_hbm(*arrays):
    return [pltpu.with_memory_space_constraint(x, pltpu.HBM) for x in arrays]


def in_vmem(*arrays):
    return [pltpu.with_memory_space_constraint(x, pltpu.VMEM) for x in arrays]


def smem():
    return pl.BlockSpec(memory_space=pltpu.SMEM)


def local(
    acts,
    grads,
    down_factor,
    up_factor_transposed,
    input_projection,
    gradient_projection,
    order,
    damping,
):
    parts = lax.axis_size("mp")
    shards = lax.axis_size("ex")
    tokens, width = acts.shape[1:]
    key_width = grads.shape[2]
    rank = down_factor.shape[1]
    sketch = input_projection.shape[1]
    examples = tokens // EXAMPLE_LENGTH
    per = rank // parts
    span = per * sketch
    scaling = 1.0 / math.sqrt(2.0 * EXAMPLE_LENGTH * parts)
    sends = pl.pallas_call(
        functools.partial(partial_kernel, parts, scaling),
        out_shape=[pltpu.VMEM((2 * examples, span), jnp.float32)] * parts,
        in_specs=[hbm()] * 7,
        out_specs=[vmem()] * parts,
        scratch_shapes=[
            pltpu.VMEM((tokens, width), acts.dtype),
            pltpu.VMEM((tokens, key_width), grads.dtype),
            pltpu.VMEM((sketch + rank, width), acts.dtype),
            pltpu.VMEM((sketch + rank, key_width), grads.dtype),
            pltpu.SMEM(order.shape[1:], order.dtype),
            pltpu.VMEM((2, rank, tokens), jnp.float32),
            pltpu.VMEM((examples * parts, 2 * tokens), jnp.float32),
            pltpu.VMEM((examples * parts, LANES), jnp.float32),
            pltpu.SemaphoreType.DMA(((width + key_width) // CHUNK, 3)),
            pltpu.SemaphoreType.DMA,
        ],
        compiler_params=pltpu.CompilerParams(vmem_limit_bytes=8 * 2**20),
        name="partials",
    )(
        *in_hbm(
            acts,
            grads,
            down_factor,
            up_factor_transposed,
            input_projection,
            gradient_projection,
            order,
        )
    )
    chunks = [exchange(sends[d], 1, d) for d in range(parts - 1, -1, -1)]
    padded = max(span, GROUP * sketch)
    columns, feature_rows = pl.pallas_call(
        sum_kernel,
        out_shape=[pltpu.VMEM((examples, padded), jnp.float32)] * 2,
        in_specs=[vmem()] * parts,
        out_specs=[vmem()] * 2,
        compiler_params=pltpu.CompilerParams(vmem_limit_bytes=2 * 2**20),
        name="sums",
    )(*in_vmem(*chunks))
    near = [columns] + [exchange(columns, d) for d in range(3, shards, 2)] + [feature_rows]
    held = pl.pallas_call(
        stack_kernel,
        out_shape=pltpu.VMEM((len(near) * examples, padded), jnp.float32),
        in_specs=[vmem()] * len(near),
        out_specs=vmem(),
        compiler_params=pltpu.CompilerParams(vmem_limit_bytes=2 * 2**20),
        name="stack",
    )(*in_vmem(*near))
    sent = exchange(held, 1)
    return pl.pallas_call(
        functools.partial(factor_kernel, parts),
        out_shape=[
            jax.ShapeDtypeStruct((examples // parts, rank * sketch), jnp.float32),
            jax.ShapeDtypeStruct((per, sketch, sketch), jnp.float32),
        ],
        in_specs=[smem()] + [vmem()] * 2,
        out_specs=[vmem()] * 2,
        compiler_params=pltpu.CompilerParams(vmem_limit_bytes=8 * 2**20),
        name="factors",
    )(damping, *in_vmem(held, sent))


def solution(mesh):
    in_specs = (
        P("mp", "ex", None),
        P("mp", "ex", None),
        P("mp", None, None),
        P("mp", None, None),
        P("mp", None, None),
        P("mp", None, None),
        P("mp", "ex", None),
        P(),
    )
    out_specs = (P(("ex", "mp"), None), P("mp", None, None))
    return jax.shard_map(
        local, mesh=mesh, in_specs=in_specs, out_specs=out_specs, check_vma=False
    )
```

```python
import functools
import math

import jax
import jax.numpy as jnp
from jax import lax
from jax.experimental import pallas as pl
from jax.experimental.pallas import tpu as pltpu
from jax.sharding import PartitionSpec as P

EXAMPLE_LENGTH = 8
LANES = 128
SLOT = 32
GROUP = LANES // SLOT
PANEL = 8
CHUNK = 1024


def dot_nt(a, b):
    return lax.dot_general(
        a, b, (((1,), (1,)), ((), ())), preferred_element_type=jnp.float32
    )


def dot_nn(a, b):
    return jnp.dot(a, b, preferred_element_type=jnp.float32)


def split(x):
    high = x.astype(jnp.bfloat16)
    return high, (x - high.astype(jnp.float32)).astype(jnp.bfloat16)


def partial_kernel(
    parts,
    scaling,
    acts_hbm,
    grads_hbm,
    down_hbm,
    up_hbm,
    proj_in_hbm,
    proj_out_hbm,
    order_hbm,
    *refs,
):
    sends, refs = refs[:parts], refs[parts:]
    acts, grads, weights_in, weights_out, order, low, mask, out, sems, order_sem = refs
    tokens, width = acts.shape
    rank = down_hbm.shape[1]
    sketch = proj_in_hbm.shape[1]
    examples = tokens // EXAMPLE_LENGTH
    per = rank // parts
    halves = sketch // SLOT

    def copies(source, target, sem, start, size):
        return pltpu.make_async_copy(
            source.at[0, :, pl.ds(start, size)],
            target.at[:, pl.ds(start, size)],
            sem,
        )

    order_copy = pltpu.make_async_copy(order_hbm.at[0], order, order_sem)
    order_copy.start()
    sources = [
        (grads_hbm, grads, proj_out_hbm, up_hbm, weights_out),
        (acts_hbm, acts, proj_in_hbm, down_hbm, weights_in),
    ]
    pending = []
    for data_hbm, data, first_hbm, second_hbm, weights in sources:
        for start in range(0, data.shape[1], CHUNK):
            n = len(pending)
            pending.append(
                [
                    copies(first_hbm, weights.at[pl.ds(0, sketch)], sems.at[n, 0], start, CHUNK),
                    copies(second_hbm, weights.at[pl.ds(sketch, rank)], sems.at[n, 1], start, CHUNK),
                    copies(data_hbm, data, sems.at[n, 2], start, CHUNK),
                ]
            )
            for copy in pending[-1]:
                copy.start()

    order_copy.wait()
    rows = examples * parts
    lane = lax.broadcasted_iota(jnp.int32, (rows, 2 * tokens), 1)
    source = (lane % tokens) // EXAMPLE_LENGTH
    target = jnp.zeros((8, 2 * tokens), jnp.int32)
    for s in range(examples):
        target = jnp.where(source[:8] == s, order[0, s], target)
    target = jnp.concatenate([target] * (rows // 8), axis=0)
    place = lax.broadcasted_iota(jnp.int32, (rows, 2 * tokens), 0) // parts
    mask[...] = jnp.where(target == place, scaling, 0.0)

    def product(first, data, weights):
        total = None
        for n in range(data.shape[1] // CHUNK):
            for copy in pending[first + n]:
                copy.wait()
            here = pl.ds(n * CHUNK, CHUNK)
            term = dot_nt(weights[:, here], data[:, here])
            total = term if total is None else total + term
        return total

    from_grads = product(0, grads, weights_out)
    from_acts = product(grads.shape[1] // CHUNK, acts, weights_in)
    sketches = jnp.concatenate([from_acts[:sketch], from_grads[:sketch]], axis=1)
    low[0] = from_grads[sketch:]
    low[1] = from_acts[sketch:]

    highs, lows = [], []
    for c in range(per):
        chosen = jnp.concatenate(
            [low[i, pl.ds(c, parts, stride=per), :] for i in range(2)], axis=1
        )
        chosen = jnp.concatenate([chosen] * examples, axis=0)
        high, rest = split(chosen * mask[...])
        highs.append(high)
        lows.append(rest)
    left_high = jnp.concatenate(highs, axis=0)
    left_low = jnp.concatenate(lows, axis=0)
    right = jnp.concatenate(
        [sketches[h * SLOT : (h + 1) * SLOT] for h in range(halves) for _ in range(per)],
        axis=0,
    )
    right_high, right_low = split(right)
    both = dot_nt(jnp.concatenate([left_high, left_low], axis=0), right_high)
    size = left_high.shape[0]
    spread = (dot_nt(left_high, right_low) + both[size:]) + both[:size]
    column = lax.broadcasted_iota(jnp.int32, (rows, per * sketch), 1)
    channel = (column // SLOT) % per
    total = spread[:rows]
    for c in range(1, per):
        total = jnp.where(channel == c, spread[c * rows : (c + 1) * rows], total)
    me = lax.axis_index("mp")
    for start in range(0, per * sketch, LANES):
        stop = min(start + LANES, per * sketch)
        out[:, : stop - start] = total[:, start:stop]
        for d in range(parts):
            g = me ^ d
            sends[d][:examples, start:stop] = out[
                pl.ds(pl.multiple_of(g * examples, examples), examples), : stop - start
            ]
            sends[d][examples:, start:stop] = out[pl.ds(g, examples, stride=parts), :][
                :, : stop - start
            ]


def sum_kernel(*refs):
    chunks, (columns, feature_rows) = refs[:-2], refs[-2:]
    examples, padded = columns.shape
    total = chunks[0][...]
    for chunk in chunks[1:]:
        total = total + chunk[...]
    width = total.shape[1]
    for ref, value in ((feature_rows, total[:examples]), (columns, total[examples:])):
        ref[:, :width] = value
        if padded > width:
            ref[:, width:] = jnp.zeros((examples, padded - width), jnp.float32)


def stack_kernel(*refs):
    rows = refs[0].shape[0]
    for n, part in enumerate(refs[:-1]):
        refs[-1][n * rows : (n + 1) * rows, :] = part[...]


def write_features(total, parts, per, features):
    rows_here, width = features.shape
    span = width // parts
    halves = span // (per * SLOT)
    natural = jnp.concatenate(
        [
            total[:, (h * per + c) * SLOT : (h * per + c + 1) * SLOT]
            for c in range(per)
            for h in range(halves)
        ],
        axis=1,
    )
    for r in range(rows_here):
        features[r : r + 1, :] = jnp.concatenate(
            [natural[r * parts + g : r * parts + g + 1, :] for g in range(parts)], axis=1
        )


def pick_lanes(x, index):
    return jnp.take_along_axis(x, index, axis=1)


def reciprocal(x):
    guess = pl.reciprocal(x, approx=True)
    return guess * (2.0 - x * guess)


def factor_kernel(parts, damping, held, sent, features, factors):
    channels, sketch, _ = factors.shape
    examples = features.shape[0] * parts
    gathered = held.shape[0] - examples
    span = features.shape[1] // parts
    write_features(sent[gathered:, :span], parts, channels, features)
    halves = sketch // SLOT
    panels = sketch // PANEL
    per_half = SLOT // PANEL
    stacked = jnp.concatenate([held[:gathered, :], sent[:gathered, :]], axis=0)
    high, rest = split(stacked)
    turned_high, turned_rest = split(jnp.transpose(stacked))
    gram = dot_nn(turned_high, rest) + dot_nn(
        jnp.concatenate([turned_rest, turned_high], axis=1),
        jnp.concatenate([high, high], axis=0),
    )
    lane = lax.broadcasted_iota(jnp.int32, (PANEL, LANES), 1)
    sub = lax.broadcasted_iota(jnp.int32, (PANEL, LANES), 0)
    slot = lane // SLOT
    within = lane % SLOT
    ridge = damping[0]
    tile = []
    for q in range(panels):
        hr, at = divmod(q, per_half)
        line = []
        for h in range(halves):
            value = None
            for c in range(GROUP):
                start = hr * LANES + c * SLOT + at * PANEL
                block = gram[start : start + PANEL, h * LANES : (h + 1) * LANES]
                value = block if c == 0 else jnp.where(slot == c, block, value)
            value = value * (1.0 / stacked.shape[0])
            if h == hr:
                value = value + jnp.where(within == at * PANEL + sub, ridge, 0.0)
            line.append(value)
        tile.append(line)

    zero = jnp.zeros((PANEL, LANES), jnp.float32)
    finished = []
    for q in range(panels):
        hq, at = divmod(q, per_half)
        column = [
            {
                j: pick_lanes(tile[j][hq], slot * SLOT + at * PANEL + r)
                for j in range(q, panels)
            }
            for r in range(PANEL)
        ]
        block = [
            [
                jnp.broadcast_to(column[r][q][s : s + 1, :], (PANEL, LANES))
                if s >= r
                else None
                for s in range(PANEL)
            ]
            for r in range(PANEL)
        ]
        line = [
            [
                jnp.broadcast_to(tile[q][h][r : r + 1, :], (PANEL, LANES))
                if h >= hq
                else None
                for h in range(halves)
            ]
            for r in range(PANEL)
        ]
        inverse = []

        def eliminate(r, s, inv):
            ratio = block[r][s] * inv
            for t in range(s, PANEL):
                block[s][t] = block[s][t] - ratio * block[r][t]
            for j in range(q + 1, panels):
                column[s][j] = column[s][j] - ratio * column[r][j]
            for h in range(hq, halves):
                line[s][h] = line[s][h] - ratio * line[r][h]

        for r in range(0, PANEL, 2):
            pivot = block[r][r]
            minor = pivot * block[r + 1][r + 1] - block[r][r + 1] * block[r][r + 1]
            inverse.append(reciprocal(pivot))
            inverse.append(pivot * reciprocal(minor))
            eliminate(r, r + 1, inverse[r])
            for s in range(r + 2, PANEL):
                eliminate(r, s, inverse[r])
                eliminate(r + 1, s, inverse[r + 1])
        result = []
        for h in range(halves):
            if h < hq:
                result.append(zero)
                continue
            value = zero
            for r in range(PANEL):
                value = jnp.where(sub == r, line[r][h] * lax.rsqrt(block[r][r]), value)
            if h == hq:
                value = jnp.where(within >= at * PANEL + sub, value, 0.0)
            result.append(value)
        finished.append(result)
        for j in range(q + 1, panels):
            weights = [column[r][j] * inverse[r] for r in range(PANEL)]
            for h in range((q + 1) // per_half, halves):
                value = tile[j][h]
                for r in range(PANEL):
                    value = value - weights[r] * line[r][h]
                tile[j][h] = value

    for q in range(panels):
        for c in range(channels):
            factors[c, q * PANEL : (q + 1) * PANEL, :] = jnp.concatenate(
                [finished[q][h][:, c * SLOT : (c + 1) * SLOT] for h in range(halves)],
                axis=1,
            )


def exchange(x, ex_distance, mp_distance=0):
    shards, parts = lax.axis_size("ex"), lax.axis_size("mp")
    return lax.ppermute(
        x,
        ("ex", "mp"),
        [
            (m * parts + b, (m ^ ex_distance) * parts + (b ^ mp_distance))
            for m in range(shards)
            for b in range(parts)
        ],
    )


def vmem():
    return pl.BlockSpec(memory_space=pltpu.VMEM)


def hbm():
    return pl.BlockSpec(memory_space=pltpu.HBM)


def in_hbm(*arrays):
    return [pltpu.with_memory_space_constraint(x, pltpu.HBM) for x in arrays]


def in_vmem(*arrays):
    return [pltpu.with_memory_space_constraint(x, pltpu.VMEM) for x in arrays]


def smem():
    return pl.BlockSpec(memory_space=pltpu.SMEM)


def local(
    acts,
    grads,
    down_factor,
    up_factor_transposed,
    input_projection,
    gradient_projection,
    order,
    damping,
):
    parts = lax.axis_size("mp")
    shards = lax.axis_size("ex")
    tokens, width = acts.shape[1:]
    key_width = grads.shape[2]
    rank = down_factor.shape[1]
    sketch = input_projection.shape[1]
    examples = tokens // EXAMPLE_LENGTH
    per = rank // parts
    span = per * sketch
    scaling = 1.0 / math.sqrt(2.0 * EXAMPLE_LENGTH * parts)
    sends = pl.pallas_call(
        functools.partial(partial_kernel, parts, scaling),
        out_shape=[pltpu.VMEM((2 * examples, span), jnp.float32)] * parts,
        in_specs=[hbm()] * 7,
        out_specs=[vmem()] * parts,
        scratch_shapes=[
            pltpu.VMEM((tokens, width), acts.dtype),
            pltpu.VMEM((tokens, key_width), grads.dtype),
            pltpu.VMEM((sketch + rank, width), acts.dtype),
            pltpu.VMEM((sketch + rank, key_width), grads.dtype),
            pltpu.SMEM(order.shape[1:], order.dtype),
            pltpu.VMEM((2, rank, tokens), jnp.float32),
            pltpu.VMEM((examples * parts, 2 * tokens), jnp.float32),
            pltpu.VMEM((examples * parts, LANES), jnp.float32),
            pltpu.SemaphoreType.DMA(((width + key_width) // CHUNK, 3)),
            pltpu.SemaphoreType.DMA,
        ],
        compiler_params=pltpu.CompilerParams(vmem_limit_bytes=8 * 2**20),
        name="partials",
    )(
        *in_hbm(
            acts,
            grads,
            down_factor,
            up_factor_transposed,
            input_projection,
            gradient_projection,
            order,
        )
    )
    chunks = [exchange(sends[d], 1, d) for d in range(parts - 1, -1, -1)]
    padded = max(span, GROUP * sketch)
    columns, feature_rows = pl.pallas_call(
        sum_kernel,
        out_shape=[pltpu.VMEM((examples, padded), jnp.float32)] * 2,
        in_specs=[vmem()] * parts,
        out_specs=[vmem()] * 2,
        compiler_params=pltpu.CompilerParams(vmem_limit_bytes=2 * 2**20),
        name="sums",
    )(*in_vmem(*chunks))
    near = [columns] + [exchange(columns, d) for d in range(3, shards, 2)] + [feature_rows]
    held = pl.pallas_call(
        stack_kernel,
        out_shape=pltpu.VMEM((len(near) * examples, padded), jnp.float32),
        in_specs=[vmem()] * len(near),
        out_specs=vmem(),
        compiler_params=pltpu.CompilerParams(vmem_limit_bytes=2 * 2**20),
        name="stack",
    )(*in_vmem(*near))
    sent = exchange(held, 1)
    return pl.pallas_call(
        functools.partial(factor_kernel, parts),
        out_shape=[
            jax.ShapeDtypeStruct((examples // parts, rank * sketch), jnp.float32),
            jax.ShapeDtypeStruct((per, sketch, sketch), jnp.float32),
        ],
        in_specs=[smem()] + [vmem()] * 2,
        out_specs=[vmem()] * 2,
        compiler_params=pltpu.CompilerParams(vmem_limit_bytes=8 * 2**20),
        name="factors",
    )(damping, *in_vmem(held, sent))


def solution(mesh):
    in_specs = (
        P("mp", "ex", None),
        P("mp", "ex", None),
        P("mp", None, None),
        P("mp", None, None),
        P("mp", None, None),
        P("mp", None, None),
        P("mp", "ex", None),
        P(),
    )
    out_specs = (P(("ex", "mp"), None), P("mp", None, None))
    return jax.shard_map(
        local, mesh=mesh, in_specs=in_specs, out_specs=out_specs, check_vma=False
    )
```

```python
import functools
import math

import jax
import jax.numpy as jnp
from jax import lax
from jax.experimental import pallas as pl
from jax.experimental.pallas import tpu as pltpu
from jax.sharding import PartitionSpec as P

EXAMPLE_LENGTH = 8
LANES = 128
SLOT = 32
GROUP = LANES // SLOT
PANEL = 8
CHUNK = 512


def dot_nt(a, b):
    return lax.dot_general(
        a, b, (((1,), (1,)), ((), ())), preferred_element_type=jnp.float32
    )


def dot_nn(a, b):
    return jnp.dot(a, b, preferred_element_type=jnp.float32)


def split(x):
    high = x.astype(jnp.bfloat16)
    return high, (x - high.astype(jnp.float32)).astype(jnp.bfloat16)


def partial_kernel(
    parts,
    scaling,
    acts_hbm,
    grads_hbm,
    down_hbm,
    up_hbm,
    proj_in_hbm,
    proj_out_hbm,
    order_hbm,
    *refs,
):
    sends, refs = refs[:parts], refs[parts:]
    acts, grads, weights_in, weights_out, order, low, mask, out, sems, order_sem = refs
    tokens, width = acts.shape
    rank = down_hbm.shape[1]
    sketch = proj_in_hbm.shape[1]
    examples = tokens // EXAMPLE_LENGTH
    per = rank // parts
    halves = sketch // SLOT

    def copies(source, target, sem, start, size):
        return pltpu.make_async_copy(
            source.at[0, :, pl.ds(start, size)],
            target.at[:, pl.ds(start, size)],
            sem,
        )

    order_copy = pltpu.make_async_copy(order_hbm.at[0], order, order_sem)
    order_copy.start()
    sources = [
        (grads_hbm, grads, proj_out_hbm, up_hbm, weights_out),
        (acts_hbm, acts, proj_in_hbm, down_hbm, weights_in),
    ]
    pending = []
    for data_hbm, data, first_hbm, second_hbm, weights in sources:
        for start in range(0, data.shape[1], CHUNK):
            n = len(pending)
            pending.append(
                [
                    copies(first_hbm, weights.at[pl.ds(0, sketch)], sems.at[n, 0], start, CHUNK),
                    copies(second_hbm, weights.at[pl.ds(sketch, rank)], sems.at[n, 1], start, CHUNK),
                    copies(data_hbm, data, sems.at[n, 2], start, CHUNK),
                ]
            )
            for copy in pending[-1]:
                copy.start()

    order_copy.wait()
    rows = examples * parts
    lane = lax.broadcasted_iota(jnp.int32, (rows, 2 * tokens), 1)
    source = (lane % tokens) // EXAMPLE_LENGTH
    target = jnp.zeros((8, 2 * tokens), jnp.int32)
    for s in range(examples):
        target = jnp.where(source[:8] == s, order[0, s], target)
    target = jnp.concatenate([target] * (rows // 8), axis=0)
    place = lax.broadcasted_iota(jnp.int32, (rows, 2 * tokens), 0) // parts
    mask[...] = jnp.where(target == place, scaling, 0.0)

    def product(first, data, weights):
        total = None
        for n in range(data.shape[1] // CHUNK):
            for copy in pending[first + n]:
                copy.wait()
            here = pl.ds(n * CHUNK, CHUNK)
            term = dot_nt(weights[:, here], data[:, here])
            total = term if total is None else total + term
        return total

    from_grads = product(0, grads, weights_out)
    from_acts = product(grads.shape[1] // CHUNK, acts, weights_in)
    sketches = jnp.concatenate([from_acts[:sketch], from_grads[:sketch]], axis=1)
    low[0] = from_grads[sketch:]
    low[1] = from_acts[sketch:]

    highs, lows = [], []
    for c in range(per):
        chosen = jnp.concatenate(
            [low[i, pl.ds(c, parts, stride=per), :] for i in range(2)], axis=1
        )
        chosen = jnp.concatenate([chosen] * examples, axis=0)
        high, rest = split(chosen * mask[...])
        highs.append(high)
        lows.append(rest)
    left_high = jnp.concatenate(highs, axis=0)
    left_low = jnp.concatenate(lows, axis=0)
    right = jnp.concatenate(
        [sketches[h * SLOT : (h + 1) * SLOT] for h in range(halves) for _ in range(per)],
        axis=0,
    )
    right_high, right_low = split(right)
    both = dot_nt(jnp.concatenate([left_high, left_low], axis=0), right_high)
    size = left_high.shape[0]
    spread = (dot_nt(left_high, right_low) + both[size:]) + both[:size]
    column = lax.broadcasted_iota(jnp.int32, (rows, per * sketch), 1)
    channel = (column // SLOT) % per
    total = spread[:rows]
    for c in range(1, per):
        total = jnp.where(channel == c, spread[c * rows : (c + 1) * rows], total)
    me = lax.axis_index("mp")
    for start in range(0, per * sketch, LANES):
        stop = min(start + LANES, per * sketch)
        out[:, : stop - start] = total[:, start:stop]
        for d in range(parts):
            g = me ^ d
            sends[d][:examples, start:stop] = out[
                pl.ds(pl.multiple_of(g * examples, examples), examples), : stop - start
            ]
            sends[d][examples:, start:stop] = out[pl.ds(g, examples, stride=parts), :][
                :, : stop - start
            ]


def sum_kernel(*refs):
    chunks, (columns, feature_rows) = refs[:-2], refs[-2:]
    examples, padded = columns.shape
    total = chunks[0][...]
    for chunk in chunks[1:]:
        total = total + chunk[...]
    width = total.shape[1]
    for ref, value in ((feature_rows, total[:examples]), (columns, total[examples:])):
        ref[:, :width] = value
        if padded > width:
            ref[:, width:] = jnp.zeros((examples, padded - width), jnp.float32)


def stack_kernel(*refs):
    rows = refs[0].shape[0]
    for n, part in enumerate(refs[:-1]):
        refs[-1][n * rows : (n + 1) * rows, :] = part[...]


def write_features(total, parts, per, features):
    rows_here, width = features.shape
    span = width // parts
    halves = span // (per * SLOT)
    natural = jnp.concatenate(
        [
            total[:, (h * per + c) * SLOT : (h * per + c + 1) * SLOT]
            for c in range(per)
            for h in range(halves)
        ],
        axis=1,
    )
    for r in range(rows_here):
        features[r : r + 1, :] = jnp.concatenate(
            [natural[r * parts + g : r * parts + g + 1, :] for g in range(parts)], axis=1
        )


def pick_lanes(x, index):
    return jnp.take_along_axis(x, index, axis=1)


def reciprocal(x):
    guess = pl.reciprocal(x, approx=True)
    return guess * (2.0 - x * guess)


def factor_kernel(parts, damping, held, sent, features, factors):
    channels, sketch, _ = factors.shape
    examples = features.shape[0] * parts
    gathered = held.shape[0] - examples
    span = features.shape[1] // parts
    write_features(sent[gathered:, :span], parts, channels, features)
    halves = sketch // SLOT
    panels = sketch // PANEL
    per_half = SLOT // PANEL
    stacked = jnp.concatenate([held[:gathered, :], sent[:gathered, :]], axis=0)
    high, rest = split(stacked)
    turned_high, turned_rest = split(jnp.transpose(stacked))
    gram = dot_nn(turned_high, rest) + dot_nn(
        jnp.concatenate([turned_rest, turned_high], axis=1),
        jnp.concatenate([high, high], axis=0),
    )
    lane = lax.broadcasted_iota(jnp.int32, (PANEL, LANES), 1)
    sub = lax.broadcasted_iota(jnp.int32, (PANEL, LANES), 0)
    slot = lane // SLOT
    within = lane % SLOT
    ridge = damping[0]
    tile = []
    for q in range(panels):
        hr, at = divmod(q, per_half)
        line = []
        for h in range(halves):
            value = None
            for c in range(GROUP):
                start = hr * LANES + c * SLOT + at * PANEL
                block = gram[start : start + PANEL, h * LANES : (h + 1) * LANES]
                value = block if c == 0 else jnp.where(slot == c, block, value)
            value = value * (1.0 / stacked.shape[0])
            if h == hr:
                value = value + jnp.where(within == at * PANEL + sub, ridge, 0.0)
            line.append(value)
        tile.append(line)

    zero = jnp.zeros((PANEL, LANES), jnp.float32)
    finished = []
    ahead = [pick_lanes(tile[0][0], slot * SLOT + r) for r in range(PANEL)]
    for q in range(panels):
        hq, at = divmod(q, per_half)
        if q + 1 < panels:
            hn, an = divmod(q + 1, per_half)
            behind = [
                pick_lanes(tile[q + 1][hn], slot * SLOT + an * PANEL + r)
                for r in range(PANEL)
            ]
        column = [
            {
                j: ahead[r]
                if j == q
                else pick_lanes(tile[j][hq], slot * SLOT + at * PANEL + r)
                for j in range(q, panels)
            }
            for r in range(PANEL)
        ]
        block = [
            [
                jnp.broadcast_to(column[r][q][s : s + 1, :], (PANEL, LANES))
                if s >= r
                else None
                for s in range(PANEL)
            ]
            for r in range(PANEL)
        ]
        line = [
            [
                jnp.broadcast_to(tile[q][h][r : r + 1, :], (PANEL, LANES))
                if h >= hq
                else None
                for h in range(halves)
            ]
            for r in range(PANEL)
        ]
        inverse = []

        def eliminate(r, s, inv):
            ratio = block[r][s] * inv
            for t in range(s, PANEL):
                block[s][t] = block[s][t] - ratio * block[r][t]
            for j in range(q + 1, panels):
                column[s][j] = column[s][j] - ratio * column[r][j]
            for h in range(hq, halves):
                line[s][h] = line[s][h] - ratio * line[r][h]

        for r in range(0, PANEL, 2):
            pivot = block[r][r]
            minor = pivot * block[r + 1][r + 1] - block[r][r + 1] * block[r][r + 1]
            inverse.append(reciprocal(pivot))
            inverse.append(pivot * reciprocal(minor))
            eliminate(r, r + 1, inverse[r])
            for s in range(r + 2, PANEL):
                eliminate(r, s, inverse[r])
                eliminate(r + 1, s, inverse[r + 1])
        result = []
        for h in range(halves):
            if h < hq:
                result.append(zero)
                continue
            value = zero
            for r in range(PANEL):
                value = jnp.where(sub == r, line[r][h] * lax.rsqrt(block[r][r]), value)
            if h == hq:
                value = jnp.where(within >= at * PANEL + sub, value, 0.0)
            result.append(value)
        finished.append(result)
        for j in range(q + 1, panels):
            weights = [column[r][j] * inverse[r] for r in range(PANEL)]
            if j == q + 1:
                ahead = behind
                for r in range(PANEL):
                    for s in range(PANEL):
                        factor = jnp.broadcast_to(
                            column[r][j][s : s + 1, :], (PANEL, LANES)
                        )
                        ahead[s] = ahead[s] - weights[r] * factor
            for h in range((q + 1) // per_half, halves):
                value = tile[j][h]
                for r in range(PANEL):
                    value = value - weights[r] * line[r][h]
                tile[j][h] = value

    for q in range(panels):
        for c in range(channels):
            factors[c, q * PANEL : (q + 1) * PANEL, :] = jnp.concatenate(
                [finished[q][h][:, c * SLOT : (c + 1) * SLOT] for h in range(halves)],
                axis=1,
            )


def exchange(x, ex_distance, mp_distance=0):
    shards, parts = lax.axis_size("ex"), lax.axis_size("mp")
    return lax.ppermute(
        x,
        ("ex", "mp"),
        [
            (m * parts + b, (m ^ ex_distance) * parts + (b ^ mp_distance))
            for m in range(shards)
            for b in range(parts)
        ],
    )


def vmem():
    return pl.BlockSpec(memory_space=pltpu.VMEM)


def hbm():
    return pl.BlockSpec(memory_space=pltpu.HBM)


def in_hbm(*arrays):
    return [pltpu.with_memory_space_constraint(x, pltpu.HBM) for x in arrays]


def in_vmem(*arrays):
    return [pltpu.with_memory_space_constraint(x, pltpu.VMEM) for x in arrays]


def smem():
    return pl.BlockSpec(memory_space=pltpu.SMEM)


def local(
    acts,
    grads,
    down_factor,
    up_factor_transposed,
    input_projection,
    gradient_projection,
    order,
    damping,
):
    parts = lax.axis_size("mp")
    shards = lax.axis_size("ex")
    tokens, width = acts.shape[1:]
    key_width = grads.shape[2]
    rank = down_factor.shape[1]
    sketch = input_projection.shape[1]
    examples = tokens // EXAMPLE_LENGTH
    per = rank // parts
    span = per * sketch
    scaling = 1.0 / math.sqrt(2.0 * EXAMPLE_LENGTH * parts)
    sends = pl.pallas_call(
        functools.partial(partial_kernel, parts, scaling),
        out_shape=[pltpu.VMEM((2 * examples, span), jnp.float32)] * parts,
        in_specs=[hbm()] * 7,
        out_specs=[vmem()] * parts,
        scratch_shapes=[
            pltpu.VMEM((tokens, width), acts.dtype),
            pltpu.VMEM((tokens, key_width), grads.dtype),
            pltpu.VMEM((sketch + rank, width), acts.dtype),
            pltpu.VMEM((sketch + rank, key_width), grads.dtype),
            pltpu.SMEM(order.shape[1:], order.dtype),
            pltpu.VMEM((2, rank, tokens), jnp.float32),
            pltpu.VMEM((examples * parts, 2 * tokens), jnp.float32),
            pltpu.VMEM((examples * parts, LANES), jnp.float32),
            pltpu.SemaphoreType.DMA(((width + key_width) // CHUNK, 3)),
            pltpu.SemaphoreType.DMA,
        ],
        compiler_params=pltpu.CompilerParams(vmem_limit_bytes=8 * 2**20),
        name="partials",
    )(
        *in_hbm(
            acts,
            grads,
            down_factor,
            up_factor_transposed,
            input_projection,
            gradient_projection,
            order,
        )
    )
    chunks = [exchange(sends[d], 1, d) for d in range(parts - 1, -1, -1)]
    padded = max(span, GROUP * sketch)
    columns, feature_rows = pl.pallas_call(
        sum_kernel,
        out_shape=[pltpu.VMEM((examples, padded), jnp.float32)] * 2,
        in_specs=[vmem()] * parts,
        out_specs=[vmem()] * 2,
        compiler_params=pltpu.CompilerParams(vmem_limit_bytes=2 * 2**20),
        name="sums",
    )(*in_vmem(*chunks))
    near = [columns] + [exchange(columns, d) for d in range(3, shards, 2)] + [feature_rows]
    held = pl.pallas_call(
        stack_kernel,
        out_shape=pltpu.VMEM((len(near) * examples, padded), jnp.float32),
        in_specs=[vmem()] * len(near),
        out_specs=vmem(),
        compiler_params=pltpu.CompilerParams(vmem_limit_bytes=2 * 2**20),
        name="stack",
    )(*in_vmem(*near))
    sent = exchange(held, 1)
    return pl.pallas_call(
        functools.partial(factor_kernel, parts),
        out_shape=[
            jax.ShapeDtypeStruct((examples // parts, rank * sketch), jnp.float32),
            jax.ShapeDtypeStruct((per, sketch, sketch), jnp.float32),
        ],
        in_specs=[smem()] + [vmem()] * 2,
        out_specs=[vmem()] * 2,
        compiler_params=pltpu.CompilerParams(vmem_limit_bytes=8 * 2**20),
        name="factors",
    )(damping, *in_vmem(held, sent))


def solution(mesh):
    in_specs = (
        P("mp", "ex", None),
        P("mp", "ex", None),
        P("mp", None, None),
        P("mp", None, None),
        P("mp", None, None),
        P("mp", None, None),
        P("mp", "ex", None),
        P(),
    )
    out_specs = (P(("ex", "mp"), None), P("mp", None, None))
    return jax.shard_map(
        local, mesh=mesh, in_specs=in_specs, out_specs=out_specs, check_vma=False
    )
```

```python
import functools
import math

import jax
import jax.numpy as jnp
from jax import lax
from jax.experimental import pallas as pl
from jax.experimental.pallas import tpu as pltpu
from jax.sharding import PartitionSpec as P

EXAMPLE_LENGTH = 8
LANES = 128
SLOT = 32
GROUP = LANES // SLOT
PANEL = 8
CHUNK = 2048


def dot_nt(a, b):
    return lax.dot_general(
        a, b, (((1,), (1,)), ((), ())), preferred_element_type=jnp.float32
    )


def dot_nn(a, b):
    return jnp.dot(a, b, preferred_element_type=jnp.float32)


def split(x):
    high = x.astype(jnp.bfloat16)
    return high, (x - high.astype(jnp.float32)).astype(jnp.bfloat16)


def partial_kernel(
    parts,
    scaling,
    acts_hbm,
    grads_hbm,
    down_hbm,
    up_hbm,
    proj_in_hbm,
    proj_out_hbm,
    order_hbm,
    *refs,
):
    sends, refs = refs[:parts], refs[parts:]
    acts, grads, weights_in, weights_out, order, low, mask, out, sems, order_sem = refs
    tokens, width = acts.shape
    rank = down_hbm.shape[1]
    sketch = proj_in_hbm.shape[1]
    examples = tokens // EXAMPLE_LENGTH
    per = rank // parts
    halves = sketch // SLOT

    def copy_in(source, target, sem):
        copy = pltpu.make_async_copy(source, target, sem)
        copy.start()
        return copy

    order_copy = copy_in(order_hbm.at[0], order, order_sem)
    pending = []
    for n, (data_hbm, data, first_hbm, second_hbm, weights) in enumerate(
        [
            (grads_hbm, grads, proj_out_hbm, up_hbm, weights_out),
            (acts_hbm, acts, proj_in_hbm, down_hbm, weights_in),
        ]
    ):
        first = [
            copy_in(first_hbm.at[0], weights.at[pl.ds(0, sketch)], sems.at[n, 0]),
            copy_in(second_hbm.at[0], weights.at[pl.ds(sketch, rank)], sems.at[n, 1]),
        ]
        chunks = []
        for start in range(0, data.shape[1], CHUNK):
            here = pl.ds(start, min(CHUNK, data.shape[1] - start))
            chunks.append(
                (
                    here,
                    copy_in(
                        data_hbm.at[0, :, here],
                        data.at[:, here],
                        sems.at[n, 2 + len(chunks)],
                    ),
                )
            )
        pending.append((first, chunks))

    order_copy.wait()
    rows = examples * parts
    lane = lax.broadcasted_iota(jnp.int32, (rows, 2 * tokens), 1)
    source = (lane % tokens) // EXAMPLE_LENGTH
    target = jnp.zeros((8, 2 * tokens), jnp.int32)
    for s in range(examples):
        target = jnp.where(source[:8] == s, order[0, s], target)
    target = jnp.concatenate([target] * (rows // 8), axis=0)
    place = lax.broadcasted_iota(jnp.int32, (rows, 2 * tokens), 0) // parts
    mask[...] = jnp.where(target == place, scaling, 0.0)

    def product(n, data, weights):
        first, chunks = pending[n]
        for copy in first:
            copy.wait()
        total = None
        for here, copy in chunks:
            copy.wait()
            term = dot_nt(weights[:, here], data[:, here])
            total = term if total is None else total + term
        return total

    from_grads = product(0, grads, weights_out)
    from_acts = product(1, acts, weights_in)
    sketches = jnp.concatenate([from_acts[:sketch], from_grads[:sketch]], axis=1)
    low[0] = from_grads[sketch:]
    low[1] = from_acts[sketch:]

    highs, lows = [], []
    for c in range(per):
        chosen = jnp.concatenate(
            [low[i, pl.ds(c, parts, stride=per), :] for i in range(2)], axis=1
        )
        chosen = jnp.concatenate([chosen] * examples, axis=0)
        high, rest = split(chosen * mask[...])
        highs.append(high)
        lows.append(rest)
    left_high = jnp.concatenate(highs, axis=0)
    left_low = jnp.concatenate(lows, axis=0)
    right = jnp.concatenate(
        [sketches[h * SLOT : (h + 1) * SLOT] for h in range(halves) for _ in range(per)],
        axis=0,
    )
    right_high, right_low = split(right)
    both = dot_nt(jnp.concatenate([left_high, left_low], axis=0), right_high)
    size = left_high.shape[0]
    spread = (dot_nt(left_high, right_low) + both[size:]) + both[:size]
    column = lax.broadcasted_iota(jnp.int32, (rows, per * sketch), 1)
    channel = (column // SLOT) % per
    total = spread[:rows]
    for c in range(1, per):
        total = jnp.where(channel == c, spread[c * rows : (c + 1) * rows], total)
    me = lax.axis_index("mp")
    for start in range(0, per * sketch, LANES):
        stop = min(start + LANES, per * sketch)
        out[:, : stop - start] = total[:, start:stop]
        for d in range(parts):
            g = me ^ d
            sends[d][:examples, start:stop] = out[
                pl.ds(pl.multiple_of(g * examples, examples), examples), : stop - start
            ]
            sends[d][examples:, start:stop] = out[pl.ds(g, examples, stride=parts), :][
                :, : stop - start
            ]


def sum_kernel(*refs):
    chunks, (columns, feature_rows) = refs[:-2], refs[-2:]
    examples, padded = columns.shape
    total = chunks[0][...]
    for chunk in chunks[1:]:
        total = total + chunk[...]
    width = total.shape[1]
    for ref, value in ((feature_rows, total[:examples]), (columns, total[examples:])):
        ref[:, :width] = value
        if padded > width:
            ref[:, width:] = jnp.zeros((examples, padded - width), jnp.float32)


def stack_kernel(*refs):
    rows = refs[0].shape[0]
    for n, part in enumerate(refs[:-1]):
        refs[-1][n * rows : (n + 1) * rows, :] = part[...]


def write_features(total, parts, per, features):
    rows_here, width = features.shape
    span = width // parts
    halves = span // (per * SLOT)
    natural = jnp.concatenate(
        [
            total[:, (h * per + c) * SLOT : (h * per + c + 1) * SLOT]
            for c in range(per)
            for h in range(halves)
        ],
        axis=1,
    )
    for r in range(rows_here):
        features[r : r + 1, :] = jnp.concatenate(
            [natural[r * parts + g : r * parts + g + 1, :] for g in range(parts)], axis=1
        )


def pick_lanes(x, index):
    return jnp.take_along_axis(x, index, axis=1)


def reciprocal(x):
    guess = pl.reciprocal(x, approx=True)
    return guess * (2.0 - x * guess)


def factor_kernel(parts, damping, held, sent, features, factors):
    channels, sketch, _ = factors.shape
    examples = features.shape[0] * parts
    gathered = held.shape[0] - examples
    span = features.shape[1] // parts
    write_features(sent[gathered:, :span], parts, channels, features)
    halves = sketch // SLOT
    panels = sketch // PANEL
    per_half = SLOT // PANEL
    stacked = jnp.concatenate([held[:gathered, :], sent[:gathered, :]], axis=0)
    high, rest = split(stacked)
    turned_high, turned_rest = split(jnp.transpose(stacked))
    gram = dot_nn(turned_high, rest) + dot_nn(
        jnp.concatenate([turned_rest, turned_high], axis=1),
        jnp.concatenate([high, high], axis=0),
    )
    lane = lax.broadcasted_iota(jnp.int32, (PANEL, LANES), 1)
    sub = lax.broadcasted_iota(jnp.int32, (PANEL, LANES), 0)
    slot = lane // SLOT
    within = lane % SLOT
    ridge = damping[0]
    tile = []
    for q in range(panels):
        hr, at = divmod(q, per_half)
        line = []
        for h in range(halves):
            value = None
            for c in range(GROUP):
                start = hr * LANES + c * SLOT + at * PANEL
                block = gram[start : start + PANEL, h * LANES : (h + 1) * LANES]
                value = block if c == 0 else jnp.where(slot == c, block, value)
            value = value * (1.0 / stacked.shape[0])
            if h == hr:
                value = value + jnp.where(within == at * PANEL + sub, ridge, 0.0)
            line.append(value)
        tile.append(line)

    zero = jnp.zeros((PANEL, LANES), jnp.float32)
    finished = []
    ahead = [pick_lanes(tile[0][0], slot * SLOT + r) for r in range(PANEL)]
    for q in range(panels):
        hq, at = divmod(q, per_half)
        if q + 1 < panels:
            hn, an = divmod(q + 1, per_half)
            behind = [
                pick_lanes(tile[q + 1][hn], slot * SLOT + an * PANEL + r)
                for r in range(PANEL)
            ]
        column = [
            {
                j: ahead[r]
                if j == q
                else pick_lanes(tile[j][hq], slot * SLOT + at * PANEL + r)
                for j in range(q, panels)
            }
            for r in range(PANEL)
        ]
        block = [
            [
                jnp.broadcast_to(column[r][q][s : s + 1, :], (PANEL, LANES))
                if s >= r
                else None
                for s in range(PANEL)
            ]
            for r in range(PANEL)
        ]
        line = [
            [
                jnp.broadcast_to(tile[q][h][r : r + 1, :], (PANEL, LANES))
                if h >= hq
                else None
                for h in range(halves)
            ]
            for r in range(PANEL)
        ]
        inverse = []

        def eliminate(r, s, inv):
            ratio = block[r][s] * inv
            for t in range(s, PANEL):
                block[s][t] = block[s][t] - ratio * block[r][t]
            for j in range(q + 1, panels):
                column[s][j] = column[s][j] - ratio * column[r][j]
            for h in range(hq, halves):
                line[s][h] = line[s][h] - ratio * line[r][h]

        for r in range(0, PANEL, 2):
            pivot = block[r][r]
            minor = pivot * block[r + 1][r + 1] - block[r][r + 1] * block[r][r + 1]
            inverse.append(reciprocal(pivot))
            inverse.append(pivot * reciprocal(minor))
            eliminate(r, r + 1, inverse[r])
            for s in range(r + 2, PANEL):
                eliminate(r, s, inverse[r])
                eliminate(r + 1, s, inverse[r + 1])
        result = []
        for h in range(halves):
            if h < hq:
                result.append(zero)
                continue
            value = zero
            for r in range(PANEL):
                value = jnp.where(sub == r, line[r][h] * lax.rsqrt(block[r][r]), value)
            if h == hq:
                value = jnp.where(within >= at * PANEL + sub, value, 0.0)
            result.append(value)
        finished.append(result)
        for j in range(q + 1, panels):
            weights = [column[r][j] * inverse[r] for r in range(PANEL)]
            if j == q + 1:
                ahead = behind
                for r in range(PANEL):
                    for s in range(PANEL):
                        factor = jnp.broadcast_to(
                            column[r][j][s : s + 1, :], (PANEL, LANES)
                        )
                        ahead[s] = ahead[s] - weights[r] * factor
            for h in range((q + 1) // per_half, halves):
                value = tile[j][h]
                for r in range(PANEL):
                    value = value - weights[r] * line[r][h]
                tile[j][h] = value

    for q in range(panels):
        for c in range(channels):
            factors[c, q * PANEL : (q + 1) * PANEL, :] = jnp.concatenate(
                [finished[q][h][:, c * SLOT : (c + 1) * SLOT] for h in range(halves)],
                axis=1,
            )


def exchange(x, ex_distance, mp_distance=0):
    shards, parts = lax.axis_size("ex"), lax.axis_size("mp")
    return lax.ppermute(
        x,
        ("ex", "mp"),
        [
            (m * parts + b, (m ^ ex_distance) * parts + (b ^ mp_distance))
            for m in range(shards)
            for b in range(parts)
        ],
    )


def vmem():
    return pl.BlockSpec(memory_space=pltpu.VMEM)


def hbm():
    return pl.BlockSpec(memory_space=pltpu.HBM)


def in_hbm(*arrays):
    return [pltpu.with_memory_space_constraint(x, pltpu.HBM) for x in arrays]


def in_vmem(*arrays):
    return [pltpu.with_memory_space_constraint(x, pltpu.VMEM) for x in arrays]


def smem():
    return pl.BlockSpec(memory_space=pltpu.SMEM)


def local(
    acts,
    grads,
    down_factor,
    up_factor_transposed,
    input_projection,
    gradient_projection,
    order,
    damping,
):
    parts = lax.axis_size("mp")
    shards = lax.axis_size("ex")
    tokens, width = acts.shape[1:]
    key_width = grads.shape[2]
    rank = down_factor.shape[1]
    sketch = input_projection.shape[1]
    examples = tokens // EXAMPLE_LENGTH
    per = rank // parts
    span = per * sketch
    scaling = 1.0 / math.sqrt(2.0 * EXAMPLE_LENGTH * parts)
    sends = pl.pallas_call(
        functools.partial(partial_kernel, parts, scaling),
        out_shape=[pltpu.VMEM((2 * examples, span), jnp.float32)] * parts,
        in_specs=[hbm()] * 7,
        out_specs=[vmem()] * parts,
        scratch_shapes=[
            pltpu.VMEM((tokens, width), acts.dtype),
            pltpu.VMEM((tokens, key_width), grads.dtype),
            pltpu.VMEM((sketch + rank, width), acts.dtype),
            pltpu.VMEM((sketch + rank, key_width), grads.dtype),
            pltpu.SMEM(order.shape[1:], order.dtype),
            pltpu.VMEM((2, rank, tokens), jnp.float32),
            pltpu.VMEM((examples * parts, 2 * tokens), jnp.float32),
            pltpu.VMEM((examples * parts, LANES), jnp.float32),
            pltpu.SemaphoreType.DMA((2, 2 + pl.cdiv(max(width, key_width), CHUNK))),
            pltpu.SemaphoreType.DMA,
        ],
        compiler_params=pltpu.CompilerParams(vmem_limit_bytes=8 * 2**20),
        name="partials",
    )(
        *in_hbm(
            acts,
            grads,
            down_factor,
            up_factor_transposed,
            input_projection,
            gradient_projection,
            order,
        )
    )
    chunks = [exchange(sends[d], 1, d) for d in range(parts - 1, -1, -1)]
    padded = max(span, GROUP * sketch)
    columns, feature_rows = pl.pallas_call(
        sum_kernel,
        out_shape=[pltpu.VMEM((examples, padded), jnp.float32)] * 2,
        in_specs=[vmem()] * parts,
        out_specs=[vmem()] * 2,
        compiler_params=pltpu.CompilerParams(vmem_limit_bytes=2 * 2**20),
        name="sums",
    )(*in_vmem(*chunks))
    near = [columns] + [exchange(columns, d) for d in range(3, shards, 2)] + [feature_rows]
    held = pl.pallas_call(
        stack_kernel,
        out_shape=pltpu.VMEM((len(near) * examples, padded), jnp.float32),
        in_specs=[vmem()] * len(near),
        out_specs=vmem(),
        compiler_params=pltpu.CompilerParams(vmem_limit_bytes=2 * 2**20),
        name="stack",
    )(*in_vmem(*near))
    sent = exchange(held, 1)
    return pl.pallas_call(
        functools.partial(factor_kernel, parts),
        out_shape=[
            jax.ShapeDtypeStruct((examples // parts, rank * sketch), jnp.float32),
            jax.ShapeDtypeStruct((per, sketch, sketch), jnp.float32),
        ],
        in_specs=[smem()] + [vmem()] * 2,
        out_specs=[vmem()] * 2,
        compiler_params=pltpu.CompilerParams(vmem_limit_bytes=8 * 2**20),
        name="factors",
    )(damping, *in_vmem(held, sent))


def solution(mesh):
    in_specs = (
        P("mp", "ex", None),
        P("mp", "ex", None),
        P("mp", None, None),
        P("mp", None, None),
        P("mp", None, None),
        P("mp", None, None),
        P("mp", "ex", None),
        P(),
    )
    out_specs = (P(("ex", "mp"), None), P("mp", None, None))
    return jax.shard_map(
        local, mesh=mesh, in_specs=in_specs, out_specs=out_specs, check_vma=False
    )
```

```python
import functools
import itertools
import math

import jax
import jax.numpy as jnp
from jax import lax
from jax.experimental import pallas as pl
from jax.experimental.pallas import tpu as pltpu
from jax.sharding import PartitionSpec as P

EXAMPLE_LENGTH = 8
LANES = 128
SLOT = 32
GROUP = LANES // SLOT
PANEL = 8
CHUNK = 1024


def dot_nt(a, b):
    return lax.dot_general(
        a, b, (((1,), (1,)), ((), ())), preferred_element_type=jnp.float32
    )


def dot_nn(a, b):
    return jnp.dot(a, b, preferred_element_type=jnp.float32)


def split(x):
    high = x.astype(jnp.bfloat16)
    return high, (x - high.astype(jnp.float32)).astype(jnp.bfloat16)


def partial_kernel(
    parts,
    scaling,
    acts_hbm,
    grads_hbm,
    down_hbm,
    up_hbm,
    proj_in_hbm,
    proj_out_hbm,
    order_hbm,
    *refs,
):
    sends, refs = refs[:parts], refs[parts:]
    acts, grads, weights_in, weights_out, order, low, mask, out, sems, order_sem = refs
    tokens, width = acts.shape
    rank = down_hbm.shape[1]
    sketch = proj_in_hbm.shape[1]
    examples = tokens // EXAMPLE_LENGTH
    per = rank // parts
    halves = sketch // SLOT

    queue = itertools.cycle((0, 1))

    def copy_in(source, target, sem):
        copy = pltpu.make_async_copy(source, target, sem)
        copy.start(priority=next(queue))
        return copy

    order_copy = copy_in(order_hbm.at[0], order, order_sem)
    pending = []
    for n, (data_hbm, data, first_hbm, second_hbm, weights) in enumerate(
        [
            (grads_hbm, grads, proj_out_hbm, up_hbm, weights_out),
            (acts_hbm, acts, proj_in_hbm, down_hbm, weights_in),
        ]
    ):
        first = [
            copy_in(first_hbm.at[0], weights.at[pl.ds(0, sketch)], sems.at[n, 0]),
            copy_in(second_hbm.at[0], weights.at[pl.ds(sketch, rank)], sems.at[n, 1]),
        ]
        chunks = []
        for start in range(0, data.shape[1], CHUNK):
            here = pl.ds(start, min(CHUNK, data.shape[1] - start))
            chunks.append(
                (
                    here,
                    copy_in(
                        data_hbm.at[0, :, here],
                        data.at[:, here],
                        sems.at[n, 2 + len(chunks)],
                    ),
                )
            )
        pending.append((first, chunks))

    order_copy.wait()
    rows = examples * parts
    lane = lax.broadcasted_iota(jnp.int32, (rows, 2 * tokens), 1)
    source = (lane % tokens) // EXAMPLE_LENGTH
    target = jnp.zeros((8, 2 * tokens), jnp.int32)
    for s in range(examples):
        target = jnp.where(source[:8] == s, order[0, s], target)
    target = jnp.concatenate([target] * (rows // 8), axis=0)
    place = lax.broadcasted_iota(jnp.int32, (rows, 2 * tokens), 0) // parts
    mask[...] = jnp.where(target == place, scaling, 0.0)

    def product(n, data, weights):
        first, chunks = pending[n]
        for copy in first:
            copy.wait()
        total = None
        for here, copy in chunks:
            copy.wait()
            term = dot_nt(weights[:, here], data[:, here])
            total = term if total is None else total + term
        return total

    from_grads = product(0, grads, weights_out)
    from_acts = product(1, acts, weights_in)
    sketches = jnp.concatenate([from_acts[:sketch], from_grads[:sketch]], axis=1)
    low[0] = from_grads[sketch:]
    low[1] = from_acts[sketch:]

    highs, lows = [], []
    for c in range(per):
        chosen = jnp.concatenate(
            [low[i, pl.ds(c, parts, stride=per), :] for i in range(2)], axis=1
        )
        chosen = jnp.concatenate([chosen] * examples, axis=0)
        high, rest = split(chosen * mask[...])
        highs.append(high)
        lows.append(rest)
    left_high = jnp.concatenate(highs, axis=0)
    left_low = jnp.concatenate(lows, axis=0)
    right = jnp.concatenate(
        [sketches[h * SLOT : (h + 1) * SLOT] for h in range(halves) for _ in range(per)],
        axis=0,
    )
    right_high, right_low = split(right)
    both = dot_nt(jnp.concatenate([left_high, left_low], axis=0), right_high)
    size = left_high.shape[0]
    spread = (dot_nt(left_high, right_low) + both[size:]) + both[:size]
    column = lax.broadcasted_iota(jnp.int32, (rows, per * sketch), 1)
    channel = (column // SLOT) % per
    total = spread[:rows]
    for c in range(1, per):
        total = jnp.where(channel == c, spread[c * rows : (c + 1) * rows], total)
    me = lax.axis_index("mp")
    for start in range(0, per * sketch, LANES):
        stop = min(start + LANES, per * sketch)
        out[:, : stop - start] = total[:, start:stop]
        for d in range(parts):
            g = me ^ d
            sends[d][:examples, start:stop] = out[
                pl.ds(pl.multiple_of(g * examples, examples), examples), : stop - start
            ]
            sends[d][examples:, start:stop] = out[pl.ds(g, examples, stride=parts), :][
                :, : stop - start
            ]


def sum_kernel(*refs):
    chunks, (columns, feature_rows) = refs[:-2], refs[-2:]
    examples, padded = columns.shape
    total = chunks[0][...]
    for chunk in chunks[1:]:
        total = total + chunk[...]
    width = total.shape[1]
    for ref, value in ((feature_rows, total[:examples]), (columns, total[examples:])):
        ref[:, :width] = value
        if padded > width:
            ref[:, width:] = jnp.zeros((examples, padded - width), jnp.float32)


def stack_kernel(*refs):
    rows = refs[0].shape[0]
    for n, part in enumerate(refs[:-1]):
        refs[-1][n * rows : (n + 1) * rows, :] = part[...]


def write_features(total, parts, per, features):
    rows_here, width = features.shape
    span = width // parts
    halves = span // (per * SLOT)
    natural = jnp.concatenate(
        [
            total[:, (h * per + c) * SLOT : (h * per + c + 1) * SLOT]
            for c in range(per)
            for h in range(halves)
        ],
        axis=1,
    )
    for r in range(rows_here):
        features[r : r + 1, :] = jnp.concatenate(
            [natural[r * parts + g : r * parts + g + 1, :] for g in range(parts)], axis=1
        )


def pick_lanes(x, index):
    return jnp.take_along_axis(x, index, axis=1)


def reciprocal(x):
    guess = pl.reciprocal(x, approx=True)
    return guess * (2.0 - x * guess)


def factor_kernel(parts, damping, held, sent, features, factors):
    channels, sketch, _ = factors.shape
    examples = features.shape[0] * parts
    gathered = held.shape[0] - examples
    span = features.shape[1] // parts
    write_features(sent[gathered:, :span], parts, channels, features)
    halves = sketch // SLOT
    panels = sketch // PANEL
    per_half = SLOT // PANEL
    stacked = jnp.concatenate([held[:gathered, :], sent[:gathered, :]], axis=0)
    high, rest = split(stacked)
    turned_high, turned_rest = split(jnp.transpose(stacked))
    gram = dot_nn(turned_high, rest) + dot_nn(
        jnp.concatenate([turned_rest, turned_high], axis=1),
        jnp.concatenate([high, high], axis=0),
    )
    lane = lax.broadcasted_iota(jnp.int32, (PANEL, LANES), 1)
    sub = lax.broadcasted_iota(jnp.int32, (PANEL, LANES), 0)
    slot = lane // SLOT
    within = lane % SLOT
    ridge = damping[0]
    tile = []
    for q in range(panels):
        hr, at = divmod(q, per_half)
        line = []
        for h in range(halves):
            value = None
            for c in range(GROUP):
                start = hr * LANES + c * SLOT + at * PANEL
                block = gram[start : start + PANEL, h * LANES : (h + 1) * LANES]
                value = block if c == 0 else jnp.where(slot == c, block, value)
            value = value * (1.0 / stacked.shape[0])
            if h == hr:
                value = value + jnp.where(within == at * PANEL + sub, ridge, 0.0)
            line.append(value)
        tile.append(line)

    zero = jnp.zeros((PANEL, LANES), jnp.float32)
    finished = []
    ahead = [pick_lanes(tile[0][0], slot * SLOT + r) for r in range(PANEL)]
    for q in range(panels):
        hq, at = divmod(q, per_half)
        if q + 1 < panels:
            hn, an = divmod(q + 1, per_half)
            behind = [
                pick_lanes(tile[q + 1][hn], slot * SLOT + an * PANEL + r)
                for r in range(PANEL)
            ]
        column = [
            {
                j: ahead[r]
                if j == q
                else pick_lanes(tile[j][hq], slot * SLOT + at * PANEL + r)
                for j in range(q, panels)
            }
            for r in range(PANEL)
        ]
        block = [
            [
                jnp.broadcast_to(column[r][q][s : s + 1, :], (PANEL, LANES))
                if s >= r
                else None
                for s in range(PANEL)
            ]
            for r in range(PANEL)
        ]
        line = [
            [
                jnp.broadcast_to(tile[q][h][r : r + 1, :], (PANEL, LANES))
                if h >= hq
                else None
                for h in range(halves)
            ]
            for r in range(PANEL)
        ]
        inverse = []

        def eliminate(r, s, inv):
            ratio = block[r][s] * inv
            for t in range(s, PANEL):
                block[s][t] = block[s][t] - ratio * block[r][t]
            for j in range(q + 1, panels):
                column[s][j] = column[s][j] - ratio * column[r][j]
            for h in range(hq, halves):
                line[s][h] = line[s][h] - ratio * line[r][h]

        for r in range(0, PANEL, 2):
            pivot = block[r][r]
            minor = pivot * block[r + 1][r + 1] - block[r][r + 1] * block[r][r + 1]
            inverse.append(reciprocal(pivot))
            inverse.append(pivot * reciprocal(minor))
            eliminate(r, r + 1, inverse[r])
            for s in range(r + 2, PANEL):
                eliminate(r, s, inverse[r])
                eliminate(r + 1, s, inverse[r + 1])
        result = []
        for h in range(halves):
            if h < hq:
                result.append(zero)
                continue
            value = zero
            for r in range(PANEL):
                value = jnp.where(sub == r, line[r][h] * lax.rsqrt(block[r][r]), value)
            if h == hq:
                value = jnp.where(within >= at * PANEL + sub, value, 0.0)
            result.append(value)
        finished.append(result)
        for j in range(q + 1, panels):
            weights = [column[r][j] * inverse[r] for r in range(PANEL)]
            if j == q + 1:
                ahead = behind
                for r in range(PANEL):
                    for s in range(PANEL):
                        factor = jnp.broadcast_to(
                            column[r][j][s : s + 1, :], (PANEL, LANES)
                        )
                        ahead[s] = ahead[s] - weights[r] * factor
            for h in range((q + 1) // per_half, halves):
                value = tile[j][h]
                for r in range(PANEL):
                    value = value - weights[r] * line[r][h]
                tile[j][h] = value

    for q in range(panels):
        for c in range(channels):
            factors[c, q * PANEL : (q + 1) * PANEL, :] = jnp.concatenate(
                [finished[q][h][:, c * SLOT : (c + 1) * SLOT] for h in range(halves)],
                axis=1,
            )


def exchange(x, ex_distance, mp_distance=0):
    shards, parts = lax.axis_size("ex"), lax.axis_size("mp")
    return lax.ppermute(
        x,
        ("ex", "mp"),
        [
            (m * parts + b, (m ^ ex_distance) * parts + (b ^ mp_distance))
            for m in range(shards)
            for b in range(parts)
        ],
    )


def vmem():
    return pl.BlockSpec(memory_space=pltpu.VMEM)


def hbm():
    return pl.BlockSpec(memory_space=pltpu.HBM)


def in_hbm(*arrays):
    return [pltpu.with_memory_space_constraint(x, pltpu.HBM) for x in arrays]


def in_vmem(*arrays):
    return [pltpu.with_memory_space_constraint(x, pltpu.VMEM) for x in arrays]


def smem():
    return pl.BlockSpec(memory_space=pltpu.SMEM)


def local(
    acts,
    grads,
    down_factor,
    up_factor_transposed,
    input_projection,
    gradient_projection,
    order,
    damping,
):
    parts = lax.axis_size("mp")
    shards = lax.axis_size("ex")
    tokens, width = acts.shape[1:]
    key_width = grads.shape[2]
    rank = down_factor.shape[1]
    sketch = input_projection.shape[1]
    examples = tokens // EXAMPLE_LENGTH
    per = rank // parts
    span = per * sketch
    scaling = 1.0 / math.sqrt(2.0 * EXAMPLE_LENGTH * parts)
    sends = pl.pallas_call(
        functools.partial(partial_kernel, parts, scaling),
        out_shape=[pltpu.VMEM((2 * examples, span), jnp.float32)] * parts,
        in_specs=[hbm()] * 7,
        out_specs=[vmem()] * parts,
        scratch_shapes=[
            pltpu.VMEM((tokens, width), acts.dtype),
            pltpu.VMEM((tokens, key_width), grads.dtype),
            pltpu.VMEM((sketch + rank, width), acts.dtype),
            pltpu.VMEM((sketch + rank, key_width), grads.dtype),
            pltpu.SMEM(order.shape[1:], order.dtype),
            pltpu.VMEM((2, rank, tokens), jnp.float32),
            pltpu.VMEM((examples * parts, 2 * tokens), jnp.float32),
            pltpu.VMEM((examples * parts, LANES), jnp.float32),
            pltpu.SemaphoreType.DMA((2, 2 + pl.cdiv(max(width, key_width), CHUNK))),
            pltpu.SemaphoreType.DMA,
        ],
        compiler_params=pltpu.CompilerParams(vmem_limit_bytes=8 * 2**20),
        name="partials",
    )(
        *in_hbm(
            acts,
            grads,
            down_factor,
            up_factor_transposed,
            input_projection,
            gradient_projection,
            order,
        )
    )
    chunks = [exchange(sends[d], 1, d) for d in range(parts - 1, -1, -1)]
    padded = max(span, GROUP * sketch)
    columns, feature_rows = pl.pallas_call(
        sum_kernel,
        out_shape=[pltpu.VMEM((examples, padded), jnp.float32)] * 2,
        in_specs=[vmem()] * parts,
        out_specs=[vmem()] * 2,
        compiler_params=pltpu.CompilerParams(vmem_limit_bytes=2 * 2**20),
        name="sums",
    )(*in_vmem(*chunks))
    near = [columns] + [exchange(columns, d) for d in range(3, shards, 2)] + [feature_rows]
    held = pl.pallas_call(
        stack_kernel,
        out_shape=pltpu.VMEM((len(near) * examples, padded), jnp.float32),
        in_specs=[vmem()] * len(near),
        out_specs=vmem(),
        compiler_params=pltpu.CompilerParams(vmem_limit_bytes=2 * 2**20),
        name="stack",
    )(*in_vmem(*near))
    sent = exchange(held, 1)
    return pl.pallas_call(
        functools.partial(factor_kernel, parts),
        out_shape=[
            jax.ShapeDtypeStruct((examples // parts, rank * sketch), jnp.float32),
            jax.ShapeDtypeStruct((per, sketch, sketch), jnp.float32),
        ],
        in_specs=[smem()] + [vmem()] * 2,
        out_specs=[vmem()] * 2,
        compiler_params=pltpu.CompilerParams(vmem_limit_bytes=8 * 2**20),
        name="factors",
    )(damping, *in_vmem(held, sent))


def solution(mesh):
    in_specs = (
        P("mp", "ex", None),
        P("mp", "ex", None),
        P("mp", None, None),
        P("mp", None, None),
        P("mp", None, None),
        P("mp", None, None),
        P("mp", "ex", None),
        P(),
    )
    out_specs = (P(("ex", "mp"), None), P("mp", None, None))
    return jax.shard_map(
        local, mesh=mesh, in_specs=in_specs, out_specs=out_specs, check_vma=False
    )
```

```python
import functools
import math

import jax
import jax.numpy as jnp
from jax import lax
from jax.experimental import pallas as pl
from jax.experimental.pallas import tpu as pltpu
from jax.sharding import PartitionSpec as P

EXAMPLE_LENGTH = 8
LANES = 128
SLOT = 32
GROUP = LANES // SLOT
PANEL = 8
CHUNK = 1024


def dot_nt(a, b):
    return lax.dot_general(
        a, b, (((1,), (1,)), ((), ())), preferred_element_type=jnp.float32
    )


def dot_nn(a, b):
    return jnp.dot(a, b, preferred_element_type=jnp.float32)


def split(x):
    high = x.astype(jnp.bfloat16)
    return high, (x - high.astype(jnp.float32)).astype(jnp.bfloat16)


def partial_kernel(
    parts,
    scaling,
    acts_hbm,
    grads_hbm,
    down_hbm,
    up_hbm,
    proj_in_hbm,
    proj_out_hbm,
    order_hbm,
    *refs,
):
    sends, refs = refs[:parts], refs[parts:]
    acts, grads, weights_in, weights_out, order, low, mask, out, sems, order_sem = refs
    tokens, width = acts.shape
    rank = down_hbm.shape[1]
    sketch = proj_in_hbm.shape[1]
    examples = tokens // EXAMPLE_LENGTH
    per = rank // parts
    halves = sketch // SLOT

    def copies(source, target, sem, start, size):
        return pltpu.make_async_copy(
            source.at[0, :, pl.ds(start, size)],
            target.at[:, pl.ds(start, size)],
            sem,
        )

    order_copy = pltpu.make_async_copy(order_hbm.at[0], order, order_sem)
    order_copy.start()
    sources = [
        (grads_hbm, grads, proj_out_hbm, up_hbm, weights_out),
        (acts_hbm, acts, proj_in_hbm, down_hbm, weights_in),
    ]
    pending = []
    for data_hbm, data, first_hbm, second_hbm, weights in sources:
        for start in range(0, data.shape[1], CHUNK):
            n = len(pending)
            pending.append(
                [
                    copies(first_hbm, weights.at[pl.ds(0, sketch)], sems.at[n, 0], start, CHUNK),
                    copies(second_hbm, weights.at[pl.ds(sketch, rank)], sems.at[n, 1], start, CHUNK),
                    copies(data_hbm, data, sems.at[n, 2], start, CHUNK),
                ]
            )
            for copy in pending[-1]:
                copy.start()

    order_copy.wait()
    rows = examples * parts
    lane = lax.broadcasted_iota(jnp.int32, (rows, 2 * tokens), 1)
    source = (lane % tokens) // EXAMPLE_LENGTH
    target = jnp.zeros((8, 2 * tokens), jnp.int32)
    for s in range(examples):
        target = jnp.where(source[:8] == s, order[0, s], target)
    target = jnp.concatenate([target] * (rows // 8), axis=0)
    place = lax.broadcasted_iota(jnp.int32, (rows, 2 * tokens), 0) // parts
    mask[...] = jnp.where(target == place, scaling, 0.0)

    def product(first, data, weights):
        total = None
        for n in range(data.shape[1] // CHUNK):
            for copy in pending[first + n]:
                copy.wait()
            here = pl.ds(n * CHUNK, CHUNK)
            term = dot_nt(data[:, here], weights[:, here])
            total = term if total is None else total + term
        return total

    from_grads = product(0, grads, weights_out)
    from_acts = product(grads.shape[1] // CHUNK, acts, weights_in)
    low[0] = jnp.transpose(from_grads)[sketch:]
    low[1] = jnp.transpose(from_acts)[sketch:]
    right_high, right_low = split(
        jnp.concatenate([from_acts[:, :sketch], from_grads[:, :sketch]], axis=0)
    )

    highs, lows = [], []
    for c in range(per):
        chosen = jnp.concatenate(
            [low[i, pl.ds(c, parts, stride=per), :] for i in range(2)], axis=1
        )
        chosen = jnp.concatenate([chosen] * examples, axis=0)
        high, rest = split(chosen * mask[...])
        highs.append(high)
        lows.append(rest)
    left_high = jnp.concatenate(highs, axis=0)
    left_low = jnp.concatenate(lows, axis=0)
    both = jnp.dot(
        jnp.concatenate([left_high, left_low], axis=0),
        right_high,
        preferred_element_type=jnp.float32,
    )
    size = left_high.shape[0]
    spread = (
        jnp.dot(left_high, right_low, preferred_element_type=jnp.float32) + both[size:]
    ) + both[:size]
    total = jnp.concatenate(
        [
            spread[c * rows : (c + 1) * rows, h * SLOT : (h + 1) * SLOT]
            for h in range(halves)
            for c in range(per)
        ],
        axis=1,
    )
    me = lax.axis_index("mp")
    for start in range(0, per * sketch, LANES):
        stop = min(start + LANES, per * sketch)
        out[:, : stop - start] = total[:, start:stop]
        for d in range(parts):
            g = me ^ d
            sends[d][:examples, start:stop] = out[
                pl.ds(pl.multiple_of(g * examples, examples), examples), : stop - start
            ]
            sends[d][examples:, start:stop] = out[pl.ds(g, examples, stride=parts), :][
                :, : stop - start
            ]


def sum_kernel(*refs):
    chunks, (columns, feature_rows) = refs[:-2], refs[-2:]
    examples, padded = columns.shape
    total = chunks[0][...]
    for chunk in chunks[1:]:
        total = total + chunk[...]
    width = total.shape[1]
    for ref, value in ((feature_rows, total[:examples]), (columns, total[examples:])):
        ref[:, :width] = value
        if padded > width:
            ref[:, width:] = jnp.zeros((examples, padded - width), jnp.float32)


def stack_kernel(*refs):
    rows = refs[0].shape[0]
    for n, part in enumerate(refs[:-1]):
        refs[-1][n * rows : (n + 1) * rows, :] = part[...]


def write_features(total, parts, per, features):
    rows_here, width = features.shape
    span = width // parts
    halves = span // (per * SLOT)
    natural = jnp.concatenate(
        [
            total[:, (h * per + c) * SLOT : (h * per + c + 1) * SLOT]
            for c in range(per)
            for h in range(halves)
        ],
        axis=1,
    )
    for r in range(rows_here):
        features[r : r + 1, :] = jnp.concatenate(
            [natural[r * parts + g : r * parts + g + 1, :] for g in range(parts)], axis=1
        )


def pick_lanes(x, index):
    return jnp.take_along_axis(x, index, axis=1)


def reciprocal(x):
    guess = pl.reciprocal(x, approx=True)
    return guess * (2.0 - x * guess)


def factor_kernel(parts, damping, held, sent, features, factors):
    channels, sketch, _ = factors.shape
    examples = features.shape[0] * parts
    gathered = held.shape[0] - examples
    span = features.shape[1] // parts
    write_features(sent[gathered:, :span], parts, channels, features)
    halves = sketch // SLOT
    panels = sketch // PANEL
    per_half = SLOT // PANEL
    stacked = jnp.concatenate([held[:gathered, :], sent[:gathered, :]], axis=0)
    high, rest = split(stacked)
    turned_high, turned_rest = split(jnp.transpose(stacked))
    gram = dot_nn(turned_high, rest) + dot_nn(
        jnp.concatenate([turned_rest, turned_high], axis=1),
        jnp.concatenate([high, high], axis=0),
    )
    lane = lax.broadcasted_iota(jnp.int32, (PANEL, LANES), 1)
    sub = lax.broadcasted_iota(jnp.int32, (PANEL, LANES), 0)
    slot = lane // SLOT
    within = lane % SLOT
    ridge = damping[0]
    tile = []
    for q in range(panels):
        hr, at = divmod(q, per_half)
        line = []
        for h in range(halves):
            value = None
            for c in range(GROUP):
                start = hr * LANES + c * SLOT + at * PANEL
                block = gram[start : start + PANEL, h * LANES : (h + 1) * LANES]
                value = block if c == 0 else jnp.where(slot == c, block, value)
            value = value * (1.0 / stacked.shape[0])
            if h == hr:
                value = value + jnp.where(within == at * PANEL + sub, ridge, 0.0)
            line.append(value)
        tile.append(line)

    zero = jnp.zeros((PANEL, LANES), jnp.float32)
    finished = []
    ahead = [pick_lanes(tile[0][0], slot * SLOT + r) for r in range(PANEL)]
    for q in range(panels):
        hq, at = divmod(q, per_half)
        if q + 1 < panels:
            hn, an = divmod(q + 1, per_half)
            behind = [
                pick_lanes(tile[q + 1][hn], slot * SLOT + an * PANEL + r)
                for r in range(PANEL)
            ]
        column = [
            {
                j: ahead[r]
                if j == q
                else pick_lanes(tile[j][hq], slot * SLOT + at * PANEL + r)
                for j in range(q, panels)
            }
            for r in range(PANEL)
        ]
        block = [
            [
                jnp.broadcast_to(column[r][q][s : s + 1, :], (PANEL, LANES))
                if s >= r
                else None
                for s in range(PANEL)
            ]
            for r in range(PANEL)
        ]
        line = [
            [
                jnp.broadcast_to(tile[q][h][r : r + 1, :], (PANEL, LANES))
                if h >= hq
                else None
                for h in range(halves)
            ]
            for r in range(PANEL)
        ]
        inverse = []

        def eliminate(r, s, inv):
            ratio = block[r][s] * inv
            for t in range(s, PANEL):
                block[s][t] = block[s][t] - ratio * block[r][t]
            for j in range(q + 1, panels):
                column[s][j] = column[s][j] - ratio * column[r][j]
            for h in range(hq, halves):
                line[s][h] = line[s][h] - ratio * line[r][h]

        for r in range(0, PANEL, 2):
            pivot = block[r][r]
            minor = pivot * block[r + 1][r + 1] - block[r][r + 1] * block[r][r + 1]
            inverse.append(reciprocal(pivot))
            inverse.append(pivot * reciprocal(minor))
            eliminate(r, r + 1, inverse[r])
            for s in range(r + 2, PANEL):
                eliminate(r, s, inverse[r])
                eliminate(r + 1, s, inverse[r + 1])
        result = []
        for h in range(halves):
            if h < hq:
                result.append(zero)
                continue
            value = zero
            for r in range(PANEL):
                value = jnp.where(sub == r, line[r][h] * lax.rsqrt(block[r][r]), value)
            if h == hq:
                value = jnp.where(within >= at * PANEL + sub, value, 0.0)
            result.append(value)
        finished.append(result)
        for j in range(q + 1, panels):
            weights = [column[r][j] * inverse[r] for r in range(PANEL)]
            if j == q + 1:
                ahead = behind
                for r in range(PANEL):
                    for s in range(PANEL):
                        factor = jnp.broadcast_to(
                            column[r][j][s : s + 1, :], (PANEL, LANES)
                        )
                        ahead[s] = ahead[s] - weights[r] * factor
            for h in range((q + 1) // per_half, halves):
                value = tile[j][h]
                for r in range(PANEL):
                    value = value - weights[r] * line[r][h]
                tile[j][h] = value

    for q in range(panels):
        for c in range(channels):
            factors[c, q * PANEL : (q + 1) * PANEL, :] = jnp.concatenate(
                [finished[q][h][:, c * SLOT : (c + 1) * SLOT] for h in range(halves)],
                axis=1,
            )


def exchange(x, ex_distance, mp_distance=0):
    shards, parts = lax.axis_size("ex"), lax.axis_size("mp")
    return lax.ppermute(
        x,
        ("ex", "mp"),
        [
            (m * parts + b, (m ^ ex_distance) * parts + (b ^ mp_distance))
            for m in range(shards)
            for b in range(parts)
        ],
    )


def vmem():
    return pl.BlockSpec(memory_space=pltpu.VMEM)


def hbm():
    return pl.BlockSpec(memory_space=pltpu.HBM)


def in_hbm(*arrays):
    return [pltpu.with_memory_space_constraint(x, pltpu.HBM) for x in arrays]


def in_vmem(*arrays):
    return [pltpu.with_memory_space_constraint(x, pltpu.VMEM) for x in arrays]


def smem():
    return pl.BlockSpec(memory_space=pltpu.SMEM)


def local(
    acts,
    grads,
    down_factor,
    up_factor_transposed,
    input_projection,
    gradient_projection,
    order,
    damping,
):
    parts = lax.axis_size("mp")
    shards = lax.axis_size("ex")
    tokens, width = acts.shape[1:]
    key_width = grads.shape[2]
    rank = down_factor.shape[1]
    sketch = input_projection.shape[1]
    examples = tokens // EXAMPLE_LENGTH
    per = rank // parts
    span = per * sketch
    scaling = 1.0 / math.sqrt(2.0 * EXAMPLE_LENGTH * parts)
    sends = pl.pallas_call(
        functools.partial(partial_kernel, parts, scaling),
        out_shape=[pltpu.VMEM((2 * examples, span), jnp.float32)] * parts,
        in_specs=[hbm()] * 7,
        out_specs=[vmem()] * parts,
        scratch_shapes=[
            pltpu.VMEM((tokens, width), acts.dtype),
            pltpu.VMEM((tokens, key_width), grads.dtype),
            pltpu.VMEM((sketch + rank, width), acts.dtype),
            pltpu.VMEM((sketch + rank, key_width), grads.dtype),
            pltpu.SMEM(order.shape[1:], order.dtype),
            pltpu.VMEM((2, rank, tokens), jnp.float32),
            pltpu.VMEM((examples * parts, 2 * tokens), jnp.float32),
            pltpu.VMEM((examples * parts, LANES), jnp.float32),
            pltpu.SemaphoreType.DMA(((width + key_width) // CHUNK, 3)),
            pltpu.SemaphoreType.DMA,
        ],
        compiler_params=pltpu.CompilerParams(vmem_limit_bytes=8 * 2**20),
        name="partials",
    )(
        *in_hbm(
            acts,
            grads,
            down_factor,
            up_factor_transposed,
            input_projection,
            gradient_projection,
            order,
        )
    )
    chunks = [exchange(sends[d], 1, d) for d in range(parts - 1, -1, -1)]
    padded = max(span, GROUP * sketch)
    columns, feature_rows = pl.pallas_call(
        sum_kernel,
        out_shape=[pltpu.VMEM((examples, padded), jnp.float32)] * 2,
        in_specs=[vmem()] * parts,
        out_specs=[vmem()] * 2,
        compiler_params=pltpu.CompilerParams(vmem_limit_bytes=2 * 2**20),
        name="sums",
    )(*in_vmem(*chunks))
    near = [columns] + [exchange(columns, d) for d in range(3, shards, 2)] + [feature_rows]
    held = pl.pallas_call(
        stack_kernel,
        out_shape=pltpu.VMEM((len(near) * examples, padded), jnp.float32),
        in_specs=[vmem()] * len(near),
        out_specs=vmem(),
        compiler_params=pltpu.CompilerParams(vmem_limit_bytes=2 * 2**20),
        name="stack",
    )(*in_vmem(*near))
    sent = exchange(held, 1)
    return pl.pallas_call(
        functools.partial(factor_kernel, parts),
        out_shape=[
            jax.ShapeDtypeStruct((examples // parts, rank * sketch), jnp.float32),
            jax.ShapeDtypeStruct((per, sketch, sketch), jnp.float32),
        ],
        in_specs=[smem()] + [vmem()] * 2,
        out_specs=[vmem()] * 2,
        compiler_params=pltpu.CompilerParams(vmem_limit_bytes=8 * 2**20),
        name="factors",
    )(damping, *in_vmem(held, sent))


def solution(mesh):
    in_specs = (
        P("mp", "ex", None),
        P("mp", "ex", None),
        P("mp", None, None),
        P("mp", None, None),
        P("mp", None, None),
        P("mp", None, None),
        P("mp", "ex", None),
        P(),
    )
    out_specs = (P(("ex", "mp"), None), P("mp", None, None))
    return jax.shard_map(
        local, mesh=mesh, in_specs=in_specs, out_specs=out_specs, check_vma=False
    )
```

```python
import functools
import math

import jax
import jax.numpy as jnp
from jax import lax
from jax.experimental import pallas as pl
from jax.experimental.pallas import tpu as pltpu
from jax.sharding import PartitionSpec as P

EXAMPLE_LENGTH = 8
LANES = 128
SLOT = 32
GROUP = LANES // SLOT
PANEL = 8
CHUNK = 1024


def dot_nt(a, b):
    return lax.dot_general(
        a, b, (((1,), (1,)), ((), ())), preferred_element_type=jnp.float32
    )


def dot_nn(a, b):
    return jnp.dot(a, b, preferred_element_type=jnp.float32)


def split(x):
    high = x.astype(jnp.bfloat16)
    return high, (x - high.astype(jnp.float32)).astype(jnp.bfloat16)


def partial_kernel(
    parts,
    scaling,
    acts_hbm,
    grads_hbm,
    down_hbm,
    up_hbm,
    proj_in_hbm,
    proj_out_hbm,
    order_hbm,
    *refs,
):
    sends, refs = refs[:parts], refs[parts:]
    acts, grads, weights_in, weights_out, order, low, mask, out, sems, order_sem = refs
    tokens, width = acts.shape
    rank = down_hbm.shape[1]
    sketch = proj_in_hbm.shape[1]
    examples = tokens // EXAMPLE_LENGTH
    per = rank // parts
    halves = sketch // SLOT

    def copies(source, target, sem, start, size):
        return pltpu.make_async_copy(
            source.at[0, :, pl.ds(start, size)],
            target.at[:, pl.ds(start, size)],
            sem,
        )

    order_copy = pltpu.make_async_copy(order_hbm.at[0], order, order_sem)
    order_copy.start()
    sources = [
        (grads_hbm, grads, proj_out_hbm, up_hbm, weights_out),
        (acts_hbm, acts, proj_in_hbm, down_hbm, weights_in),
    ]
    pending = []
    for data_hbm, data, first_hbm, second_hbm, weights in sources:
        for start in range(0, data.shape[1], CHUNK):
            n = len(pending)
            pending.append(
                [
                    copies(first_hbm, weights.at[pl.ds(0, sketch)], sems.at[n, 0], start, CHUNK),
                    copies(second_hbm, weights.at[pl.ds(sketch, rank)], sems.at[n, 1], start, CHUNK),
                    copies(data_hbm, data, sems.at[n, 2], start, CHUNK),
                ]
            )
            for copy in pending[-1]:
                copy.start()

    order_copy.wait()
    rows = examples * parts
    source = lax.broadcasted_iota(jnp.int32, (8, tokens), 1) // EXAMPLE_LENGTH
    target = jnp.zeros((8, tokens), jnp.int32)
    for s in range(examples):
        target = jnp.where(source == s, order[0, s], target)
    target = jnp.concatenate([target] * (rows // 8), axis=0)
    place = lax.broadcasted_iota(jnp.int32, (rows, tokens), 0) // parts
    mask[...] = jnp.where(target == place, scaling, 0.0)

    def product(first, data, weights):
        total = None
        for n in range(data.shape[1] // CHUNK):
            for copy in pending[first + n]:
                copy.wait()
            here = pl.ds(n * CHUNK, CHUNK)
            term = dot_nt(weights[:, here], data[:, here])
            total = term if total is None else total + term
        return total

    def spread_low(values, n):
        low[n] = values
        tiles = []
        for c in range(per):
            chosen = low[n, pl.ds(c, parts, stride=per), :]
            chosen = jnp.concatenate([chosen] * max(1, 8 // parts), axis=0)
            chosen = jnp.concatenate([chosen] * (rows // chosen.shape[0]), axis=0)
            tiles.append(split(chosen * mask[...]))
        return [jnp.concatenate(half, axis=0) for half in zip(*tiles)]

    def spread_sketch(values):
        return split(
            jnp.concatenate(
                [values[h * SLOT : (h + 1) * SLOT] for h in range(halves) for _ in range(per)],
                axis=0,
            )
        )

    from_grads = product(0, grads, weights_out)
    left_grads = spread_low(from_grads[sketch:], 0)
    right_grads = spread_sketch(from_grads[:sketch])
    from_acts = product(grads.shape[1] // CHUNK, acts, weights_in)
    left_acts = spread_low(from_acts[sketch:], 1)
    right_acts = spread_sketch(from_acts[:sketch])
    left_high, left_low = [
        jnp.concatenate(pair, axis=1) for pair in zip(left_grads, left_acts)
    ]
    right_high, right_low = [
        jnp.concatenate(pair, axis=1) for pair in zip(right_acts, right_grads)
    ]
    both = dot_nt(jnp.concatenate([left_high, left_low], axis=0), right_high)
    size = left_high.shape[0]
    spread = (dot_nt(left_high, right_low) + both[size:]) + both[:size]
    column = lax.broadcasted_iota(jnp.int32, (rows, per * sketch), 1)
    channel = (column // SLOT) % per
    total = spread[:rows]
    for c in range(1, per):
        total = jnp.where(channel == c, spread[c * rows : (c + 1) * rows], total)
    me = lax.axis_index("mp")
    for start in range(0, per * sketch, LANES):
        stop = min(start + LANES, per * sketch)
        out[:, : stop - start] = total[:, start:stop]
        for d in range(parts):
            g = me ^ d
            sends[d][:examples, start:stop] = out[
                pl.ds(pl.multiple_of(g * examples, examples), examples), : stop - start
            ]
            sends[d][examples:, start:stop] = out[pl.ds(g, examples, stride=parts), :][
                :, : stop - start
            ]


def sum_kernel(*refs):
    chunks, (columns, feature_rows) = refs[:-2], refs[-2:]
    examples, padded = columns.shape
    total = chunks[0][...]
    for chunk in chunks[1:]:
        total = total + chunk[...]
    width = total.shape[1]
    for ref, value in ((feature_rows, total[:examples]), (columns, total[examples:])):
        ref[:, :width] = value
        if padded > width:
            ref[:, width:] = jnp.zeros((examples, padded - width), jnp.float32)


def stack_kernel(*refs):
    rows = refs[0].shape[0]
    for n, part in enumerate(refs[:-1]):
        refs[-1][n * rows : (n + 1) * rows, :] = part[...]


def write_features(total, parts, per, features):
    rows_here, width = features.shape
    span = width // parts
    halves = span // (per * SLOT)
    natural = jnp.concatenate(
        [
            total[:, (h * per + c) * SLOT : (h * per + c + 1) * SLOT]
            for c in range(per)
            for h in range(halves)
        ],
        axis=1,
    )
    for r in range(rows_here):
        features[r : r + 1, :] = jnp.concatenate(
            [natural[r * parts + g : r * parts + g + 1, :] for g in range(parts)], axis=1
        )


def pick_lanes(x, index):
    return jnp.take_along_axis(x, index, axis=1)


def reciprocal(x):
    guess = pl.reciprocal(x, approx=True)
    return guess * (2.0 - x * guess)


def factor_kernel(parts, damping, held, sent, features, factors):
    channels, sketch, _ = factors.shape
    examples = features.shape[0] * parts
    gathered = held.shape[0] - examples
    span = features.shape[1] // parts
    write_features(sent[gathered:, :span], parts, channels, features)
    halves = sketch // SLOT
    panels = sketch // PANEL
    per_half = SLOT // PANEL
    stacked = jnp.concatenate([held[:gathered, :], sent[:gathered, :]], axis=0)
    high, rest = split(stacked)
    turned_high, turned_rest = split(jnp.transpose(stacked))
    gram = dot_nn(turned_high, rest) + dot_nn(
        jnp.concatenate([turned_rest, turned_high], axis=1),
        jnp.concatenate([high, high], axis=0),
    )
    lane = lax.broadcasted_iota(jnp.int32, (PANEL, LANES), 1)
    sub = lax.broadcasted_iota(jnp.int32, (PANEL, LANES), 0)
    slot = lane // SLOT
    within = lane % SLOT
    ridge = damping[0]
    tile = []
    for q in range(panels):
        hr, at = divmod(q, per_half)
        line = []
        for h in range(halves):
            value = None
            for c in range(GROUP):
                start = hr * LANES + c * SLOT + at * PANEL
                block = gram[start : start + PANEL, h * LANES : (h + 1) * LANES]
                value = block if c == 0 else jnp.where(slot == c, block, value)
            value = value * (1.0 / stacked.shape[0])
            if h == hr:
                value = value + jnp.where(within == at * PANEL + sub, ridge, 0.0)
            line.append(value)
        tile.append(line)

    zero = jnp.zeros((PANEL, LANES), jnp.float32)
    finished = []
    ahead = [pick_lanes(tile[0][0], slot * SLOT + r) for r in range(PANEL)]
    for q in range(panels):
        hq, at = divmod(q, per_half)
        if q + 1 < panels:
            hn, an = divmod(q + 1, per_half)
            behind = [
                pick_lanes(tile[q + 1][hn], slot * SLOT + an * PANEL + r)
                for r in range(PANEL)
            ]
        column = [
            {
                j: ahead[r]
                if j == q
                else pick_lanes(tile[j][hq], slot * SLOT + at * PANEL + r)
                for j in range(q, panels)
            }
            for r in range(PANEL)
        ]
        block = [
            [
                jnp.broadcast_to(column[r][q][s : s + 1, :], (PANEL, LANES))
                if s >= r
                else None
                for s in range(PANEL)
            ]
            for r in range(PANEL)
        ]
        line = [
            [
                jnp.broadcast_to(tile[q][h][r : r + 1, :], (PANEL, LANES))
                if h >= hq
                else None
                for h in range(halves)
            ]
            for r in range(PANEL)
        ]
        inverse = []

        def eliminate(r, s, inv):
            ratio = block[r][s] * inv
            for t in range(s, PANEL):
                block[s][t] = block[s][t] - ratio * block[r][t]
            for j in range(q + 1, panels):
                column[s][j] = column[s][j] - ratio * column[r][j]
            for h in range(hq, halves):
                line[s][h] = line[s][h] - ratio * line[r][h]

        for r in range(0, PANEL, 2):
            pivot = block[r][r]
            minor = pivot * block[r + 1][r + 1] - block[r][r + 1] * block[r][r + 1]
            inverse.append(reciprocal(pivot))
            inverse.append(pivot * reciprocal(minor))
            eliminate(r, r + 1, inverse[r])
            for s in range(r + 2, PANEL):
                eliminate(r, s, inverse[r])
                eliminate(r + 1, s, inverse[r + 1])
        result = []
        for h in range(halves):
            if h < hq:
                result.append(zero)
                continue
            value = zero
            for r in range(PANEL):
                value = jnp.where(sub == r, line[r][h] * lax.rsqrt(block[r][r]), value)
            if h == hq:
                value = jnp.where(within >= at * PANEL + sub, value, 0.0)
            result.append(value)
        finished.append(result)
        for j in range(q + 1, panels):
            weights = [column[r][j] * inverse[r] for r in range(PANEL)]
            if j == q + 1:
                ahead = behind
                for r in range(PANEL):
                    for s in range(PANEL):
                        factor = jnp.broadcast_to(
                            column[r][j][s : s + 1, :], (PANEL, LANES)
                        )
                        ahead[s] = ahead[s] - weights[r] * factor
            for h in range((q + 1) // per_half, halves):
                value = tile[j][h]
                for r in range(PANEL):
                    value = value - weights[r] * line[r][h]
                tile[j][h] = value

    for q in range(panels):
        for c in range(channels):
            factors[c, q * PANEL : (q + 1) * PANEL, :] = jnp.concatenate(
                [finished[q][h][:, c * SLOT : (c + 1) * SLOT] for h in range(halves)],
                axis=1,
            )


def exchange(x, ex_distance, mp_distance=0):
    shards, parts = lax.axis_size("ex"), lax.axis_size("mp")
    return lax.ppermute(
        x,
        ("ex", "mp"),
        [
            (m * parts + b, (m ^ ex_distance) * parts + (b ^ mp_distance))
            for m in range(shards)
            for b in range(parts)
        ],
    )


def vmem():
    return pl.BlockSpec(memory_space=pltpu.VMEM)


def hbm():
    return pl.BlockSpec(memory_space=pltpu.HBM)


def in_hbm(*arrays):
    return [pltpu.with_memory_space_constraint(x, pltpu.HBM) for x in arrays]


def in_vmem(*arrays):
    return [pltpu.with_memory_space_constraint(x, pltpu.VMEM) for x in arrays]


def smem():
    return pl.BlockSpec(memory_space=pltpu.SMEM)


def local(
    acts,
    grads,
    down_factor,
    up_factor_transposed,
    input_projection,
    gradient_projection,
    order,
    damping,
):
    parts = lax.axis_size("mp")
    shards = lax.axis_size("ex")
    tokens, width = acts.shape[1:]
    key_width = grads.shape[2]
    rank = down_factor.shape[1]
    sketch = input_projection.shape[1]
    examples = tokens // EXAMPLE_LENGTH
    per = rank // parts
    span = per * sketch
    scaling = 1.0 / math.sqrt(2.0 * EXAMPLE_LENGTH * parts)
    sends = pl.pallas_call(
        functools.partial(partial_kernel, parts, scaling),
        out_shape=[pltpu.VMEM((2 * examples, span), jnp.float32)] * parts,
        in_specs=[hbm()] * 7,
        out_specs=[vmem()] * parts,
        scratch_shapes=[
            pltpu.VMEM((tokens, width), acts.dtype),
            pltpu.VMEM((tokens, key_width), grads.dtype),
            pltpu.VMEM((sketch + rank, width), acts.dtype),
            pltpu.VMEM((sketch + rank, key_width), grads.dtype),
            pltpu.SMEM(order.shape[1:], order.dtype),
            pltpu.VMEM((2, rank, tokens), jnp.float32),
            pltpu.VMEM((examples * parts, tokens), jnp.float32),
            pltpu.VMEM((examples * parts, LANES), jnp.float32),
            pltpu.SemaphoreType.DMA(((width + key_width) // CHUNK, 3)),
            pltpu.SemaphoreType.DMA,
        ],
        compiler_params=pltpu.CompilerParams(vmem_limit_bytes=8 * 2**20),
        name="partials",
    )(
        *in_hbm(
            acts,
            grads,
            down_factor,
            up_factor_transposed,
            input_projection,
            gradient_projection,
            order,
        )
    )
    chunks = [exchange(sends[d], 1, d) for d in range(parts - 1, -1, -1)]
    padded = max(span, GROUP * sketch)
    columns, feature_rows = pl.pallas_call(
        sum_kernel,
        out_shape=[pltpu.VMEM((examples, padded), jnp.float32)] * 2,
        in_specs=[vmem()] * parts,
        out_specs=[vmem()] * 2,
        compiler_params=pltpu.CompilerParams(vmem_limit_bytes=2 * 2**20),
        name="sums",
    )(*in_vmem(*chunks))
    near = [columns] + [exchange(columns, d) for d in range(3, shards, 2)] + [feature_rows]
    held = pl.pallas_call(
        stack_kernel,
        out_shape=pltpu.VMEM((len(near) * examples, padded), jnp.float32),
        in_specs=[vmem()] * len(near),
        out_specs=vmem(),
        compiler_params=pltpu.CompilerParams(vmem_limit_bytes=2 * 2**20),
        name="stack",
    )(*in_vmem(*near))
    sent = exchange(held, 1)
    return pl.pallas_call(
        functools.partial(factor_kernel, parts),
        out_shape=[
            jax.ShapeDtypeStruct((examples // parts, rank * sketch), jnp.float32),
            jax.ShapeDtypeStruct((per, sketch, sketch), jnp.float32),
        ],
        in_specs=[smem()] + [vmem()] * 2,
        out_specs=[vmem()] * 2,
        compiler_params=pltpu.CompilerParams(vmem_limit_bytes=8 * 2**20),
        name="factors",
    )(damping, *in_vmem(held, sent))


def solution(mesh):
    in_specs = (
        P("mp", "ex", None),
        P("mp", "ex", None),
        P("mp", None, None),
        P("mp", None, None),
        P("mp", None, None),
        P("mp", None, None),
        P("mp", "ex", None),
        P(),
    )
    out_specs = (P(("ex", "mp"), None), P("mp", None, None))
    return jax.shard_map(
        local, mesh=mesh, in_specs=in_specs, out_specs=out_specs, check_vma=False
    )
```

```python
import functools
import math

import jax
import jax.numpy as jnp
from jax import lax
from jax.experimental import pallas as pl
from jax.experimental.pallas import tpu as pltpu
from jax.sharding import PartitionSpec as P

EXAMPLE_LENGTH = 8
LANES = 128
SLOT = 32
GROUP = LANES // SLOT
PANEL = 8
CHUNK = 1024


def dot_nt(a, b):
    return lax.dot_general(
        a, b, (((1,), (1,)), ((), ())), preferred_element_type=jnp.float32
    )


def dot_nn(a, b):
    return jnp.dot(a, b, preferred_element_type=jnp.float32)


def split(x):
    high = x.astype(jnp.bfloat16)
    return high, (x - high.astype(jnp.float32)).astype(jnp.bfloat16)


def partial_kernel(
    parts,
    scaling,
    acts_hbm,
    grads_hbm,
    down_hbm,
    up_hbm,
    proj_in_hbm,
    proj_out_hbm,
    order_hbm,
    *refs,
):
    sends, refs = refs[:parts], refs[parts:]
    acts, grads, weights_in, weights_out, order, low, mask, out, sems, order_sem = refs
    tokens, width = acts.shape
    rank = down_hbm.shape[1]
    sketch = proj_in_hbm.shape[1]
    examples = tokens // EXAMPLE_LENGTH
    per = rank // parts
    halves = sketch // SLOT

    def copy_in(source, target, sem):
        copy = pltpu.make_async_copy(source, target, sem)
        copy.start()
        return copy

    order_copy = copy_in(order_hbm.at[0], order, order_sem)
    pending = []
    for n, (data_hbm, data, first_hbm, second_hbm, weights) in enumerate(
        [
            (grads_hbm, grads, proj_out_hbm, up_hbm, weights_out),
            (acts_hbm, acts, proj_in_hbm, down_hbm, weights_in),
        ]
    ):
        first = [
            copy_in(first_hbm.at[0], weights.at[pl.ds(0, sketch)], sems.at[n, 0]),
            copy_in(second_hbm.at[0], weights.at[pl.ds(sketch, rank)], sems.at[n, 1]),
        ]
        chunks = []
        for start in range(0, data.shape[1], CHUNK):
            here = pl.ds(start, min(CHUNK, data.shape[1] - start))
            chunks.append(
                (
                    here,
                    copy_in(
                        data_hbm.at[0, :, here],
                        data.at[:, here],
                        sems.at[n, 2 + len(chunks)],
                    ),
                )
            )
        pending.append((first, chunks))

    order_copy.wait()
    rows = examples * parts
    source = lax.broadcasted_iota(jnp.int32, (8, tokens), 1) // EXAMPLE_LENGTH
    target = jnp.zeros((8, tokens), jnp.int32)
    for s in range(examples):
        target = jnp.where(source == s, order[0, s], target)
    target = jnp.concatenate([target] * (rows // 8), axis=0)
    place = lax.broadcasted_iota(jnp.int32, (rows, tokens), 0) // parts
    mask[...] = jnp.where(target == place, scaling, 0.0)

    def product(n, data, weights):
        first, chunks = pending[n]
        for copy in first:
            copy.wait()
        total = None
        for here, copy in chunks:
            copy.wait()
            term = dot_nt(weights[:, here], data[:, here])
            total = term if total is None else total + term
        return total

    def spread_low(values, n):
        low[n] = values
        tiles = []
        for c in range(per):
            chosen = low[n, pl.ds(c, parts, stride=per), :]
            chosen = jnp.concatenate([chosen] * max(1, 8 // parts), axis=0)
            chosen = jnp.concatenate([chosen] * (rows // chosen.shape[0]), axis=0)
            tiles.append(split(chosen * mask[...]))
        return [jnp.concatenate(half, axis=0) for half in zip(*tiles)]

    def spread_sketch(values):
        return split(
            jnp.concatenate(
                [values[h * SLOT : (h + 1) * SLOT] for h in range(halves) for _ in range(per)],
                axis=0,
            )
        )

    from_grads = product(0, grads, weights_out)
    left_grads = spread_low(from_grads[sketch:], 0)
    right_grads = spread_sketch(from_grads[:sketch])
    from_acts = product(1, acts, weights_in)
    left_acts = spread_low(from_acts[sketch:], 1)
    right_acts = spread_sketch(from_acts[:sketch])
    left_high, left_low = [
        jnp.concatenate(pair, axis=1) for pair in zip(left_grads, left_acts)
    ]
    right_high, right_low = [
        jnp.concatenate(pair, axis=1) for pair in zip(right_acts, right_grads)
    ]
    both = dot_nt(jnp.concatenate([left_high, left_low], axis=0), right_high)
    size = left_high.shape[0]
    spread = (dot_nt(left_high, right_low) + both[size:]) + both[:size]
    column = lax.broadcasted_iota(jnp.int32, (rows, per * sketch), 1)
    channel = (column // SLOT) % per
    total = spread[:rows]
    for c in range(1, per):
        total = jnp.where(channel == c, spread[c * rows : (c + 1) * rows], total)
    me = lax.axis_index("mp")
    for start in range(0, per * sketch, LANES):
        stop = min(start + LANES, per * sketch)
        out[:, : stop - start] = total[:, start:stop]
        for d in range(parts):
            g = me ^ d
            sends[d][:examples, start:stop] = out[
                pl.ds(pl.multiple_of(g * examples, examples), examples), : stop - start
            ]
            sends[d][examples:, start:stop] = out[pl.ds(g, examples, stride=parts), :][
                :, : stop - start
            ]


def sum_kernel(*refs):
    chunks, (columns, feature_rows) = refs[:-2], refs[-2:]
    examples, padded = columns.shape
    total = chunks[0][...]
    for chunk in chunks[1:]:
        total = total + chunk[...]
    width = total.shape[1]
    for ref, value in ((feature_rows, total[:examples]), (columns, total[examples:])):
        ref[:, :width] = value
        if padded > width:
            ref[:, width:] = jnp.zeros((examples, padded - width), jnp.float32)


def stack_kernel(*refs):
    rows = refs[0].shape[0]
    for n, part in enumerate(refs[:-1]):
        refs[-1][n * rows : (n + 1) * rows, :] = part[...]


def write_features(total, parts, per, features):
    rows_here, width = features.shape
    span = width // parts
    halves = span // (per * SLOT)
    natural = jnp.concatenate(
        [
            total[:, (h * per + c) * SLOT : (h * per + c + 1) * SLOT]
            for c in range(per)
            for h in range(halves)
        ],
        axis=1,
    )
    for r in range(rows_here):
        features[r : r + 1, :] = jnp.concatenate(
            [natural[r * parts + g : r * parts + g + 1, :] for g in range(parts)], axis=1
        )


def pick_lanes(x, index):
    return jnp.take_along_axis(x, index, axis=1)


def reciprocal(x, scale=None):
    guess = pl.reciprocal(x, approx=True)
    rest = 2.0 - x * guess
    return (guess if scale is None else scale * guess) * rest


def factor_kernel(parts, damping, held, sent, features, factors):
    channels, sketch, _ = factors.shape
    examples = features.shape[0] * parts
    gathered = held.shape[0] - examples
    span = features.shape[1] // parts
    write_features(sent[gathered:, :span], parts, channels, features)
    halves = sketch // SLOT
    panels = sketch // PANEL
    per_half = SLOT // PANEL
    stacked = jnp.concatenate([held[:gathered, :], sent[:gathered, :]], axis=0)
    high, rest = split(stacked)
    turned_high, turned_rest = split(jnp.transpose(stacked))
    gram = dot_nn(turned_high, rest) + dot_nn(
        jnp.concatenate([turned_rest, turned_high], axis=1),
        jnp.concatenate([high, high], axis=0),
    )
    lane = lax.broadcasted_iota(jnp.int32, (PANEL, LANES), 1)
    sub = lax.broadcasted_iota(jnp.int32, (PANEL, LANES), 0)
    slot = lane // SLOT
    within = lane % SLOT
    ridge = damping[0]
    tile = []
    for q in range(panels):
        hr, at = divmod(q, per_half)
        line = []
        for h in range(halves):
            value = None
            for c in range(GROUP):
                start = hr * LANES + c * SLOT + at * PANEL
                block = gram[start : start + PANEL, h * LANES : (h + 1) * LANES]
                value = block if c == 0 else jnp.where(slot == c, block, value)
            value = value * (1.0 / stacked.shape[0])
            if h == hr:
                value = value + jnp.where(within == at * PANEL + sub, ridge, 0.0)
            line.append(value)
        tile.append(line)

    zero = jnp.zeros((PANEL, LANES), jnp.float32)
    finished = []
    ahead = [pick_lanes(tile[0][0], slot * SLOT + r) for r in range(PANEL)]
    for q in range(panels):
        hq, at = divmod(q, per_half)
        if q + 1 < panels:
            hn, an = divmod(q + 1, per_half)
            behind = [
                pick_lanes(tile[q + 1][hn], slot * SLOT + an * PANEL + r)
                for r in range(PANEL)
            ]
        column = [
            {
                j: ahead[r]
                if j == q
                else pick_lanes(tile[j][hq], slot * SLOT + at * PANEL + r)
                for j in range(q, panels)
            }
            for r in range(PANEL)
        ]
        block = [
            [
                jnp.broadcast_to(column[r][q][s : s + 1, :], (PANEL, LANES))
                if s >= r
                else None
                for s in range(PANEL)
            ]
            for r in range(PANEL)
        ]
        line = [
            [
                jnp.broadcast_to(tile[q][h][r : r + 1, :], (PANEL, LANES))
                if h >= hq
                else None
                for h in range(halves)
            ]
            for r in range(PANEL)
        ]
        inverse = []

        def eliminate(r, s, inv, near=()):
            ratio = block[r][s] * inv
            for t in range(s, PANEL):
                step = (block[r][s] * block[r][t]) * inv if t in near else ratio * block[r][t]
                block[s][t] = block[s][t] - step
            for j in range(q + 1, panels):
                column[s][j] = column[s][j] - ratio * column[r][j]
            for h in range(hq, halves):
                line[s][h] = line[s][h] - ratio * line[r][h]

        for r in range(0, PANEL, 2):
            pivot = block[r][r]
            minor = pivot * block[r + 1][r + 1] - block[r][r + 1] * block[r][r + 1]
            inverse.append(reciprocal(pivot))
            inverse.append(reciprocal(minor, pivot))
            eliminate(r, r + 1, inverse[r])
            for s in range(r + 2, PANEL):
                near = (r + 2, r + 3) if s < r + 4 else ()
                eliminate(r, s, inverse[r], near)
                eliminate(r + 1, s, inverse[r + 1], near)
        result = []
        for h in range(halves):
            if h < hq:
                result.append(zero)
                continue
            value = zero
            for r in range(PANEL):
                value = jnp.where(sub == r, line[r][h] * lax.rsqrt(block[r][r]), value)
            if h == hq:
                value = jnp.where(within >= at * PANEL + sub, value, 0.0)
            result.append(value)
        finished.append(result)
        for j in range(q + 1, panels):
            weights = [column[r][j] * inverse[r] for r in range(PANEL)]
            if j == q + 1:
                ahead = behind
                for r in range(PANEL):
                    for s in range(PANEL):
                        factor = jnp.broadcast_to(
                            column[r][j][s : s + 1, :], (PANEL, LANES)
                        )
                        step = (
                            (column[r][j] * factor) * inverse[r]
                            if r >= PANEL - 2
                            else weights[r] * factor
                        )
                        ahead[s] = ahead[s] - step
            for h in range((q + 1) // per_half, halves):
                value = tile[j][h]
                for r in range(PANEL):
                    value = value - weights[r] * line[r][h]
                tile[j][h] = value

    for q in range(panels):
        for c in range(channels):
            factors[c, q * PANEL : (q + 1) * PANEL, :] = jnp.concatenate(
                [finished[q][h][:, c * SLOT : (c + 1) * SLOT] for h in range(halves)],
                axis=1,
            )


def exchange(x, ex_distance, mp_distance=0):
    shards, parts = lax.axis_size("ex"), lax.axis_size("mp")
    return lax.ppermute(
        x,
        ("ex", "mp"),
        [
            (m * parts + b, (m ^ ex_distance) * parts + (b ^ mp_distance))
            for m in range(shards)
            for b in range(parts)
        ],
    )


def vmem():
    return pl.BlockSpec(memory_space=pltpu.VMEM)


def hbm():
    return pl.BlockSpec(memory_space=pltpu.HBM)


def in_hbm(*arrays):
    return [pltpu.with_memory_space_constraint(x, pltpu.HBM) for x in arrays]


def in_vmem(*arrays):
    return [pltpu.with_memory_space_constraint(x, pltpu.VMEM) for x in arrays]


def smem():
    return pl.BlockSpec(memory_space=pltpu.SMEM)


def local(
    acts,
    grads,
    down_factor,
    up_factor_transposed,
    input_projection,
    gradient_projection,
    order,
    damping,
):
    parts = lax.axis_size("mp")
    shards = lax.axis_size("ex")
    tokens, width = acts.shape[1:]
    key_width = grads.shape[2]
    rank = down_factor.shape[1]
    sketch = input_projection.shape[1]
    examples = tokens // EXAMPLE_LENGTH
    per = rank // parts
    span = per * sketch
    scaling = 1.0 / math.sqrt(2.0 * EXAMPLE_LENGTH * parts)
    sends = pl.pallas_call(
        functools.partial(partial_kernel, parts, scaling),
        out_shape=[pltpu.VMEM((2 * examples, span), jnp.float32)] * parts,
        in_specs=[hbm()] * 7,
        out_specs=[vmem()] * parts,
        scratch_shapes=[
            pltpu.VMEM((tokens, width), acts.dtype),
            pltpu.VMEM((tokens, key_width), grads.dtype),
            pltpu.VMEM((sketch + rank, width), acts.dtype),
            pltpu.VMEM((sketch + rank, key_width), grads.dtype),
            pltpu.SMEM(order.shape[1:], order.dtype),
            pltpu.VMEM((2, rank, tokens), jnp.float32),
            pltpu.VMEM((examples * parts, tokens), jnp.float32),
            pltpu.VMEM((examples * parts, LANES), jnp.float32),
            pltpu.SemaphoreType.DMA((2, 2 + pl.cdiv(max(width, key_width), CHUNK))),
            pltpu.SemaphoreType.DMA,
        ],
        compiler_params=pltpu.CompilerParams(vmem_limit_bytes=8 * 2**20),
        name="partials",
    )(
        *in_hbm(
            acts,
            grads,
            down_factor,
            up_factor_transposed,
            input_projection,
            gradient_projection,
            order,
        )
    )
    chunks = [exchange(sends[d], 1, d) for d in range(parts - 1, -1, -1)]
    padded = max(span, GROUP * sketch)
    columns, feature_rows = pl.pallas_call(
        sum_kernel,
        out_shape=[pltpu.VMEM((examples, padded), jnp.float32)] * 2,
        in_specs=[vmem()] * parts,
        out_specs=[vmem()] * 2,
        compiler_params=pltpu.CompilerParams(vmem_limit_bytes=2 * 2**20),
        name="sums",
    )(*in_vmem(*chunks))
    near = [columns] + [exchange(columns, d) for d in range(3, shards, 2)] + [feature_rows]
    held = pl.pallas_call(
        stack_kernel,
        out_shape=pltpu.VMEM((len(near) * examples, padded), jnp.float32),
        in_specs=[vmem()] * len(near),
        out_specs=vmem(),
        compiler_params=pltpu.CompilerParams(vmem_limit_bytes=2 * 2**20),
        name="stack",
    )(*in_vmem(*near))
    sent = exchange(held, 1)
    return pl.pallas_call(
        functools.partial(factor_kernel, parts),
        out_shape=[
            jax.ShapeDtypeStruct((examples // parts, rank * sketch), jnp.float32),
            jax.ShapeDtypeStruct((per, sketch, sketch), jnp.float32),
        ],
        in_specs=[smem()] + [vmem()] * 2,
        out_specs=[vmem()] * 2,
        compiler_params=pltpu.CompilerParams(vmem_limit_bytes=8 * 2**20),
        name="factors",
    )(damping, *in_vmem(held, sent))


def solution(mesh):
    in_specs = (
        P("mp", "ex", None),
        P("mp", "ex", None),
        P("mp", None, None),
        P("mp", None, None),
        P("mp", None, None),
        P("mp", None, None),
        P("mp", "ex", None),
        P(),
    )
    out_specs = (P(("ex", "mp"), None), P("mp", None, None))
    return jax.shard_map(
        local, mesh=mesh, in_specs=in_specs, out_specs=out_specs, check_vma=False
    )
```

```python
import functools
import math

import jax
import jax.numpy as jnp
from jax import lax
from jax.experimental import pallas as pl
from jax.experimental.pallas import tpu as pltpu
from jax.sharding import PartitionSpec as P

EXAMPLE_LENGTH = 8
LANES = 128
SLOT = 32
GROUP = LANES // SLOT
PANEL = 8
CHUNK = 1024


def dot_nt(a, b):
    return lax.dot_general(
        a, b, (((1,), (1,)), ((), ())), preferred_element_type=jnp.float32
    )


def dot_nn(a, b):
    return jnp.dot(a, b, preferred_element_type=jnp.float32)


def split(x):
    high = x.astype(jnp.bfloat16)
    return high, (x - high.astype(jnp.float32)).astype(jnp.bfloat16)


def partial_kernel(
    parts,
    scaling,
    acts_hbm,
    grads_hbm,
    down_hbm,
    up_hbm,
    proj_in_hbm,
    proj_out_hbm,
    order_hbm,
    *refs,
):
    sends, refs = refs[:parts], refs[parts:]
    acts, grads, weights_in, weights_out, order, sketches, out, line, sems, order_sem = refs
    tokens, width = acts.shape
    rank = down_hbm.shape[1]
    sketch = proj_in_hbm.shape[1]
    examples = tokens // EXAMPLE_LENGTH
    per = rank // parts
    halves = sketch // SLOT

    def copy_in(source, target, sem):
        copy = pltpu.make_async_copy(source, target, sem)
        copy.start()
        return copy

    order_copy = copy_in(order_hbm.at[0], order, order_sem)
    pending = []
    for n, (data_hbm, data, first_hbm, second_hbm, weights) in enumerate(
        [
            (grads_hbm, grads, up_hbm, proj_out_hbm, weights_out),
            (acts_hbm, acts, proj_in_hbm, down_hbm, weights_in),
        ]
    ):
        first = [
            copy_in(
                first_hbm.at[0], weights.at[pl.ds(0, first_hbm.shape[1])], sems.at[n, 0]
            ),
            copy_in(
                second_hbm.at[0],
                weights.at[pl.ds(sketch, second_hbm.shape[1])],
                sems.at[n, 1],
            ),
        ]
        chunks = []
        for start in range(0, data.shape[1], CHUNK):
            here = pl.ds(start, min(CHUNK, data.shape[1] - start))
            chunks.append(
                (
                    here,
                    copy_in(
                        data_hbm.at[0, :, here],
                        data.at[:, here],
                        sems.at[n, 2 + len(chunks)],
                    ),
                )
            )
        pending.append((first, chunks))
    for weights, rows in ((weights_in, sketch + rank), (weights_out, rank)):
        stop = LANES if rows > sketch else sketch
        weights[rows:stop, :] = jnp.zeros((stop - rows, weights.shape[1]), weights.dtype)

    def product(n, data, weights):
        first, chunks = pending[n]
        for copy in first:
            copy.wait()
        total = None
        for here, copy in chunks:
            copy.wait()
            term = dot_nt(data[:, here], weights[:, here])
            total = term if total is None else total + term
        return total

    from_grads = product(0, grads, weights_out)
    from_acts = product(1, acts, weights_in)
    lane = lax.broadcasted_iota(jnp.int32, (tokens, LANES), 1)
    sketches[...] = jnp.where(lane < sketch, from_acts, from_grads)
    lows = jnp.transpose(jnp.where(lane < sketch, from_grads, from_acts)) * scaling
    low_out, low_in = lows[:rank], lows[sketch : sketch + rank]
    first = lax.broadcasted_iota(jnp.int32, (rank, LANES), 1) < sketch
    low = [
        jnp.where(first, low_out, pltpu.roll(low_in, sketch, 1)),
        jnp.where(first, pltpu.roll(low_out, sketch, 1), low_in),
    ]
    half = lax.broadcasted_iota(jnp.int32, (8, LANES), 1) // sketch * sketch
    order_copy.wait()
    for s in range(examples):
        sums = [None] * (rank // 8)
        for t in range(s * EXAMPLE_LENGTH, (s + 1) * EXAMPLE_LENGTH):
            row = jnp.broadcast_to(sketches[t : t + 1, :], (8, LANES))
            for c in range(rank // 8):
                part = low[t // sketch][c * 8 : (c + 1) * 8]
                term = pick_lanes(part, half + t % sketch) * row
                sums[c] = term if sums[c] is None else sums[c] + term
        for c, value in enumerate(sums):
            start = pl.multiple_of(order[0, s] * rank + c * 8, 8)
            out[pl.ds(start, 8), :] = value + pltpu.roll(value, sketch, 1)

    rows = examples * parts
    slot = lax.broadcasted_iota(jnp.int32, (rows, LANES), 1) // SLOT
    me = lax.axis_index("mp")
    picked = [
        out[pl.ds(c, rows, stride=per), :] if per > 1 else out[...] for c in range(per)
    ]
    for h in range(halves):
        total = None
        for c, value in enumerate(picked):
            if (c - h) * SLOT % sketch:
                value = pltpu.roll(value, SLOT, 1)
            total = value if c == 0 else jnp.where(slot == c, value, total)
        span = per * SLOT
        here = pl.ds(h * span, span)
        line[...] = total
        for d in range(parts):
            g = me ^ d
            by_row = line[pl.ds(pl.multiple_of(g * examples, examples), examples), :]
            by_column = line[pl.ds(g, examples, stride=parts), :]
            sends[d][:examples, here] = by_row[:, :span]
            sends[d][examples:, here] = by_column[:, :span]


def sum_kernel(*refs):
    chunks, (columns, feature_rows) = refs[:-2], refs[-2:]
    examples, padded = columns.shape
    total = chunks[0][...]
    for chunk in chunks[1:]:
        total = total + chunk[...]
    width = total.shape[1]
    for ref, value in ((feature_rows, total[:examples]), (columns, total[examples:])):
        ref[:, :width] = value
        if padded > width:
            ref[:, width:] = jnp.zeros((examples, padded - width), jnp.float32)


def stack_kernel(*refs):
    rows = refs[0].shape[0]
    for n, part in enumerate(refs[:-1]):
        refs[-1][n * rows : (n + 1) * rows, :] = part[...]


def write_features(total, parts, per, features):
    rows_here, width = features.shape
    span = width // parts
    halves = span // (per * SLOT)
    natural = jnp.concatenate(
        [
            total[:, (h * per + c) * SLOT : (h * per + c + 1) * SLOT]
            for c in range(per)
            for h in range(halves)
        ],
        axis=1,
    )
    for r in range(rows_here):
        features[r : r + 1, :] = jnp.concatenate(
            [natural[r * parts + g : r * parts + g + 1, :] for g in range(parts)], axis=1
        )


def pick_lanes(x, index):
    return jnp.take_along_axis(x, index, axis=1)


def reciprocal(x, scale=None):
    guess = pl.reciprocal(x, approx=True)
    rest = 2.0 - x * guess
    return (guess if scale is None else scale * guess) * rest


def factor_kernel(parts, damping, held, sent, features, factors):
    channels, sketch, _ = factors.shape
    examples = features.shape[0] * parts
    gathered = held.shape[0] - examples
    span = features.shape[1] // parts
    write_features(sent[gathered:, :span], parts, channels, features)
    halves = sketch // SLOT
    panels = sketch // PANEL
    per_half = SLOT // PANEL
    stacked = jnp.concatenate([held[:gathered, :], sent[:gathered, :]], axis=0)
    high, rest = split(stacked)
    turned_high, turned_rest = split(jnp.transpose(stacked))
    gram = dot_nn(turned_high, rest) + dot_nn(
        jnp.concatenate([turned_rest, turned_high], axis=1),
        jnp.concatenate([high, high], axis=0),
    )
    lane = lax.broadcasted_iota(jnp.int32, (PANEL, LANES), 1)
    sub = lax.broadcasted_iota(jnp.int32, (PANEL, LANES), 0)
    slot = lane // SLOT
    within = lane % SLOT
    ridge = damping[0]
    tile = []
    for q in range(panels):
        hr, at = divmod(q, per_half)
        line = []
        for h in range(halves):
            value = None
            for c in range(GROUP):
                start = hr * LANES + c * SLOT + at * PANEL
                block = gram[start : start + PANEL, h * LANES : (h + 1) * LANES]
                value = block if c == 0 else jnp.where(slot == c, block, value)
            value = value * (1.0 / stacked.shape[0])
            if h == hr:
                value = value + jnp.where(within == at * PANEL + sub, ridge, 0.0)
            line.append(value)
        tile.append(line)

    zero = jnp.zeros((PANEL, LANES), jnp.float32)
    finished = []
    ahead = [pick_lanes(tile[0][0], slot * SLOT + r) for r in range(PANEL)]
    for q in range(panels):
        hq, at = divmod(q, per_half)
        if q + 1 < panels:
            hn, an = divmod(q + 1, per_half)
            behind = [
                pick_lanes(tile[q + 1][hn], slot * SLOT + an * PANEL + r)
                for r in range(PANEL)
            ]
        column = [
            {
                j: ahead[r]
                if j == q
                else pick_lanes(tile[j][hq], slot * SLOT + at * PANEL + r)
                for j in range(q, panels)
            }
            for r in range(PANEL)
        ]
        block = [
            [
                jnp.broadcast_to(column[r][q][s : s + 1, :], (PANEL, LANES))
                if s >= r
                else None
                for s in range(PANEL)
            ]
            for r in range(PANEL)
        ]
        line = [
            [
                jnp.broadcast_to(tile[q][h][r : r + 1, :], (PANEL, LANES))
                if h >= hq
                else None
                for h in range(halves)
            ]
            for r in range(PANEL)
        ]
        inverse = []

        def eliminate(r, s, inv, near=()):
            ratio = block[r][s] * inv
            for t in range(s, PANEL):
                step = (block[r][s] * block[r][t]) * inv if t in near else ratio * block[r][t]
                block[s][t] = block[s][t] - step
            for j in range(q + 1, panels):
                column[s][j] = column[s][j] - ratio * column[r][j]
            for h in range(hq, halves):
                line[s][h] = line[s][h] - ratio * line[r][h]

        for r in range(0, PANEL, 2):
            pivot = block[r][r]
            minor = pivot * block[r + 1][r + 1] - block[r][r + 1] * block[r][r + 1]
            inverse.append(reciprocal(pivot))
            inverse.append(reciprocal(minor, pivot))
            eliminate(r, r + 1, inverse[r])
            for s in range(r + 2, PANEL):
                near = (r + 2, r + 3) if s < r + 4 else ()
                eliminate(r, s, inverse[r], near)
                eliminate(r + 1, s, inverse[r + 1], near)
        result = []
        for h in range(halves):
            if h < hq:
                result.append(zero)
                continue
            value = zero
            for r in range(PANEL):
                value = jnp.where(sub == r, line[r][h] * lax.rsqrt(block[r][r]), value)
            if h == hq:
                value = jnp.where(within >= at * PANEL + sub, value, 0.0)
            result.append(value)
        finished.append(result)
        for j in range(q + 1, panels):
            weights = [column[r][j] * inverse[r] for r in range(PANEL)]
            if j == q + 1:
                ahead = behind
                for r in range(PANEL):
                    for s in range(PANEL):
                        factor = jnp.broadcast_to(
                            column[r][j][s : s + 1, :], (PANEL, LANES)
                        )
                        step = (
                            (column[r][j] * factor) * inverse[r]
                            if r >= PANEL - 2
                            else weights[r] * factor
                        )
                        ahead[s] = ahead[s] - step
            for h in range((q + 1) // per_half, halves):
                value = tile[j][h]
                for r in range(PANEL):
                    value = value - weights[r] * line[r][h]
                tile[j][h] = value

    for q in range(panels):
        for c in range(channels):
            factors[c, q * PANEL : (q + 1) * PANEL, :] = jnp.concatenate(
                [finished[q][h][:, c * SLOT : (c + 1) * SLOT] for h in range(halves)],
                axis=1,
            )


def exchange(x, ex_distance, mp_distance=0):
    shards, parts = lax.axis_size("ex"), lax.axis_size("mp")
    return lax.ppermute(
        x,
        ("ex", "mp"),
        [
            (m * parts + b, (m ^ ex_distance) * parts + (b ^ mp_distance))
            for m in range(shards)
            for b in range(parts)
        ],
    )


def vmem():
    return pl.BlockSpec(memory_space=pltpu.VMEM)


def hbm():
    return pl.BlockSpec(memory_space=pltpu.HBM)


def in_hbm(*arrays):
    return [pltpu.with_memory_space_constraint(x, pltpu.HBM) for x in arrays]


def in_vmem(*arrays):
    return [pltpu.with_memory_space_constraint(x, pltpu.VMEM) for x in arrays]


def smem():
    return pl.BlockSpec(memory_space=pltpu.SMEM)


def local(
    acts,
    grads,
    down_factor,
    up_factor_transposed,
    input_projection,
    gradient_projection,
    order,
    damping,
):
    parts = lax.axis_size("mp")
    shards = lax.axis_size("ex")
    tokens, width = acts.shape[1:]
    key_width = grads.shape[2]
    rank = down_factor.shape[1]
    sketch = input_projection.shape[1]
    examples = tokens // EXAMPLE_LENGTH
    per = rank // parts
    span = per * sketch
    scaling = 1.0 / math.sqrt(2.0 * EXAMPLE_LENGTH * parts)
    sends = pl.pallas_call(
        functools.partial(partial_kernel, parts, scaling),
        out_shape=[pltpu.VMEM((2 * examples, span), jnp.float32)] * parts,
        in_specs=[hbm()] * 7,
        out_specs=[vmem()] * parts,
        scratch_shapes=[
            pltpu.VMEM((tokens, width), acts.dtype),
            pltpu.VMEM((tokens, key_width), grads.dtype),
            pltpu.VMEM((LANES, width), acts.dtype),
            pltpu.VMEM((LANES, key_width), grads.dtype),
            pltpu.SMEM(order.shape[1:], order.dtype),
            pltpu.VMEM((tokens, LANES), jnp.float32),
            pltpu.VMEM((examples * rank, LANES), jnp.float32),
            pltpu.VMEM((examples * parts, LANES), jnp.float32),
            pltpu.SemaphoreType.DMA((2, 2 + pl.cdiv(max(width, key_width), CHUNK))),
            pltpu.SemaphoreType.DMA,
        ],
        compiler_params=pltpu.CompilerParams(vmem_limit_bytes=8 * 2**20),
        name="partials",
    )(
        *in_hbm(
            acts,
            grads,
            down_factor,
            up_factor_transposed,
            input_projection,
            gradient_projection,
            order,
        )
    )
    chunks = [exchange(sends[d], 1, d) for d in range(parts - 1, -1, -1)]
    padded = max(span, GROUP * sketch)
    columns, feature_rows = pl.pallas_call(
        sum_kernel,
        out_shape=[pltpu.VMEM((examples, padded), jnp.float32)] * 2,
        in_specs=[vmem()] * parts,
        out_specs=[vmem()] * 2,
        compiler_params=pltpu.CompilerParams(vmem_limit_bytes=2 * 2**20),
        name="sums",
    )(*in_vmem(*chunks))
    near = [columns] + [exchange(columns, d) for d in range(3, shards, 2)] + [feature_rows]
    held = pl.pallas_call(
        stack_kernel,
        out_shape=pltpu.VMEM((len(near) * examples, padded), jnp.float32),
        in_specs=[vmem()] * len(near),
        out_specs=vmem(),
        compiler_params=pltpu.CompilerParams(vmem_limit_bytes=2 * 2**20),
        name="stack",
    )(*in_vmem(*near))
    sent = exchange(held, 1)
    return pl.pallas_call(
        functools.partial(factor_kernel, parts),
        out_shape=[
            jax.ShapeDtypeStruct((examples // parts, rank * sketch), jnp.float32),
            jax.ShapeDtypeStruct((per, sketch, sketch), jnp.float32),
        ],
        in_specs=[smem()] + [vmem()] * 2,
        out_specs=[vmem()] * 2,
        compiler_params=pltpu.CompilerParams(vmem_limit_bytes=8 * 2**20),
        name="factors",
    )(damping, *in_vmem(held, sent))


def solution(mesh):
    in_specs = (
        P("mp", "ex", None),
        P("mp", "ex", None),
        P("mp", None, None),
        P("mp", None, None),
        P("mp", None, None),
        P("mp", None, None),
        P("mp", "ex", None),
        P(),
    )
    out_specs = (P(("ex", "mp"), None), P("mp", None, None))
    return jax.shard_map(
        local, mesh=mesh, in_specs=in_specs, out_specs=out_specs, check_vma=False
    )
```

```python
import functools
import math

import jax
import jax.numpy as jnp
from jax import lax
from jax.experimental import pallas as pl
from jax.experimental.pallas import tpu as pltpu
from jax.sharding import PartitionSpec as P

EXAMPLE_LENGTH = 8
LANES = 128
SLOT = 32
GROUP = LANES // SLOT
PANEL = 8
CHUNK = 1024


def dot_nt(a, b):
    return lax.dot_general(
        a, b, (((1,), (1,)), ((), ())), preferred_element_type=jnp.float32
    )


def dot_nn(a, b):
    return jnp.dot(a, b, preferred_element_type=jnp.float32)


def split(x):
    high = x.astype(jnp.bfloat16)
    return high, (x - high.astype(jnp.float32)).astype(jnp.bfloat16)


def partial_kernel(
    parts,
    scaling,
    acts_hbm,
    grads_hbm,
    down_hbm,
    up_hbm,
    proj_in_hbm,
    proj_out_hbm,
    order_hbm,
    *refs,
):
    sends, refs = refs[:parts], refs[parts:]
    acts, grads, weights_in, weights_out, order, low, mask, out, sems, order_sem = refs
    tokens, width = acts.shape
    rank = down_hbm.shape[1]
    sketch = proj_in_hbm.shape[1]
    examples = tokens // EXAMPLE_LENGTH
    per = rank // parts
    halves = sketch // SLOT

    def copies(source, target, sem, start, size):
        return pltpu.make_async_copy(
            source.at[0, :, pl.ds(start, size)],
            target.at[:, pl.ds(start, size)],
            sem,
        )

    order_copy = pltpu.make_async_copy(order_hbm.at[0], order, order_sem)
    order_copy.start()
    sources = [
        (grads_hbm, grads, proj_out_hbm, up_hbm, weights_out),
        (acts_hbm, acts, proj_in_hbm, down_hbm, weights_in),
    ]
    pending = []
    for data_hbm, data, first_hbm, second_hbm, weights in sources:
        for start in range(0, data.shape[1], CHUNK):
            n = len(pending)
            pending.append(
                [
                    copies(first_hbm, weights.at[pl.ds(0, sketch)], sems.at[n, 0], start, CHUNK),
                    copies(second_hbm, weights.at[pl.ds(sketch, rank)], sems.at[n, 1], start, CHUNK),
                    copies(data_hbm, data, sems.at[n, 2], start, CHUNK),
                ]
            )
            for copy in pending[-1]:
                copy.start()

    order_copy.wait()
    rows = examples * parts
    source = lax.broadcasted_iota(jnp.int32, (8, tokens), 1) // EXAMPLE_LENGTH
    target = jnp.zeros((8, tokens), jnp.int32)
    for s in range(examples):
        target = jnp.where(source == s, order[0, s], target)
    target = jnp.concatenate([target] * (rows // 8), axis=0)
    place = lax.broadcasted_iota(jnp.int32, (rows, tokens), 0) // parts
    mask[...] = jnp.where(target == place, scaling, 0.0)

    def product(first, data, weights):
        total = None
        for n in range(data.shape[1] // CHUNK):
            for copy in pending[first + n]:
                copy.wait()
            here = pl.ds(n * CHUNK, CHUNK)
            term = dot_nt(weights[:, here], data[:, here])
            total = term if total is None else total + term
        return total

    def spread_low(values, n):
        low[n] = values
        tiles = []
        for c in range(per):
            chosen = low[n, pl.ds(c, parts, stride=per), :]
            chosen = jnp.concatenate([chosen] * max(1, 8 // parts), axis=0)
            chosen = jnp.concatenate([chosen] * (rows // chosen.shape[0]), axis=0)
            tiles.append(split(chosen * mask[...]))
        return [jnp.concatenate(half, axis=0) for half in zip(*tiles)]

    def spread_sketch(values):
        return split(
            jnp.concatenate(
                [values[h * SLOT : (h + 1) * SLOT] for h in range(halves) for _ in range(per)],
                axis=0,
            )
        )

    from_grads = product(0, grads, weights_out)
    left_grads = spread_low(from_grads[sketch:], 0)
    right_grads = spread_sketch(from_grads[:sketch])
    from_acts = product(grads.shape[1] // CHUNK, acts, weights_in)
    left_acts = spread_low(from_acts[sketch:], 1)
    right_acts = spread_sketch(from_acts[:sketch])
    left_high, left_low = [
        jnp.concatenate(pair, axis=1) for pair in zip(left_grads, left_acts)
    ]
    right_high, right_low = [
        jnp.concatenate(pair, axis=1) for pair in zip(right_acts, right_grads)
    ]
    both = dot_nt(jnp.concatenate([left_high, left_low], axis=0), right_high)
    size = left_high.shape[0]
    spread = (dot_nt(left_high, right_low) + both[size:]) + both[:size]
    column = lax.broadcasted_iota(jnp.int32, (rows, per * sketch), 1)
    channel = (column // SLOT) % per
    total = spread[:rows]
    for c in range(1, per):
        total = jnp.where(channel == c, spread[c * rows : (c + 1) * rows], total)
    me = lax.axis_index("mp")
    for start in range(0, per * sketch, LANES):
        stop = min(start + LANES, per * sketch)
        out[:, : stop - start] = total[:, start:stop]
        for d in range(parts):
            g = me ^ d
            sends[d][:examples, start:stop] = out[
                pl.ds(pl.multiple_of(g * examples, examples), examples), : stop - start
            ]
            sends[d][examples:, start:stop] = out[pl.ds(g, examples, stride=parts), :][
                :, : stop - start
            ]


def sum_kernel(*refs):
    chunks, (columns, feature_rows) = refs[:-2], refs[-2:]
    examples, padded = columns.shape
    total = chunks[0][...]
    for chunk in chunks[1:]:
        total = total + chunk[...]
    width = total.shape[1]
    for ref, value in ((feature_rows, total[:examples]), (columns, total[examples:])):
        ref[:, :width] = value
        if padded > width:
            ref[:, width:] = jnp.zeros((examples, padded - width), jnp.float32)


def stack_kernel(*refs):
    rows = refs[0].shape[0]
    for n, part in enumerate(refs[:-1]):
        refs[-1][n * rows : (n + 1) * rows, :] = part[...]


def write_features(total, parts, per, features):
    rows_here, width = features.shape
    span = width // parts
    halves = span // (per * SLOT)
    natural = jnp.concatenate(
        [
            total[:, (h * per + c) * SLOT : (h * per + c + 1) * SLOT]
            for c in range(per)
            for h in range(halves)
        ],
        axis=1,
    )
    for r in range(rows_here):
        features[r : r + 1, :] = jnp.concatenate(
            [natural[r * parts + g : r * parts + g + 1, :] for g in range(parts)], axis=1
        )


def pick_lanes(x, index, offset):
    if offset:
        x = pltpu.roll(x, LANES - offset, 1)
    return jnp.take_along_axis(x, index, axis=1)


def reciprocal(x, scale=None):
    guess = pl.reciprocal(x, approx=True)
    rest = 2.0 - x * guess
    return (guess if scale is None else scale * guess) * rest


def factor_kernel(parts, damping, held, sent, features, factors):
    channels, sketch, _ = factors.shape
    examples = features.shape[0] * parts
    gathered = held.shape[0] - examples
    span = features.shape[1] // parts
    write_features(sent[gathered:, :span], parts, channels, features)
    halves = sketch // SLOT
    panels = sketch // PANEL
    per_half = SLOT // PANEL
    stacked = jnp.concatenate([held[:gathered, :], sent[:gathered, :]], axis=0)
    high, rest = split(stacked)
    turned_high, turned_rest = split(jnp.transpose(stacked))
    gram = dot_nn(turned_high, rest) + dot_nn(
        jnp.concatenate([turned_rest, turned_high], axis=1),
        jnp.concatenate([high, high], axis=0),
    )
    lane = lax.broadcasted_iota(jnp.int32, (PANEL, LANES), 1)
    sub = lax.broadcasted_iota(jnp.int32, (PANEL, LANES), 0)
    slot = lane // SLOT
    within = lane % SLOT
    ridge = damping[0]
    tile = []
    for q in range(panels):
        hr, at = divmod(q, per_half)
        line = []
        for h in range(halves):
            value = None
            for c in range(GROUP):
                start = hr * LANES + c * SLOT + at * PANEL
                block = gram[start : start + PANEL, h * LANES : (h + 1) * LANES]
                value = block if c == 0 else jnp.where(slot == c, block, value)
            value = value * (1.0 / stacked.shape[0])
            if h == hr:
                value = value + jnp.where(within == at * PANEL + sub, ridge, 0.0)
            line.append(value)
        tile.append(line)

    zero = jnp.zeros((PANEL, LANES), jnp.float32)
    finished = []
    ahead = [pick_lanes(tile[0][0], slot * SLOT, r) for r in range(PANEL)]
    for q in range(panels):
        hq, at = divmod(q, per_half)
        if q + 1 < panels:
            hn, an = divmod(q + 1, per_half)
            behind = [
                pick_lanes(tile[q + 1][hn], slot * SLOT, an * PANEL + r)
                for r in range(PANEL)
            ]
        column = [
            {
                j: ahead[r]
                if j == q
                else pick_lanes(tile[j][hq], slot * SLOT, at * PANEL + r)
                for j in range(q, panels)
            }
            for r in range(PANEL)
        ]
        block = [
            [
                jnp.broadcast_to(column[r][q][s : s + 1, :], (PANEL, LANES))
                if s >= r
                else None
                for s in range(PANEL)
            ]
            for r in range(PANEL)
        ]
        line = [
            [
                jnp.broadcast_to(tile[q][h][r : r + 1, :], (PANEL, LANES))
                if h >= hq
                else None
                for h in range(halves)
            ]
            for r in range(PANEL)
        ]
        inverse = []

        def eliminate(r, s, inv, near=()):
            ratio = block[r][s] * inv
            for t in range(s, PANEL):
                step = (block[r][s] * block[r][t]) * inv if t in near else ratio * block[r][t]
                block[s][t] = block[s][t] - step
            for j in range(q + 1, panels):
                column[s][j] = column[s][j] - ratio * column[r][j]
            for h in range(hq, halves):
                line[s][h] = line[s][h] - ratio * line[r][h]

        for r in range(0, PANEL, 2):
            pivot = block[r][r]
            minor = pivot * block[r + 1][r + 1] - block[r][r + 1] * block[r][r + 1]
            inverse.append(reciprocal(pivot))
            inverse.append(reciprocal(minor, pivot))
            eliminate(r, r + 1, inverse[r])
            for s in range(r + 2, PANEL):
                near = (r + 2, r + 3) if s < r + 4 else ()
                eliminate(r, s, inverse[r], near)
                eliminate(r + 1, s, inverse[r + 1], near)
        result = []
        for h in range(halves):
            if h < hq:
                result.append(zero)
                continue
            value = zero
            for r in range(PANEL):
                value = jnp.where(sub == r, line[r][h] * lax.rsqrt(block[r][r]), value)
            if h == hq:
                value = jnp.where(within >= at * PANEL + sub, value, 0.0)
            result.append(value)
        finished.append(result)
        for j in range(q + 1, panels):
            weights = [column[r][j] * inverse[r] for r in range(PANEL)]
            if j == q + 1:
                ahead = behind
                for r in range(PANEL):
                    for s in range(PANEL):
                        factor = jnp.broadcast_to(
                            column[r][j][s : s + 1, :], (PANEL, LANES)
                        )
                        step = (
                            (column[r][j] * factor) * inverse[r]
                            if r >= PANEL - 2
                            else weights[r] * factor
                        )
                        ahead[s] = ahead[s] - step
            for h in range((q + 1) // per_half, halves):
                value = tile[j][h]
                for r in range(PANEL):
                    value = value - weights[r] * line[r][h]
                tile[j][h] = value

    for q in range(panels):
        for c in range(channels):
            factors[c, q * PANEL : (q + 1) * PANEL, :] = jnp.concatenate(
                [finished[q][h][:, c * SLOT : (c + 1) * SLOT] for h in range(halves)],
                axis=1,
            )


def exchange(x, ex_distance, mp_distance=0):
    shards, parts = lax.axis_size("ex"), lax.axis_size("mp")
    return lax.ppermute(
        x,
        ("ex", "mp"),
        [
            (m * parts + b, (m ^ ex_distance) * parts + (b ^ mp_distance))
            for m in range(shards)
            for b in range(parts)
        ],
    )


def vmem():
    return pl.BlockSpec(memory_space=pltpu.VMEM)


def hbm():
    return pl.BlockSpec(memory_space=pltpu.HBM)


def in_hbm(*arrays):
    return [pltpu.with_memory_space_constraint(x, pltpu.HBM) for x in arrays]


def in_vmem(*arrays):
    return [pltpu.with_memory_space_constraint(x, pltpu.VMEM) for x in arrays]


def smem():
    return pl.BlockSpec(memory_space=pltpu.SMEM)


def local(
    acts,
    grads,
    down_factor,
    up_factor_transposed,
    input_projection,
    gradient_projection,
    order,
    damping,
):
    parts = lax.axis_size("mp")
    shards = lax.axis_size("ex")
    tokens, width = acts.shape[1:]
    key_width = grads.shape[2]
    rank = down_factor.shape[1]
    sketch = input_projection.shape[1]
    examples = tokens // EXAMPLE_LENGTH
    per = rank // parts
    span = per * sketch
    scaling = 1.0 / math.sqrt(2.0 * EXAMPLE_LENGTH * parts)
    sends = pl.pallas_call(
        functools.partial(partial_kernel, parts, scaling),
        out_shape=[pltpu.VMEM((2 * examples, span), jnp.float32)] * parts,
        in_specs=[hbm()] * 7,
        out_specs=[vmem()] * parts,
        scratch_shapes=[
            pltpu.VMEM((tokens, width), acts.dtype),
            pltpu.VMEM((tokens, key_width), grads.dtype),
            pltpu.VMEM((sketch + rank, width), acts.dtype),
            pltpu.VMEM((sketch + rank, key_width), grads.dtype),
            pltpu.SMEM(order.shape[1:], order.dtype),
            pltpu.VMEM((2, rank, tokens), jnp.float32),
            pltpu.VMEM((examples * parts, tokens), jnp.float32),
            pltpu.VMEM((examples * parts, LANES), jnp.float32),
            pltpu.SemaphoreType.DMA(((width + key_width) // CHUNK, 3)),
            pltpu.SemaphoreType.DMA,
        ],
        compiler_params=pltpu.CompilerParams(vmem_limit_bytes=8 * 2**20),
        name="partials",
    )(
        *in_hbm(
            acts,
            grads,
            down_factor,
            up_factor_transposed,
            input_projection,
            gradient_projection,
            order,
        )
    )
    chunks = [exchange(sends[d], 1, d) for d in range(parts - 1, -1, -1)]
    padded = max(span, GROUP * sketch)
    columns, feature_rows = pl.pallas_call(
        sum_kernel,
        out_shape=[pltpu.VMEM((examples, padded), jnp.float32)] * 2,
        in_specs=[vmem()] * parts,
        out_specs=[vmem()] * 2,
        compiler_params=pltpu.CompilerParams(vmem_limit_bytes=2 * 2**20),
        name="sums",
    )(*in_vmem(*chunks))
    near = [columns] + [exchange(columns, d) for d in range(3, shards, 2)] + [feature_rows]
    held = pl.pallas_call(
        stack_kernel,
        out_shape=pltpu.VMEM((len(near) * examples, padded), jnp.float32),
        in_specs=[vmem()] * len(near),
        out_specs=vmem(),
        compiler_params=pltpu.CompilerParams(vmem_limit_bytes=2 * 2**20),
        name="stack",
    )(*in_vmem(*near))
    sent = exchange(held, 1)
    return pl.pallas_call(
        functools.partial(factor_kernel, parts),
        out_shape=[
            jax.ShapeDtypeStruct((examples // parts, rank * sketch), jnp.float32),
            jax.ShapeDtypeStruct((per, sketch, sketch), jnp.float32),
        ],
        in_specs=[smem()] + [vmem()] * 2,
        out_specs=[vmem()] * 2,
        compiler_params=pltpu.CompilerParams(vmem_limit_bytes=8 * 2**20),
        name="factors",
    )(damping, *in_vmem(held, sent))


def solution(mesh):
    in_specs = (
        P("mp", "ex", None),
        P("mp", "ex", None),
        P("mp", None, None),
        P("mp", None, None),
        P("mp", None, None),
        P("mp", None, None),
        P("mp", "ex", None),
        P(),
    )
    out_specs = (P(("ex", "mp"), None), P("mp", None, None))
    return jax.shard_map(
        local, mesh=mesh, in_specs=in_specs, out_specs=out_specs, check_vma=False
    )
```

```python
import functools
import itertools
import math

import jax
import jax.numpy as jnp
from jax import lax
from jax.experimental import pallas as pl
from jax.experimental.pallas import tpu as pltpu
from jax.sharding import PartitionSpec as P

EXAMPLE_LENGTH = 8
LANES = 128
SLOT = 32
GROUP = LANES // SLOT
PANEL = 8
CHUNK = 1024


def dot_nt(a, b):
    return lax.dot_general(
        a, b, (((1,), (1,)), ((), ())), preferred_element_type=jnp.float32
    )


def dot_nn(a, b):
    return jnp.dot(a, b, preferred_element_type=jnp.float32)


def split(x):
    high = x.astype(jnp.bfloat16)
    return high, (x - high.astype(jnp.float32)).astype(jnp.bfloat16)


def partial_kernel(
    parts,
    scaling,
    acts_hbm,
    grads_hbm,
    down_hbm,
    up_hbm,
    proj_in_hbm,
    proj_out_hbm,
    order_hbm,
    *refs,
):
    sends, refs = refs[:parts], refs[parts:]
    acts, grads, weights_in, weights_out, order, low, mask, out, sems, order_sem = refs
    tokens, width = acts.shape
    rank = down_hbm.shape[1]
    sketch = proj_in_hbm.shape[1]
    examples = tokens // EXAMPLE_LENGTH
    per = rank // parts
    halves = sketch // SLOT

    def copies(source, target, sem, start, size):
        return pltpu.make_async_copy(
            source.at[0, :, pl.ds(start, size)],
            target.at[:, pl.ds(start, size)],
            sem,
        )

    order_copy = pltpu.make_async_copy(order_hbm.at[0], order, order_sem)
    order_copy.start()
    sources = [
        (grads_hbm, grads, proj_out_hbm, up_hbm, weights_out),
        (acts_hbm, acts, proj_in_hbm, down_hbm, weights_in),
    ]
    pending = []
    for data_hbm, data, first_hbm, second_hbm, weights in sources:
        for start in range(0, data.shape[1], CHUNK):
            n = len(pending)
            pending.append(
                [
                    copies(first_hbm, weights.at[pl.ds(0, sketch)], sems.at[n, 0], start, CHUNK),
                    copies(second_hbm, weights.at[pl.ds(sketch, rank)], sems.at[n, 1], start, CHUNK),
                    copies(data_hbm, data, sems.at[n, 2], start, CHUNK),
                ]
            )
            for copy in pending[-1]:
                copy.start()

    order_copy.wait()
    rows = examples * parts
    source = lax.broadcasted_iota(jnp.int32, (8, tokens), 1) // EXAMPLE_LENGTH
    target = jnp.zeros((8, tokens), jnp.int32)
    for s in range(examples):
        target = jnp.where(source == s, order[0, s], target)
    target = jnp.concatenate([target] * (rows // 8), axis=0)
    place = lax.broadcasted_iota(jnp.int32, (rows, tokens), 0) // parts
    mask[...] = jnp.where(target == place, scaling, 0.0)

    def product(first, data, weights):
        total = None
        for n in range(data.shape[1] // CHUNK):
            for copy in pending[first + n]:
                copy.wait()
            here = pl.ds(n * CHUNK, CHUNK)
            term = dot_nt(weights[:, here], data[:, here])
            total = term if total is None else total + term
        return total

    def spread_low(values, n):
        low[n] = values
        tiles = []
        for c in range(per):
            chosen = low[n, pl.ds(c, parts, stride=per), :]
            chosen = jnp.concatenate([chosen] * max(1, 8 // parts), axis=0)
            chosen = jnp.concatenate([chosen] * (rows // chosen.shape[0]), axis=0)
            tiles.append(split(chosen * mask[...]))
        return [jnp.concatenate(half, axis=0) for half in zip(*tiles)]

    def spread_sketch(values):
        return split(
            jnp.concatenate(
                [values[h * SLOT : (h + 1) * SLOT] for h in range(halves) for _ in range(per)],
                axis=0,
            )
        )

    from_grads = product(0, grads, weights_out)
    left_grads = spread_low(from_grads[sketch:], 0)
    right_grads = spread_sketch(from_grads[:sketch])
    from_acts = product(grads.shape[1] // CHUNK, acts, weights_in)
    left_acts = spread_low(from_acts[sketch:], 1)
    right_acts = spread_sketch(from_acts[:sketch])
    left_high, left_low = [
        jnp.concatenate(pair, axis=1) for pair in zip(left_grads, left_acts)
    ]
    right_high, right_low = [
        jnp.concatenate(pair, axis=1) for pair in zip(right_acts, right_grads)
    ]
    both = dot_nt(jnp.concatenate([left_high, left_low], axis=0), right_high)
    size = left_high.shape[0]
    spread = (dot_nt(left_high, right_low) + both[size:]) + both[:size]
    column = lax.broadcasted_iota(jnp.int32, (rows, per * sketch), 1)
    channel = (column // SLOT) % per
    total = spread[:rows]
    for c in range(1, per):
        total = jnp.where(channel == c, spread[c * rows : (c + 1) * rows], total)
    me = lax.axis_index("mp")
    for start in range(0, per * sketch, LANES):
        stop = min(start + LANES, per * sketch)
        out[:, : stop - start] = total[:, start:stop]
        for d in range(parts):
            g = me ^ d
            sends[d][:examples, start:stop] = out[
                pl.ds(pl.multiple_of(g * examples, examples), examples), : stop - start
            ]
            sends[d][examples:, start:stop] = out[pl.ds(g, examples, stride=parts), :][
                :, : stop - start
            ]


def sum_kernel(*refs):
    chunks, (columns, feature_rows) = refs[:-2], refs[-2:]
    examples, padded = columns.shape
    total = chunks[0][...]
    for chunk in chunks[1:]:
        total = total + chunk[...]
    width = total.shape[1]
    for ref, value in ((feature_rows, total[:examples]), (columns, total[examples:])):
        ref[:, :width] = value
        if padded > width:
            ref[:, width:] = jnp.zeros((examples, padded - width), jnp.float32)


def stack_kernel(*refs):
    rows = refs[0].shape[0]
    for n, part in enumerate(refs[:-1]):
        refs[-1][n * rows : (n + 1) * rows, :] = part[...]


def write_features(total, parts, per, features):
    rows_here, width = features.shape
    span = width // parts
    halves = span // (per * SLOT)
    natural = jnp.concatenate(
        [
            total[:, (h * per + c) * SLOT : (h * per + c + 1) * SLOT]
            for c in range(per)
            for h in range(halves)
        ],
        axis=1,
    )
    for r in range(rows_here):
        features[r : r + 1, :] = jnp.concatenate(
            [natural[r * parts + g : r * parts + g + 1, :] for g in range(parts)], axis=1
        )


def pick_lanes(x, index):
    return jnp.take_along_axis(x, index, axis=1)


def reciprocal(x, scale=None):
    guess = pl.reciprocal(x, approx=True)
    rest = 2.0 - x * guess
    return (guess if scale is None else scale * guess) * rest


def factor_kernel(parts, damping, held, sent, features, factors, kept):
    channels, sketch, _ = factors.shape
    examples = features.shape[0] * parts
    gathered = held.shape[0] - examples
    span = features.shape[1] // parts
    write_features(sent[gathered:, :span], parts, channels, features)
    halves = sketch // SLOT
    panels = sketch // PANEL
    per_half = SLOT // PANEL
    stacked = jnp.concatenate([held[:gathered, :], sent[:gathered, :]], axis=0)
    high, rest = split(stacked)
    turned_high, turned_rest = split(jnp.transpose(stacked))
    gram = dot_nn(turned_high, rest) + dot_nn(
        jnp.concatenate([turned_rest, turned_high], axis=1),
        jnp.concatenate([high, high], axis=0),
    )
    lane = lax.broadcasted_iota(jnp.int32, (PANEL, LANES), 1)
    sub = lax.broadcasted_iota(jnp.int32, (PANEL, LANES), 0)
    slot = lane // SLOT
    within = lane % SLOT
    ridge = damping[0]
    tile = []
    for q in range(panels):
        hr, at = divmod(q, per_half)
        line = []
        for h in range(halves):
            value = None
            for c in range(GROUP):
                start = hr * LANES + c * SLOT + at * PANEL
                block = gram[start : start + PANEL, h * LANES : (h + 1) * LANES]
                value = block if c == 0 else jnp.where(slot == c, block, value)
            value = value * (1.0 / stacked.shape[0])
            if h == hr:
                value = value + jnp.where(within == at * PANEL + sub, ridge, 0.0)
            line.append(value)
        tile.append(line)

    places = itertools.count(0, PANEL)

    def rows_of(x):
        place = next(places)
        kept[place : place + PANEL, :] = x
        return [kept[pl.ds(place + s, PANEL, stride=0), :] for s in range(PANEL)]

    zero = jnp.zeros((PANEL, LANES), jnp.float32)
    finished = []
    ahead = [pick_lanes(tile[0][0], slot * SLOT + r) for r in range(PANEL)]
    for q in range(panels):
        hq, at = divmod(q, per_half)
        if q + 1 < panels:
            hn, an = divmod(q + 1, per_half)
            behind = [
                pick_lanes(tile[q + 1][hn], slot * SLOT + an * PANEL + r)
                for r in range(PANEL)
            ]
        column = [
            {
                j: ahead[r]
                if j == q
                else pick_lanes(tile[j][hq], slot * SLOT + at * PANEL + r)
                for j in range(q, panels)
            }
            for r in range(PANEL)
        ]
        block = [rows_of(column[r][q]) for r in range(PANEL)]
        lines = [rows_of(tile[q][h]) if h >= hq else [None] * PANEL for h in range(halves)]
        line = [list(group) for group in zip(*lines)]
        inverse = []

        def eliminate(r, s, inv, near=()):
            ratio = block[r][s] * inv
            for t in range(s, PANEL):
                step = (block[r][s] * block[r][t]) * inv if t in near else ratio * block[r][t]
                block[s][t] = block[s][t] - step
            for j in range(q + 1, panels):
                column[s][j] = column[s][j] - ratio * column[r][j]
            for h in range(hq, halves):
                line[s][h] = line[s][h] - ratio * line[r][h]

        for r in range(0, PANEL, 2):
            pivot = block[r][r]
            minor = pivot * block[r + 1][r + 1] - block[r][r + 1] * block[r][r + 1]
            inverse.append(reciprocal(pivot))
            inverse.append(reciprocal(minor, pivot))
            eliminate(r, r + 1, inverse[r])
            for s in range(r + 2, PANEL):
                near = (r + 2, r + 3) if s < r + 4 else ()
                eliminate(r, s, inverse[r], near)
                eliminate(r + 1, s, inverse[r + 1], near)
        result = []
        for h in range(halves):
            if h < hq:
                result.append(zero)
                continue
            value = zero
            for r in range(PANEL):
                value = jnp.where(sub == r, line[r][h] * lax.rsqrt(block[r][r]), value)
            if h == hq:
                value = jnp.where(within >= at * PANEL + sub, value, 0.0)
            result.append(value)
        finished.append(result)
        for j in range(q + 1, panels):
            weights = [column[r][j] * inverse[r] for r in range(PANEL)]
            if j == q + 1:
                ahead = behind
                for r in range(PANEL):
                    for s, factor in enumerate(rows_of(column[r][j])):
                        step = (
                            (column[r][j] * factor) * inverse[r]
                            if r >= PANEL - 2
                            else weights[r] * factor
                        )
                        ahead[s] = ahead[s] - step
            for h in range((q + 1) // per_half, halves):
                value = tile[j][h]
                for r in range(PANEL):
                    value = value - weights[r] * line[r][h]
                tile[j][h] = value

    for q in range(panels):
        for c in range(channels):
            factors[c, q * PANEL : (q + 1) * PANEL, :] = jnp.concatenate(
                [finished[q][h][:, c * SLOT : (c + 1) * SLOT] for h in range(halves)],
                axis=1,
            )


def exchange(x, ex_distance, mp_distance=0):
    shards, parts = lax.axis_size("ex"), lax.axis_size("mp")
    return lax.ppermute(
        x,
        ("ex", "mp"),
        [
            (m * parts + b, (m ^ ex_distance) * parts + (b ^ mp_distance))
            for m in range(shards)
            for b in range(parts)
        ],
    )


def vmem():
    return pl.BlockSpec(memory_space=pltpu.VMEM)


def hbm():
    return pl.BlockSpec(memory_space=pltpu.HBM)


def in_hbm(*arrays):
    return [pltpu.with_memory_space_constraint(x, pltpu.HBM) for x in arrays]


def in_vmem(*arrays):
    return [pltpu.with_memory_space_constraint(x, pltpu.VMEM) for x in arrays]


def smem():
    return pl.BlockSpec(memory_space=pltpu.SMEM)


def local(
    acts,
    grads,
    down_factor,
    up_factor_transposed,
    input_projection,
    gradient_projection,
    order,
    damping,
):
    parts = lax.axis_size("mp")
    shards = lax.axis_size("ex")
    tokens, width = acts.shape[1:]
    key_width = grads.shape[2]
    rank = down_factor.shape[1]
    sketch = input_projection.shape[1]
    examples = tokens // EXAMPLE_LENGTH
    per = rank // parts
    span = per * sketch
    scaling = 1.0 / math.sqrt(2.0 * EXAMPLE_LENGTH * parts)
    sends = pl.pallas_call(
        functools.partial(partial_kernel, parts, scaling),
        out_shape=[pltpu.VMEM((2 * examples, span), jnp.float32)] * parts,
        in_specs=[hbm()] * 7,
        out_specs=[vmem()] * parts,
        scratch_shapes=[
            pltpu.VMEM((tokens, width), acts.dtype),
            pltpu.VMEM((tokens, key_width), grads.dtype),
            pltpu.VMEM((sketch + rank, width), acts.dtype),
            pltpu.VMEM((sketch + rank, key_width), grads.dtype),
            pltpu.SMEM(order.shape[1:], order.dtype),
            pltpu.VMEM((2, rank, tokens), jnp.float32),
            pltpu.VMEM((examples * parts, tokens), jnp.float32),
            pltpu.VMEM((examples * parts, LANES), jnp.float32),
            pltpu.SemaphoreType.DMA(((width + key_width) // CHUNK, 3)),
            pltpu.SemaphoreType.DMA,
        ],
        compiler_params=pltpu.CompilerParams(vmem_limit_bytes=8 * 2**20),
        name="partials",
    )(
        *in_hbm(
            acts,
            grads,
            down_factor,
            up_factor_transposed,
            input_projection,
            gradient_projection,
            order,
        )
    )
    chunks = [exchange(sends[d], 1, d) for d in range(parts - 1, -1, -1)]
    padded = max(span, GROUP * sketch)
    columns, feature_rows = pl.pallas_call(
        sum_kernel,
        out_shape=[pltpu.VMEM((examples, padded), jnp.float32)] * 2,
        in_specs=[vmem()] * parts,
        out_specs=[vmem()] * 2,
        compiler_params=pltpu.CompilerParams(vmem_limit_bytes=2 * 2**20),
        name="sums",
    )(*in_vmem(*chunks))
    near = [columns] + [exchange(columns, d) for d in range(3, shards, 2)] + [feature_rows]
    held = pl.pallas_call(
        stack_kernel,
        out_shape=pltpu.VMEM((len(near) * examples, padded), jnp.float32),
        in_specs=[vmem()] * len(near),
        out_specs=vmem(),
        compiler_params=pltpu.CompilerParams(vmem_limit_bytes=2 * 2**20),
        name="stack",
    )(*in_vmem(*near))
    sent = exchange(held, 1)
    return pl.pallas_call(
        functools.partial(factor_kernel, parts),
        out_shape=[
            jax.ShapeDtypeStruct((examples // parts, rank * sketch), jnp.float32),
            jax.ShapeDtypeStruct((per, sketch, sketch), jnp.float32),
        ],
        in_specs=[smem()] + [vmem()] * 2,
        out_specs=[vmem()] * 2,
        scratch_shapes=[
            pltpu.VMEM(
                (sketch * (2 * PANEL + sketch // SLOT) + PANEL, LANES), jnp.float32
            )
        ],
        compiler_params=pltpu.CompilerParams(vmem_limit_bytes=8 * 2**20),
        name="factors",
    )(damping, *in_vmem(held, sent))


def solution(mesh):
    in_specs = (
        P("mp", "ex", None),
        P("mp", "ex", None),
        P("mp", None, None),
        P("mp", None, None),
        P("mp", None, None),
        P("mp", None, None),
        P("mp", "ex", None),
        P(),
    )
    out_specs = (P(("ex", "mp"), None), P("mp", None, None))
    return jax.shard_map(
        local, mesh=mesh, in_specs=in_specs, out_specs=out_specs, check_vma=False
    )
```

```python
import functools
import itertools
import math

import jax
import jax.numpy as jnp
from jax import lax
from jax.experimental import pallas as pl
from jax.experimental.pallas import tpu as pltpu
from jax.sharding import PartitionSpec as P

EXAMPLE_LENGTH = 8
LANES = 128
SLOT = 32
GROUP = LANES // SLOT
PANEL = 8
PIECES = 4


def dot_nt(a, b):
    return lax.dot_general(
        a, b, (((1,), (1,)), ((), ())), preferred_element_type=jnp.float32
    )


def dot_nn(a, b):
    return jnp.dot(a, b, preferred_element_type=jnp.float32)


def split(x):
    high = x.astype(jnp.bfloat16)
    return high, (x - high.astype(jnp.float32)).astype(jnp.bfloat16)


def partial_kernel(
    parts,
    scaling,
    acts_hbm,
    grads_hbm,
    down_hbm,
    up_hbm,
    proj_in_hbm,
    proj_out_hbm,
    order_hbm,
    *refs,
):
    sends, refs = refs[:parts], refs[parts:]
    acts, grads, weights_in, weights_out, order, low, mask, out, sems, order_sem = refs
    tokens, width = acts.shape
    rank = down_hbm.shape[1]
    sketch = proj_in_hbm.shape[1]
    examples = tokens // EXAMPLE_LENGTH
    per = rank // parts
    halves = sketch // SLOT

    def copy_in(source, target, sem):
        copy = pltpu.make_async_copy(source, target, sem)
        copy.start()
        return copy

    order_copy = copy_in(order_hbm.at[0], order, order_sem)
    pending = []
    for n, (data_hbm, data, first_hbm, second_hbm, weights, count) in enumerate(
        [
            (grads_hbm, grads, proj_out_hbm, up_hbm, weights_out, 1),
            (acts_hbm, acts, proj_in_hbm, down_hbm, weights_in, PIECES),
        ]
    ):
        first = [
            copy_in(first_hbm.at[0], weights.at[pl.ds(0, sketch)], sems.at[n, 0]),
            copy_in(second_hbm.at[0], weights.at[pl.ds(sketch, rank)], sems.at[n, 1]),
        ]
        pieces = []
        for i in range(count):
            here = pl.ds(i * (tokens // count), tokens // count)
            pieces.append(
                (here, copy_in(data_hbm.at[0, here], data.at[here], sems.at[n, 2 + i]))
            )
        pending.append((first, pieces))
    def product(n, data, weights):
        first, pieces = pending[n]
        for copy in first:
            copy.wait()
        terms = []
        for here, copy in pieces:
            copy.wait()
            terms.append(dot_nt(data[here, :], weights[...]))
        return jnp.concatenate(terms, axis=0)

    from_grads = product(0, grads, weights_out)
    order_copy.wait()
    rows = examples * parts
    lane = lax.broadcasted_iota(jnp.int32, (rows, 2 * tokens), 1)
    source = (lane % tokens) // EXAMPLE_LENGTH
    target = jnp.zeros((8, 2 * tokens), jnp.int32)
    for s in range(examples):
        target = jnp.where(source[:8] == s, order[0, s], target)
    target = jnp.concatenate([target] * (rows // 8), axis=0)
    place = lax.broadcasted_iota(jnp.int32, (rows, 2 * tokens), 0) // parts
    mask[...] = jnp.where(target == place, scaling, 0.0)

    from_acts = product(1, acts, weights_in)
    low[0] = jnp.transpose(from_grads)[sketch:]
    low[1] = jnp.transpose(from_acts)[sketch:]
    right_high, right_low = split(
        jnp.concatenate([from_acts[:, :sketch], from_grads[:, :sketch]], axis=0)
    )

    highs, lows = [], []
    for c in range(per):
        chosen = jnp.concatenate(
            [low[i, pl.ds(c, parts, stride=per), :] for i in range(2)], axis=1
        )
        chosen = jnp.concatenate([chosen] * max(1, 8 // parts), axis=0)
        chosen = jnp.concatenate([chosen] * (rows // chosen.shape[0]), axis=0)
        high, rest = split(chosen * mask[...])
        highs.append(high)
        lows.append(rest)
    left_high = jnp.concatenate(highs, axis=0)
    left_low = jnp.concatenate(lows, axis=0)
    both = jnp.dot(
        jnp.concatenate([left_high, left_low], axis=0),
        right_high,
        preferred_element_type=jnp.float32,
    )
    size = left_high.shape[0]
    spread = (
        jnp.dot(left_high, right_low, preferred_element_type=jnp.float32) + both[size:]
    ) + both[:size]
    total = jnp.concatenate(
        [
            spread[c * rows : (c + 1) * rows, h * SLOT : (h + 1) * SLOT]
            for h in range(halves)
            for c in range(per)
        ],
        axis=1,
    )
    me = lax.axis_index("mp")
    for start in range(0, per * sketch, LANES):
        stop = min(start + LANES, per * sketch)
        out[:, : stop - start] = total[:, start:stop]
        for d in range(parts):
            g = me ^ d
            sends[d][:examples, start:stop] = out[
                pl.ds(pl.multiple_of(g * examples, examples), examples), : stop - start
            ]
            sends[d][examples:, start:stop] = out[pl.ds(g, examples, stride=parts), :][
                :, : stop - start
            ]


def sum_kernel(*refs):
    chunks, (columns, feature_rows) = refs[:-2], refs[-2:]
    examples, padded = columns.shape
    total = chunks[0][...]
    for chunk in chunks[1:]:
        total = total + chunk[...]
    width = total.shape[1]
    for ref, value in ((feature_rows, total[:examples]), (columns, total[examples:])):
        ref[:, :width] = value
        if padded > width:
            ref[:, width:] = jnp.zeros((examples, padded - width), jnp.float32)


def stack_kernel(*refs):
    rows = refs[0].shape[0]
    for n, part in enumerate(refs[:-1]):
        refs[-1][n * rows : (n + 1) * rows, :] = part[...]


def write_features(total, parts, per, features):
    rows_here, width = features.shape
    span = width // parts
    halves = span // (per * SLOT)
    natural = jnp.concatenate(
        [
            total[:, (h * per + c) * SLOT : (h * per + c + 1) * SLOT]
            for c in range(per)
            for h in range(halves)
        ],
        axis=1,
    )
    for r in range(rows_here):
        features[r : r + 1, :] = jnp.concatenate(
            [natural[r * parts + g : r * parts + g + 1, :] for g in range(parts)], axis=1
        )


def pick_lanes(x, index):
    return jnp.take_along_axis(x, index, axis=1)


def reciprocal(x, scale=None):
    guess = pl.reciprocal(x, approx=True)
    rest = 2.0 - x * guess
    return (guess if scale is None else scale * guess) * rest


def factor_kernel(parts, damping, held, sent, features, factors, kept):
    channels, sketch, _ = factors.shape
    examples = features.shape[0] * parts
    gathered = held.shape[0] - examples
    span = features.shape[1] // parts
    write_features(sent[gathered:, :span], parts, channels, features)
    halves = sketch // SLOT
    panels = sketch // PANEL
    per_half = SLOT // PANEL
    stacked = jnp.concatenate([held[:gathered, :], sent[:gathered, :]], axis=0)
    high, rest = split(stacked)
    turned_high, turned_rest = split(jnp.transpose(stacked))
    gram = dot_nn(turned_high, rest) + dot_nn(
        jnp.concatenate([turned_rest, turned_high], axis=1),
        jnp.concatenate([high, high], axis=0),
    )
    lane = lax.broadcasted_iota(jnp.int32, (PANEL, LANES), 1)
    sub = lax.broadcasted_iota(jnp.int32, (PANEL, LANES), 0)
    slot = lane // SLOT
    within = lane % SLOT
    ridge = damping[0]
    tile = []
    for q in range(panels):
        hr, at = divmod(q, per_half)
        line = []
        for h in range(halves):
            value = None
            for c in range(GROUP):
                start = hr * LANES + c * SLOT + at * PANEL
                block = gram[start : start + PANEL, h * LANES : (h + 1) * LANES]
                value = block if c == 0 else jnp.where(slot == c, block, value)
            value = value * (1.0 / stacked.shape[0])
            if h == hr:
                value = value + jnp.where(within == at * PANEL + sub, ridge, 0.0)
            line.append(value)
        tile.append(line)

    places = itertools.count(0, PANEL)

    def rows_of(x):
        place = next(places)
        kept[place : place + PANEL, :] = x
        return [kept[pl.ds(place + s, PANEL, stride=0), :] for s in range(PANEL)]

    zero = jnp.zeros((PANEL, LANES), jnp.float32)
    finished = []
    ahead = [pick_lanes(tile[0][0], slot * SLOT + r) for r in range(PANEL)]
    for q in range(panels):
        hq, at = divmod(q, per_half)
        if q + 1 < panels:
            hn, an = divmod(q + 1, per_half)
            behind = [
                pick_lanes(tile[q + 1][hn], slot * SLOT + an * PANEL + r)
                for r in range(PANEL)
            ]
        column = [
            {
                j: ahead[r]
                if j == q
                else pick_lanes(tile[j][hq], slot * SLOT + at * PANEL + r)
                for j in range(q, panels)
            }
            for r in range(PANEL)
        ]
        block = [rows_of(column[r][q]) for r in range(PANEL)]
        lines = [rows_of(tile[q][h]) if h >= hq else [None] * PANEL for h in range(halves)]
        line = [list(group) for group in zip(*lines)]
        inverse = []

        def eliminate(r, s, inv, near=()):
            ratio = block[r][s] * inv
            for t in range(s, PANEL):
                step = (block[r][s] * block[r][t]) * inv if t in near else ratio * block[r][t]
                block[s][t] = block[s][t] - step
            for j in range(q + 1, panels):
                column[s][j] = column[s][j] - ratio * column[r][j]
            for h in range(hq, halves):
                line[s][h] = line[s][h] - ratio * line[r][h]

        for r in range(0, PANEL, 2):
            pivot = block[r][r]
            minor = pivot * block[r + 1][r + 1] - block[r][r + 1] * block[r][r + 1]
            inverse.append(reciprocal(pivot))
            inverse.append(reciprocal(minor, pivot))
            eliminate(r, r + 1, inverse[r])
            for s in range(r + 2, PANEL):
                near = (r + 2, r + 3) if s < r + 4 else ()
                eliminate(r, s, inverse[r], near)
                eliminate(r + 1, s, inverse[r + 1], near)
        result = []
        for h in range(halves):
            if h < hq:
                result.append(zero)
                continue
            value = zero
            for r in range(PANEL):
                value = jnp.where(sub == r, line[r][h] * lax.rsqrt(block[r][r]), value)
            if h == hq:
                value = jnp.where(within >= at * PANEL + sub, value, 0.0)
            result.append(value)
        finished.append(result)
        for j in range(q + 1, panels):
            weights = [column[r][j] * inverse[r] for r in range(PANEL)]
            if j == q + 1:
                ahead = behind
                for r in range(PANEL):
                    for s, factor in enumerate(rows_of(column[r][j])):
                        step = (
                            (column[r][j] * factor) * inverse[r]
                            if r >= PANEL - 2
                            else weights[r] * factor
                        )
                        ahead[s] = ahead[s] - step
            for h in range((q + 1) // per_half, halves):
                value = tile[j][h]
                for r in range(PANEL):
                    value = value - weights[r] * line[r][h]
                tile[j][h] = value

    for q in range(panels):
        for c in range(channels):
            factors[c, q * PANEL : (q + 1) * PANEL, :] = jnp.concatenate(
                [finished[q][h][:, c * SLOT : (c + 1) * SLOT] for h in range(halves)],
                axis=1,
            )


def exchange(x, ex_distance, mp_distance=0):
    shards, parts = lax.axis_size("ex"), lax.axis_size("mp")
    return lax.ppermute(
        x,
        ("ex", "mp"),
        [
            (m * parts + b, (m ^ ex_distance) * parts + (b ^ mp_distance))
            for m in range(shards)
            for b in range(parts)
        ],
    )


def vmem():
    return pl.BlockSpec(memory_space=pltpu.VMEM)


def hbm():
    return pl.BlockSpec(memory_space=pltpu.HBM)


def in_hbm(*arrays):
    return [pltpu.with_memory_space_constraint(x, pltpu.HBM) for x in arrays]


def in_vmem(*arrays):
    return [pltpu.with_memory_space_constraint(x, pltpu.VMEM) for x in arrays]


def smem():
    return pl.BlockSpec(memory_space=pltpu.SMEM)


def local(
    acts,
    grads,
    down_factor,
    up_factor_transposed,
    input_projection,
    gradient_projection,
    order,
    damping,
):
    parts = lax.axis_size("mp")
    shards = lax.axis_size("ex")
    tokens, width = acts.shape[1:]
    key_width = grads.shape[2]
    rank = down_factor.shape[1]
    sketch = input_projection.shape[1]
    examples = tokens // EXAMPLE_LENGTH
    per = rank // parts
    span = per * sketch
    scaling = 1.0 / math.sqrt(2.0 * EXAMPLE_LENGTH * parts)
    sends = pl.pallas_call(
        functools.partial(partial_kernel, parts, scaling),
        out_shape=[pltpu.VMEM((2 * examples, span), jnp.float32)] * parts,
        in_specs=[hbm()] * 7,
        out_specs=[vmem()] * parts,
        scratch_shapes=[
            pltpu.VMEM((tokens, width), acts.dtype),
            pltpu.VMEM((tokens, key_width), grads.dtype),
            pltpu.VMEM((sketch + rank, width), acts.dtype),
            pltpu.VMEM((sketch + rank, key_width), grads.dtype),
            pltpu.SMEM(order.shape[1:], order.dtype),
            pltpu.VMEM((2, rank, tokens), jnp.float32),
            pltpu.VMEM((examples * parts, 2 * tokens), jnp.float32),
            pltpu.VMEM((examples * parts, LANES), jnp.float32),
            pltpu.SemaphoreType.DMA((2, 2 + PIECES)),
            pltpu.SemaphoreType.DMA,
        ],
        compiler_params=pltpu.CompilerParams(vmem_limit_bytes=8 * 2**20),
        name="partials",
    )(
        *in_hbm(
            acts,
            grads,
            down_factor,
            up_factor_transposed,
            input_projection,
            gradient_projection,
            order,
        )
    )
    chunks = [exchange(sends[d], 1, d) for d in range(parts - 1, -1, -1)]
    padded = max(span, GROUP * sketch)
    columns, feature_rows = pl.pallas_call(
        sum_kernel,
        out_shape=[pltpu.VMEM((examples, padded), jnp.float32)] * 2,
        in_specs=[vmem()] * parts,
        out_specs=[vmem()] * 2,
        compiler_params=pltpu.CompilerParams(vmem_limit_bytes=2 * 2**20),
        name="sums",
    )(*in_vmem(*chunks))
    near = [columns] + [exchange(columns, d) for d in range(3, shards, 2)] + [feature_rows]
    held = pl.pallas_call(
        stack_kernel,
        out_shape=pltpu.VMEM((len(near) * examples, padded), jnp.float32),
        in_specs=[vmem()] * len(near),
        out_specs=vmem(),
        compiler_params=pltpu.CompilerParams(vmem_limit_bytes=2 * 2**20),
        name="stack",
    )(*in_vmem(*near))
    sent = exchange(held, 1)
    return pl.pallas_call(
        functools.partial(factor_kernel, parts),
        out_shape=[
            jax.ShapeDtypeStruct((examples // parts, rank * sketch), jnp.float32),
            jax.ShapeDtypeStruct((per, sketch, sketch), jnp.float32),
        ],
        in_specs=[smem()] + [vmem()] * 2,
        out_specs=[vmem()] * 2,
        scratch_shapes=[
            pltpu.VMEM(
                (sketch * (2 * PANEL + sketch // SLOT) + PANEL, LANES), jnp.float32
            )
        ],
        compiler_params=pltpu.CompilerParams(vmem_limit_bytes=8 * 2**20),
        name="factors",
    )(damping, *in_vmem(held, sent))


def solution(mesh):
    in_specs = (
        P("mp", "ex", None),
        P("mp", "ex", None),
        P("mp", None, None),
        P("mp", None, None),
        P("mp", None, None),
        P("mp", None, None),
        P("mp", "ex", None),
        P(),
    )
    out_specs = (P(("ex", "mp"), None), P("mp", None, None))
    return jax.shard_map(
        local, mesh=mesh, in_specs=in_specs, out_specs=out_specs, check_vma=False
    )
```

```python
import functools
import itertools
import math

import jax
import jax.numpy as jnp
from jax import lax
from jax.experimental import pallas as pl
from jax.experimental.pallas import tpu as pltpu
from jax.sharding import PartitionSpec as P

EXAMPLE_LENGTH = 8
LANES = 128
SLOT = 32
GROUP = LANES // SLOT
PANEL = 8
CHUNK = 1024


def dot_nt(a, b):
    return lax.dot_general(
        a, b, (((1,), (1,)), ((), ())), preferred_element_type=jnp.float32
    )


def dot_nn(a, b):
    return jnp.dot(a, b, preferred_element_type=jnp.float32)


def split(x):
    high = x.astype(jnp.bfloat16)
    return high, (x - high.astype(jnp.float32)).astype(jnp.bfloat16)


def partial_kernel(
    parts,
    scaling,
    acts_hbm,
    grads_hbm,
    down_hbm,
    up_hbm,
    proj_in_hbm,
    proj_out_hbm,
    order_hbm,
    *refs,
):
    sends, refs = refs[:parts], refs[parts:]
    acts, grads, weights_in, weights_out, turned_in, turned_out, order, low, mask, out, sems = refs
    tokens, width = acts.shape
    rank = down_hbm.shape[1]
    sketch = proj_in_hbm.shape[1]
    examples = tokens // EXAMPLE_LENGTH
    per = rank // parts
    halves = sketch // SLOT

    number = itertools.count()

    def copy_in(source, target):
        copy = pltpu.make_async_copy(source, target, sems.at[next(number)])
        copy.start()
        return copy

    def weight_copies(first_hbm, second_hbm, weights):
        return [
            copy_in(first_hbm.at[0], weights.at[pl.ds(0, sketch)]),
            copy_in(second_hbm.at[0], weights.at[pl.ds(sketch, rank)]),
        ]

    order_copy = copy_in(order_hbm.at[0], order)
    out_copies = weight_copies(proj_out_hbm, up_hbm, weights_out)
    grads_copy = copy_in(grads_hbm.at[0], grads)
    in_copies = weight_copies(proj_in_hbm, down_hbm, weights_in)
    strips = [pl.ds(start, CHUNK) for start in range(0, width, CHUNK)]
    acts_copies = [copy_in(acts_hbm.at[0, :, here], acts.at[:, here]) for here in strips]

    rows = examples * parts
    order_copy.wait()
    source = lax.broadcasted_iota(jnp.int32, (8, tokens), 1) // EXAMPLE_LENGTH
    target = jnp.zeros((8, tokens), jnp.int32)
    for s in range(examples):
        target = jnp.where(source == s, order[0, s], target)
    target = jnp.concatenate([target] * (rows // 8), axis=0)
    place = lax.broadcasted_iota(jnp.int32, (rows, tokens), 0) // parts
    mask[...] = jnp.where(target == place, scaling, 0.0)

    def spread_low(values, n):
        low[n] = jnp.transpose(values)[sketch:]
        tiles = []
        for c in range(per):
            chosen = low[n, pl.ds(c, parts, stride=per), :]
            chosen = jnp.concatenate([chosen] * max(1, 8 // parts), axis=0)
            chosen = jnp.concatenate([chosen] * (rows // chosen.shape[0]), axis=0)
            tiles.append(split(chosen * mask[...]))
        return [jnp.concatenate(half, axis=0) for half in zip(*tiles)]

    for copy in out_copies:
        copy.wait()
    turned_out[...] = jnp.transpose(weights_out[...])
    grads_copy.wait()
    from_grads = dot_nn(grads[...], turned_out[...])
    left_grads = spread_low(from_grads, 0)
    for copy in in_copies:
        copy.wait()
    for here in strips:
        turned_in[here, :] = jnp.transpose(weights_in[:, here])
    from_acts = None
    for here, copy in zip(strips, acts_copies):
        copy.wait()
        term = dot_nn(acts[:, here], turned_in[here, :])
        from_acts = term if from_acts is None else from_acts + term
    left_acts = spread_low(from_acts, 1)
    left_high, left_low = [
        jnp.concatenate(pair, axis=1) for pair in zip(left_grads, left_acts)
    ]
    right_high, right_low = split(
        jnp.concatenate([from_acts[:, :sketch], from_grads[:, :sketch]], axis=0)
    )
    both = jnp.dot(
        jnp.concatenate([left_high, left_low], axis=0),
        right_high,
        preferred_element_type=jnp.float32,
    )
    size = left_high.shape[0]
    spread = (
        jnp.dot(left_high, right_low, preferred_element_type=jnp.float32) + both[size:]
    ) + both[:size]
    total = jnp.concatenate(
        [
            spread[c * rows : (c + 1) * rows, h * SLOT : (h + 1) * SLOT]
            for h in range(halves)
            for c in range(per)
        ],
        axis=1,
    )
    me = lax.axis_index("mp")
    for start in range(0, per * sketch, LANES):
        stop = min(start + LANES, per * sketch)
        out[:, : stop - start] = total[:, start:stop]
        for d in range(parts):
            g = me ^ d
            sends[d][:examples, start:stop] = out[
                pl.ds(pl.multiple_of(g * examples, examples), examples), : stop - start
            ]
            sends[d][examples:, start:stop] = out[pl.ds(g, examples, stride=parts), :][
                :, : stop - start
            ]


def sum_kernel(*refs):
    chunks, (columns, feature_rows) = refs[:-2], refs[-2:]
    examples, padded = columns.shape
    total = chunks[0][...]
    for chunk in chunks[1:]:
        total = total + chunk[...]
    width = total.shape[1]
    for ref, value in ((feature_rows, total[:examples]), (columns, total[examples:])):
        ref[:, :width] = value
        if padded > width:
            ref[:, width:] = jnp.zeros((examples, padded - width), jnp.float32)


def stack_kernel(*refs):
    rows = refs[0].shape[0]
    for n, part in enumerate(refs[:-1]):
        refs[-1][n * rows : (n + 1) * rows, :] = part[...]


def write_features(total, parts, per, features):
    rows_here, width = features.shape
    span = width // parts
    halves = span // (per * SLOT)
    natural = jnp.concatenate(
        [
            total[:, (h * per + c) * SLOT : (h * per + c + 1) * SLOT]
            for c in range(per)
            for h in range(halves)
        ],
        axis=1,
    )
    for r in range(rows_here):
        features[r : r + 1, :] = jnp.concatenate(
            [natural[r * parts + g : r * parts + g + 1, :] for g in range(parts)], axis=1
        )


def pick_lanes(x, index):
    return jnp.take_along_axis(x, index, axis=1)


def reciprocal(x, scale=None):
    guess = pl.reciprocal(x, approx=True)
    rest = 2.0 - x * guess
    return (guess if scale is None else scale * guess) * rest


def factor_kernel(parts, damping, held, sent, features, factors, kept):
    channels, sketch, _ = factors.shape
    examples = features.shape[0] * parts
    gathered = held.shape[0] - examples
    span = features.shape[1] // parts
    write_features(sent[gathered:, :span], parts, channels, features)
    halves = sketch // SLOT
    panels = sketch // PANEL
    per_half = SLOT // PANEL
    stacked = jnp.concatenate([held[:gathered, :], sent[:gathered, :]], axis=0)
    high, rest = split(stacked)
    turned_high, turned_rest = split(jnp.transpose(stacked))
    gram = dot_nn(turned_high, rest) + dot_nn(
        jnp.concatenate([turned_rest, turned_high], axis=1),
        jnp.concatenate([high, high], axis=0),
    )
    lane = lax.broadcasted_iota(jnp.int32, (PANEL, LANES), 1)
    sub = lax.broadcasted_iota(jnp.int32, (PANEL, LANES), 0)
    slot = lane // SLOT
    within = lane % SLOT
    ridge = damping[0]
    tile = []
    for q in range(panels):
        hr, at = divmod(q, per_half)
        line = []
        for h in range(halves):
            value = None
            for c in range(GROUP):
                start = hr * LANES + c * SLOT + at * PANEL
                block = gram[start : start + PANEL, h * LANES : (h + 1) * LANES]
                value = block if c == 0 else jnp.where(slot == c, block, value)
            value = value * (1.0 / stacked.shape[0])
            if h == hr:
                value = value + jnp.where(within == at * PANEL + sub, ridge, 0.0)
            line.append(value)
        tile.append(line)

    places = itertools.count(0, PANEL)

    def rows_of(x):
        place = next(places)
        kept[place : place + PANEL, :] = x
        return [kept[pl.ds(place + s, PANEL, stride=0), :] for s in range(PANEL)]

    zero = jnp.zeros((PANEL, LANES), jnp.float32)
    finished = []
    ahead = [pick_lanes(tile[0][0], slot * SLOT + r) for r in range(PANEL)]
    for q in range(panels):
        hq, at = divmod(q, per_half)
        if q + 1 < panels:
            hn, an = divmod(q + 1, per_half)
            behind = [
                pick_lanes(tile[q + 1][hn], slot * SLOT + an * PANEL + r)
                for r in range(PANEL)
            ]
        column = [
            {
                j: ahead[r]
                if j == q
                else pick_lanes(tile[j][hq], slot * SLOT + at * PANEL + r)
                for j in range(q, panels)
            }
            for r in range(PANEL)
        ]
        block = [rows_of(column[r][q]) for r in range(PANEL)]
        lines = [rows_of(tile[q][h]) if h >= hq else [None] * PANEL for h in range(halves)]
        line = [list(group) for group in zip(*lines)]
        inverse = []

        def eliminate(r, s, inv, near=()):
            ratio = block[r][s] * inv
            for t in range(s, PANEL):
                step = (block[r][s] * block[r][t]) * inv if t in near else ratio * block[r][t]
                block[s][t] = block[s][t] - step
            for j in range(q + 1, panels):
                column[s][j] = column[s][j] - ratio * column[r][j]
            for h in range(hq, halves):
                line[s][h] = line[s][h] - ratio * line[r][h]

        for r in range(0, PANEL, 2):
            pivot = block[r][r]
            minor = pivot * block[r + 1][r + 1] - block[r][r + 1] * block[r][r + 1]
            inverse.append(reciprocal(pivot))
            inverse.append(reciprocal(minor, pivot))
            eliminate(r, r + 1, inverse[r])
            for s in range(r + 2, PANEL):
                near = (r + 2, r + 3) if s < r + 4 else ()
                eliminate(r, s, inverse[r], near)
                eliminate(r + 1, s, inverse[r + 1], near)
        result = []
        for h in range(halves):
            if h < hq:
                result.append(zero)
                continue
            value = zero
            for r in range(PANEL):
                value = jnp.where(sub == r, line[r][h] * lax.rsqrt(block[r][r]), value)
            if h == hq:
                value = jnp.where(within >= at * PANEL + sub, value, 0.0)
            result.append(value)
        finished.append(result)
        for j in range(q + 1, panels):
            weights = [column[r][j] * inverse[r] for r in range(PANEL)]
            if j == q + 1:
                ahead = behind
                for r in range(PANEL):
                    for s, factor in enumerate(rows_of(column[r][j])):
                        step = (
                            (column[r][j] * factor) * inverse[r]
                            if r >= PANEL - 2
                            else weights[r] * factor
                        )
                        ahead[s] = ahead[s] - step
            for h in range((q + 1) // per_half, halves):
                value = tile[j][h]
                for r in range(PANEL):
                    value = value - weights[r] * line[r][h]
                tile[j][h] = value

    for q in range(panels):
        for c in range(channels):
            factors[c, q * PANEL : (q + 1) * PANEL, :] = jnp.concatenate(
                [finished[q][h][:, c * SLOT : (c + 1) * SLOT] for h in range(halves)],
                axis=1,
            )


def exchange(x, ex_distance, mp_distance=0):
    shards, parts = lax.axis_size("ex"), lax.axis_size("mp")
    return lax.ppermute(
        x,
        ("ex", "mp"),
        [
            (m * parts + b, (m ^ ex_distance) * parts + (b ^ mp_distance))
            for m in range(shards)
            for b in range(parts)
        ],
    )


def vmem():
    return pl.BlockSpec(memory_space=pltpu.VMEM)


def hbm():
    return pl.BlockSpec(memory_space=pltpu.HBM)


def in_hbm(*arrays):
    return [pltpu.with_memory_space_constraint(x, pltpu.HBM) for x in arrays]


def in_vmem(*arrays):
    return [pltpu.with_memory_space_constraint(x, pltpu.VMEM) for x in arrays]


def smem():
    return pl.BlockSpec(memory_space=pltpu.SMEM)


def local(
    acts,
    grads,
    down_factor,
    up_factor_transposed,
    input_projection,
    gradient_projection,
    order,
    damping,
):
    parts = lax.axis_size("mp")
    shards = lax.axis_size("ex")
    tokens, width = acts.shape[1:]
    key_width = grads.shape[2]
    rank = down_factor.shape[1]
    sketch = input_projection.shape[1]
    examples = tokens // EXAMPLE_LENGTH
    per = rank // parts
    span = per * sketch
    scaling = 1.0 / math.sqrt(2.0 * EXAMPLE_LENGTH * parts)
    sends = pl.pallas_call(
        functools.partial(partial_kernel, parts, scaling),
        out_shape=[pltpu.VMEM((2 * examples, span), jnp.float32)] * parts,
        in_specs=[hbm()] * 7,
        out_specs=[vmem()] * parts,
        scratch_shapes=[
            pltpu.VMEM((tokens, width), acts.dtype),
            pltpu.VMEM((tokens, key_width), grads.dtype),
            pltpu.VMEM((sketch + rank, width), acts.dtype),
            pltpu.VMEM((sketch + rank, key_width), grads.dtype),
            pltpu.VMEM((width, sketch + rank), acts.dtype),
            pltpu.VMEM((key_width, sketch + rank), grads.dtype),
            pltpu.SMEM(order.shape[1:], order.dtype),
            pltpu.VMEM((2, rank, tokens), jnp.float32),
            pltpu.VMEM((examples * parts, tokens), jnp.float32),
            pltpu.VMEM((examples * parts, LANES), jnp.float32),
            pltpu.SemaphoreType.DMA((6 + width // CHUNK,)),
        ],
        compiler_params=pltpu.CompilerParams(vmem_limit_bytes=8 * 2**20),
        name="partials",
    )(
        *in_hbm(
            acts,
            grads,
            down_factor,
            up_factor_transposed,
            input_projection,
            gradient_projection,
            order,
        )
    )
    chunks = [exchange(sends[d], 1, d) for d in range(parts - 1, -1, -1)]
    padded = max(span, GROUP * sketch)
    columns, feature_rows = pl.pallas_call(
        sum_kernel,
        out_shape=[pltpu.VMEM((examples, padded), jnp.float32)] * 2,
        in_specs=[vmem()] * parts,
        out_specs=[vmem()] * 2,
        compiler_params=pltpu.CompilerParams(vmem_limit_bytes=2 * 2**20),
        name="sums",
    )(*in_vmem(*chunks))
    near = [columns] + [exchange(columns, d) for d in range(3, shards, 2)] + [feature_rows]
    held = pl.pallas_call(
        stack_kernel,
        out_shape=pltpu.VMEM((len(near) * examples, padded), jnp.float32),
        in_specs=[vmem()] * len(near),
        out_specs=vmem(),
        compiler_params=pltpu.CompilerParams(vmem_limit_bytes=2 * 2**20),
        name="stack",
    )(*in_vmem(*near))
    sent = exchange(held, 1)
    return pl.pallas_call(
        functools.partial(factor_kernel, parts),
        out_shape=[
            jax.ShapeDtypeStruct((examples // parts, rank * sketch), jnp.float32),
            jax.ShapeDtypeStruct((per, sketch, sketch), jnp.float32),
        ],
        in_specs=[smem()] + [vmem()] * 2,
        out_specs=[vmem()] * 2,
        scratch_shapes=[
            pltpu.VMEM(
                (sketch * (2 * PANEL + sketch // SLOT) + PANEL, LANES), jnp.float32
            )
        ],
        compiler_params=pltpu.CompilerParams(vmem_limit_bytes=8 * 2**20),
        name="factors",
    )(damping, *in_vmem(held, sent))


def solution(mesh):
    in_specs = (
        P("mp", "ex", None),
        P("mp", "ex", None),
        P("mp", None, None),
        P("mp", None, None),
        P("mp", None, None),
        P("mp", None, None),
        P("mp", "ex", None),
        P(),
    )
    out_specs = (P(("ex", "mp"), None), P("mp", None, None))
    return jax.shard_map(
        local, mesh=mesh, in_specs=in_specs, out_specs=out_specs, check_vma=False
    )
```

```python
import functools
import math

import jax
import jax.numpy as jnp
from jax import lax
from jax.experimental import pallas as pl
from jax.experimental.pallas import tpu as pltpu
from jax.sharding import PartitionSpec as P

EXAMPLE_LENGTH = 8
LANES = 128
SLOT = 32
GROUP = LANES // SLOT
PANEL = 8
CHUNK = 1024


def dot_nt(a, b):
    return lax.dot_general(
        a, b, (((1,), (1,)), ((), ())), preferred_element_type=jnp.float32
    )


def dot_nn(a, b):
    return jnp.dot(a, b, preferred_element_type=jnp.float32)


def split(x):
    high = x.astype(jnp.bfloat16)
    return high, (x - high.astype(jnp.float32)).astype(jnp.bfloat16)


def partial_kernel(
    parts,
    scaling,
    acts_hbm,
    grads_hbm,
    down_hbm,
    up_hbm,
    proj_in_hbm,
    proj_out_hbm,
    order_hbm,
    *refs,
):
    sends, refs = refs[:parts], refs[parts:]
    acts, grads, weights_in, weights_out, order, low, mask, out, sems, order_sem = refs
    tokens, width = acts.shape
    rank = down_hbm.shape[1]
    sketch = proj_in_hbm.shape[1]
    examples = tokens // EXAMPLE_LENGTH
    per = rank // parts
    halves = sketch // SLOT

    def copies(source, target, sem, start, size):
        return pltpu.make_async_copy(
            source.at[0, :, pl.ds(start, size)],
            target.at[:, pl.ds(start, size)],
            sem,
        )

    order_copy = pltpu.make_async_copy(order_hbm.at[0], order, order_sem)
    order_copy.start()
    sources = [
        (grads_hbm, grads, proj_out_hbm, up_hbm, weights_out),
        (acts_hbm, acts, proj_in_hbm, down_hbm, weights_in),
    ]
    pending = []
    for data_hbm, data, first_hbm, second_hbm, weights in sources:
        for start in range(0, data.shape[1], CHUNK):
            n = len(pending)
            pending.append(
                [
                    copies(first_hbm, weights.at[pl.ds(0, sketch)], sems.at[n, 0], start, CHUNK),
                    copies(second_hbm, weights.at[pl.ds(sketch, rank)], sems.at[n, 1], start, CHUNK),
                    copies(data_hbm, data, sems.at[n, 2], start, CHUNK),
                ]
            )
            for copy in pending[-1]:
                copy.start()

    order_copy.wait()
    rows = examples * parts
    source = lax.broadcasted_iota(jnp.int32, (8, tokens), 1) // EXAMPLE_LENGTH
    target = jnp.zeros((8, tokens), jnp.int32)
    for s in range(examples):
        target = jnp.where(source == s, order[0, s], target)
    target = jnp.concatenate([target] * (rows // 8), axis=0)
    place = lax.broadcasted_iota(jnp.int32, (rows, tokens), 0) // parts
    mask[...] = jnp.where(target == place, scaling, 0.0)

    def product(first, data, weights):
        total = None
        for n in range(data.shape[1] // CHUNK):
            for copy in pending[first + n]:
                copy.wait()
            here = pl.ds(n * CHUNK, CHUNK)
            term = dot_nt(weights[:, here], data[:, here])
            total = term if total is None else total + term
        return total

    def spread_low(values, n):
        low[n] = values
        tiles = []
        for c in range(per):
            chosen = low[n, pl.ds(c, parts, stride=per), :]
            chosen = jnp.concatenate([chosen] * max(1, 8 // parts), axis=0)
            chosen = jnp.concatenate([chosen] * (rows // chosen.shape[0]), axis=0)
            tiles.append(split(chosen * mask[...]))
        return [jnp.concatenate(half, axis=0) for half in zip(*tiles)]

    def spread_sketch(values):
        return split(
            jnp.concatenate(
                [values[h * SLOT : (h + 1) * SLOT] for h in range(halves) for _ in range(per)],
                axis=0,
            )
        )

    from_grads = product(0, grads, weights_out)
    left_grads = spread_low(from_grads[sketch:], 0)
    right_grads = spread_sketch(from_grads[:sketch])
    from_acts = product(grads.shape[1] // CHUNK, acts, weights_in)
    left_acts = spread_low(from_acts[sketch:], 1)
    right_acts = spread_sketch(from_acts[:sketch])
    left_high, left_low = [
        jnp.concatenate(pair, axis=1) for pair in zip(left_grads, left_acts)
    ]
    right_high, right_low = [
        jnp.concatenate(pair, axis=1) for pair in zip(right_acts, right_grads)
    ]
    both = dot_nt(jnp.concatenate([left_high, left_low], axis=0), right_high)
    size = left_high.shape[0]
    spread = (dot_nt(left_high, right_low) + both[size:]) + both[:size]
    column = lax.broadcasted_iota(jnp.int32, (rows, per * sketch), 1)
    channel = (column // SLOT) % per
    total = spread[:rows]
    for c in range(1, per):
        total = jnp.where(channel == c, spread[c * rows : (c + 1) * rows], total)
    me = lax.axis_index("mp")
    for start in range(0, per * sketch, LANES):
        stop = min(start + LANES, per * sketch)
        out[:, : stop - start] = total[:, start:stop]
        for d in range(parts):
            g = me ^ d
            sends[d][:examples, start:stop] = out[
                pl.ds(pl.multiple_of(g * examples, examples), examples), : stop - start
            ]
            sends[d][examples:, start:stop] = out[pl.ds(g, examples, stride=parts), :][
                :, : stop - start
            ]


def sum_kernel(*refs):
    chunks, (columns, feature_rows) = refs[:-2], refs[-2:]
    examples, padded = columns.shape
    total = chunks[0][...]
    for chunk in chunks[1:]:
        total = total + chunk[...]
    width = total.shape[1]
    for ref, value in ((feature_rows, total[:examples]), (columns, total[examples:])):
        ref[:, :width] = value
        if padded > width:
            ref[:, width:] = jnp.zeros((examples, padded - width), jnp.float32)


def stack_kernel(*refs):
    rows = refs[0].shape[0]
    for n, part in enumerate(refs[:-1]):
        refs[-1][n * rows : (n + 1) * rows, :] = part[...]


def write_features(total, parts, per, features):
    rows_here, width = features.shape
    span = width // parts
    halves = span // (per * SLOT)
    natural = jnp.concatenate(
        [
            total[:, (h * per + c) * SLOT : (h * per + c + 1) * SLOT]
            for c in range(per)
            for h in range(halves)
        ],
        axis=1,
    )
    for r in range(rows_here):
        features[r : r + 1, :] = jnp.concatenate(
            [natural[r * parts + g : r * parts + g + 1, :] for g in range(parts)], axis=1
        )


def pick_lanes(x, index):
    return jnp.take_along_axis(x, index, axis=1)


def reciprocal(x):
    guess = pl.reciprocal(x, approx=True)
    return guess * (2.0 - x * guess)


def gram_tiles(rows):
    halves = rows.shape[1] // LANES
    per_half = SLOT // PANEL
    high, rest = split(rows)
    turned_high, turned_rest = split(jnp.transpose(rows))
    gram = dot_nn(turned_high, rest) + dot_nn(
        jnp.concatenate([turned_rest, turned_high], axis=1),
        jnp.concatenate([high, high], axis=0),
    )
    slot = lax.broadcasted_iota(jnp.int32, (PANEL, LANES), 1) // SLOT
    tiles = []
    for q in range(halves * per_half):
        hr, at = divmod(q, per_half)
        line = []
        for h in range(halves):
            value = None
            for c in range(GROUP):
                start = hr * LANES + c * SLOT + at * PANEL
                block = gram[start : start + PANEL, h * LANES : (h + 1) * LANES]
                value = block if c == 0 else jnp.where(slot == c, block, value)
            line.append(value)
        tiles.append(line)
    return tiles


def gram_kernel(gathered, held, own_tiles):
    for q, line in enumerate(gram_tiles(held[:gathered, :])):
        for h, value in enumerate(line):
            own_tiles[q * PANEL : (q + 1) * PANEL, h * LANES : (h + 1) * LANES] = value


def factor_kernel(parts, gathered, damping, own_tiles, sent, features, factors):
    channels, sketch, _ = factors.shape
    halves = sketch // SLOT
    panels = sketch // PANEL
    per_half = SLOT // PANEL
    span = features.shape[1] // parts
    write_features(sent[gathered:, :span], parts, channels, features)
    lane = lax.broadcasted_iota(jnp.int32, (PANEL, LANES), 1)
    sub = lax.broadcasted_iota(jnp.int32, (PANEL, LANES), 0)
    slot = lane // SLOT
    within = lane % SLOT
    ridge = damping[0]
    tile = gram_tiles(sent[:gathered, :])
    for q in range(panels):
        hr, at = divmod(q, per_half)
        for h in range(halves):
            own = own_tiles[q * PANEL : (q + 1) * PANEL, h * LANES : (h + 1) * LANES]
            value = (tile[q][h] + own) * (1.0 / (2 * gathered))
            if h == hr:
                value = value + jnp.where(within == at * PANEL + sub, ridge, 0.0)
            tile[q][h] = value

    zero = jnp.zeros((PANEL, LANES), jnp.float32)
    finished = []
    ahead = [pick_lanes(tile[0][0], slot * SLOT + r) for r in range(PANEL)]
    for q in range(panels):
        hq, at = divmod(q, per_half)
        if q + 1 < panels:
            hn, an = divmod(q + 1, per_half)
            behind = [
                pick_lanes(tile[q + 1][hn], slot * SLOT + an * PANEL + r)
                for r in range(PANEL)
            ]
        column = [
            {
                j: ahead[r]
                if j == q
                else pick_lanes(tile[j][hq], slot * SLOT + at * PANEL + r)
                for j in range(q, panels)
            }
            for r in range(PANEL)
        ]
        block = [
            [
                jnp.broadcast_to(column[r][q][s : s + 1, :], (PANEL, LANES))
                if s >= r
                else None
                for s in range(PANEL)
            ]
            for r in range(PANEL)
        ]
        line = [
            [
                jnp.broadcast_to(tile[q][h][r : r + 1, :], (PANEL, LANES))
                if h >= hq
                else None
                for h in range(halves)
            ]
            for r in range(PANEL)
        ]
        inverse = []

        def eliminate(r, s, inv):
            ratio = block[r][s] * inv
            for t in range(s, PANEL):
                block[s][t] = block[s][t] - ratio * block[r][t]
            for j in range(q + 1, panels):
                column[s][j] = column[s][j] - ratio * column[r][j]
            for h in range(hq, halves):
                line[s][h] = line[s][h] - ratio * line[r][h]

        for r in range(0, PANEL, 2):
            pivot = block[r][r]
            minor = pivot * block[r + 1][r + 1] - block[r][r + 1] * block[r][r + 1]
            inverse.append(reciprocal(pivot))
            inverse.append(pivot * reciprocal(minor))
            eliminate(r, r + 1, inverse[r])
            for s in range(r + 2, PANEL):
                eliminate(r, s, inverse[r])
                eliminate(r + 1, s, inverse[r + 1])
        result = []
        for h in range(halves):
            if h < hq:
                result.append(zero)
                continue
            value = zero
            for r in range(PANEL):
                value = jnp.where(sub == r, line[r][h] * lax.rsqrt(block[r][r]), value)
            if h == hq:
                value = jnp.where(within >= at * PANEL + sub, value, 0.0)
            result.append(value)
        finished.append(result)
        for j in range(q + 1, panels):
            weights = [column[r][j] * inverse[r] for r in range(PANEL)]
            if j == q + 1:
                ahead = behind
                for r in range(PANEL):
                    for s in range(PANEL):
                        factor = jnp.broadcast_to(
                            column[r][j][s : s + 1, :], (PANEL, LANES)
                        )
                        ahead[s] = ahead[s] - weights[r] * factor
            for h in range((q + 1) // per_half, halves):
                value = tile[j][h]
                for r in range(PANEL):
                    value = value - weights[r] * line[r][h]
                tile[j][h] = value

    for q in range(panels):
        for c in range(channels):
            factors[c, q * PANEL : (q + 1) * PANEL, :] = jnp.concatenate(
                [finished[q][h][:, c * SLOT : (c + 1) * SLOT] for h in range(halves)],
                axis=1,
            )


def exchange(x, ex_distance, mp_distance=0):
    shards, parts = lax.axis_size("ex"), lax.axis_size("mp")
    return lax.ppermute(
        x,
        ("ex", "mp"),
        [
            (m * parts + b, (m ^ ex_distance) * parts + (b ^ mp_distance))
            for m in range(shards)
            for b in range(parts)
        ],
    )


def vmem():
    return pl.BlockSpec(memory_space=pltpu.VMEM)


def hbm():
    return pl.BlockSpec(memory_space=pltpu.HBM)


def in_hbm(*arrays):
    return [pltpu.with_memory_space_constraint(x, pltpu.HBM) for x in arrays]


def in_vmem(*arrays):
    return [pltpu.with_memory_space_constraint(x, pltpu.VMEM) for x in arrays]


def smem():
    return pl.BlockSpec(memory_space=pltpu.SMEM)


def local(
    acts,
    grads,
    down_factor,
    up_factor_transposed,
    input_projection,
    gradient_projection,
    order,
    damping,
):
    parts = lax.axis_size("mp")
    shards = lax.axis_size("ex")
    tokens, width = acts.shape[1:]
    key_width = grads.shape[2]
    rank = down_factor.shape[1]
    sketch = input_projection.shape[1]
    examples = tokens // EXAMPLE_LENGTH
    per = rank // parts
    span = per * sketch
    scaling = 1.0 / math.sqrt(2.0 * EXAMPLE_LENGTH * parts)
    sends = pl.pallas_call(
        functools.partial(partial_kernel, parts, scaling),
        out_shape=[pltpu.VMEM((2 * examples, span), jnp.float32)] * parts,
        in_specs=[hbm()] * 7,
        out_specs=[vmem()] * parts,
        scratch_shapes=[
            pltpu.VMEM((tokens, width), acts.dtype),
            pltpu.VMEM((tokens, key_width), grads.dtype),
            pltpu.VMEM((sketch + rank, width), acts.dtype),
            pltpu.VMEM((sketch + rank, key_width), grads.dtype),
            pltpu.SMEM(order.shape[1:], order.dtype),
            pltpu.VMEM((2, rank, tokens), jnp.float32),
            pltpu.VMEM((examples * parts, tokens), jnp.float32),
            pltpu.VMEM((examples * parts, LANES), jnp.float32),
            pltpu.SemaphoreType.DMA(((width + key_width) // CHUNK, 3)),
            pltpu.SemaphoreType.DMA,
        ],
        compiler_params=pltpu.CompilerParams(vmem_limit_bytes=8 * 2**20),
        name="partials",
    )(
        *in_hbm(
            acts,
            grads,
            down_factor,
            up_factor_transposed,
            input_projection,
            gradient_projection,
            order,
        )
    )
    chunks = [exchange(sends[d], 1, d) for d in range(parts - 1, -1, -1)]
    padded = max(span, GROUP * sketch)
    columns, feature_rows = pl.pallas_call(
        sum_kernel,
        out_shape=[pltpu.VMEM((examples, padded), jnp.float32)] * 2,
        in_specs=[vmem()] * parts,
        out_specs=[vmem()] * 2,
        compiler_params=pltpu.CompilerParams(vmem_limit_bytes=2 * 2**20),
        name="sums",
    )(*in_vmem(*chunks))
    near = [columns] + [exchange(columns, d) for d in range(3, shards, 2)] + [feature_rows]
    held = pl.pallas_call(
        stack_kernel,
        out_shape=pltpu.VMEM((len(near) * examples, padded), jnp.float32),
        in_specs=[vmem()] * len(near),
        out_specs=vmem(),
        compiler_params=pltpu.CompilerParams(vmem_limit_bytes=2 * 2**20),
        name="stack",
    )(*in_vmem(*near))
    sent = exchange(held, 1)
    gathered = held.shape[0] - examples
    own_tiles = pl.pallas_call(
        functools.partial(gram_kernel, gathered),
        out_shape=pltpu.VMEM((sketch, padded), jnp.float32),
        in_specs=[vmem()],
        out_specs=vmem(),
        compiler_params=pltpu.CompilerParams(vmem_limit_bytes=8 * 2**20),
        cost_estimate=pl.CostEstimate(
            flops=6 * gathered * padded * padded, bytes_accessed=0, transcendentals=0
        ),
        name="gram",
    )(*in_vmem(held))
    return pl.pallas_call(
        functools.partial(factor_kernel, parts, gathered),
        out_shape=[
            jax.ShapeDtypeStruct((examples // parts, rank * sketch), jnp.float32),
            jax.ShapeDtypeStruct((per, sketch, sketch), jnp.float32),
        ],
        in_specs=[smem()] + [vmem()] * 2,
        out_specs=[vmem()] * 2,
        compiler_params=pltpu.CompilerParams(vmem_limit_bytes=8 * 2**20),
        name="factors",
    )(damping, *in_vmem(own_tiles, sent))


def solution(mesh):
    in_specs = (
        P("mp", "ex", None),
        P("mp", "ex", None),
        P("mp", None, None),
        P("mp", None, None),
        P("mp", None, None),
        P("mp", None, None),
        P("mp", "ex", None),
        P(),
    )
    out_specs = (P(("ex", "mp"), None), P("mp", None, None))
    return jax.shard_map(
        local, mesh=mesh, in_specs=in_specs, out_specs=out_specs, check_vma=False
    )
```

```python
import functools
import math

import jax
import jax.numpy as jnp
from jax import lax
from jax.experimental import pallas as pl
from jax.experimental.pallas import tpu as pltpu
from jax.sharding import PartitionSpec as P

EXAMPLE_LENGTH = 8
LANES = 128
SLOT = 32
GROUP = LANES // SLOT
PANEL = 8
CHUNK = 1024


def dot_nt(a, b):
    return lax.dot_general(
        a, b, (((1,), (1,)), ((), ())), preferred_element_type=jnp.float32
    )


def dot_nn(a, b):
    return jnp.dot(a, b, preferred_element_type=jnp.float32)


def split(x):
    high = x.astype(jnp.bfloat16)
    return high, (x - high.astype(jnp.float32)).astype(jnp.bfloat16)


def partial_kernel(
    parts,
    scaling,
    acts_hbm,
    grads_hbm,
    down_hbm,
    up_hbm,
    proj_in_hbm,
    proj_out_hbm,
    order_hbm,
    *refs,
):
    sends, refs = refs[:parts], refs[parts:]
    acts, grads, weights_in, weights_out, order, low, mask, out, sems, order_sem = refs
    tokens, width = acts.shape
    rank = down_hbm.shape[1]
    sketch = proj_in_hbm.shape[1]
    examples = tokens // EXAMPLE_LENGTH
    per = rank // parts
    halves = sketch // SLOT

    def copies(source, target, sem, start, size):
        return pltpu.make_async_copy(
            source.at[0, :, pl.ds(start, size)],
            target.at[:, pl.ds(start, size)],
            sem,
        )

    order_copy = pltpu.make_async_copy(order_hbm.at[0], order, order_sem)
    order_copy.start()
    sources = [
        (grads_hbm, grads, proj_out_hbm, up_hbm, weights_out),
        (acts_hbm, acts, proj_in_hbm, down_hbm, weights_in),
    ]
    pending = []
    for data_hbm, data, first_hbm, second_hbm, weights in sources:
        for start in range(0, data.shape[1], CHUNK):
            n = len(pending)
            pending.append(
                [
                    copies(first_hbm, weights.at[pl.ds(0, sketch)], sems.at[n, 0], start, CHUNK),
                    copies(second_hbm, weights.at[pl.ds(sketch, rank)], sems.at[n, 1], start, CHUNK),
                    copies(data_hbm, data, sems.at[n, 2], start, CHUNK),
                ]
            )
            for copy in pending[-1]:
                copy.start()

    order_copy.wait()
    rows = examples * parts
    source = lax.broadcasted_iota(jnp.int32, (8, tokens), 1) // EXAMPLE_LENGTH
    target = jnp.zeros((8, tokens), jnp.int32)
    for s in range(examples):
        target = jnp.where(source == s, order[0, s], target)
    target = jnp.concatenate([target] * (rows // 8), axis=0)
    place = lax.broadcasted_iota(jnp.int32, (rows, tokens), 0) // parts
    mask[...] = jnp.where(target == place, scaling, 0.0)

    def product(first, data, weights):
        total = None
        for n in range(data.shape[1] // CHUNK):
            for copy in pending[first + n]:
                copy.wait()
            here = pl.ds(n * CHUNK, CHUNK)
            term = dot_nt(weights[:, here], data[:, here])
            total = term if total is None else total + term
        return total

    def spread_low(values, n):
        low[n] = values
        tiles = []
        for c in range(per):
            chosen = low[n, pl.ds(c, parts, stride=per), :]
            chosen = jnp.concatenate([chosen] * max(1, 8 // parts), axis=0)
            chosen = jnp.concatenate([chosen] * (rows // chosen.shape[0]), axis=0)
            tiles.append(split(chosen * mask[...]))
        return [jnp.concatenate(half, axis=0) for half in zip(*tiles)]

    def spread_sketch(values):
        return split(
            jnp.concatenate(
                [values[h * SLOT : (h + 1) * SLOT] for h in range(halves) for _ in range(per)],
                axis=0,
            )
        )

    from_grads = product(0, grads, weights_out)
    left_grads = spread_low(from_grads[sketch:], 0)
    right_grads = spread_sketch(from_grads[:sketch])
    from_acts = product(grads.shape[1] // CHUNK, acts, weights_in)
    left_acts = spread_low(from_acts[sketch:], 1)
    right_acts = spread_sketch(from_acts[:sketch])
    left_high, left_low = [
        jnp.concatenate(pair, axis=1) for pair in zip(left_grads, left_acts)
    ]
    right_high, right_low = [
        jnp.concatenate(pair, axis=1) for pair in zip(right_acts, right_grads)
    ]
    both = dot_nt(jnp.concatenate([left_high, left_low], axis=0), right_high)
    size = left_high.shape[0]
    spread = (dot_nt(left_high, right_low) + both[size:]) + both[:size]
    column = lax.broadcasted_iota(jnp.int32, (rows, per * sketch), 1)
    channel = (column // SLOT) % per
    total = spread[:rows]
    for c in range(1, per):
        total = jnp.where(channel == c, spread[c * rows : (c + 1) * rows], total)
    me = lax.axis_index("mp")
    for start in range(0, per * sketch, LANES):
        stop = min(start + LANES, per * sketch)
        out[:, : stop - start] = total[:, start:stop]
        for d in range(parts):
            g = me ^ d
            sends[d][:examples, start:stop] = out[
                pl.ds(pl.multiple_of(g * examples, examples), examples), : stop - start
            ]
            sends[d][examples:, start:stop] = out[pl.ds(g, examples, stride=parts), :][
                :, : stop - start
            ]


def sum_kernel(*refs):
    chunks, (columns, feature_rows) = refs[:-2], refs[-2:]
    examples, padded = columns.shape
    total = chunks[0][...]
    for chunk in chunks[1:]:
        total = total + chunk[...]
    width = total.shape[1]
    for ref, value in ((feature_rows, total[:examples]), (columns, total[examples:])):
        ref[:, :width] = value
        if padded > width:
            ref[:, width:] = jnp.zeros((examples, padded - width), jnp.float32)


def stack_kernel(*refs):
    rows = refs[0].shape[0]
    for n, part in enumerate(refs[:-1]):
        refs[-1][n * rows : (n + 1) * rows, :] = part[...]


def write_features(total, parts, per, features):
    rows_here, width = features.shape
    span = width // parts
    halves = span // (per * SLOT)
    natural = jnp.concatenate(
        [
            total[:, (h * per + c) * SLOT : (h * per + c + 1) * SLOT]
            for c in range(per)
            for h in range(halves)
        ],
        axis=1,
    )
    for r in range(rows_here):
        features[r : r + 1, :] = jnp.concatenate(
            [natural[r * parts + g : r * parts + g + 1, :] for g in range(parts)], axis=1
        )


def pick_lanes(x, index):
    return jnp.take_along_axis(x, index, axis=1)


def reciprocal(x):
    guess = pl.reciprocal(x, approx=True)
    return guess * (2.0 - x * guess)


def factor_kernel(parts, damping, held, sent, features, factors):
    channels, sketch, _ = factors.shape
    examples = features.shape[0] * parts
    gathered = held.shape[0] - examples
    span = features.shape[1] // parts
    write_features(sent[gathered:, :span], parts, channels, features)
    halves = sketch // SLOT
    panels = sketch // PANEL
    per_half = SLOT // PANEL
    stacked = jnp.concatenate([held[:gathered, :], sent[:gathered, :]], axis=0)
    high, rest = split(stacked)
    turned_high, turned_rest = split(jnp.transpose(stacked))
    gram = dot_nn(turned_high, rest) + dot_nn(
        jnp.concatenate([turned_rest, turned_high], axis=1),
        jnp.concatenate([high, high], axis=0),
    )
    lane = lax.broadcasted_iota(jnp.int32, (PANEL, LANES), 1)
    sub = lax.broadcasted_iota(jnp.int32, (PANEL, LANES), 0)
    slot = lane // SLOT
    within = lane % SLOT
    ridge = damping[0]
    tile = []
    for q in range(panels):
        hr, at = divmod(q, per_half)
        line = []
        for h in range(halves):
            value = None
            for c in range(GROUP):
                start = hr * LANES + c * SLOT + at * PANEL
                block = gram[start : start + PANEL, h * LANES : (h + 1) * LANES]
                value = block if c == 0 else jnp.where(slot == c, block, value)
            value = value * (1.0 / stacked.shape[0])
            if h == hr:
                value = value + jnp.where(within == at * PANEL + sub, ridge, 0.0)
            line.append(value)
        tile.append(line)

    zero = jnp.zeros((PANEL, LANES), jnp.float32)
    finished = []
    ahead = [pick_lanes(tile[0][0], slot * SLOT + r) for r in range(PANEL)]
    for q in range(panels):
        hq, at = divmod(q, per_half)
        if q + 1 < panels:
            hn, an = divmod(q + 1, per_half)
            behind = [
                pick_lanes(tile[q + 1][hn], slot * SLOT + an * PANEL + r)
                for r in range(PANEL)
            ]
        column = [
            {
                j: ahead[r]
                if j == q
                else pick_lanes(tile[j][hq], slot * SLOT + at * PANEL + r)
                for j in range(q, min(q + 3, panels))
            }
            for r in range(PANEL)
        ]
        block = [
            [
                jnp.broadcast_to(column[r][q][s : s + 1, :], (PANEL, LANES))
                if s >= r
                else None
                for s in range(PANEL)
            ]
            for r in range(PANEL)
        ]
        line = [
            [
                jnp.broadcast_to(tile[q][h][r : r + 1, :], (PANEL, LANES))
                if h >= hq
                else None
                for h in range(halves)
            ]
            for r in range(PANEL)
        ]
        inverse = []
        ratios = {}

        def eliminate(r, s, inv):
            ratio = ratios[r, s] = block[r][s] * inv
            for t in range(s, PANEL):
                block[s][t] = block[s][t] - ratio * block[r][t]
            for j in range(q + 1, min(q + 3, panels)):
                column[s][j] = column[s][j] - ratio * column[r][j]
            for h in range(hq, halves):
                line[s][h] = line[s][h] - ratio * line[r][h]

        for r in range(0, PANEL, 2):
            pivot = block[r][r]
            minor = pivot * block[r + 1][r + 1] - block[r][r + 1] * block[r][r + 1]
            inverse.append(reciprocal(pivot))
            inverse.append(pivot * reciprocal(minor))
            eliminate(r, r + 1, inverse[r])
            for s in range(r + 2, PANEL):
                eliminate(r, s, inverse[r])
                eliminate(r + 1, s, inverse[r + 1])
        result = []
        for h in range(halves):
            if h < hq:
                result.append(zero)
                continue
            value = zero
            for r in range(PANEL):
                value = jnp.where(sub == r, line[r][h] * lax.rsqrt(block[r][r]), value)
            if h == hq:
                value = jnp.where(within >= at * PANEL + sub, value, 0.0)
            result.append(value)
        finished.append(result)
        far = range(q + 3, panels)
        if far:
            raw = [tile[j][hq] for j in far] + [zero] * (len(far) % 2)
            raw_high, raw_low = split(jnp.concatenate(raw, axis=0))
            raw_both = jnp.concatenate([raw_high, raw_low], axis=0)
            for h in range((q + 1) // per_half, halves):
                solved = [None] * PANEL
                packed = zero
                for r in reversed(range(PANEL)):
                    value = line[r][h] * inverse[r]
                    for s in range(r + 1, PANEL):
                        value = value - ratios[r, s] * solved[s]
                    solved[r] = value
                    packed = jnp.where(sub == r, value, packed)
                right_high, right_low = split(
                    jnp.concatenate(
                        [
                            jnp.where(slot == c, packed, 0.0) if a == at else zero
                            for c in range(GROUP)
                            for a in range(per_half)
                        ],
                        axis=0,
                    )
                )
                both = dot_nn(raw_both, right_high)
                size = raw_high.shape[0]
                change = (dot_nn(raw_high, right_low) + both[size:]) + both[:size]
                for n, j in enumerate(far):
                    tile[j][h] = tile[j][h] - change[n * PANEL : (n + 1) * PANEL]
        for j in range(q + 1, min(q + 3, panels)):
            weights = [column[r][j] * inverse[r] for r in range(PANEL)]
            if j == q + 1:
                ahead = behind
                for r in range(PANEL):
                    for s in range(PANEL):
                        factor = jnp.broadcast_to(
                            column[r][j][s : s + 1, :], (PANEL, LANES)
                        )
                        ahead[s] = ahead[s] - weights[r] * factor
            for h in range((q + 1) // per_half, halves):
                value = tile[j][h]
                for r in range(PANEL):
                    value = value - weights[r] * line[r][h]
                tile[j][h] = value

    for q in range(panels):
        for c in range(channels):
            factors[c, q * PANEL : (q + 1) * PANEL, :] = jnp.concatenate(
                [finished[q][h][:, c * SLOT : (c + 1) * SLOT] for h in range(halves)],
                axis=1,
            )


def exchange(x, ex_distance, mp_distance=0):
    shards, parts = lax.axis_size("ex"), lax.axis_size("mp")
    return lax.ppermute(
        x,
        ("ex", "mp"),
        [
            (m * parts + b, (m ^ ex_distance) * parts + (b ^ mp_distance))
            for m in range(shards)
            for b in range(parts)
        ],
    )


def vmem():
    return pl.BlockSpec(memory_space=pltpu.VMEM)


def hbm():
    return pl.BlockSpec(memory_space=pltpu.HBM)


def in_hbm(*arrays):
    return [pltpu.with_memory_space_constraint(x, pltpu.HBM) for x in arrays]


def in_vmem(*arrays):
    return [pltpu.with_memory_space_constraint(x, pltpu.VMEM) for x in arrays]


def smem():
    return pl.BlockSpec(memory_space=pltpu.SMEM)


def local(
    acts,
    grads,
    down_factor,
    up_factor_transposed,
    input_projection,
    gradient_projection,
    order,
    damping,
):
    parts = lax.axis_size("mp")
    shards = lax.axis_size("ex")
    tokens, width = acts.shape[1:]
    key_width = grads.shape[2]
    rank = down_factor.shape[1]
    sketch = input_projection.shape[1]
    examples = tokens // EXAMPLE_LENGTH
    per = rank // parts
    span = per * sketch
    scaling = 1.0 / math.sqrt(2.0 * EXAMPLE_LENGTH * parts)
    sends = pl.pallas_call(
        functools.partial(partial_kernel, parts, scaling),
        out_shape=[pltpu.VMEM((2 * examples, span), jnp.float32)] * parts,
        in_specs=[hbm()] * 7,
        out_specs=[vmem()] * parts,
        scratch_shapes=[
            pltpu.VMEM((tokens, width), acts.dtype),
            pltpu.VMEM((tokens, key_width), grads.dtype),
            pltpu.VMEM((sketch + rank, width), acts.dtype),
            pltpu.VMEM((sketch + rank, key_width), grads.dtype),
            pltpu.SMEM(order.shape[1:], order.dtype),
            pltpu.VMEM((2, rank, tokens), jnp.float32),
            pltpu.VMEM((examples * parts, tokens), jnp.float32),
            pltpu.VMEM((examples * parts, LANES), jnp.float32),
            pltpu.SemaphoreType.DMA(((width + key_width) // CHUNK, 3)),
            pltpu.SemaphoreType.DMA,
        ],
        compiler_params=pltpu.CompilerParams(vmem_limit_bytes=8 * 2**20),
        name="partials",
    )(
        *in_hbm(
            acts,
            grads,
            down_factor,
            up_factor_transposed,
            input_projection,
            gradient_projection,
            order,
        )
    )
    chunks = [exchange(sends[d], 1, d) for d in range(parts - 1, -1, -1)]
    padded = max(span, GROUP * sketch)
    columns, feature_rows = pl.pallas_call(
        sum_kernel,
        out_shape=[pltpu.VMEM((examples, padded), jnp.float32)] * 2,
        in_specs=[vmem()] * parts,
        out_specs=[vmem()] * 2,
        compiler_params=pltpu.CompilerParams(vmem_limit_bytes=2 * 2**20),
        name="sums",
    )(*in_vmem(*chunks))
    near = [columns] + [exchange(columns, d) for d in range(3, shards, 2)] + [feature_rows]
    held = pl.pallas_call(
        stack_kernel,
        out_shape=pltpu.VMEM((len(near) * examples, padded), jnp.float32),
        in_specs=[vmem()] * len(near),
        out_specs=vmem(),
        compiler_params=pltpu.CompilerParams(vmem_limit_bytes=2 * 2**20),
        name="stack",
    )(*in_vmem(*near))
    sent = exchange(held, 1)
    return pl.pallas_call(
        functools.partial(factor_kernel, parts),
        out_shape=[
            jax.ShapeDtypeStruct((examples // parts, rank * sketch), jnp.float32),
            jax.ShapeDtypeStruct((per, sketch, sketch), jnp.float32),
        ],
        in_specs=[smem()] + [vmem()] * 2,
        out_specs=[vmem()] * 2,
        compiler_params=pltpu.CompilerParams(vmem_limit_bytes=8 * 2**20),
        name="factors",
    )(damping, *in_vmem(held, sent))


def solution(mesh):
    in_specs = (
        P("mp", "ex", None),
        P("mp", "ex", None),
        P("mp", None, None),
        P("mp", None, None),
        P("mp", None, None),
        P("mp", None, None),
        P("mp", "ex", None),
        P(),
    )
    out_specs = (P(("ex", "mp"), None), P("mp", None, None))
    return jax.shard_map(
        local, mesh=mesh, in_specs=in_specs, out_specs=out_specs, check_vma=False
    )
```

```python
import functools
import math

import jax
import jax.numpy as jnp
from jax import lax
from jax.experimental import pallas as pl
from jax.experimental.pallas import tpu as pltpu
from jax.sharding import PartitionSpec as P

EXAMPLE_LENGTH = 8
LANES = 128
SLOT = 32
GROUP = LANES // SLOT
PANEL = 8
CHUNK = 1024


def dot_nt(a, b):
    return lax.dot_general(
        a, b, (((1,), (1,)), ((), ())), preferred_element_type=jnp.float32
    )


def dot_nn(a, b):
    return jnp.dot(a, b, preferred_element_type=jnp.float32)


def split(x):
    high = x.astype(jnp.bfloat16)
    return high, (x - high.astype(jnp.float32)).astype(jnp.bfloat16)


def partial_kernel(
    parts,
    scaling,
    acts_hbm,
    grads_hbm,
    down_hbm,
    up_hbm,
    proj_in_hbm,
    proj_out_hbm,
    order_hbm,
    *refs,
):
    sends, refs = refs[:parts], refs[parts:]
    acts, grads, weights_in, weights_out, order, low, mask, out, sems, order_sem = refs
    tokens, width = acts.shape
    rank = down_hbm.shape[1]
    sketch = proj_in_hbm.shape[1]
    examples = tokens // EXAMPLE_LENGTH
    per = rank // parts
    halves = sketch // SLOT

    def copies(source, target, sem, start, size):
        return pltpu.make_async_copy(
            source.at[0, :, pl.ds(start, size)],
            target.at[:, pl.ds(start, size)],
            sem,
        )

    order_copy = pltpu.make_async_copy(order_hbm.at[0], order, order_sem)
    order_copy.start()
    sources = [
        (grads_hbm, grads, proj_out_hbm, up_hbm, weights_out),
        (acts_hbm, acts, proj_in_hbm, down_hbm, weights_in),
    ]
    pending = []
    for data_hbm, data, first_hbm, second_hbm, weights in sources:
        for start in range(0, data.shape[1], CHUNK):
            n = len(pending)
            pending.append(
                [
                    copies(first_hbm, weights.at[pl.ds(0, sketch)], sems.at[n, 0], start, CHUNK),
                    copies(second_hbm, weights.at[pl.ds(sketch, rank)], sems.at[n, 1], start, CHUNK),
                    copies(data_hbm, data, sems.at[n, 2], start, CHUNK),
                ]
            )
            for copy in pending[-1]:
                copy.start()

    order_copy.wait()
    rows = examples * parts
    source = lax.broadcasted_iota(jnp.int32, (8, tokens), 1) // EXAMPLE_LENGTH
    target = jnp.zeros((8, tokens), jnp.int32)
    for s in range(examples):
        target = jnp.where(source == s, order[0, s], target)
    target = jnp.concatenate([target] * (rows // 8), axis=0)
    place = lax.broadcasted_iota(jnp.int32, (rows, tokens), 0) // parts
    mask[...] = jnp.where(target == place, scaling, 0.0)

    def product(first, data, weights):
        total = None
        for n in range(data.shape[1] // CHUNK):
            for copy in pending[first + n]:
                copy.wait()
            here = pl.ds(n * CHUNK, CHUNK)
            term = dot_nt(weights[:, here], data[:, here])
            total = term if total is None else total + term
        return total

    def spread_low(values, n):
        low[n] = values
        tiles = []
        for c in range(per):
            chosen = low[n, pl.ds(c, parts, stride=per), :]
            chosen = jnp.concatenate([chosen] * max(1, 8 // parts), axis=0)
            chosen = jnp.concatenate([chosen] * (rows // chosen.shape[0]), axis=0)
            tiles.append(split(chosen * mask[...]))
        return [jnp.concatenate(half, axis=0) for half in zip(*tiles)]

    def spread_sketch(values):
        return split(
            jnp.concatenate(
                [values[h * SLOT : (h + 1) * SLOT] for h in range(halves) for _ in range(per)],
                axis=0,
            )
        )

    from_grads = product(0, grads, weights_out)
    left_grads = spread_low(from_grads[sketch:], 0)
    right_grads = spread_sketch(from_grads[:sketch])
    from_acts = product(grads.shape[1] // CHUNK, acts, weights_in)
    left_acts = spread_low(from_acts[sketch:], 1)
    right_acts = spread_sketch(from_acts[:sketch])
    left_high, left_low = [
        jnp.concatenate(pair, axis=1) for pair in zip(left_grads, left_acts)
    ]
    right_high, right_low = [
        jnp.concatenate(pair, axis=1) for pair in zip(right_acts, right_grads)
    ]
    both = dot_nt(jnp.concatenate([left_high, left_low], axis=0), right_high)
    size = left_high.shape[0]
    spread = (dot_nt(left_high, right_low) + both[size:]) + both[:size]
    column = lax.broadcasted_iota(jnp.int32, (rows, per * sketch), 1)
    channel = (column // SLOT) % per
    total = spread[:rows]
    for c in range(1, per):
        total = jnp.where(channel == c, spread[c * rows : (c + 1) * rows], total)
    me = lax.axis_index("mp")
    for start in range(0, per * sketch, LANES):
        stop = min(start + LANES, per * sketch)
        out[:, : stop - start] = total[:, start:stop]
        for d in range(parts):
            g = me ^ d
            sends[d][:examples, start:stop] = out[
                pl.ds(pl.multiple_of(g * examples, examples), examples), : stop - start
            ]
            sends[d][examples:, start:stop] = out[pl.ds(g, examples, stride=parts), :][
                :, : stop - start
            ]


def sum_kernel(*refs):
    chunks, (columns, feature_rows) = refs[:-2], refs[-2:]
    examples, padded = columns.shape
    total = chunks[0][...]
    for chunk in chunks[1:]:
        total = total + chunk[...]
    width = total.shape[1]
    for ref, value in ((feature_rows, total[:examples]), (columns, total[examples:])):
        ref[:, :width] = value
        if padded > width:
            ref[:, width:] = jnp.zeros((examples, padded - width), jnp.float32)


def stack_kernel(*refs):
    rows = refs[0].shape[0]
    for n, part in enumerate(refs[:-1]):
        refs[-1][n * rows : (n + 1) * rows, :] = part[...]


def write_features(total, parts, per, features):
    rows_here, width = features.shape
    span = width // parts
    halves = span // (per * SLOT)
    natural = jnp.concatenate(
        [
            total[:, (h * per + c) * SLOT : (h * per + c + 1) * SLOT]
            for c in range(per)
            for h in range(halves)
        ],
        axis=1,
    )
    for r in range(rows_here):
        features[r : r + 1, :] = jnp.concatenate(
            [natural[r * parts + g : r * parts + g + 1, :] for g in range(parts)], axis=1
        )


def pick_lanes(x, index):
    return jnp.take_along_axis(x, index, axis=1)


def reciprocal(x):
    guess = pl.reciprocal(x, approx=True)
    return guess * (2.0 - x * guess)


def factor_kernel(parts, damping, held, sent, features, factors):
    channels, sketch, _ = factors.shape
    examples = features.shape[0] * parts
    gathered = held.shape[0] - examples
    span = features.shape[1] // parts
    write_features(sent[gathered:, :span], parts, channels, features)
    halves = sketch // SLOT
    panels = sketch // PANEL
    per_half = SLOT // PANEL
    stacked = jnp.concatenate([held[:gathered, :], sent[:gathered, :]], axis=0)
    high, rest = split(stacked)
    turned_high, turned_rest = split(jnp.transpose(stacked))
    gram = dot_nn(turned_high, rest) + dot_nn(
        jnp.concatenate([turned_rest, turned_high], axis=1),
        jnp.concatenate([high, high], axis=0),
    )
    lane = lax.broadcasted_iota(jnp.int32, (PANEL, LANES), 1)
    sub = lax.broadcasted_iota(jnp.int32, (PANEL, LANES), 0)
    slot = lane // SLOT
    within = lane % SLOT
    ridge = damping[0]
    tile = []
    for q in range(panels):
        hr, at = divmod(q, per_half)
        line = []
        for h in range(halves):
            value = None
            for c in range(GROUP):
                start = hr * LANES + c * SLOT + at * PANEL
                block = gram[start : start + PANEL, h * LANES : (h + 1) * LANES]
                value = block if c == 0 else jnp.where(slot == c, block, value)
            value = value * (1.0 / stacked.shape[0])
            if h == hr:
                value = value + jnp.where(within == at * PANEL + sub, ridge, 0.0)
            line.append(value)
        tile.append(line)

    zero = jnp.zeros((PANEL, LANES), jnp.float32)
    finished = []
    ahead = [pick_lanes(tile[0][0], slot * SLOT + r) for r in range(PANEL)]
    for q in range(panels):
        hq, at = divmod(q, per_half)
        if q + 1 < panels:
            hn, an = divmod(q + 1, per_half)
            behind = [
                pick_lanes(tile[q + 1][hn], slot * SLOT + an * PANEL + r)
                for r in range(PANEL)
            ]
        column = [
            {
                j: ahead[r]
                if j == q
                else pick_lanes(tile[j][hq], slot * SLOT + at * PANEL + r)
                for j in range(q, panels)
            }
            for r in range(PANEL)
        ]
        block = [
            [
                jnp.broadcast_to(column[r][q][s : s + 1, :], (PANEL, LANES))
                if s >= r
                else None
                for s in range(PANEL)
            ]
            for r in range(PANEL)
        ]
        line = [
            [
                jnp.broadcast_to(tile[q][h][r : r + 1, :], (PANEL, LANES))
                if h >= hq
                else None
                for h in range(halves)
            ]
            for r in range(PANEL)
        ]
        inverse = []

        def eliminate(r, s, inv):
            ratio = block[r][s] * inv
            for t in range(s, PANEL):
                block[s][t] = block[s][t] - ratio * block[r][t]
            for j in range(q + 1, panels):
                column[s][j] = column[s][j] - ratio * column[r][j]
            for h in range(hq, halves):
                line[s][h] = line[s][h] - ratio * line[r][h]

        for r in range(0, PANEL, 2):
            pivot = block[r][r]
            minor = pivot * block[r + 1][r + 1] - block[r][r + 1] * block[r][r + 1]
            inverse.append(reciprocal(pivot))
            inverse.append(pivot * reciprocal(minor))
            eliminate(r, r + 1, inverse[r])
            for s in range(r + 2, PANEL):
                eliminate(r, s, inverse[r])
                eliminate(r + 1, s, inverse[r + 1])
        result = []
        for h in range(halves):
            if h < hq:
                result.append(zero)
                continue
            value = zero
            for r in range(PANEL):
                value = jnp.where(sub == r, line[r][h] * lax.rsqrt(block[r][r]), value)
            if h == hq:
                value = jnp.where(within >= at * PANEL + sub, value, 0.0)
            result.append(value)
        finished.append(result)
        for j in range(q + 1, panels):
            weights = [column[r][j] * inverse[r] for r in range(PANEL)]
            if j == q + 1:
                ahead = behind
                for r in range(PANEL):
                    for s in range(PANEL):
                        factor = jnp.broadcast_to(
                            column[r][j][s : s + 1, :], (PANEL, LANES)
                        )
                        ahead[s] = ahead[s] - weights[r] * factor
            for h in range((q + 1) // per_half, halves):
                value = tile[j][h]
                for r in range(PANEL):
                    value = value - weights[r] * line[r][h]
                tile[j][h] = value

    for q in range(panels):
        for c in range(channels):
            factors[c, q * PANEL : (q + 1) * PANEL, :] = jnp.concatenate(
                [finished[q][h][:, c * SLOT : (c + 1) * SLOT] for h in range(halves)],
                axis=1,
            )


def permute(x, source):
    shards, parts = lax.axis_size("ex"), lax.axis_size("mp")
    pairs = []
    for m in range(shards):
        for b in range(parts):
            sm, sb = source(m, b)
            pairs.append((sm * parts + sb, m * parts + b))
    return lax.ppermute(x, ("ex", "mp"), sorted(pairs))


def exchange(x, ex_distance, mp_distance=0):
    return permute(x, lambda m, b: (m ^ ex_distance, b ^ mp_distance))


def shift_chips(x, distance):
    shards = lax.axis_size("ex")
    return permute(x, lambda m, b: ((m - 2 * distance) % shards ^ 1, b))


def vmem():
    return pl.BlockSpec(memory_space=pltpu.VMEM)


def hbm():
    return pl.BlockSpec(memory_space=pltpu.HBM)


def in_hbm(*arrays):
    return [pltpu.with_memory_space_constraint(x, pltpu.HBM) for x in arrays]


def in_vmem(*arrays):
    return [pltpu.with_memory_space_constraint(x, pltpu.VMEM) for x in arrays]


def smem():
    return pl.BlockSpec(memory_space=pltpu.SMEM)


def local(
    acts,
    grads,
    down_factor,
    up_factor_transposed,
    input_projection,
    gradient_projection,
    order,
    damping,
):
    parts = lax.axis_size("mp")
    shards = lax.axis_size("ex")
    tokens, width = acts.shape[1:]
    key_width = grads.shape[2]
    rank = down_factor.shape[1]
    sketch = input_projection.shape[1]
    examples = tokens // EXAMPLE_LENGTH
    per = rank // parts
    span = per * sketch
    scaling = 1.0 / math.sqrt(2.0 * EXAMPLE_LENGTH * parts)
    sends = pl.pallas_call(
        functools.partial(partial_kernel, parts, scaling),
        out_shape=[pltpu.VMEM((2 * examples, span), jnp.float32)] * parts,
        in_specs=[hbm()] * 7,
        out_specs=[vmem()] * parts,
        scratch_shapes=[
            pltpu.VMEM((tokens, width), acts.dtype),
            pltpu.VMEM((tokens, key_width), grads.dtype),
            pltpu.VMEM((sketch + rank, width), acts.dtype),
            pltpu.VMEM((sketch + rank, key_width), grads.dtype),
            pltpu.SMEM(order.shape[1:], order.dtype),
            pltpu.VMEM((2, rank, tokens), jnp.float32),
            pltpu.VMEM((examples * parts, tokens), jnp.float32),
            pltpu.VMEM((examples * parts, LANES), jnp.float32),
            pltpu.SemaphoreType.DMA(((width + key_width) // CHUNK, 3)),
            pltpu.SemaphoreType.DMA,
        ],
        compiler_params=pltpu.CompilerParams(vmem_limit_bytes=8 * 2**20),
        name="partials",
    )(
        *in_hbm(
            acts,
            grads,
            down_factor,
            up_factor_transposed,
            input_projection,
            gradient_projection,
            order,
        )
    )
    chunks = [exchange(sends[d], 1, d) for d in range(parts - 1, -1, -1)]
    padded = max(span, GROUP * sketch)
    columns, feature_rows = pl.pallas_call(
        sum_kernel,
        out_shape=[pltpu.VMEM((examples, padded), jnp.float32)] * 2,
        in_specs=[vmem()] * parts,
        out_specs=[vmem()] * 2,
        compiler_params=pltpu.CompilerParams(vmem_limit_bytes=2 * 2**20),
        name="sums",
    )(*in_vmem(*chunks))
    shifts = sorted(range(1, shards // 2), key=lambda d: (-min(d, shards // 2 - d), -d))
    near = [columns] + [shift_chips(columns, d) for d in shifts] + [feature_rows]
    held = pl.pallas_call(
        stack_kernel,
        out_shape=pltpu.VMEM((len(near) * examples, padded), jnp.float32),
        in_specs=[vmem()] * len(near),
        out_specs=vmem(),
        compiler_params=pltpu.CompilerParams(vmem_limit_bytes=2 * 2**20),
        name="stack",
    )(*in_vmem(*near))
    sent = exchange(held, 1)
    return pl.pallas_call(
        functools.partial(factor_kernel, parts),
        out_shape=[
            jax.ShapeDtypeStruct((examples // parts, rank * sketch), jnp.float32),
            jax.ShapeDtypeStruct((per, sketch, sketch), jnp.float32),
        ],
        in_specs=[smem()] + [vmem()] * 2,
        out_specs=[vmem()] * 2,
        compiler_params=pltpu.CompilerParams(vmem_limit_bytes=8 * 2**20),
        name="factors",
    )(damping, *in_vmem(held, sent))


def solution(mesh):
    in_specs = (
        P("mp", "ex", None),
        P("mp", "ex", None),
        P("mp", None, None),
        P("mp", None, None),
        P("mp", None, None),
        P("mp", None, None),
        P("mp", "ex", None),
        P(),
    )
    out_specs = (P(("ex", "mp"), None), P("mp", None, None))
    return jax.shard_map(
        local, mesh=mesh, in_specs=in_specs, out_specs=out_specs, check_vma=False
    )
```

```python
import functools
import math

import jax
import jax.numpy as jnp
from jax import lax
from jax.experimental import pallas as pl
from jax.experimental.pallas import tpu as pltpu
from jax.sharding import PartitionSpec as P

EXAMPLE_LENGTH = 8
LANES = 128
SLOT = 32
GROUP = LANES // SLOT
PANEL = 8
CHUNK = 1024


def dot_nt(a, b):
    return lax.dot_general(
        a, b, (((1,), (1,)), ((), ())), preferred_element_type=jnp.float32
    )


def dot_nn(a, b):
    return jnp.dot(a, b, preferred_element_type=jnp.float32)


def split(x):
    high = x.astype(jnp.bfloat16)
    return high, (x - high.astype(jnp.float32)).astype(jnp.bfloat16)


def partial_kernel(
    parts,
    scaling,
    acts_hbm,
    grads_hbm,
    down_hbm,
    up_hbm,
    proj_in_hbm,
    proj_out_hbm,
    order_hbm,
    *refs,
):
    sends, refs = refs[:parts], refs[parts:]
    acts, grads, weights_in, weights_out, order, low, mask, out, sems, order_sem = refs
    tokens, width = acts.shape
    rank = down_hbm.shape[1]
    sketch = proj_in_hbm.shape[1]
    examples = tokens // EXAMPLE_LENGTH
    per = rank // parts
    halves = sketch // SLOT

    def copies(source, target, sem, start, size):
        return pltpu.make_async_copy(
            source.at[0, :, pl.ds(start, size)],
            target.at[:, pl.ds(start, size)],
            sem,
        )

    order_copy = pltpu.make_async_copy(order_hbm.at[0], order, order_sem)
    order_copy.start()
    sources = [
        (grads_hbm, grads, proj_out_hbm, up_hbm, weights_out),
        (acts_hbm, acts, proj_in_hbm, down_hbm, weights_in),
    ]
    pending = []
    for data_hbm, data, first_hbm, second_hbm, weights in sources:
        for start in range(0, data.shape[1], CHUNK):
            n = len(pending)
            pending.append(
                [
                    copies(first_hbm, weights.at[pl.ds(0, sketch)], sems.at[n, 0], start, CHUNK),
                    copies(second_hbm, weights.at[pl.ds(sketch, rank)], sems.at[n, 1], start, CHUNK),
                    copies(data_hbm, data, sems.at[n, 2], start, CHUNK),
                ]
            )
            for copy in pending[-1]:
                copy.start()

    order_copy.wait()
    rows = examples * parts
    source = lax.broadcasted_iota(jnp.int32, (8, tokens), 1) // EXAMPLE_LENGTH
    target = jnp.zeros((8, tokens), jnp.int32)
    for s in range(examples):
        target = jnp.where(source == s, order[0, s], target)
    target = jnp.concatenate([target] * (rows // 8), axis=0)
    place = lax.broadcasted_iota(jnp.int32, (rows, tokens), 0) // parts
    mask[...] = jnp.where(target == place, scaling, 0.0)

    def product(first, data, weights):
        total = None
        for n in range(data.shape[1] // CHUNK):
            for copy in pending[first + n]:
                copy.wait()
            here = pl.ds(n * CHUNK, CHUNK)
            term = dot_nt(weights[:, here], data[:, here])
            total = term if total is None else total + term
        return total

    def spread_low(values, n):
        low[n] = values
        tiles = []
        for c in range(per):
            chosen = low[n, pl.ds(c, parts, stride=per), :]
            chosen = jnp.concatenate([chosen] * max(1, 8 // parts), axis=0)
            chosen = jnp.concatenate([chosen] * (rows // chosen.shape[0]), axis=0)
            tiles.append(split(chosen * mask[...]))
        return [jnp.concatenate(half, axis=0) for half in zip(*tiles)]

    def spread_sketch(values):
        return split(
            jnp.concatenate(
                [values[h * SLOT : (h + 1) * SLOT] for h in range(halves) for _ in range(per)],
                axis=0,
            )
        )

    from_grads = product(0, grads, weights_out)
    left_grads = spread_low(from_grads[sketch:], 0)
    right_grads = spread_sketch(from_grads[:sketch])
    from_acts = product(grads.shape[1] // CHUNK, acts, weights_in)
    left_acts = spread_low(from_acts[sketch:], 1)
    right_acts = spread_sketch(from_acts[:sketch])
    left_high, left_low = [
        jnp.concatenate(pair, axis=1) for pair in zip(left_grads, left_acts)
    ]
    right_high, right_low = [
        jnp.concatenate(pair, axis=1) for pair in zip(right_acts, right_grads)
    ]
    both = dot_nt(jnp.concatenate([left_high, left_low], axis=0), right_high)
    size = left_high.shape[0]
    spread = (dot_nt(left_high, right_low) + both[size:]) + both[:size]
    column = lax.broadcasted_iota(jnp.int32, (rows, per * sketch), 1)
    channel = (column // SLOT) % per
    total = spread[:rows]
    for c in range(1, per):
        total = jnp.where(channel == c, spread[c * rows : (c + 1) * rows], total)
    me = lax.axis_index("mp")
    for start in range(0, per * sketch, LANES):
        stop = min(start + LANES, per * sketch)
        out[:, : stop - start] = total[:, start:stop]
        for d in range(parts):
            g = me ^ d
            sends[d][:examples, start:stop] = out[
                pl.ds(pl.multiple_of(g * examples, examples), examples), : stop - start
            ]
            sends[d][examples:, start:stop] = out[pl.ds(g, examples, stride=parts), :][
                :, : stop - start
            ]


def sum_kernel(*refs):
    chunks, (columns, feature_rows) = refs[:-2], refs[-2:]
    examples, padded = columns.shape
    total = chunks[0][...]
    for chunk in chunks[1:]:
        total = total + chunk[...]
    width = total.shape[1]
    for ref, value in ((feature_rows, total[:examples]), (columns, total[examples:])):
        ref[:, :width] = value
        if padded > width:
            ref[:, width:] = jnp.zeros((examples, padded - width), jnp.float32)


def stack_kernel(*refs):
    rows = refs[0].shape[0]
    for n, part in enumerate(refs[:-1]):
        refs[-1][n * rows : (n + 1) * rows, :] = part[...]


def write_features(total, parts, per, features):
    rows_here, width = features.shape
    span = width // parts
    halves = span // (per * SLOT)
    natural = jnp.concatenate(
        [
            total[:, (h * per + c) * SLOT : (h * per + c + 1) * SLOT]
            for c in range(per)
            for h in range(halves)
        ],
        axis=1,
    )
    for r in range(rows_here):
        features[r : r + 1, :] = jnp.concatenate(
            [natural[r * parts + g : r * parts + g + 1, :] for g in range(parts)], axis=1
        )


def pick_lanes(x, index):
    return jnp.take_along_axis(x, index, axis=1)


def reciprocal(x):
    guess = pl.reciprocal(x, approx=True)
    return guess * (2.0 - x * guess)


def factor_kernel(parts, damping, held, sent, features, factors):
    channels, sketch, _ = factors.shape
    examples = features.shape[0] * parts
    gathered = held.shape[0] - examples
    span = features.shape[1] // parts
    write_features(sent[gathered:, :span], parts, channels, features)
    halves = sketch // SLOT
    panels = sketch // PANEL
    per_half = SLOT // PANEL
    stacked = jnp.concatenate([held[:gathered, :], sent[:gathered, :]], axis=0)
    high, rest = split(stacked)
    turned_high, turned_rest = split(jnp.transpose(stacked))
    gram = dot_nn(turned_high, rest) + dot_nn(
        jnp.concatenate([turned_rest, turned_high], axis=1),
        jnp.concatenate([high, high], axis=0),
    )
    lane = lax.broadcasted_iota(jnp.int32, (PANEL, LANES), 1)
    sub = lax.broadcasted_iota(jnp.int32, (PANEL, LANES), 0)
    slot = lane // SLOT
    within = lane % SLOT
    ridge = damping[0]
    tile = []
    for q in range(panels):
        hr, at = divmod(q, per_half)
        line = []
        for h in range(halves):
            value = None
            for c in range(GROUP):
                start = hr * LANES + c * SLOT + at * PANEL
                block = gram[start : start + PANEL, h * LANES : (h + 1) * LANES]
                value = block if c == 0 else jnp.where(slot == c, block, value)
            value = value * (1.0 / stacked.shape[0])
            if h == hr:
                value = value + jnp.where(within == at * PANEL + sub, ridge, 0.0)
            line.append(value)
        tile.append(line)

    zero = jnp.zeros((PANEL, LANES), jnp.float32)
    finished = []
    ahead = [pick_lanes(tile[0][0], slot * SLOT + r) for r in range(PANEL)]
    for q in range(panels):
        hq, at = divmod(q, per_half)
        if q + 1 < panels:
            hn, an = divmod(q + 1, per_half)
            behind = [
                pick_lanes(tile[q + 1][hn], slot * SLOT + an * PANEL + r)
                for r in range(PANEL)
            ]
        column = [
            {
                j: ahead[r]
                if j == q
                else pick_lanes(tile[j][hq], slot * SLOT + at * PANEL + r)
                for j in range(q, panels)
            }
            for r in range(PANEL)
        ]
        block = [
            [
                jnp.broadcast_to(column[r][q][s : s + 1, :], (PANEL, LANES))
                if s >= r
                else None
                for s in range(PANEL)
            ]
            for r in range(PANEL)
        ]
        line = [
            [
                jnp.broadcast_to(tile[q][h][r : r + 1, :], (PANEL, LANES))
                if h >= hq
                else None
                for h in range(halves)
            ]
            for r in range(PANEL)
        ]
        inverse = []

        def eliminate(r, s, inv):
            ratio = block[r][s] * inv
            for t in range(s, PANEL):
                block[s][t] = block[s][t] - ratio * block[r][t]
            for j in range(q + 1, panels):
                column[s][j] = column[s][j] - ratio * column[r][j]
            for h in range(hq, halves):
                line[s][h] = line[s][h] - ratio * line[r][h]

        for r in range(0, PANEL, 2):
            pivot = block[r][r]
            minor = pivot * block[r + 1][r + 1] - block[r][r + 1] * block[r][r + 1]
            inverse.append(reciprocal(pivot))
            inverse.append(pivot * reciprocal(minor))
            eliminate(r, r + 1, inverse[r])
            for s in range(r + 2, PANEL):
                eliminate(r, s, inverse[r])
                eliminate(r + 1, s, inverse[r + 1])
        result = []
        for h in range(halves):
            if h < hq:
                result.append(zero)
                continue
            value = zero
            for r in range(PANEL):
                value = jnp.where(sub == r, line[r][h] * lax.rsqrt(block[r][r]), value)
            if h == hq:
                value = jnp.where(within >= at * PANEL + sub, value, 0.0)
            result.append(value)
        finished.append(result)
        for j in range(q + 1, panels):
            weights = [column[r][j] * inverse[r] for r in range(PANEL)]
            if j == q + 1:
                ahead = behind
                for r in range(PANEL):
                    for s in range(PANEL):
                        factor = jnp.broadcast_to(
                            column[r][j][s : s + 1, :], (PANEL, LANES)
                        )
                        ahead[s] = ahead[s] - weights[r] * factor
            for h in range((q + 1) // per_half, halves):
                value = tile[j][h]
                for r in range(PANEL):
                    value = value - weights[r] * line[r][h]
                tile[j][h] = value

    for q in range(panels):
        for c in range(channels):
            factors[c, q * PANEL : (q + 1) * PANEL, :] = jnp.concatenate(
                [finished[q][h][:, c * SLOT : (c + 1) * SLOT] for h in range(halves)],
                axis=1,
            )


def permute(x, source):
    shards, parts = lax.axis_size("ex"), lax.axis_size("mp")
    pairs = []
    for m in range(shards):
        for b in range(parts):
            sm, sb = source(m, b)
            pairs.append((sm * parts + sb, m * parts + b))
    return lax.ppermute(x, ("ex", "mp"), sorted(pairs))


def exchange(x, ex_distance, mp_distance=0):
    return permute(x, lambda m, b: (m ^ ex_distance, b ^ mp_distance))


def shift_chips(x, distance):
    chips = lax.axis_size("ex") // 2
    ring = [i ^ i >> 1 for i in range(chips)]
    place = {chip: i for i, chip in enumerate(ring)}

    def source(m, b):
        return 2 * ring[(place[m // 2] - distance) % chips] + (1 - m % 2), b

    return permute(x, source)


def vmem():
    return pl.BlockSpec(memory_space=pltpu.VMEM)


def hbm():
    return pl.BlockSpec(memory_space=pltpu.HBM)


def in_hbm(*arrays):
    return [pltpu.with_memory_space_constraint(x, pltpu.HBM) for x in arrays]


def in_vmem(*arrays):
    return [pltpu.with_memory_space_constraint(x, pltpu.VMEM) for x in arrays]


def smem():
    return pl.BlockSpec(memory_space=pltpu.SMEM)


def local(
    acts,
    grads,
    down_factor,
    up_factor_transposed,
    input_projection,
    gradient_projection,
    order,
    damping,
):
    parts = lax.axis_size("mp")
    shards = lax.axis_size("ex")
    tokens, width = acts.shape[1:]
    key_width = grads.shape[2]
    rank = down_factor.shape[1]
    sketch = input_projection.shape[1]
    examples = tokens // EXAMPLE_LENGTH
    per = rank // parts
    span = per * sketch
    scaling = 1.0 / math.sqrt(2.0 * EXAMPLE_LENGTH * parts)
    sends = pl.pallas_call(
        functools.partial(partial_kernel, parts, scaling),
        out_shape=[pltpu.VMEM((2 * examples, span), jnp.float32)] * parts,
        in_specs=[hbm()] * 7,
        out_specs=[vmem()] * parts,
        scratch_shapes=[
            pltpu.VMEM((tokens, width), acts.dtype),
            pltpu.VMEM((tokens, key_width), grads.dtype),
            pltpu.VMEM((sketch + rank, width), acts.dtype),
            pltpu.VMEM((sketch + rank, key_width), grads.dtype),
            pltpu.SMEM(order.shape[1:], order.dtype),
            pltpu.VMEM((2, rank, tokens), jnp.float32),
            pltpu.VMEM((examples * parts, tokens), jnp.float32),
            pltpu.VMEM((examples * parts, LANES), jnp.float32),
            pltpu.SemaphoreType.DMA(((width + key_width) // CHUNK, 3)),
            pltpu.SemaphoreType.DMA,
        ],
        compiler_params=pltpu.CompilerParams(vmem_limit_bytes=8 * 2**20),
        name="partials",
    )(
        *in_hbm(
            acts,
            grads,
            down_factor,
            up_factor_transposed,
            input_projection,
            gradient_projection,
            order,
        )
    )
    distances = sorted(range(1, parts), key=lambda d: (d < parts // 2, d))
    chunks = [exchange(sends[d], 1, d) for d in [*distances, 0]]
    padded = max(span, GROUP * sketch)
    columns, feature_rows = pl.pallas_call(
        sum_kernel,
        out_shape=[pltpu.VMEM((examples, padded), jnp.float32)] * 2,
        in_specs=[vmem()] * parts,
        out_specs=[vmem()] * 2,
        compiler_params=pltpu.CompilerParams(vmem_limit_bytes=2 * 2**20),
        name="sums",
    )(*in_vmem(*chunks))
    shifts = sorted(range(1, shards // 2), key=lambda d: (-min(d, shards // 2 - d), -d))
    near = [columns] + [shift_chips(columns, d) for d in shifts] + [feature_rows]
    held = pl.pallas_call(
        stack_kernel,
        out_shape=pltpu.VMEM((len(near) * examples, padded), jnp.float32),
        in_specs=[vmem()] * len(near),
        out_specs=vmem(),
        compiler_params=pltpu.CompilerParams(vmem_limit_bytes=2 * 2**20),
        name="stack",
    )(*in_vmem(*near))
    sent = exchange(held, 1)
    return pl.pallas_call(
        functools.partial(factor_kernel, parts),
        out_shape=[
            jax.ShapeDtypeStruct((examples // parts, rank * sketch), jnp.float32),
            jax.ShapeDtypeStruct((per, sketch, sketch), jnp.float32),
        ],
        in_specs=[smem()] + [vmem()] * 2,
        out_specs=[vmem()] * 2,
        compiler_params=pltpu.CompilerParams(vmem_limit_bytes=8 * 2**20),
        name="factors",
    )(damping, *in_vmem(held, sent))


def solution(mesh):
    in_specs = (
        P("mp", "ex", None),
        P("mp", "ex", None),
        P("mp", None, None),
        P("mp", None, None),
        P("mp", None, None),
        P("mp", None, None),
        P("mp", "ex", None),
        P(),
    )
    out_specs = (P(("ex", "mp"), None), P("mp", None, None))
    return jax.shard_map(
        local, mesh=mesh, in_specs=in_specs, out_specs=out_specs, check_vma=False
    )
```

```python
import functools
import math

import jax
import jax.numpy as jnp
from jax import lax
from jax.experimental import pallas as pl
from jax.experimental.pallas import tpu as pltpu
from jax.sharding import PartitionSpec as P

EXAMPLE_LENGTH = 8
LANES = 128
SLOT = 32
GROUP = LANES // SLOT
PANEL = 8
CHUNK = 1024


def dot_nt(a, b):
    return lax.dot_general(
        a, b, (((1,), (1,)), ((), ())), preferred_element_type=jnp.float32
    )


def dot_nn(a, b):
    return jnp.dot(a, b, preferred_element_type=jnp.float32)


def split(x):
    high = x.astype(jnp.bfloat16)
    return high, (x - high.astype(jnp.float32)).astype(jnp.bfloat16)


def partial_kernel(
    parts,
    scaling,
    acts_hbm,
    grads_hbm,
    down_hbm,
    up_hbm,
    proj_in_hbm,
    proj_out_hbm,
    order_hbm,
    *refs,
):
    sends, refs = refs[:parts], refs[parts:]
    acts, grads, weights_in, weights_out, order, low, mask, out, sems, order_sem = refs
    tokens, width = acts.shape
    rank = down_hbm.shape[1]
    sketch = proj_in_hbm.shape[1]
    examples = tokens // EXAMPLE_LENGTH
    per = rank // parts
    halves = sketch // SLOT

    def copies(source, target, sem, start, size):
        return pltpu.make_async_copy(
            source.at[0, :, pl.ds(start, size)],
            target.at[:, pl.ds(start, size)],
            sem,
        )

    order_copy = pltpu.make_async_copy(order_hbm.at[0], order, order_sem)
    order_copy.start()
    sources = [
        (grads_hbm, grads, proj_out_hbm, up_hbm, weights_out),
        (acts_hbm, acts, proj_in_hbm, down_hbm, weights_in),
    ]
    pending = []
    for data_hbm, data, first_hbm, second_hbm, weights in sources:
        for start in range(0, data.shape[1], CHUNK):
            n = len(pending)
            pending.append(
                [
                    copies(first_hbm, weights.at[pl.ds(0, sketch)], sems.at[n, 0], start, CHUNK),
                    copies(second_hbm, weights.at[pl.ds(sketch, rank)], sems.at[n, 1], start, CHUNK),
                    copies(data_hbm, data, sems.at[n, 2], start, CHUNK),
                ]
            )
            for copy in pending[-1]:
                copy.start()

    rows = examples * parts

    def product(total, n, data, weights, stages):
        for stage in stages:
            for copy in pending[n + stage]:
                copy.wait()
            here = pl.ds(stage * CHUNK, CHUNK)
            term = dot_nt(weights[:, here], data[:, here])
            total = term if total is None else total + term
        return total

    def spread_low(values, n):
        low[n] = values
        tiles = []
        for c in range(per):
            chosen = low[n, pl.ds(c, parts, stride=per), :]
            chosen = jnp.concatenate([chosen] * max(1, 8 // parts), axis=0)
            chosen = jnp.concatenate([chosen] * (rows // chosen.shape[0]), axis=0)
            tiles.append(split(chosen * mask[...]))
        return [jnp.concatenate(half, axis=0) for half in zip(*tiles)]

    def spread_sketch(values):
        return [
            jnp.concatenate(
                [part[h * SLOT : (h + 1) * SLOT] for h in range(halves) for _ in range(per)],
                axis=0,
            )
            for part in split(values)
        ]

    out_stages, in_stages = grads.shape[1] // CHUNK, width // CHUNK
    from_grads = product(None, 0, grads, weights_out, range(out_stages))
    from_acts = product(None, out_stages, acts, weights_in, range(in_stages // 2))

    order_copy.wait()
    source = lax.broadcasted_iota(jnp.int32, (8, tokens), 1) // EXAMPLE_LENGTH
    target = jnp.zeros((8, tokens), jnp.int32)
    for s in range(examples):
        target = jnp.where(source == s, order[0, s], target)
    target = jnp.concatenate([target] * (rows // 8), axis=0)
    place = lax.broadcasted_iota(jnp.int32, (rows, tokens), 0) // parts
    mask[...] = jnp.where(target == place, scaling, 0.0)
    left_grads = spread_low(from_grads[sketch:], 0)
    right_grads = spread_sketch(from_grads[:sketch])

    from_acts = product(
        from_acts, out_stages, acts, weights_in, range(in_stages // 2, in_stages)
    )
    left_acts = spread_low(from_acts[sketch:], 1)
    right_acts = spread_sketch(from_acts[:sketch])
    left_high, left_low = [
        jnp.concatenate(pair, axis=1) for pair in zip(left_grads, left_acts)
    ]
    right_high, right_low = [
        jnp.concatenate(pair, axis=1) for pair in zip(right_acts, right_grads)
    ]
    both = dot_nt(jnp.concatenate([left_high, left_low], axis=0), right_high)
    size = left_high.shape[0]
    spread = (dot_nt(left_high, right_low) + both[size:]) + both[:size]
    column = lax.broadcasted_iota(jnp.int32, (rows, per * sketch), 1)
    channel = (column // SLOT) % per
    total = spread[:rows]
    for c in range(1, per):
        total = jnp.where(channel == c, spread[c * rows : (c + 1) * rows], total)
    me = lax.axis_index("mp")
    for start in range(0, per * sketch, LANES):
        stop = min(start + LANES, per * sketch)
        out[:, : stop - start] = total[:, start:stop]
        for d in range(parts):
            g = me ^ d
            sends[d][:examples, start:stop] = out[
                pl.ds(pl.multiple_of(g * examples, examples), examples), : stop - start
            ]
            sends[d][examples:, start:stop] = out[pl.ds(g, examples, stride=parts), :][
                :, : stop - start
            ]


def sum_kernel(*refs):
    chunks, (columns, feature_rows) = refs[:-2], refs[-2:]
    examples, padded = columns.shape
    total = chunks[0][...]
    for chunk in chunks[1:]:
        total = total + chunk[...]
    width = total.shape[1]
    for ref, value in ((feature_rows, total[:examples]), (columns, total[examples:])):
        ref[:, :width] = value
        if padded > width:
            ref[:, width:] = jnp.zeros((examples, padded - width), jnp.float32)


def stack_kernel(*refs):
    rows = refs[0].shape[0]
    for n, part in enumerate(refs[:-1]):
        refs[-1][n * rows : (n + 1) * rows, :] = part[...]


def write_features(total, parts, per, features):
    rows_here, width = features.shape
    span = width // parts
    halves = span // (per * SLOT)
    natural = jnp.concatenate(
        [
            total[:, (h * per + c) * SLOT : (h * per + c + 1) * SLOT]
            for c in range(per)
            for h in range(halves)
        ],
        axis=1,
    )
    for r in range(rows_here):
        features[r : r + 1, :] = jnp.concatenate(
            [natural[r * parts + g : r * parts + g + 1, :] for g in range(parts)], axis=1
        )


def pick_lanes(x, index):
    return jnp.take_along_axis(x, index, axis=1)


def reciprocal(x):
    guess = pl.reciprocal(x, approx=True)
    return guess * (2.0 - x * guess)


def factor_kernel(parts, damping, held, sent, features, factors):
    channels, sketch, _ = factors.shape
    examples = features.shape[0] * parts
    gathered = held.shape[0] - examples
    span = features.shape[1] // parts
    write_features(sent[gathered:, :span], parts, channels, features)
    halves = sketch // SLOT
    panels = sketch // PANEL
    per_half = SLOT // PANEL
    stacked = jnp.concatenate([held[:gathered, :], sent[:gathered, :]], axis=0)
    high, rest = split(stacked)
    turned_high, turned_rest = split(jnp.transpose(stacked))
    gram = dot_nn(turned_high, rest) + dot_nn(
        jnp.concatenate([turned_rest, turned_high], axis=1),
        jnp.concatenate([high, high], axis=0),
    )
    lane = lax.broadcasted_iota(jnp.int32, (PANEL, LANES), 1)
    sub = lax.broadcasted_iota(jnp.int32, (PANEL, LANES), 0)
    slot = lane // SLOT
    within = lane % SLOT
    ridge = damping[0]
    tile = []
    for q in range(panels):
        hr, at = divmod(q, per_half)
        line = []
        for h in range(halves):
            value = None
            for c in range(GROUP):
                start = hr * LANES + c * SLOT + at * PANEL
                block = gram[start : start + PANEL, h * LANES : (h + 1) * LANES]
                value = block if c == 0 else jnp.where(slot == c, block, value)
            value = value * (1.0 / stacked.shape[0])
            if h == hr:
                value = value + jnp.where(within == at * PANEL + sub, ridge, 0.0)
            line.append(value)
        tile.append(line)

    zero = jnp.zeros((PANEL, LANES), jnp.float32)
    finished = []
    ahead = [pick_lanes(tile[0][0], slot * SLOT + r) for r in range(PANEL)]
    for q in range(panels):
        hq, at = divmod(q, per_half)
        if q + 1 < panels:
            hn, an = divmod(q + 1, per_half)
            behind = [
                pick_lanes(tile[q + 1][hn], slot * SLOT + an * PANEL + r)
                for r in range(PANEL)
            ]
        column = [
            {
                j: ahead[r]
                if j == q
                else pick_lanes(tile[j][hq], slot * SLOT + at * PANEL + r)
                for j in range(q, panels)
            }
            for r in range(PANEL)
        ]
        block = [
            [
                jnp.broadcast_to(column[r][q][s : s + 1, :], (PANEL, LANES))
                if s >= r
                else None
                for s in range(PANEL)
            ]
            for r in range(PANEL)
        ]
        line = [
            [
                jnp.broadcast_to(tile[q][h][r : r + 1, :], (PANEL, LANES))
                if h >= hq
                else None
                for h in range(halves)
            ]
            for r in range(PANEL)
        ]
        inverse = []

        def eliminate(r, s, inv):
            ratio = block[r][s] * inv
            for t in range(s, PANEL):
                block[s][t] = block[s][t] - ratio * block[r][t]
            for j in range(q + 1, panels):
                column[s][j] = column[s][j] - ratio * column[r][j]
            for h in range(hq, halves):
                line[s][h] = line[s][h] - ratio * line[r][h]

        for r in range(0, PANEL, 2):
            pivot = block[r][r]
            minor = pivot * block[r + 1][r + 1] - block[r][r + 1] * block[r][r + 1]
            inverse.append(reciprocal(pivot))
            inverse.append(pivot * reciprocal(minor))
            eliminate(r, r + 1, inverse[r])
            for s in range(r + 2, PANEL):
                eliminate(r, s, inverse[r])
                eliminate(r + 1, s, inverse[r + 1])
        result = []
        for h in range(halves):
            if h < hq:
                result.append(zero)
                continue
            value = zero
            for r in range(PANEL):
                value = jnp.where(sub == r, line[r][h] * lax.rsqrt(block[r][r]), value)
            if h == hq:
                value = jnp.where(within >= at * PANEL + sub, value, 0.0)
            result.append(value)
        finished.append(result)
        for j in range(q + 1, panels):
            weights = [column[r][j] * inverse[r] for r in range(PANEL)]
            if j == q + 1:
                ahead = behind
                for r in range(PANEL):
                    for s in range(PANEL):
                        factor = jnp.broadcast_to(
                            column[r][j][s : s + 1, :], (PANEL, LANES)
                        )
                        ahead[s] = ahead[s] - weights[r] * factor
            for h in range((q + 1) // per_half, halves):
                value = tile[j][h]
                for r in range(PANEL):
                    value = value - weights[r] * line[r][h]
                tile[j][h] = value

    for q in range(panels):
        for c in range(channels):
            factors[c, q * PANEL : (q + 1) * PANEL, :] = jnp.concatenate(
                [finished[q][h][:, c * SLOT : (c + 1) * SLOT] for h in range(halves)],
                axis=1,
            )


def permute(x, source):
    shards, parts = lax.axis_size("ex"), lax.axis_size("mp")
    pairs = []
    for m in range(shards):
        for b in range(parts):
            sm, sb = source(m, b)
            pairs.append((sm * parts + sb, m * parts + b))
    return lax.ppermute(x, ("ex", "mp"), sorted(pairs))


def exchange(x, ex_distance, mp_distance=0):
    return permute(x, lambda m, b: (m ^ ex_distance, b ^ mp_distance))


def shift_chips(x, distance):
    shards = lax.axis_size("ex")
    return permute(x, lambda m, b: ((m - 2 * distance) % shards ^ 1, b))


def vmem():
    return pl.BlockSpec(memory_space=pltpu.VMEM)


def hbm():
    return pl.BlockSpec(memory_space=pltpu.HBM)


def in_hbm(*arrays):
    return [pltpu.with_memory_space_constraint(x, pltpu.HBM) for x in arrays]


def in_vmem(*arrays):
    return [pltpu.with_memory_space_constraint(x, pltpu.VMEM) for x in arrays]


def smem():
    return pl.BlockSpec(memory_space=pltpu.SMEM)


def local(
    acts,
    grads,
    down_factor,
    up_factor_transposed,
    input_projection,
    gradient_projection,
    order,
    damping,
):
    parts = lax.axis_size("mp")
    shards = lax.axis_size("ex")
    tokens, width = acts.shape[1:]
    key_width = grads.shape[2]
    rank = down_factor.shape[1]
    sketch = input_projection.shape[1]
    examples = tokens // EXAMPLE_LENGTH
    per = rank // parts
    span = per * sketch
    scaling = 1.0 / math.sqrt(2.0 * EXAMPLE_LENGTH * parts)
    sends = pl.pallas_call(
        functools.partial(partial_kernel, parts, scaling),
        out_shape=[pltpu.VMEM((2 * examples, span), jnp.float32)] * parts,
        in_specs=[hbm()] * 7,
        out_specs=[vmem()] * parts,
        scratch_shapes=[
            pltpu.VMEM((tokens, width), acts.dtype),
            pltpu.VMEM((tokens, key_width), grads.dtype),
            pltpu.VMEM((sketch + rank, width), acts.dtype),
            pltpu.VMEM((sketch + rank, key_width), grads.dtype),
            pltpu.SMEM(order.shape[1:], order.dtype),
            pltpu.VMEM((2, rank, tokens), jnp.float32),
            pltpu.VMEM((examples * parts, tokens), jnp.float32),
            pltpu.VMEM((examples * parts, LANES), jnp.float32),
            pltpu.SemaphoreType.DMA(((width + key_width) // CHUNK, 3)),
            pltpu.SemaphoreType.DMA,
        ],
        compiler_params=pltpu.CompilerParams(vmem_limit_bytes=8 * 2**20),
        name="partials",
    )(
        *in_hbm(
            acts,
            grads,
            down_factor,
            up_factor_transposed,
            input_projection,
            gradient_projection,
            order,
        )
    )
    chunks = [exchange(sends[d], 1, d) for d in range(parts - 1, -1, -1)]
    padded = max(span, GROUP * sketch)
    columns, feature_rows = pl.pallas_call(
        sum_kernel,
        out_shape=[pltpu.VMEM((examples, padded), jnp.float32)] * 2,
        in_specs=[vmem()] * parts,
        out_specs=[vmem()] * 2,
        compiler_params=pltpu.CompilerParams(vmem_limit_bytes=2 * 2**20),
        name="sums",
    )(*in_vmem(*chunks))
    shifts = sorted(range(1, shards // 2), key=lambda d: (-min(d, shards // 2 - d), -d))
    near = [columns] + [shift_chips(columns, d) for d in shifts] + [feature_rows]
    held = pl.pallas_call(
        stack_kernel,
        out_shape=pltpu.VMEM((len(near) * examples, padded), jnp.float32),
        in_specs=[vmem()] * len(near),
        out_specs=vmem(),
        compiler_params=pltpu.CompilerParams(vmem_limit_bytes=2 * 2**20),
        name="stack",
    )(*in_vmem(*near))
    sent = exchange(held, 1)
    return pl.pallas_call(
        functools.partial(factor_kernel, parts),
        out_shape=[
            jax.ShapeDtypeStruct((examples // parts, rank * sketch), jnp.float32),
            jax.ShapeDtypeStruct((per, sketch, sketch), jnp.float32),
        ],
        in_specs=[smem()] + [vmem()] * 2,
        out_specs=[vmem()] * 2,
        compiler_params=pltpu.CompilerParams(vmem_limit_bytes=8 * 2**20),
        name="factors",
    )(damping, *in_vmem(held, sent))


def solution(mesh):
    in_specs = (
        P("mp", "ex", None),
        P("mp", "ex", None),
        P("mp", None, None),
        P("mp", None, None),
        P("mp", None, None),
        P("mp", None, None),
        P("mp", "ex", None),
        P(),
    )
    out_specs = (P(("ex", "mp"), None), P("mp", None, None))
    return jax.shard_map(
        local, mesh=mesh, in_specs=in_specs, out_specs=out_specs, check_vma=False
    )
```

```python
import functools
import math

import jax
import jax.numpy as jnp
from jax import lax
from jax.experimental import pallas as pl
from jax.experimental.pallas import tpu as pltpu
from jax.sharding import PartitionSpec as P

EXAMPLE_LENGTH = 8
LANES = 128
SLOT = 32
GROUP = LANES // SLOT
PANEL = 8
CHUNK = 1024


def dot_nt(a, b):
    return lax.dot_general(
        a, b, (((1,), (1,)), ((), ())), preferred_element_type=jnp.float32
    )


def dot_nn(a, b):
    return jnp.dot(a, b, preferred_element_type=jnp.float32)


def split(x):
    high = x.astype(jnp.bfloat16)
    return high, (x - high.astype(jnp.float32)).astype(jnp.bfloat16)


def partial_kernel(
    parts,
    scaling,
    acts_hbm,
    grads_hbm,
    down_hbm,
    up_hbm,
    proj_in_hbm,
    proj_out_hbm,
    order_hbm,
    *refs,
):
    sends, refs = refs[:parts], refs[parts:]
    acts, grads, weights_in, weights_out, order, low, mask, out, sems, order_sem = refs
    tokens, width = acts.shape
    rank = down_hbm.shape[1]
    sketch = proj_in_hbm.shape[1]
    examples = tokens // EXAMPLE_LENGTH
    per = rank // parts
    halves = sketch // SLOT

    def copies(source, target, sem, start, size):
        return pltpu.make_async_copy(
            source.at[0, :, pl.ds(start, size)],
            target.at[:, pl.ds(start, size)],
            sem,
        )

    order_copy = pltpu.make_async_copy(order_hbm.at[0], order, order_sem)
    order_copy.start()
    sources = [
        (grads_hbm, grads, proj_out_hbm, up_hbm, weights_out),
        (acts_hbm, acts, proj_in_hbm, down_hbm, weights_in),
    ]
    pending = []
    for data_hbm, data, first_hbm, second_hbm, weights in sources:
        for start in range(0, data.shape[1], CHUNK):
            n = len(pending)
            pending.append(
                [
                    copies(first_hbm, weights.at[pl.ds(0, sketch)], sems.at[n, 0], start, CHUNK),
                    copies(second_hbm, weights.at[pl.ds(sketch, rank)], sems.at[n, 1], start, CHUNK),
                    copies(data_hbm, data, sems.at[n, 2], start, CHUNK),
                ]
            )
            for copy in pending[-1]:
                copy.start()

    order_copy.wait()
    rows = examples * parts
    source = lax.broadcasted_iota(jnp.int32, (8, tokens), 1) // EXAMPLE_LENGTH
    target = jnp.zeros((8, tokens), jnp.int32)
    for s in range(examples):
        target = jnp.where(source == s, order[0, s], target)
    target = jnp.concatenate([target] * (rows // 8), axis=0)
    place = lax.broadcasted_iota(jnp.int32, (rows, tokens), 0) // parts
    mask[...] = jnp.where(target == place, scaling, 0.0)

    def product(first, data, weights):
        total = None
        for n in range(data.shape[1] // CHUNK):
            for copy in pending[first + n]:
                copy.wait()
            here = pl.ds(n * CHUNK, CHUNK)
            term = dot_nt(weights[:, here], data[:, here])
            total = term if total is None else total + term
        return total

    def spread_low(values, n):
        low[n] = values
        tiles = []
        for c in range(per):
            chosen = low[n, pl.ds(c, parts, stride=per), :]
            chosen = jnp.concatenate([chosen] * max(1, 8 // parts), axis=0)
            chosen = jnp.concatenate([chosen] * (rows // chosen.shape[0]), axis=0)
            tiles.append(split(chosen * mask[...]))
        return [jnp.concatenate(half, axis=0) for half in zip(*tiles)]

    def spread_sketch(values):
        return split(
            jnp.concatenate(
                [values[h * SLOT : (h + 1) * SLOT] for h in range(halves) for _ in range(per)],
                axis=0,
            )
        )

    from_grads = product(0, grads, weights_out)
    left_grads = spread_low(from_grads[sketch:], 0)
    right_grads = spread_sketch(from_grads[:sketch])
    from_acts = product(grads.shape[1] // CHUNK, acts, weights_in)
    left_acts = spread_low(from_acts[sketch:], 1)
    right_acts = spread_sketch(from_acts[:sketch])
    left_high, left_low = [
        jnp.concatenate(pair, axis=1) for pair in zip(left_grads, left_acts)
    ]
    right_high, right_low = [
        jnp.concatenate(pair, axis=1) for pair in zip(right_acts, right_grads)
    ]
    both = dot_nt(jnp.concatenate([left_high, left_low], axis=0), right_high)
    size = left_high.shape[0]
    spread = (dot_nt(left_high, right_low) + both[size:]) + both[:size]
    column = lax.broadcasted_iota(jnp.int32, (rows, per * sketch), 1)
    channel = (column // SLOT) % per
    total = spread[:rows]
    for c in range(1, per):
        total = jnp.where(channel == c, spread[c * rows : (c + 1) * rows], total)
    me = lax.axis_index("mp")
    for start in range(0, per * sketch, LANES):
        stop = min(start + LANES, per * sketch)
        out[:, : stop - start] = total[:, start:stop]
        for d in range(parts):
            g = me ^ d
            sends[d][:examples, start:stop] = out[
                pl.ds(pl.multiple_of(g * examples, examples), examples), : stop - start
            ]
            sends[d][examples:, start:stop] = out[pl.ds(g, examples, stride=parts), :][
                :, : stop - start
            ]


def sum_kernel(damping, *refs):
    chunks, (columns, feature_rows, ridge) = refs[:-3], refs[-3:]
    ridge[...] = jnp.full(ridge.shape, damping[0], jnp.float32)
    examples, padded = columns.shape
    total = chunks[0][...]
    for chunk in chunks[1:]:
        total = total + chunk[...]
    width = total.shape[1]
    for ref, value in ((feature_rows, total[:examples]), (columns, total[examples:])):
        ref[:, :width] = value
        if padded > width:
            ref[:, width:] = jnp.zeros((examples, padded - width), jnp.float32)


def stack_kernel(*refs):
    rows = refs[0].shape[0]
    for n, part in enumerate(refs[:-1]):
        refs[-1][n * rows : (n + 1) * rows, :] = part[...]


def write_features(total, parts, per, features):
    rows_here, width = features.shape
    span = width // parts
    halves = span // (per * SLOT)
    natural = jnp.concatenate(
        [
            total[:, (h * per + c) * SLOT : (h * per + c + 1) * SLOT]
            for c in range(per)
            for h in range(halves)
        ],
        axis=1,
    )
    for r in range(rows_here):
        features[r : r + 1, :] = jnp.concatenate(
            [natural[r * parts + g : r * parts + g + 1, :] for g in range(parts)], axis=1
        )


def pick_lanes(x, index):
    return jnp.take_along_axis(x, index, axis=1)


def reciprocal(x):
    guess = pl.reciprocal(x, approx=True)
    return guess * (2.0 - x * guess)


def factor_kernel(parts, ridge, held, sent, features, factors):
    channels, sketch, _ = factors.shape
    examples = features.shape[0] * parts
    gathered = held.shape[0] - examples
    span = features.shape[1] // parts
    write_features(sent[gathered:, :span], parts, channels, features)
    halves = sketch // SLOT
    panels = sketch // PANEL
    per_half = SLOT // PANEL
    stacked = jnp.concatenate([held[:gathered, :], sent[:gathered, :]], axis=0)
    high, rest = split(stacked)
    turned_high, turned_rest = split(jnp.transpose(stacked))
    gram = dot_nn(turned_high, rest) + dot_nn(
        jnp.concatenate([turned_rest, turned_high], axis=1),
        jnp.concatenate([high, high], axis=0),
    )
    lane = lax.broadcasted_iota(jnp.int32, (PANEL, LANES), 1)
    sub = lax.broadcasted_iota(jnp.int32, (PANEL, LANES), 0)
    slot = lane // SLOT
    within = lane % SLOT
    tile = []
    for q in range(panels):
        hr, at = divmod(q, per_half)
        line = []
        for h in range(halves):
            value = None
            for c in range(GROUP):
                start = hr * LANES + c * SLOT + at * PANEL
                block = gram[start : start + PANEL, h * LANES : (h + 1) * LANES]
                value = block if c == 0 else jnp.where(slot == c, block, value)
            value = value * (1.0 / stacked.shape[0])
            if h == hr:
                value = value + jnp.where(within == at * PANEL + sub, ridge[...], 0.0)
            line.append(value)
        tile.append(line)

    zero = jnp.zeros((PANEL, LANES), jnp.float32)
    finished = []
    ahead = [pick_lanes(tile[0][0], slot * SLOT + r) for r in range(PANEL)]
    for q in range(panels):
        hq, at = divmod(q, per_half)
        if q + 1 < panels:
            hn, an = divmod(q + 1, per_half)
            behind = [
                pick_lanes(tile[q + 1][hn], slot * SLOT + an * PANEL + r)
                for r in range(PANEL)
            ]
        column = [
            {
                j: ahead[r]
                if j == q
                else pick_lanes(tile[j][hq], slot * SLOT + at * PANEL + r)
                for j in range(q, panels)
            }
            for r in range(PANEL)
        ]
        block = [
            [
                jnp.broadcast_to(column[r][q][s : s + 1, :], (PANEL, LANES))
                if s >= r
                else None
                for s in range(PANEL)
            ]
            for r in range(PANEL)
        ]
        line = [
            [
                jnp.broadcast_to(tile[q][h][r : r + 1, :], (PANEL, LANES))
                if h >= hq
                else None
                for h in range(halves)
            ]
            for r in range(PANEL)
        ]
        inverse = []

        def eliminate(r, s, inv):
            ratio = block[r][s] * inv
            for t in range(s, PANEL):
                block[s][t] = block[s][t] - ratio * block[r][t]
            for j in range(q + 1, panels):
                column[s][j] = column[s][j] - ratio * column[r][j]
            for h in range(hq, halves):
                line[s][h] = line[s][h] - ratio * line[r][h]

        for r in range(0, PANEL, 2):
            pivot = block[r][r]
            minor = pivot * block[r + 1][r + 1] - block[r][r + 1] * block[r][r + 1]
            inverse.append(reciprocal(pivot))
            inverse.append(pivot * reciprocal(minor))
            eliminate(r, r + 1, inverse[r])
            for s in range(r + 2, PANEL):
                eliminate(r, s, inverse[r])
                eliminate(r + 1, s, inverse[r + 1])
        result = []
        for h in range(halves):
            if h < hq:
                result.append(zero)
                continue
            value = zero
            for r in range(PANEL):
                value = jnp.where(sub == r, line[r][h] * lax.rsqrt(block[r][r]), value)
            if h == hq:
                value = jnp.where(within >= at * PANEL + sub, value, 0.0)
            result.append(value)
        finished.append(result)
        for j in range(q + 1, panels):
            weights = [column[r][j] * inverse[r] for r in range(PANEL)]
            if j == q + 1:
                ahead = behind
                for r in range(PANEL):
                    for s in range(PANEL):
                        factor = jnp.broadcast_to(
                            column[r][j][s : s + 1, :], (PANEL, LANES)
                        )
                        ahead[s] = ahead[s] - weights[r] * factor
            for h in range((q + 1) // per_half, halves):
                value = tile[j][h]
                for r in range(PANEL):
                    value = value - weights[r] * line[r][h]
                tile[j][h] = value

    for q in range(panels):
        for c in range(channels):
            factors[c, q * PANEL : (q + 1) * PANEL, :] = jnp.concatenate(
                [finished[q][h][:, c * SLOT : (c + 1) * SLOT] for h in range(halves)],
                axis=1,
            )


def permute(x, source):
    shards, parts = lax.axis_size("ex"), lax.axis_size("mp")
    pairs = []
    for m in range(shards):
        for b in range(parts):
            sm, sb = source(m, b)
            pairs.append((sm * parts + sb, m * parts + b))
    return lax.ppermute(x, ("ex", "mp"), sorted(pairs))


def exchange(x, ex_distance, mp_distance=0):
    return permute(x, lambda m, b: (m ^ ex_distance, b ^ mp_distance))


def shift_chips(x, distance):
    shards = lax.axis_size("ex")
    return permute(x, lambda m, b: ((m - 2 * distance) % shards ^ 1, b))


def vmem():
    return pl.BlockSpec(memory_space=pltpu.VMEM)


def hbm():
    return pl.BlockSpec(memory_space=pltpu.HBM)


def in_hbm(*arrays):
    return [pltpu.with_memory_space_constraint(x, pltpu.HBM) for x in arrays]


def in_vmem(*arrays):
    return [pltpu.with_memory_space_constraint(x, pltpu.VMEM) for x in arrays]


def smem():
    return pl.BlockSpec(memory_space=pltpu.SMEM)


def local(
    acts,
    grads,
    down_factor,
    up_factor_transposed,
    input_projection,
    gradient_projection,
    order,
    damping,
):
    parts = lax.axis_size("mp")
    shards = lax.axis_size("ex")
    tokens, width = acts.shape[1:]
    key_width = grads.shape[2]
    rank = down_factor.shape[1]
    sketch = input_projection.shape[1]
    examples = tokens // EXAMPLE_LENGTH
    per = rank // parts
    span = per * sketch
    scaling = 1.0 / math.sqrt(2.0 * EXAMPLE_LENGTH * parts)
    sends = pl.pallas_call(
        functools.partial(partial_kernel, parts, scaling),
        out_shape=[pltpu.VMEM((2 * examples, span), jnp.float32)] * parts,
        in_specs=[hbm()] * 7,
        out_specs=[vmem()] * parts,
        scratch_shapes=[
            pltpu.VMEM((tokens, width), acts.dtype),
            pltpu.VMEM((tokens, key_width), grads.dtype),
            pltpu.VMEM((sketch + rank, width), acts.dtype),
            pltpu.VMEM((sketch + rank, key_width), grads.dtype),
            pltpu.SMEM(order.shape[1:], order.dtype),
            pltpu.VMEM((2, rank, tokens), jnp.float32),
            pltpu.VMEM((examples * parts, tokens), jnp.float32),
            pltpu.VMEM((examples * parts, LANES), jnp.float32),
            pltpu.SemaphoreType.DMA(((width + key_width) // CHUNK, 3)),
            pltpu.SemaphoreType.DMA,
        ],
        compiler_params=pltpu.CompilerParams(vmem_limit_bytes=8 * 2**20),
        name="partials",
    )(
        *in_hbm(
            acts,
            grads,
            down_factor,
            up_factor_transposed,
            input_projection,
            gradient_projection,
            order,
        )
    )
    chunks = [exchange(sends[d], 1, d) for d in range(parts - 1, -1, -1)]
    padded = max(span, GROUP * sketch)
    columns, feature_rows, ridge = pl.pallas_call(
        sum_kernel,
        out_shape=[pltpu.VMEM((examples, padded), jnp.float32)] * 2
        + [pltpu.VMEM((PANEL, LANES), jnp.float32)],
        in_specs=[smem()] + [vmem()] * parts,
        out_specs=[vmem()] * 3,
        compiler_params=pltpu.CompilerParams(vmem_limit_bytes=2 * 2**20),
        name="sums",
    )(damping, *in_vmem(*chunks))
    shifts = sorted(range(1, shards // 2), key=lambda d: (-min(d, shards // 2 - d), -d))
    near = [columns] + [shift_chips(columns, d) for d in shifts] + [feature_rows]
    held = pl.pallas_call(
        stack_kernel,
        out_shape=pltpu.VMEM((len(near) * examples, padded), jnp.float32),
        in_specs=[vmem()] * len(near),
        out_specs=vmem(),
        compiler_params=pltpu.CompilerParams(vmem_limit_bytes=2 * 2**20),
        name="stack",
    )(*in_vmem(*near))
    sent = exchange(held, 1)
    return pl.pallas_call(
        functools.partial(factor_kernel, parts),
        out_shape=[
            jax.ShapeDtypeStruct((examples // parts, rank * sketch), jnp.float32),
            jax.ShapeDtypeStruct((per, sketch, sketch), jnp.float32),
        ],
        in_specs=[vmem()] * 3,
        out_specs=[vmem()] * 2,
        compiler_params=pltpu.CompilerParams(vmem_limit_bytes=8 * 2**20),
        name="factors",
    )(*in_vmem(ridge, held, sent))


def solution(mesh):
    in_specs = (
        P("mp", "ex", None),
        P("mp", "ex", None),
        P("mp", None, None),
        P("mp", None, None),
        P("mp", None, None),
        P("mp", None, None),
        P("mp", "ex", None),
        P(),
    )
    out_specs = (P(("ex", "mp"), None), P("mp", None, None))
    return jax.shard_map(
        local, mesh=mesh, in_specs=in_specs, out_specs=out_specs, check_vma=False
    )
```

```python
import functools
import math

import jax
import jax.numpy as jnp
from jax import lax
from jax.experimental import pallas as pl
from jax.experimental.pallas import tpu as pltpu
from jax.sharding import PartitionSpec as P

EXAMPLE_LENGTH = 8
LANES = 128
SLOT = 32
GROUP = LANES // SLOT
PANEL = 8
BOUNDS = ((0, 8), (0, 3, 5, 7, 8))


def dot_nt(a, b):
    return lax.dot_general(
        a, b, (((1,), (1,)), ((), ())), preferred_element_type=jnp.float32
    )


def dot_nn(a, b):
    return jnp.dot(a, b, preferred_element_type=jnp.float32)


def split(x):
    high = x.astype(jnp.bfloat16)
    return high, (x - high.astype(jnp.float32)).astype(jnp.bfloat16)


def partial_kernel(
    parts,
    scaling,
    acts_hbm,
    grads_hbm,
    down_hbm,
    up_hbm,
    proj_in_hbm,
    proj_out_hbm,
    order_hbm,
    *refs,
):
    sends, refs = refs[:parts], refs[parts:]
    acts, grads, weights_in, weights_out, order, low, mask, out, sems, order_sem = refs
    tokens, width = acts.shape
    rank = down_hbm.shape[1]
    sketch = proj_in_hbm.shape[1]
    examples = tokens // EXAMPLE_LENGTH
    per = rank // parts
    halves = sketch // SLOT

    def copies(source, target, sem, here):
        return pltpu.make_async_copy(source.at[0, :, here], target.at[:, here], sem)

    order_copy = pltpu.make_async_copy(order_hbm.at[0], order, order_sem)
    order_copy.start()
    sources = [
        (grads_hbm, grads, proj_out_hbm, up_hbm, weights_out),
        (acts_hbm, acts, proj_in_hbm, down_hbm, weights_in),
    ]
    pending = []
    for (data_hbm, data, first_hbm, second_hbm, weights), bounds in zip(sources, BOUNDS):
        stages = []
        edges = [data.shape[1] * edge // 8 for edge in bounds]
        for start, stop in zip(edges, edges[1:]):
            here = pl.ds(start, stop - start)
            sem = sems.at[len(pending), len(stages)]
            stage = [
                copies(first_hbm, weights.at[pl.ds(0, sketch)], sem.at[0], here),
                copies(second_hbm, weights.at[pl.ds(sketch, rank)], sem.at[1], here),
                copies(data_hbm, data, sem.at[2], here),
            ]
            for copy in stage:
                copy.start()
            stages.append((here, stage))
        pending.append(stages)

    order_copy.wait()
    rows = examples * parts
    source = lax.broadcasted_iota(jnp.int32, (8, tokens), 1) // EXAMPLE_LENGTH
    target = jnp.zeros((8, tokens), jnp.int32)
    for s in range(examples):
        target = jnp.where(source == s, order[0, s], target)
    target = jnp.concatenate([target] * (rows // 8), axis=0)
    place = lax.broadcasted_iota(jnp.int32, (rows, tokens), 0) // parts
    mask[...] = jnp.where(target == place, scaling, 0.0)

    def product(n, data, weights):
        total = None
        for here, stage in pending[n]:
            for copy in stage:
                copy.wait()
            term = dot_nt(weights[:, here], data[:, here])
            total = term if total is None else total + term
        return total

    def spread_low(values, n):
        low[n] = values
        tiles = []
        for c in range(per):
            chosen = low[n, pl.ds(c, parts, stride=per), :]
            chosen = jnp.concatenate([chosen] * max(1, 8 // parts), axis=0)
            chosen = jnp.concatenate([chosen] * (rows // chosen.shape[0]), axis=0)
            tiles.append(split(chosen * mask[...]))
        return [jnp.concatenate(half, axis=0) for half in zip(*tiles)]

    def spread_sketch(values):
        return split(
            jnp.concatenate(
                [values[h * SLOT : (h + 1) * SLOT] for h in range(halves) for _ in range(per)],
                axis=0,
            )
        )

    from_grads = product(0, grads, weights_out)
    left_grads = spread_low(from_grads[sketch:], 0)
    right_grads = spread_sketch(from_grads[:sketch])
    from_acts = product(1, acts, weights_in)
    left_acts = spread_low(from_acts[sketch:], 1)
    right_acts = spread_sketch(from_acts[:sketch])
    left_high, left_low = [
        jnp.concatenate(pair, axis=1) for pair in zip(left_grads, left_acts)
    ]
    right_high, right_low = [
        jnp.concatenate(pair, axis=1) for pair in zip(right_acts, right_grads)
    ]
    both = dot_nt(jnp.concatenate([left_high, left_low], axis=0), right_high)
    size = left_high.shape[0]
    spread = (dot_nt(left_high, right_low) + both[size:]) + both[:size]
    column = lax.broadcasted_iota(jnp.int32, (rows, per * sketch), 1)
    channel = (column // SLOT) % per
    total = spread[:rows]
    for c in range(1, per):
        total = jnp.where(channel == c, spread[c * rows : (c + 1) * rows], total)
    me = lax.axis_index("mp")
    for start in range(0, per * sketch, LANES):
        stop = min(start + LANES, per * sketch)
        out[:, : stop - start] = total[:, start:stop]
        for d in range(parts):
            g = me ^ d
            sends[d][:examples, start:stop] = out[
                pl.ds(pl.multiple_of(g * examples, examples), examples), : stop - start
            ]
            sends[d][examples:, start:stop] = out[pl.ds(g, examples, stride=parts), :][
                :, : stop - start
            ]


def sum_kernel(damping, *refs):
    chunks, (columns, feature_rows, ridge) = refs[:-3], refs[-3:]
    ridge[...] = jnp.full(ridge.shape, damping[0], jnp.float32)
    examples, padded = columns.shape
    total = chunks[0][...]
    for chunk in chunks[1:]:
        total = total + chunk[...]
    width = total.shape[1]
    for ref, value in ((feature_rows, total[:examples]), (columns, total[examples:])):
        ref[:, :width] = value
        if padded > width:
            ref[:, width:] = jnp.zeros((examples, padded - width), jnp.float32)


def stack_kernel(*refs):
    rows = refs[0].shape[0]
    for n, part in enumerate(refs[:-1]):
        refs[-1][n * rows : (n + 1) * rows, :] = part[...]


def write_features(total, parts, per, features):
    rows_here, width = features.shape
    span = width // parts
    halves = span // (per * SLOT)
    natural = jnp.concatenate(
        [
            total[:, (h * per + c) * SLOT : (h * per + c + 1) * SLOT]
            for c in range(per)
            for h in range(halves)
        ],
        axis=1,
    )
    for r in range(rows_here):
        features[r : r + 1, :] = jnp.concatenate(
            [natural[r * parts + g : r * parts + g + 1, :] for g in range(parts)], axis=1
        )


def pick_lanes(x, index):
    return jnp.take_along_axis(x, index, axis=1)


def reciprocal(x):
    guess = pl.reciprocal(x, approx=True)
    return guess * (2.0 - x * guess)


def factor_kernel(parts, ridge, held, sent, features, factors):
    channels, sketch, _ = factors.shape
    examples = features.shape[0] * parts
    gathered = held.shape[0] - examples
    span = features.shape[1] // parts
    write_features(sent[gathered:, :span], parts, channels, features)
    halves = sketch // SLOT
    panels = sketch // PANEL
    per_half = SLOT // PANEL
    stacked = jnp.concatenate([held[:gathered, :], sent[:gathered, :]], axis=0)
    high, rest = split(stacked)
    turned_high, turned_rest = split(jnp.transpose(stacked))
    gram = dot_nn(turned_high, rest) + dot_nn(
        jnp.concatenate([turned_rest, turned_high], axis=1),
        jnp.concatenate([high, high], axis=0),
    )
    lane = lax.broadcasted_iota(jnp.int32, (PANEL, LANES), 1)
    sub = lax.broadcasted_iota(jnp.int32, (PANEL, LANES), 0)
    slot = lane // SLOT
    within = lane % SLOT
    tile = []
    for q in range(panels):
        hr, at = divmod(q, per_half)
        line = []
        for h in range(halves):
            value = None
            for c in range(GROUP):
                start = hr * LANES + c * SLOT + at * PANEL
                block = gram[start : start + PANEL, h * LANES : (h + 1) * LANES]
                value = block if c == 0 else jnp.where(slot == c, block, value)
            value = value * (1.0 / stacked.shape[0])
            if h == hr:
                value = value + jnp.where(within == at * PANEL + sub, ridge[...], 0.0)
            line.append(value)
        tile.append(line)

    zero = jnp.zeros((PANEL, LANES), jnp.float32)
    finished = []
    ahead = [pick_lanes(tile[0][0], slot * SLOT + r) for r in range(PANEL)]
    for q in range(panels):
        hq, at = divmod(q, per_half)
        if q + 1 < panels:
            hn, an = divmod(q + 1, per_half)
            behind = [
                pick_lanes(tile[q + 1][hn], slot * SLOT + an * PANEL + r)
                for r in range(PANEL)
            ]
        column = [
            {
                j: ahead[r]
                if j == q
                else pick_lanes(tile[j][hq], slot * SLOT + at * PANEL + r)
                for j in range(q, panels)
            }
            for r in range(PANEL)
        ]
        block = [
            [
                jnp.broadcast_to(column[r][q][s : s + 1, :], (PANEL, LANES))
                if s >= r
                else None
                for s in range(PANEL)
            ]
            for r in range(PANEL)
        ]
        line = [
            [
                jnp.broadcast_to(tile[q][h][r : r + 1, :], (PANEL, LANES))
                if h >= hq
                else None
                for h in range(halves)
            ]
            for r in range(PANEL)
        ]
        inverse = []

        def eliminate(r, s, inv):
            ratio = block[r][s] * inv
            for t in range(s, PANEL):
                block[s][t] = block[s][t] - ratio * block[r][t]
            for j in range(q + 1, panels):
                column[s][j] = column[s][j] - ratio * column[r][j]
            for h in range(hq, halves):
                line[s][h] = line[s][h] - ratio * line[r][h]

        for r in range(0, PANEL, 2):
            pivot = block[r][r]
            minor = pivot * block[r + 1][r + 1] - block[r][r + 1] * block[r][r + 1]
            inverse.append(reciprocal(pivot))
            inverse.append(pivot * reciprocal(minor))
            eliminate(r, r + 1, inverse[r])
            for s in range(r + 2, PANEL):
                eliminate(r, s, inverse[r])
                eliminate(r + 1, s, inverse[r + 1])
        result = []
        for h in range(halves):
            if h < hq:
                result.append(zero)
                continue
            value = zero
            for r in range(PANEL):
                value = jnp.where(sub == r, line[r][h] * lax.rsqrt(block[r][r]), value)
            if h == hq:
                value = jnp.where(within >= at * PANEL + sub, value, 0.0)
            result.append(value)
        finished.append(result)
        for j in range(q + 1, panels):
            weights = [column[r][j] * inverse[r] for r in range(PANEL)]
            if j == q + 1:
                ahead = behind
                for r in range(PANEL):
                    for s in range(PANEL):
                        factor = jnp.broadcast_to(
                            column[r][j][s : s + 1, :], (PANEL, LANES)
                        )
                        ahead[s] = ahead[s] - weights[r] * factor
            for h in range((q + 1) // per_half, halves):
                value = tile[j][h]
                for r in range(PANEL):
                    value = value - weights[r] * line[r][h]
                tile[j][h] = value

    for q in range(panels):
        for c in range(channels):
            factors[c, q * PANEL : (q + 1) * PANEL, :] = jnp.concatenate(
                [finished[q][h][:, c * SLOT : (c + 1) * SLOT] for h in range(halves)],
                axis=1,
            )


def permute(x, source):
    shards, parts = lax.axis_size("ex"), lax.axis_size("mp")
    pairs = []
    for m in range(shards):
        for b in range(parts):
            sm, sb = source(m, b)
            pairs.append((sm * parts + sb, m * parts + b))
    return lax.ppermute(x, ("ex", "mp"), sorted(pairs))


def exchange(x, ex_distance, mp_distance=0):
    return permute(x, lambda m, b: (m ^ ex_distance, b ^ mp_distance))


def shift_chips(x, distance):
    shards = lax.axis_size("ex")
    return permute(x, lambda m, b: ((m - 2 * distance) % shards ^ 1, b))


def vmem():
    return pl.BlockSpec(memory_space=pltpu.VMEM)


def hbm():
    return pl.BlockSpec(memory_space=pltpu.HBM)


def in_hbm(*arrays):
    return [pltpu.with_memory_space_constraint(x, pltpu.HBM) for x in arrays]


def in_vmem(*arrays):
    return [pltpu.with_memory_space_constraint(x, pltpu.VMEM) for x in arrays]


def smem():
    return pl.BlockSpec(memory_space=pltpu.SMEM)


def local(
    acts,
    grads,
    down_factor,
    up_factor_transposed,
    input_projection,
    gradient_projection,
    order,
    damping,
):
    parts = lax.axis_size("mp")
    shards = lax.axis_size("ex")
    tokens, width = acts.shape[1:]
    key_width = grads.shape[2]
    rank = down_factor.shape[1]
    sketch = input_projection.shape[1]
    examples = tokens // EXAMPLE_LENGTH
    per = rank // parts
    span = per * sketch
    scaling = 1.0 / math.sqrt(2.0 * EXAMPLE_LENGTH * parts)
    sends = pl.pallas_call(
        functools.partial(partial_kernel, parts, scaling),
        out_shape=[pltpu.VMEM((2 * examples, span), jnp.float32)] * parts,
        in_specs=[hbm()] * 7,
        out_specs=[vmem()] * parts,
        scratch_shapes=[
            pltpu.VMEM((tokens, width), acts.dtype),
            pltpu.VMEM((tokens, key_width), grads.dtype),
            pltpu.VMEM((sketch + rank, width), acts.dtype),
            pltpu.VMEM((sketch + rank, key_width), grads.dtype),
            pltpu.SMEM(order.shape[1:], order.dtype),
            pltpu.VMEM((2, rank, tokens), jnp.float32),
            pltpu.VMEM((examples * parts, tokens), jnp.float32),
            pltpu.VMEM((examples * parts, LANES), jnp.float32),
            pltpu.SemaphoreType.DMA((2, len(BOUNDS[1]) - 1, 3)),
            pltpu.SemaphoreType.DMA,
        ],
        compiler_params=pltpu.CompilerParams(vmem_limit_bytes=8 * 2**20),
        name="partials",
    )(
        *in_hbm(
            acts,
            grads,
            down_factor,
            up_factor_transposed,
            input_projection,
            gradient_projection,
            order,
        )
    )
    chunks = [exchange(sends[d], 1, d) for d in range(parts - 1, -1, -1)]
    padded = max(span, GROUP * sketch)
    columns, feature_rows, ridge = pl.pallas_call(
        sum_kernel,
        out_shape=[pltpu.VMEM((examples, padded), jnp.float32)] * 2
        + [pltpu.VMEM((PANEL, LANES), jnp.float32)],
        in_specs=[smem()] + [vmem()] * parts,
        out_specs=[vmem()] * 3,
        compiler_params=pltpu.CompilerParams(vmem_limit_bytes=2 * 2**20),
        name="sums",
    )(damping, *in_vmem(*chunks))
    shifts = sorted(range(1, shards // 2), key=lambda d: (-min(d, shards // 2 - d), -d))
    near = [columns] + [shift_chips(columns, d) for d in shifts] + [feature_rows]
    held = pl.pallas_call(
        stack_kernel,
        out_shape=pltpu.VMEM((len(near) * examples, padded), jnp.float32),
        in_specs=[vmem()] * len(near),
        out_specs=vmem(),
        compiler_params=pltpu.CompilerParams(vmem_limit_bytes=2 * 2**20),
        name="stack",
    )(*in_vmem(*near))
    sent = exchange(held, 1)
    return pl.pallas_call(
        functools.partial(factor_kernel, parts),
        out_shape=[
            jax.ShapeDtypeStruct((examples // parts, rank * sketch), jnp.float32),
            jax.ShapeDtypeStruct((per, sketch, sketch), jnp.float32),
        ],
        in_specs=[vmem()] * 3,
        out_specs=[vmem()] * 2,
        compiler_params=pltpu.CompilerParams(vmem_limit_bytes=8 * 2**20),
        name="factors",
    )(*in_vmem(ridge, held, sent))


def solution(mesh):
    in_specs = (
        P("mp", "ex", None),
        P("mp", "ex", None),
        P("mp", None, None),
        P("mp", None, None),
        P("mp", None, None),
        P("mp", None, None),
        P("mp", "ex", None),
        P(),
    )
    out_specs = (P(("ex", "mp"), None), P("mp", None, None))
    return jax.shard_map(
        local, mesh=mesh, in_specs=in_specs, out_specs=out_specs, check_vma=False
    )
```

```python
import functools
import math

import jax
import jax.numpy as jnp
from jax import lax
from jax.experimental import pallas as pl
from jax.experimental.pallas import tpu as pltpu
from jax.sharding import PartitionSpec as P

EXAMPLE_LENGTH = 8
LANES = 128
SLOT = 32
GROUP = LANES // SLOT
PANEL = 8
BOUNDS = ((0, 8), (0, 1, 3, 5, 8))


def dot_nt(a, b):
    return lax.dot_general(
        a, b, (((1,), (1,)), ((), ())), preferred_element_type=jnp.float32
    )


def dot_nn(a, b):
    return jnp.dot(a, b, preferred_element_type=jnp.float32)


def split(x):
    high = x.astype(jnp.bfloat16)
    return high, (x - high.astype(jnp.float32)).astype(jnp.bfloat16)


def partial_kernel(
    parts,
    scaling,
    acts_hbm,
    grads_hbm,
    down_hbm,
    up_hbm,
    proj_in_hbm,
    proj_out_hbm,
    order_hbm,
    *refs,
):
    sends, refs = refs[:parts], refs[parts:]
    acts, grads, weights_in, weights_out, order, low, mask, out, sems, order_sem = refs
    tokens, width = acts.shape
    rank = down_hbm.shape[1]
    sketch = proj_in_hbm.shape[1]
    examples = tokens // EXAMPLE_LENGTH
    per = rank // parts
    halves = sketch // SLOT

    def copies(source, target, sem, here):
        return pltpu.make_async_copy(source.at[0, :, here], target.at[:, here], sem)

    order_copy = pltpu.make_async_copy(order_hbm.at[0], order, order_sem)
    order_copy.start()
    sources = [
        (grads_hbm, grads, proj_out_hbm, up_hbm, weights_out),
        (acts_hbm, acts, proj_in_hbm, down_hbm, weights_in),
    ]
    pending = []
    for (data_hbm, data, first_hbm, second_hbm, weights), bounds in zip(sources, BOUNDS):
        stages = []
        edges = [data.shape[1] * edge // 8 for edge in bounds]
        for start, stop in zip(edges, edges[1:]):
            here = pl.ds(start, stop - start)
            sem = sems.at[len(pending), len(stages)]
            stage = [
                copies(first_hbm, weights.at[pl.ds(0, sketch)], sem.at[0], here),
                copies(second_hbm, weights.at[pl.ds(sketch, rank)], sem.at[1], here),
                copies(data_hbm, data, sem.at[2], here),
            ]
            for copy in stage:
                copy.start()
            stages.append((here, stage))
        pending.append(stages)

    order_copy.wait()
    rows = examples * parts
    source = lax.broadcasted_iota(jnp.int32, (8, tokens), 1) // EXAMPLE_LENGTH
    target = jnp.zeros((8, tokens), jnp.int32)
    for s in range(examples):
        target = jnp.where(source == s, order[0, s], target)
    target = jnp.concatenate([target] * (rows // 8), axis=0)
    place = lax.broadcasted_iota(jnp.int32, (rows, tokens), 0) // parts
    mask[...] = jnp.where(target == place, scaling, 0.0)

    def product(n, data, weights):
        total = None
        for here, stage in pending[n]:
            for copy in stage:
                copy.wait()
            term = dot_nt(weights[:, here], data[:, here])
            total = term if total is None else total + term
        return total

    def spread_low(values, n):
        low[n] = values
        tiles = []
        for c in range(per):
            chosen = low[n, pl.ds(c, parts, stride=per), :]
            chosen = jnp.concatenate([chosen] * max(1, 8 // parts), axis=0)
            chosen = jnp.concatenate([chosen] * (rows // chosen.shape[0]), axis=0)
            tiles.append(split(chosen * mask[...]))
        return [jnp.concatenate(half, axis=0) for half in zip(*tiles)]

    def spread_sketch(values):
        return split(
            jnp.concatenate(
                [values[h * SLOT : (h + 1) * SLOT] for h in range(halves) for _ in range(per)],
                axis=0,
            )
        )

    from_grads = product(0, grads, weights_out)
    left_grads = spread_low(from_grads[sketch:], 0)
    right_grads = spread_sketch(from_grads[:sketch])
    from_acts = product(1, acts, weights_in)
    left_acts = spread_low(from_acts[sketch:], 1)
    right_acts = spread_sketch(from_acts[:sketch])
    left_high, left_low = [
        jnp.concatenate(pair, axis=1) for pair in zip(left_grads, left_acts)
    ]
    right_high, right_low = [
        jnp.concatenate(pair, axis=1) for pair in zip(right_acts, right_grads)
    ]
    both = dot_nt(jnp.concatenate([left_high, left_low], axis=0), right_high)
    size = left_high.shape[0]
    spread = (dot_nt(left_high, right_low) + both[size:]) + both[:size]
    column = lax.broadcasted_iota(jnp.int32, (rows, per * sketch), 1)
    channel = (column // SLOT) % per
    total = spread[:rows]
    for c in range(1, per):
        total = jnp.where(channel == c, spread[c * rows : (c + 1) * rows], total)
    me = lax.axis_index("mp")
    for start in range(0, per * sketch, LANES):
        stop = min(start + LANES, per * sketch)
        out[:, : stop - start] = total[:, start:stop]
        for d in range(parts):
            g = me ^ d
            sends[d][:examples, start:stop] = out[
                pl.ds(pl.multiple_of(g * examples, examples), examples), : stop - start
            ]
            sends[d][examples:, start:stop] = out[pl.ds(g, examples, stride=parts), :][
                :, : stop - start
            ]


def sum_kernel(damping, *refs):
    chunks, (columns, feature_rows, ridge) = refs[:-3], refs[-3:]
    ridge[...] = jnp.full(ridge.shape, damping[0], jnp.float32)
    examples, padded = columns.shape
    total = chunks[0][...]
    for chunk in chunks[1:]:
        total = total + chunk[...]
    width = total.shape[1]
    for ref, value in ((feature_rows, total[:examples]), (columns, total[examples:])):
        ref[:, :width] = value
        if padded > width:
            ref[:, width:] = jnp.zeros((examples, padded - width), jnp.float32)


def stack_kernel(*refs):
    rows = refs[0].shape[0]
    for n, part in enumerate(refs[:-1]):
        refs[-1][n * rows : (n + 1) * rows, :] = part[...]


def write_features(total, parts, per, features):
    rows_here, width = features.shape
    span = width // parts
    halves = span // (per * SLOT)
    natural = jnp.concatenate(
        [
            total[:, (h * per + c) * SLOT : (h * per + c + 1) * SLOT]
            for c in range(per)
            for h in range(halves)
        ],
        axis=1,
    )
    for r in range(rows_here):
        features[r : r + 1, :] = jnp.concatenate(
            [natural[r * parts + g : r * parts + g + 1, :] for g in range(parts)], axis=1
        )


def pick_lanes(x, index):
    return jnp.take_along_axis(x, index, axis=1)


def reciprocal(x):
    guess = pl.reciprocal(x, approx=True)
    return guess * (2.0 - x * guess)


def factor_kernel(parts, ridge, held, sent, features, factors):
    channels, sketch, _ = factors.shape
    examples = features.shape[0] * parts
    gathered = held.shape[0] - examples
    span = features.shape[1] // parts
    write_features(sent[gathered:, :span], parts, channels, features)
    halves = sketch // SLOT
    panels = sketch // PANEL
    per_half = SLOT // PANEL
    stacked = jnp.concatenate([held[:gathered, :], sent[:gathered, :]], axis=0)
    high, rest = split(stacked)
    turned_high, turned_rest = split(jnp.transpose(stacked))
    gram = dot_nn(turned_high, rest) + dot_nn(
        jnp.concatenate([turned_rest, turned_high], axis=1),
        jnp.concatenate([high, high], axis=0),
    )
    lane = lax.broadcasted_iota(jnp.int32, (PANEL, LANES), 1)
    sub = lax.broadcasted_iota(jnp.int32, (PANEL, LANES), 0)
    slot = lane // SLOT
    within = lane % SLOT
    tile = []
    for q in range(panels):
        hr, at = divmod(q, per_half)
        line = []
        for h in range(halves):
            value = None
            for c in range(GROUP):
                start = hr * LANES + c * SLOT + at * PANEL
                block = gram[start : start + PANEL, h * LANES : (h + 1) * LANES]
                value = block if c == 0 else jnp.where(slot == c, block, value)
            value = value * (1.0 / stacked.shape[0])
            if h == hr:
                value = value + jnp.where(within == at * PANEL + sub, ridge[...], 0.0)
            line.append(value)
        tile.append(line)

    zero = jnp.zeros((PANEL, LANES), jnp.float32)
    finished = []
    ahead = [pick_lanes(tile[0][0], slot * SLOT + r) for r in range(PANEL)]
    for q in range(panels):
        hq, at = divmod(q, per_half)
        if q + 1 < panels:
            hn, an = divmod(q + 1, per_half)
            behind = [
                pick_lanes(tile[q + 1][hn], slot * SLOT + an * PANEL + r)
                for r in range(PANEL)
            ]
        column = [
            {
                j: ahead[r]
                if j == q
                else pick_lanes(tile[j][hq], slot * SLOT + at * PANEL + r)
                for j in range(q, panels)
            }
            for r in range(PANEL)
        ]
        block = [
            [
                jnp.broadcast_to(column[r][q][s : s + 1, :], (PANEL, LANES))
                if s >= r
                else None
                for s in range(PANEL)
            ]
            for r in range(PANEL)
        ]
        line = [
            [
                jnp.broadcast_to(tile[q][h][r : r + 1, :], (PANEL, LANES))
                if h >= hq
                else None
                for h in range(halves)
            ]
            for r in range(PANEL)
        ]
        inverse = []

        def eliminate(r, s, inv):
            ratio = block[r][s] * inv
            for t in range(s, PANEL):
                block[s][t] = block[s][t] - ratio * block[r][t]
            for j in range(q + 1, panels):
                column[s][j] = column[s][j] - ratio * column[r][j]
            for h in range(hq, halves):
                line[s][h] = line[s][h] - ratio * line[r][h]

        for r in range(0, PANEL, 2):
            pivot = block[r][r]
            minor = pivot * block[r + 1][r + 1] - block[r][r + 1] * block[r][r + 1]
            inverse.append(reciprocal(pivot))
            inverse.append(pivot * reciprocal(minor))
            eliminate(r, r + 1, inverse[r])
            for s in range(r + 2, PANEL):
                eliminate(r, s, inverse[r])
                eliminate(r + 1, s, inverse[r + 1])
        result = []
        for h in range(halves):
            if h < hq:
                result.append(zero)
                continue
            value = zero
            for r in range(PANEL):
                value = jnp.where(sub == r, line[r][h] * lax.rsqrt(block[r][r]), value)
            if h == hq:
                value = jnp.where(within >= at * PANEL + sub, value, 0.0)
            result.append(value)
        finished.append(result)
        for j in range(q + 1, panels):
            weights = [column[r][j] * inverse[r] for r in range(PANEL)]
            if j == q + 1:
                ahead = behind
                for r in range(PANEL):
                    for s in range(PANEL):
                        factor = jnp.broadcast_to(
                            column[r][j][s : s + 1, :], (PANEL, LANES)
                        )
                        ahead[s] = ahead[s] - weights[r] * factor
            for h in range((q + 1) // per_half, halves):
                value = tile[j][h]
                for r in range(PANEL):
                    value = value - weights[r] * line[r][h]
                tile[j][h] = value

    for q in range(panels):
        for c in range(channels):
            factors[c, q * PANEL : (q + 1) * PANEL, :] = jnp.concatenate(
                [finished[q][h][:, c * SLOT : (c + 1) * SLOT] for h in range(halves)],
                axis=1,
            )


def permute(x, source):
    shards, parts = lax.axis_size("ex"), lax.axis_size("mp")
    pairs = []
    for m in range(shards):
        for b in range(parts):
            sm, sb = source(m, b)
            pairs.append((sm * parts + sb, m * parts + b))
    return lax.ppermute(x, ("ex", "mp"), sorted(pairs))


def exchange(x, ex_distance, mp_distance=0):
    return permute(x, lambda m, b: (m ^ ex_distance, b ^ mp_distance))


def shift_chips(x, distance):
    shards = lax.axis_size("ex")
    return permute(x, lambda m, b: ((m - 2 * distance) % shards ^ 1, b))


def vmem():
    return pl.BlockSpec(memory_space=pltpu.VMEM)


def hbm():
    return pl.BlockSpec(memory_space=pltpu.HBM)


def in_hbm(*arrays):
    return [pltpu.with_memory_space_constraint(x, pltpu.HBM) for x in arrays]


def in_vmem(*arrays):
    return [pltpu.with_memory_space_constraint(x, pltpu.VMEM) for x in arrays]


def smem():
    return pl.BlockSpec(memory_space=pltpu.SMEM)


def local(
    acts,
    grads,
    down_factor,
    up_factor_transposed,
    input_projection,
    gradient_projection,
    order,
    damping,
):
    parts = lax.axis_size("mp")
    shards = lax.axis_size("ex")
    tokens, width = acts.shape[1:]
    key_width = grads.shape[2]
    rank = down_factor.shape[1]
    sketch = input_projection.shape[1]
    examples = tokens // EXAMPLE_LENGTH
    per = rank // parts
    span = per * sketch
    scaling = 1.0 / math.sqrt(2.0 * EXAMPLE_LENGTH * parts)
    sends = pl.pallas_call(
        functools.partial(partial_kernel, parts, scaling),
        out_shape=[pltpu.VMEM((2 * examples, span), jnp.float32)] * parts,
        in_specs=[hbm()] * 7,
        out_specs=[vmem()] * parts,
        scratch_shapes=[
            pltpu.VMEM((tokens, width), acts.dtype),
            pltpu.VMEM((tokens, key_width), grads.dtype),
            pltpu.VMEM((sketch + rank, width), acts.dtype),
            pltpu.VMEM((sketch + rank, key_width), grads.dtype),
            pltpu.SMEM(order.shape[1:], order.dtype),
            pltpu.VMEM((2, rank, tokens), jnp.float32),
            pltpu.VMEM((examples * parts, tokens), jnp.float32),
            pltpu.VMEM((examples * parts, LANES), jnp.float32),
            pltpu.SemaphoreType.DMA((2, len(BOUNDS[1]) - 1, 3)),
            pltpu.SemaphoreType.DMA,
        ],
        compiler_params=pltpu.CompilerParams(vmem_limit_bytes=8 * 2**20),
        name="partials",
    )(
        *in_hbm(
            acts,
            grads,
            down_factor,
            up_factor_transposed,
            input_projection,
            gradient_projection,
            order,
        )
    )
    chunks = [exchange(sends[d], 1, d) for d in range(parts - 1, -1, -1)]
    padded = max(span, GROUP * sketch)
    columns, feature_rows, ridge = pl.pallas_call(
        sum_kernel,
        out_shape=[pltpu.VMEM((examples, padded), jnp.float32)] * 2
        + [pltpu.VMEM((PANEL, LANES), jnp.float32)],
        in_specs=[smem()] + [vmem()] * parts,
        out_specs=[vmem()] * 3,
        compiler_params=pltpu.CompilerParams(vmem_limit_bytes=2 * 2**20),
        name="sums",
    )(damping, *in_vmem(*chunks))
    shifts = sorted(range(1, shards // 2), key=lambda d: (-min(d, shards // 2 - d), -d))
    near = [columns] + [shift_chips(columns, d) for d in shifts] + [feature_rows]
    held = pl.pallas_call(
        stack_kernel,
        out_shape=pltpu.VMEM((len(near) * examples, padded), jnp.float32),
        in_specs=[vmem()] * len(near),
        out_specs=vmem(),
        compiler_params=pltpu.CompilerParams(vmem_limit_bytes=2 * 2**20),
        name="stack",
    )(*in_vmem(*near))
    sent = exchange(held, 1)
    return pl.pallas_call(
        functools.partial(factor_kernel, parts),
        out_shape=[
            jax.ShapeDtypeStruct((examples // parts, rank * sketch), jnp.float32),
            jax.ShapeDtypeStruct((per, sketch, sketch), jnp.float32),
        ],
        in_specs=[vmem()] * 3,
        out_specs=[vmem()] * 2,
        compiler_params=pltpu.CompilerParams(vmem_limit_bytes=8 * 2**20),
        name="factors",
    )(*in_vmem(ridge, held, sent))


def solution(mesh):
    in_specs = (
        P("mp", "ex", None),
        P("mp", "ex", None),
        P("mp", None, None),
        P("mp", None, None),
        P("mp", None, None),
        P("mp", None, None),
        P("mp", "ex", None),
        P(),
    )
    out_specs = (P(("ex", "mp"), None), P("mp", None, None))
    return jax.shard_map(
        local, mesh=mesh, in_specs=in_specs, out_specs=out_specs, check_vma=False
    )
```

```python
import functools
import math

import jax
import jax.numpy as jnp
from jax import lax
from jax.experimental import pallas as pl
from jax.experimental.pallas import tpu as pltpu
from jax.sharding import PartitionSpec as P

EXAMPLE_LENGTH = 8
LANES = 128
SLOT = 32
GROUP = LANES // SLOT
PANEL = 8
CHUNK = 1024


def dot_nt(a, b):
    return lax.dot_general(
        a, b, (((1,), (1,)), ((), ())), preferred_element_type=jnp.float32
    )


def dot_nn(a, b):
    return jnp.dot(a, b, preferred_element_type=jnp.float32)


def split(x):
    high = x.astype(jnp.bfloat16)
    return high, (x - high.astype(jnp.float32)).astype(jnp.bfloat16)


def partial_kernel(
    parts,
    scaling,
    acts_hbm,
    grads_hbm,
    down_hbm,
    up_hbm,
    proj_in_hbm,
    proj_out_hbm,
    order_hbm,
    *refs,
):
    sends, refs = refs[:parts], refs[parts:]
    acts, grads, weights_in, weights_out, order, low, mask, out, sems, order_sem = refs
    tokens, width = acts.shape
    rank = down_hbm.shape[1]
    sketch = proj_in_hbm.shape[1]
    examples = tokens // EXAMPLE_LENGTH
    per = rank // parts
    halves = sketch // SLOT

    def copies(source, target, sem, start, size):
        return pltpu.make_async_copy(
            source.at[0, :, pl.ds(start, size)],
            target.at[:, pl.ds(start, size)],
            sem,
        )

    order_copy = pltpu.make_async_copy(order_hbm.at[0], order, order_sem)
    order_copy.start()
    sources = [
        (grads_hbm, grads, proj_out_hbm, up_hbm, weights_out),
        (acts_hbm, acts, proj_in_hbm, down_hbm, weights_in),
    ]
    pending = []
    for data_hbm, data, first_hbm, second_hbm, weights in sources:
        for start in range(0, data.shape[1], CHUNK):
            n = len(pending)
            pending.append(
                [
                    copies(first_hbm, weights.at[pl.ds(0, sketch)], sems.at[n, 0], start, CHUNK),
                    copies(second_hbm, weights.at[pl.ds(sketch, rank)], sems.at[n, 1], start, CHUNK),
                    copies(data_hbm, data, sems.at[n, 2], start, CHUNK),
                ]
            )
            for copy in pending[-1]:
                copy.start()

    order_copy.wait()
    rows = examples * parts
    source = lax.broadcasted_iota(jnp.int32, (8, tokens), 1) // EXAMPLE_LENGTH
    target = jnp.zeros((8, tokens), jnp.int32)
    for s in range(examples):
        target = jnp.where(source == s, order[0, s], target)
    target = jnp.concatenate([target] * (rows // 8), axis=0)
    place = lax.broadcasted_iota(jnp.int32, (rows, tokens), 0) // parts
    mask[...] = jnp.where(target == place, scaling, 0.0)

    def product(first, data, weights):
        total = None
        for n in range(data.shape[1] // CHUNK):
            for copy in pending[first + n]:
                copy.wait()
            here = pl.ds(n * CHUNK, CHUNK)
            term = dot_nt(weights[:, here], data[:, here])
            total = term if total is None else total + term
        return total

    def spread_low(values, n):
        low[n] = values
        tiles = []
        for c in range(per):
            chosen = low[n, pl.ds(c, parts, stride=per), :]
            chosen = jnp.concatenate([chosen] * max(1, 8 // parts), axis=0)
            chosen = jnp.concatenate([chosen] * (rows // chosen.shape[0]), axis=0)
            tiles.append(split(chosen * mask[...]))
        return [jnp.concatenate(half, axis=0) for half in zip(*tiles)]

    def spread_sketch(values):
        return split(
            jnp.concatenate(
                [values[h * SLOT : (h + 1) * SLOT] for h in range(halves) for _ in range(per)],
                axis=0,
            )
        )

    from_grads = product(0, grads, weights_out)
    left_grads = spread_low(from_grads[sketch:], 0)
    right_grads = spread_sketch(from_grads[:sketch])
    from_acts = product(grads.shape[1] // CHUNK, acts, weights_in)
    left_acts = spread_low(from_acts[sketch:], 1)
    right_acts = spread_sketch(from_acts[:sketch])
    left_high, left_low = [
        jnp.concatenate(pair, axis=1) for pair in zip(left_grads, left_acts)
    ]
    right_high, right_low = [
        jnp.concatenate(pair, axis=1) for pair in zip(right_acts, right_grads)
    ]
    both = dot_nt(jnp.concatenate([left_high, left_low], axis=0), right_high)
    size = left_high.shape[0]
    spread = (dot_nt(left_high, right_low) + both[size:]) + both[:size]
    column = lax.broadcasted_iota(jnp.int32, (rows, per * sketch), 1)
    channel = (column // SLOT) % per
    total = spread[:rows]
    for c in range(1, per):
        total = jnp.where(channel == c, spread[c * rows : (c + 1) * rows], total)
    me = lax.axis_index("mp")
    for start in range(0, per * sketch, LANES):
        stop = min(start + LANES, per * sketch)
        out[:, : stop - start] = total[:, start:stop]
        for d in range(parts):
            g = me ^ d
            sends[d][:examples, start:stop] = out[
                pl.ds(pl.multiple_of(g * examples, examples), examples), : stop - start
            ]
            sends[d][examples:, start:stop] = out[pl.ds(g, examples, stride=parts), :][
                :, : stop - start
            ]


def sum_kernel(damping, *refs):
    chunks, (columns, feature_rows, ridge) = refs[:-3], refs[-3:]
    ridge[...] = jnp.full(ridge.shape, damping[0], jnp.float32)
    examples, padded = columns.shape
    total = chunks[0][...]
    for chunk in chunks[1:]:
        total = total + chunk[...]
    width = total.shape[1]
    for ref, value in ((feature_rows, total[:examples]), (columns, total[examples:])):
        ref[:, :width] = value
        if padded > width:
            ref[:, width:] = jnp.zeros((examples, padded - width), jnp.float32)


def stack_kernel(*refs):
    rows = refs[0].shape[0]
    for n, part in enumerate(refs[:-1]):
        refs[-1][n * rows : (n + 1) * rows, :] = part[...]


def write_features(total, parts, per, features):
    rows_here, width = features.shape
    span = width // parts
    halves = span // (per * SLOT)
    natural = jnp.concatenate(
        [
            total[:, (h * per + c) * SLOT : (h * per + c + 1) * SLOT]
            for c in range(per)
            for h in range(halves)
        ],
        axis=1,
    )
    for r in range(rows_here):
        features[r : r + 1, :] = jnp.concatenate(
            [natural[r * parts + g : r * parts + g + 1, :] for g in range(parts)], axis=1
        )


def pick_lanes(x, index):
    return jnp.take_along_axis(x, index, axis=1)


def reciprocal(x):
    guess = pl.reciprocal(x, approx=True)
    return guess * (2.0 - x * guess)


def factor_kernel(parts, ridge, held, sent, features, factors):
    channels, sketch, _ = factors.shape
    examples = features.shape[0] * parts
    gathered = held.shape[0] - examples
    span = features.shape[1] // parts
    write_features(sent[gathered:, :span], parts, channels, features)
    halves = sketch // SLOT
    panels = sketch // PANEL
    per_half = SLOT // PANEL
    stacked = jnp.concatenate([held[:gathered, :], sent[:gathered, :]], axis=0)
    high, rest = split(stacked)
    turned_high, turned_rest = split(jnp.transpose(stacked))
    gram = dot_nn(turned_high, rest) + dot_nn(
        jnp.concatenate([turned_rest, turned_high], axis=1),
        jnp.concatenate([high, high], axis=0),
    )
    lane = lax.broadcasted_iota(jnp.int32, (PANEL, LANES), 1)
    sub = lax.broadcasted_iota(jnp.int32, (PANEL, LANES), 0)
    slot = lane // SLOT
    within = lane % SLOT
    tile = []
    for q in range(panels):
        hr, at = divmod(q, per_half)
        line = []
        for h in range(halves):
            value = None
            for c in range(GROUP):
                start = hr * LANES + c * SLOT + at * PANEL
                block = gram[start : start + PANEL, h * LANES : (h + 1) * LANES]
                value = block if c == 0 else jnp.where(slot == c, block, value)
            value = value * (1.0 / stacked.shape[0])
            if h == hr:
                value = value + jnp.where(within == at * PANEL + sub, ridge[...], 0.0)
            line.append(value)
        tile.append(line)

    zero = jnp.zeros((PANEL, LANES), jnp.float32)
    finished = []
    ahead = [pick_lanes(tile[0][0], slot * SLOT + r) for r in range(PANEL)]
    for q in range(panels):
        hq, at = divmod(q, per_half)
        if q + 1 < panels:
            hn, an = divmod(q + 1, per_half)
            behind = [
                pick_lanes(tile[q + 1][hn], slot * SLOT + an * PANEL + r)
                for r in range(PANEL)
            ]
        column = [
            {
                j: ahead[r]
                if j == q
                else pick_lanes(tile[j][hq], slot * SLOT + at * PANEL + r)
                for j in range(q, panels)
            }
            for r in range(PANEL)
        ]
        block = [
            [
                jnp.broadcast_to(column[r][q][s : s + 1, :], (PANEL, LANES))
                if s >= r
                else None
                for s in range(PANEL)
            ]
            for r in range(PANEL)
        ]
        line = [
            [
                jnp.broadcast_to(tile[q][h][r : r + 1, :], (PANEL, LANES))
                if h >= hq
                else None
                for h in range(halves)
            ]
            for r in range(PANEL)
        ]
        inverse = []

        def eliminate(r, s, inv):
            ratio = block[r][s] * inv
            for t in range(s, PANEL):
                block[s][t] = block[s][t] - ratio * block[r][t]
            for j in range(q + 1, panels):
                column[s][j] = column[s][j] - ratio * column[r][j]
            for h in range(hq, halves):
                line[s][h] = line[s][h] - ratio * line[r][h]

        for r in range(0, PANEL, 2):
            pivot = block[r][r]
            minor = pivot * block[r + 1][r + 1] - block[r][r + 1] * block[r][r + 1]
            inverse.append(reciprocal(pivot))
            inverse.append(pivot * reciprocal(minor))
            eliminate(r, r + 1, inverse[r])
            for s in range(r + 2, PANEL):
                eliminate(r, s, inverse[r])
                eliminate(r + 1, s, inverse[r + 1])
        result = []
        for h in range(halves):
            if h < hq:
                result.append(zero)
                continue
            value = zero
            for r in range(PANEL):
                value = jnp.where(sub == r, line[r][h] * lax.rsqrt(block[r][r]), value)
            if h == hq:
                value = jnp.where(within >= at * PANEL + sub, value, 0.0)
            result.append(value)
        finished.append(result)
        for j in range(q + 1, panels):
            weights = [column[r][j] * inverse[r] for r in range(PANEL)]
            if j == q + 1:
                ahead = behind
                for r in range(PANEL):
                    for s in range(PANEL):
                        factor = jnp.broadcast_to(
                            column[r][j][s : s + 1, :], (PANEL, LANES)
                        )
                        ahead[s] = ahead[s] - weights[r] * factor
            for h in range((q + 1) // per_half, halves):
                value = tile[j][h]
                for r in range(PANEL):
                    value = value - weights[r] * line[r][h]
                tile[j][h] = value

    for q in range(panels):
        for c in range(channels):
            factors[c, q * PANEL : (q + 1) * PANEL, :] = jnp.concatenate(
                [finished[q][h][:, c * SLOT : (c + 1) * SLOT] for h in range(halves)],
                axis=1,
            )


def permute(x, source):
    shards, parts = lax.axis_size("ex"), lax.axis_size("mp")
    pairs = []
    for m in range(shards):
        for b in range(parts):
            sm, sb = source(m, b)
            pairs.append((sm * parts + sb, m * parts + b))
    return lax.ppermute(x, ("ex", "mp"), sorted(pairs))


def exchange(x, ex_distance, mp_distance=0):
    return permute(x, lambda m, b: (m ^ ex_distance, b ^ mp_distance))


def shift_chips(x, distance):
    shards = lax.axis_size("ex")
    return permute(x, lambda m, b: ((m - 2 * distance) % shards ^ 1, b))


def vmem():
    return pl.BlockSpec(memory_space=pltpu.VMEM)


def hbm():
    return pl.BlockSpec(memory_space=pltpu.HBM)


def in_hbm(*arrays):
    return [pltpu.with_memory_space_constraint(x, pltpu.HBM) for x in arrays]


def in_vmem(*arrays):
    return [pltpu.with_memory_space_constraint(x, pltpu.VMEM) for x in arrays]


def smem():
    return pl.BlockSpec(memory_space=pltpu.SMEM)


def local(
    acts,
    grads,
    down_factor,
    up_factor_transposed,
    input_projection,
    gradient_projection,
    order,
    damping,
):
    parts = lax.axis_size("mp")
    shards = lax.axis_size("ex")
    tokens, width = acts.shape[1:]
    key_width = grads.shape[2]
    rank = down_factor.shape[1]
    sketch = input_projection.shape[1]
    examples = tokens // EXAMPLE_LENGTH
    per = rank // parts
    span = per * sketch
    scaling = 1.0 / math.sqrt(2.0 * EXAMPLE_LENGTH * parts)
    sends = pl.pallas_call(
        functools.partial(partial_kernel, parts, scaling),
        out_shape=[pltpu.VMEM((2 * examples, span), jnp.float32)] * parts,
        in_specs=[hbm()] * 7,
        out_specs=[vmem()] * parts,
        scratch_shapes=[
            pltpu.VMEM((tokens, width), acts.dtype),
            pltpu.VMEM((tokens, key_width), grads.dtype),
            pltpu.VMEM((sketch + rank, width), acts.dtype),
            pltpu.VMEM((sketch + rank, key_width), grads.dtype),
            pltpu.SMEM(order.shape[1:], order.dtype),
            pltpu.VMEM((2, rank, tokens), jnp.float32),
            pltpu.VMEM((examples * parts, tokens), jnp.float32),
            pltpu.VMEM((examples * parts, LANES), jnp.float32),
            pltpu.SemaphoreType.DMA(((width + key_width) // CHUNK, 3)),
            pltpu.SemaphoreType.DMA,
        ],
        compiler_params=pltpu.CompilerParams(vmem_limit_bytes=8 * 2**20),
        name="partials",
    )(
        *in_hbm(
            acts,
            grads,
            down_factor,
            up_factor_transposed,
            input_projection,
            gradient_projection,
            order,
        )
    )
    chunks = [exchange(sends[d], 1, d) for d in range(parts - 1, -1, -1)]
    padded = max(span, GROUP * sketch)
    columns, feature_rows, ridge = pl.pallas_call(
        sum_kernel,
        out_shape=[pltpu.VMEM((examples, padded), jnp.float32)] * 2
        + [pltpu.VMEM((PANEL, LANES), jnp.float32)],
        in_specs=[smem()] + [vmem()] * parts,
        out_specs=[vmem()] * 3,
        compiler_params=pltpu.CompilerParams(vmem_limit_bytes=2 * 2**20),
        name="sums",
    )(damping, *in_vmem(*chunks))
    shifts = sorted(range(1, shards // 2), key=lambda d: (-min(d, shards // 2 - d), d))
    near = [columns] + [shift_chips(columns, d) for d in shifts] + [feature_rows]
    held = pl.pallas_call(
        stack_kernel,
        out_shape=pltpu.VMEM((len(near) * examples, padded), jnp.float32),
        in_specs=[vmem()] * len(near),
        out_specs=vmem(),
        compiler_params=pltpu.CompilerParams(vmem_limit_bytes=2 * 2**20),
        name="stack",
    )(*in_vmem(*near))
    sent = exchange(held, 1)
    return pl.pallas_call(
        functools.partial(factor_kernel, parts),
        out_shape=[
            jax.ShapeDtypeStruct((examples // parts, rank * sketch), jnp.float32),
            jax.ShapeDtypeStruct((per, sketch, sketch), jnp.float32),
        ],
        in_specs=[vmem()] * 3,
        out_specs=[vmem()] * 2,
        compiler_params=pltpu.CompilerParams(vmem_limit_bytes=8 * 2**20),
        name="factors",
    )(*in_vmem(ridge, held, sent))


def solution(mesh):
    in_specs = (
        P("mp", "ex", None),
        P("mp", "ex", None),
        P("mp", None, None),
        P("mp", None, None),
        P("mp", None, None),
        P("mp", None, None),
        P("mp", "ex", None),
        P(),
    )
    out_specs = (P(("ex", "mp"), None), P("mp", None, None))
    return jax.shard_map(
        local, mesh=mesh, in_specs=in_specs, out_specs=out_specs, check_vma=False
    )
```
